32 devices in a mesh: dp: 8 (over z, x), mp: 4 (over y, core).
Axes of the slice: x: 2, y: 2, z: 4, core: 2. Of those that a mesh axis runs over, the one named last changes fastest.
Arguments:
- tokens: bfloat16 [16384, 768], P('dp')
- latents: bfloat16 [512, 768], P('dp'), may hold values from -6 to 6
- image_of_group: int32 [64], replicated, may hold values from 0 to 4, as said below
- token_valid: int32 [16384], P('dp'), may hold values from 0 to 1, as said below
- norm1_gain: float32 [768], replicated, may hold values from 0.5 to 1.5
- norm1_shift: float32 [768], replicated, may hold values from -2 to 2
- w_qkv: bfloat16 [3, 768, 768], P(None, None, 'mp'), may hold values from -0.21875 to 0.21875
- b_qv: float32 [2, 768], P(None, 'mp'), may hold values from -2 to 2
- w_out: bfloat16 [768, 768], P('mp'), may hold values from -0.875 to 0.875
- b_out: float32 [768], replicated, may hold values from -2 to 2
- norm2_gain: float32 [768], replicated, may hold values from 0.5 to 1.5
- norm2_shift: float32 [768], replicated, may hold values from -2 to 2
- w_up: bfloat16 [768, 3072], P(None, 'mp'), may hold values from -0.21875 to 0.21875
- b_up: float32 [3072], P('mp'), may hold values from -3 to 3
- w_down: bfloat16 [3072, 768], P('mp'), may hold values from -0.21875 to 0.21875
- b_down: float32 [768], replicated, may hold values from -2 to 2
- cot_tokens: bfloat16 [16384, 768], P('dp'), may hold values from -6 to 6
- cot_latents: bfloat16 [512, 768], P('dp'), may hold values from -6 to 6
Outputs:
- out_tokens: bfloat16 [16384, 768], P('dp')
- out_latents: bfloat16 [512, 768], P('dp')
- grad_tokens: bfloat16 [16384, 768], P('dp')
- grad_latents: bfloat16 [512, 768], P('dp')
- grad_norm1_gain: float32 [768], replicated
- grad_norm1_shift: float32 [768], replicated
- grad_w_qkv: float32 [3, 768, 768], P(None, None, 'mp')
- grad_b_qv: float32 [2, 768], P(None, 'mp')
- grad_w_out: float32 [768, 768], P('mp')
- grad_b_out: float32 [768], replicated
- grad_norm2_gain: float32 [768], replicated
- grad_norm2_shift: float32 [768], replicated
- grad_w_up: float32 [768, 3072], P(None, 'mp')
- grad_b_up: float32 [3072], P('mp')
- grad_w_down: float32 [3072, 768], P('mp')
- grad_b_down: float32 [768], replicated
- root_means: float32 [3], replicated
The draws below stay inside these ranges and needn't reach their ends.
Inputs may be any that keep to these rules, and one draw needn't show every extreme that they name: Each image's groups are the groups g with image_of_group[g] equal to it; every image has at least one group. `token_valid`: within a group the real tokens are a prefix; every group of an image is full except the image's highest-numbered group, which holds 1 to 256 real tokens.
All inputs are finite; a program needn't handle non-finite values.
Results may differ from the reference program's by a relative error of at most 0.018.
Values may be sent and summed in bfloat16 or wider, within the bound.
No kernel may reach another device: no remote copies, remote signals or barrier semaphores. Data moves between devices by JAX's collectives and lax.ppermute only.
A program may use at most 256 MiB of HBM per device.

```python
import jax
import jax.numpy as jnp
from jax import lax

D = 768
HEADS = 12
HEAD = 64
FF = 3072
GROUP = 256
LAT = 8
GROUPS_DEV = 8
GROUPS = 64
TOKENS = 16384
LATENTS = 512
IMAGES = 5


def group_layout(key):
    key_cut = jax.random.fold_in(key, 101)
    key_fill = jax.random.fold_in(key, 102)
    device_count = GROUPS // GROUPS_DEV
    spare_slots = GROUPS - device_count
    other_images = IMAGES - 1
    shuffled = jax.random.permutation(key_cut, spare_slots - 1) + 1
    cut_flags = jnp.zeros((spare_slots,), jnp.int32).at[shuffled[:other_images - 1]].set(1)
    slot_image = 1 + jnp.cumsum(cut_flags).astype(jnp.int32)
    slot_index = jnp.arange(spare_slots, dtype=jnp.int32)
    slot_group = slot_index // (GROUPS_DEV - 1) * GROUPS_DEV + 1 + slot_index % (GROUPS_DEV - 1)
    owner = jnp.zeros((GROUPS,), jnp.int32).at[slot_group].set(slot_image)
    group_index = jnp.arange(GROUPS, dtype=jnp.int32)
    later_same = (group_index[None, :] > group_index[:, None]) & (owner[None, :] == owner[:, None])
    is_last = jnp.logical_not(jnp.any(later_same, axis=1))
    partial_fill = jax.random.randint(key_fill, (GROUPS,), 1, GROUP + 1)
    fill_count = jnp.where(is_last, partial_fill, GROUP)
    valid_flags = (jnp.arange(GROUP, dtype=jnp.int32)[None, :] < fill_count[:, None]).astype(jnp.int32).reshape(-1)
    return (owner, valid_flags)


def draw_image_of_group(key, part):
    owner, valid_flags = group_layout(key)
    return owner


def draw_token_valid(key, part):
    owner, valid_flags = group_layout(key)
    return valid_flags


def draw_tokens(key, part):
    key = jax.random.fold_in(key, 7)
    key_row = jax.random.fold_in(key, 1)
    key_value = jax.random.fold_in(key, 2)
    rising = 1.0 + 2.0 * jnp.arange(TOKENS, dtype=jnp.float32) / (TOKENS - 1)
    jitter = jnp.exp(jax.random.uniform(key_row, (TOKENS, 1), jnp.float32, -0.3, 0.3))
    base = jax.random.normal(key_value, (TOKENS, D), jnp.float32)
    return (base * rising[:, None] * jitter).astype(jnp.bfloat16)


def level_of(stream_key, dims, shards, low, high):
    def one(position, blocks):
        draws = jax.random.uniform(jax.random.fold_in(jax.random.fold_in(stream_key, 6), position), (blocks,), jnp.float32, low / len(shards), high / len(shards))
        return jnp.repeat(jnp.exp(draws), dims[position] // blocks).reshape((-1,) + (1,) * (len(dims) - position - 1))

    factor_of = one(*shards[0])
    for cut in shards[1:]:
        factor_of = factor_of * one(*cut)
    return factor_of


def noise(key, extent, deviation, bound, shards=(), held_as=jnp.bfloat16):
    level = level_of(key, extent, shards, -0.22, 0.18) if shards else 1.0
    entries = jax.random.normal(key, extent, jnp.float32) * deviation * level
    return jnp.minimum(jnp.maximum(entries, -bound), bound).astype(held_as)


def setup_inputs(seed: int = 0) -> dict:
    arg_keys = jax.random.split(jax.random.key(seed), 19)
    tokens = draw_tokens(jax.random.fold_in(arg_keys[18], 71), 0)
    latents = noise(arg_keys[1], (LATENTS, D), 1.0, 6.0, ((0, 8),))
    image_of_group = draw_image_of_group(jax.random.fold_in(arg_keys[18], 71), 0)
    token_valid = draw_token_valid(jax.random.fold_in(arg_keys[18], 71), 0)
    norm1_gain = jnp.clip(1.0 + 0.1 * jax.random.normal(arg_keys[4], (D,), jnp.float32), 0.5, 1.5)
    norm1_shift = noise(arg_keys[5], (D,), 0.3, 2.0, (), jnp.float32)
    w_qkv = noise(arg_keys[6], (3, D, D), D ** -0.5, 0.21875, ((2, 4),))
    b_qv = noise(arg_keys[7], (2, D), 0.3, 2.0, ((1, 4),), jnp.float32)
    w_out = noise(arg_keys[8], (D, D), (D // 16) ** -0.5, 0.875, ((0, 4),))
    b_out = noise(arg_keys[9], (D,), 0.3, 2.0, (), jnp.float32)
    norm2_gain = jnp.clip(1.0 + 0.1 * jax.random.normal(arg_keys[10], (D,), jnp.float32), 0.5, 1.5)
    norm2_shift = noise(arg_keys[11], (D,), 0.3, 2.0, (), jnp.float32)
    w_up = noise(arg_keys[12], (D, FF), D ** -0.5, 0.21875, ((1, 4),))
    b_up = noise(arg_keys[13], (FF,), 0.5, 3.0, ((0, 4),), jnp.float32)
    w_down = noise(arg_keys[14], (FF, D), (FF // 4) ** -0.5, 0.21875, ((0, 4),))
    b_down = noise(arg_keys[15], (D,), 0.3, 2.0, (), jnp.float32)
    cot_tokens = noise(arg_keys[16], (TOKENS, D), 1.0, 6.0, ((0, 8),))
    cot_latents = noise(arg_keys[17], (LATENTS, D), 1.0, 6.0, ((0, 8),))
    return {"tokens": tokens, "latents": latents, "image_of_group": image_of_group, "token_valid": token_valid, "norm1_gain": norm1_gain, "norm1_shift": norm1_shift, "w_qkv": w_qkv, "b_qv": b_qv, "w_out": w_out, "b_out": b_out, "norm2_gain": norm2_gain, "norm2_shift": norm2_shift, "w_up": w_up, "b_up": b_up, "w_down": w_down, "b_down": b_down, "cot_tokens": cot_tokens, "cot_latents": cot_latents}


@jax.custom_vjp
def low(v):
    return lax.optimization_barrier(v.astype(jnp.bfloat16)).astype(jnp.float32)

@jax.custom_vjp
def low_back(v):
    return v

def low_keep(v):
    return (low(v), None)

def low_pass(kept, grad):
    return (grad,)

def back_keep(v):
    return (v, None)

def back_low(kept, grad):
    return (low(grad),)
low.defvjp(low_keep, low_pass)
low_back.defvjp(back_keep, back_low)

def layer_norm(values, gain, shift):
    center = values - lax.optimization_barrier(jnp.mean(values, axis=-1, keepdims=True))
    spread = lax.optimization_barrier(jnp.mean(center * center, axis=-1, keepdims=True))
    return center * lax.rsqrt(spread + 1e-06) * gain + shift

def gelu_tanh(values):
    return 0.5 * values * (1.0 + jnp.tanh(0.7978845608028654 * (values + 0.044715 * values * values * values)))

def mix_heads(queries, key_rows, value_rows, allowed):
    scores = low_back(jnp.einsum('qhe,khe->hqk', queries, key_rows, precision=lax.Precision.HIGHEST) * 0.125)
    scores = jnp.where(allowed[None, None, :], scores, -1e+30)
    row_top = lax.optimization_barrier(jnp.max(scores, axis=-1, keepdims=True))
    expo_terms = jnp.exp(scores - row_top)
    weights = expo_terms / lax.optimization_barrier(jnp.sum(expo_terms, axis=-1, keepdims=True))
    return jnp.einsum('hqk,khe->qhe', low(weights), value_rows, precision=lax.Precision.HIGHEST)

def forward(tokens, latents, norm1_gain, norm1_shift, w_qkv, b_qv, w_out, b_out, norm2_gain, norm2_shift, w_up, b_up, w_down, b_down, token_valid, image_of_group):
    highest = lax.Precision.HIGHEST
    tok_total = GROUPS * GROUP
    stream = jnp.concatenate([tokens, latents], 0)
    normed = low(layer_norm(stream, norm1_gain, norm1_shift))
    project = jnp.einsum('rd,tde->tre', normed, w_qkv, precision=highest)
    queries = low(low_back(project[0] + b_qv[0]))
    key_rows = low(low_back(project[1]))
    value_rows = low(low_back(project[2] + b_qv[1]))

    def split_heads(values):
        return (values[:tok_total].reshape(GROUPS, GROUP, HEADS, HEAD), values[tok_total:].reshape(GROUPS, LAT, HEADS, HEAD))
    query_tok, query_lat = split_heads(queries)
    key_tok, key_lat = split_heads(key_rows)
    value_tok, value_lat = split_heads(value_rows)
    every_keys = key_lat.reshape(LATENTS, HEADS, HEAD)
    every_values = value_lat.reshape(LATENTS, HEADS, HEAD)
    every_image = jnp.repeat(image_of_group, LAT)
    valid_bool = token_valid.reshape(GROUPS, GROUP) > 0

    def one_group(pieces):
        q_tok, k_tok, v_tok, q_lat, k_lat, v_lat, real_rows, image_here = pieces
        near = mix_heads(q_tok, jnp.concatenate([k_tok, k_lat], 0), jnp.concatenate([v_tok, v_lat], 0), jnp.concatenate([real_rows, jnp.ones((LAT,), jnp.bool_)], 0))
        far = mix_heads(q_lat, jnp.concatenate([k_tok, every_keys], 0), jnp.concatenate([v_tok, every_values], 0), jnp.concatenate([real_rows, every_image == image_here], 0))
        return (near, far)
    near_rows, far_rows = lax.map(jax.checkpoint(one_group), (query_tok, key_tok, value_tok, query_lat, key_lat, value_lat, valid_bool, image_of_group))
    mixed_rows = low(low_back(jnp.concatenate([near_rows.reshape(tok_total, D), far_rows.reshape(LATENTS, D)], 0)))
    attn_branch = low_back(jnp.dot(mixed_rows, w_out, precision=highest) + b_out)
    residual = stream + attn_branch
    normed_two = low(layer_norm(residual, norm2_gain, norm2_shift))
    up_pre = low_back(jnp.dot(normed_two, w_up, precision=highest) + b_up)
    activated = low(gelu_tanh(up_pre))
    mlp_branch = low_back(jnp.dot(activated, w_down, precision=highest) + b_down)
    output = residual + mlp_branch
    return ((output[:tok_total], output[tok_total:]), (output[:tok_total], attn_branch[:tok_total], mlp_branch[:tok_total]))

def reference(tokens, latents, image_of_group, token_valid, norm1_gain, norm1_shift, w_qkv, b_qv, w_out, b_out, norm2_gain, norm2_shift, w_up, b_up, w_down, b_down, cot_tokens, cot_latents):
    params = tuple((w.astype(jnp.float32) for w in (norm1_gain, norm1_shift, w_qkv, b_qv, w_out, b_out, norm2_gain, norm2_shift, w_up, b_up, w_down, b_down)))

    def wrapped(tok_in, lat_in, *weights):
        return forward(tok_in, lat_in, *weights, token_valid, image_of_group)
    outputs, pull, extras = jax.vjp(wrapped, tokens.astype(jnp.float32), latents.astype(jnp.float32), *params, has_aux=True)
    grads = pull((cot_tokens.astype(jnp.float32), cot_latents.astype(jnp.float32)))
    real_flags = token_valid.astype(jnp.float32)
    real_count = jnp.sum(real_flags)
    root_means = jnp.stack([jnp.sqrt(jnp.sum(real_flags * lax.optimization_barrier(jnp.sum(piece * piece, -1))) / (real_count * D)) for piece in extras])
    return (outputs[0].astype(jnp.bfloat16), outputs[1].astype(jnp.bfloat16), grads[0].astype(jnp.bfloat16), grads[1].astype(jnp.bfloat16), grads[2], grads[3], grads[4], grads[5], grads[6], grads[7], grads[8], grads[9], grads[10], grads[11], grads[12], grads[13], root_means)
```

```python
import jax
import jax.numpy as jnp
from jax import lax
from jax.experimental import pallas as pl
from jax.experimental.pallas import tpu as pltpu
from jax.sharding import PartitionSpec as P

HEAD = 64
GROUP = 256
LAT = 8
BF = jnp.bfloat16
F32 = jnp.float32
FAR = -1e30
MIB = 1 << 20


def dot(a, b, ca, cb):
    return lax.dot_general(a, b, (((ca,), (cb,)), ((), ())), preferred_element_type=F32)


def norm_parts(values):
    center = values - jnp.mean(values, axis=-1, keepdims=True)
    spread = jnp.mean(center * center, axis=-1, keepdims=True)
    inverse = lax.rsqrt(spread + 1e-06)
    return center * inverse, inverse


def norm_back(grad, unit, inverse, gain):
    scaled = grad * gain
    inner = jnp.mean(scaled * unit, axis=-1, keepdims=True)
    return inverse * (scaled - jnp.mean(scaled, axis=-1, keepdims=True) - unit * inner)


def gelu_both(values):
    square = values * values
    inner = jnp.tanh(values * (0.7978845608028654 + 0.035677408136300125 * square))
    half = 0.5 + 0.5 * inner
    slope = values * (0.3989422804014327 + 0.05351611220494518 * square)
    return values * half, half + (1.0 - inner * inner) * slope


def split3(v):
    hi = v.astype(BF)
    mid = (v - hi.astype(F32)).astype(BF)
    low = (v - hi.astype(F32) - mid.astype(F32)).astype(BF)
    return hi, mid, low


def head_lanes(v, h):
    lane = lax.broadcasted_iota(jnp.int32, v.shape, v.ndim - 1)
    return jnp.where((lane >= h * HEAD) & (lane < (h + 1) * HEAD), v, jnp.zeros_like(v))


def whole(shape):
    return pl.BlockSpec(shape, lambda *_: (0,) * len(shape), pipeline_mode=pl.Buffered(1))


def kept(shape):
    return pl.BlockSpec(shape, lambda *_: (0,) * len(shape))


def call(body, *, grid, scalars, ins, outs, name, scratch=(), flops=0, moved=0):
    def run(*args):
        return pl.pallas_call(
            body,
            name=name,
            out_shape=[jax.ShapeDtypeStruct(s, d) for s, d, _ in outs],
            grid_spec=pltpu.PrefetchScalarGridSpec(
                num_scalar_prefetch=scalars,
                grid=grid,
                in_specs=ins,
                out_specs=[spec for _, _, spec in outs],
                scratch_shapes=list(scratch),
            ),
            compiler_params=pltpu.CompilerParams(
                dimension_semantics=("arbitrary",) * len(grid), vmem_limit_bytes=56 * MIB
            ),
            cost_estimate=pl.CostEstimate(flops=flops, bytes_accessed=moved, transcendentals=0),
        )(*args)

    return run


def key_stack(tok, lat8):
    pad = jnp.concatenate([lat8, jnp.zeros_like(lat8)], 0).astype(BF)
    return jnp.concatenate([tok, pad], 0)


def near_mask(count, columns):
    row = lax.broadcasted_iota(jnp.int32, (GROUP + 2 * LAT, columns), 0)
    return (row < count) | ((row >= GROUP) & (row < GROUP + LAT))


def forward_near(order, count, tok, lat, gain, shift, w, bias, normed, q, k, v, m0, m1, m2, m3, log, ql, kl, vl):
    step = pl.program_id(0)
    wide = w.shape[1]

    def project(rows):
        unit, _ = norm_parts(rows.astype(F32))
        rows = (unit * gain[...] + shift[...]).astype(BF)
        return (
            rows,
            (dot(rows, w[0], 1, 1) + bias[0:1]).astype(BF),
            dot(rows, w[1], 1, 1).astype(BF),
            (dot(rows, w[2], 1, 1) + bias[1:2]).astype(BF),
        )

    @pl.when(step == 0)
    def _():
        _, a, b, c = project(lat[...])
        ql[...], kl[...], vl[...] = a.astype(F32), b.astype(F32), c.astype(F32)

    rows, qs, ks, vs = project(tok[...])
    normed[...], q[...], k[...], v[...] = rows, qs, ks, vs
    here = pl.ds(pl.multiple_of(step * LAT, LAT), LAT)
    keys = key_stack(ks, kl[here, :])
    values = key_stack(vs, vl[here, :]).T
    mask = near_mask(count[step], GROUP)
    qs = qs * jnp.asarray(0.125, BF)
    logs, outs = [], []
    for h in range(wide // HEAD):
        s = jnp.where(mask, dot(head_lanes(keys, h), qs, 1, 1), FAR)
        top = jnp.max(s, 0, keepdims=True)
        e = jnp.exp(s - top)
        total = jnp.sum(e, 0, keepdims=True)
        logs.append(top + jnp.log(total))
        outs.append(dot(values[h * HEAD : (h + 1) * HEAD], e.astype(BF), 1, 0) * (1.0 / total))
    log[0] = jnp.concatenate(logs + [jnp.zeros((8 - len(logs), GROUP), F32)], 0)
    mixed = jnp.concatenate(outs, 0).T.astype(BF)
    for slot, ref in enumerate((m0, m1, m2, m3)):

        @pl.when(step // 2 == slot)
        def _(ref=ref):
            ref[...] = mixed


def forward_far(count, lat, gain, shift, w, bias, own_im, key_im, k, v, normed, qa, ka, va, m0, m1, m2, m3, far, logs_out):
    step = pl.program_id(0)
    wide = w.shape[1]
    rows_step = lat.shape[0]
    own = normed.shape[0]
    unit, _ = norm_parts(lat[...].astype(F32))
    rows = (unit * gain[...] + shift[...]).astype(BF)
    here = pl.ds(pl.multiple_of(step * rows_step, rows_step), rows_step)
    qa[here, :] = (dot(rows, w[0], 1, 1) + bias[0:1]).astype(BF)
    ka[here, :] = dot(rows, w[1], 1, 1).astype(BF)
    va[here, :] = (dot(rows, w[2], 1, 1) + bias[1:2]).astype(BF)

    @pl.when(step == 0)
    def _():
        normed[...] = rows[:own]

    @pl.when(step == pl.num_programs(0) - 1)
    def _():
        q = qa[0:own, :] * jnp.asarray(0.125, BF)
        q32 = q.astype(F32)
        groups = own // LAT
        mask = own_im[...] == key_im[...]
        lane = lax.broadcasted_iota(jnp.int32, (LAT, GROUP), 1)
        full = jnp.zeros((own, wide), F32)
        logs = []
        for h in range(wide // HEAD):
            qh = head_lanes(q32, h)
            s_lat = jnp.where(mask, dot(qh.astype(BF), ka[...], 1, 1), FAR)
            s_tok = jnp.concatenate(
                [
                    jnp.where(
                        lane < count[g],
                        dot(qh[g * LAT : (g + 1) * LAT].astype(BF), k[g * GROUP : (g + 1) * GROUP, :], 1, 1),
                        FAR,
                    )
                    for g in range(groups)
                ],
                0,
            )
            top = jnp.maximum(jnp.max(s_lat, 1, keepdims=True), jnp.max(s_tok, 1, keepdims=True))
            e_lat, e_tok = jnp.exp(s_lat - top), jnp.exp(s_tok - top)
            total = jnp.sum(e_lat, 1, keepdims=True) + jnp.sum(e_tok, 1, keepdims=True)
            logs.append(top + jnp.log(total))
            near = jnp.concatenate(
                [
                    dot(e_tok[g * LAT : (g + 1) * LAT].astype(BF), v[g * GROUP : (g + 1) * GROUP, :], 1, 0)
                    for g in range(groups)
                ],
                0,
            )
            full = full + head_lanes((dot(e_lat.astype(BF), va[...], 1, 0) + near) * (1.0 / total), h)
        mixed = full.astype(BF)
        for slot, ref in enumerate((m0, m1, m2, m3)):
            n = own // 4
            ref[...] = mixed[slot * n : (slot + 1) * n]
        parts = [split3(x) for x in logs]
        cols = [p[i] for i in range(3) for p in parts]
        lane = lax.broadcasted_iota(jnp.int32, (own, 2 * HEAD), 1)
        extra = jnp.zeros((own, 2 * HEAD), F32)
        for i, c in enumerate(cols):
            extra = jnp.where(lane == i, c.astype(F32), extra)
        far[...] = mixed
        logs_out[...] = extra.astype(BF)


def hidden_part(n2, cot, up_w, down_w, bias, branch, back, act_out, grad_out, bias_out):
    cut = 256
    for at in range(0, up_w.shape[1], cut):
        cols = slice(at, at + cut)
        wu, wd = up_w[:, cols], down_w[cols, :]
        up = dot(n2, wu, 1, 0) + bias[:, cols]
        active, slope = gelu_both(up)
        active = active.astype(BF)
        branch[...] += dot(active, wd, 1, 0)
        grad_up = (dot(cot, wd, 1, 1) * slope).astype(BF)
        back[...] += dot(grad_up, wu, 1, 1)
        act_out[:, cols] = active
        grad_out[:, cols] = grad_up
        bias_out[:, cols] = jnp.sum(grad_up.astype(F32), 0, keepdims=True)


def bias_row(pack, base):
    rows = pack[base : base + 16, :].astype(F32)
    return rows[0:1] + rows[1:2] + rows[2:3]


def valid_rows(count, at, rows):
    row = lax.broadcasted_iota(jnp.int32, (rows, 1), 0)
    first = (row < GROUP) & (row < count[at])
    return first | ((row >= GROUP) & (row < GROUP + count[at + 1]))


def middle_one(
    where, count, t0, t1, t2, t3, l0, l1, l2, l3, o0, o1, o2, o3, tok, lat, cot_tok, cot_lat, b_out, gain, shift,
    up0, down0, up1, down1, residual, n2_out, branch, back, cot, stats, bsum, pack0, pack1, act, grad,
):
    width = tok.shape[1]
    n, m = tok.shape[0], lat.shape[0]
    wide = t0.shape[1]
    attn_tok = dot(t0[...], o0[0:wide, :], 1, 0)
    attn_lat = dot(l0[...], o0[0:wide, :], 1, 0)
    for t, l, o in ((t1, l1, o1), (t2, l2, o2), (t3, l3, o3)):
        attn_tok += dot(t[...], o[0:wide, :], 1, 0)
        attn_lat += dot(l[...], o[0:wide, :], 1, 0)
    attn_tok += b_out[...]
    attn_lat += b_out[...]
    real = valid_rows(count, 0, n)
    stats[...] = jnp.zeros_like(stats)
    stats[0:1, :] = jnp.sum(jnp.where(real, attn_tok * attn_tok, 0.0), 0, keepdims=True)
    residual[0:n, :] = tok[...].astype(F32) + attn_tok
    residual[n : n + m, :] = lat[...].astype(F32) + attn_lat
    unit, _ = norm_parts(residual[...])
    n2_out[...] = (unit * gain[...] + shift[...]).astype(BF)
    cot[0:n, :] = cot_tok[...]
    cot[n : n + m, :] = cot_lat[...]
    branch[...] = jnp.zeros_like(branch)
    back[...] = jnp.zeros_like(back)
    n2, ct = n2_out[...], cot[...]
    n2_t = n2.T
    for i, (up_w, down_w, o, pack) in enumerate(((up0, down0, o0, pack0), (up1, down1, o1, pack1))):
        hidden = up_w.shape[1]
        hidden_part(n2, ct, up_w, down_w, bias_row(o, wide), branch, back, act, grad, bsum.at[i : i + 1])
        pack[0:width, :] = dot(n2_t, grad[...], 1, 0).astype(BF)
        pack[width : width + hidden, :] = dot(act[...], ct, 0, 0).astype(BF)


def middle_two(
    count, residual, n2, cot, branch_in, back_in, o0, o1, o2, o3, p2, p3, b_down, gain,
    out_rows, grad_res, g0, g1, g2, g3, grad_attn, act2, grad2, act3, grad3, stats, bsum, branch, back,
):
    width = residual.shape[1]
    wide = g0.shape[1]
    hidden = p2.shape[0] - width
    branch[...] = branch_in[...]
    back[...] = back_in[...]
    nn, ct = n2[...], cot[...]
    for i, (p, o, act, grad) in enumerate(((p2, o2, act2, grad2), (p3, o3, act3, grad3))):
        up_w, down_w = p.at[0:width], p.at[width : width + hidden]
        hidden_part(nn, ct, up_w, down_w, bias_row(o, wide), branch, back, act, grad, bsum.at[i : i + 1])
    res = residual[...]
    br = branch[...] + b_down[...]
    out = res + br
    out_rows[...] = out.astype(BF)
    tok_rows = 2 * GROUP
    real = valid_rows(count, 0, tok_rows)
    stats[...] = jnp.zeros_like(stats)
    for i, x in enumerate((out, br)):
        x = x[0:tok_rows]
        stats[i : i + 1, :] = jnp.sum(jnp.where(real, x * x, 0.0), 0, keepdims=True)
    unit, inverse = norm_parts(res)
    bk = back[...]
    stats[2:3, :] = jnp.sum(bk * unit, 0, keepdims=True)
    stats[3:4, :] = jnp.sum(bk, 0, keepdims=True)
    cot32 = ct.astype(F32)
    gr = cot32 + norm_back(bk, unit, inverse, gain[...])
    grad_res[...] = gr
    ga = gr.astype(BF)
    grad_attn[...] = ga
    stats[4:5, :] = jnp.sum(ga.astype(F32), 0, keepdims=True)
    stats[5:6, :] = jnp.sum(cot32, 0, keepdims=True)
    for o, g in ((o0, g0), (o1, g1), (o2, g2), (o3, g3)):
        g[...] = dot(ga, o[0:wide, :], 1, 1).astype(BF)


def middle_grads(n2, cot, grad_attn, t0, t1, t2, t3, l0, l1, l2, l3, act2, grad2, act3, grad3, own_out, send_out, pair_out):
    width = n2.shape[1]
    hidden = act2.shape[1]
    wide = t0.shape[1]
    tok_rows = t0.shape[0]
    n2_t = n2[...].T
    ct, ga = cot[...], grad_attn[...]

    def out_grad(t, l):
        return (dot(t[...], ga[0:tok_rows], 0, 0) + dot(l[...], ga[tok_rows:], 0, 0)).astype(BF)

    for act, grad, dst, t, l in ((act3, grad3, send_out, t3, l3), (act2, grad2, pair_out, t2, l2)):
        dst[0:width, :] = dot(n2_t, grad[...], 1, 0).astype(BF)
        dst[width : width + hidden, :] = dot(act[...], ct, 0, 0).astype(BF)
        dst[width + hidden : width + hidden + wide, :] = out_grad(t, l)
    send_out[width + hidden + wide : width + hidden + 2 * wide, :] = out_grad(t1, l1)
    own_out[...] = out_grad(t0, l0)


def backward_near(
    order, count, normed, q, k, v, ql, kl, vl, log, far, logs_far, da, db, la, lb, w,
    part, grad_w, bias, dq_far, dk_near, dv_near,
):
    step = pl.program_id(0)
    wide = q.shape[1]
    heads = wide // HEAD
    first = step < 2
    d_tok = jnp.where(first, da[...], db[...])
    d_lat16 = jnp.where(first, la[...], lb[...]).astype(F32)
    d_lat = jnp.where(step % 2 == 0, d_lat16[0:LAT], d_lat16[LAT : 2 * LAT])
    number = count[step]
    eighth = jnp.asarray(0.125, BF)
    qs, ks, vs = q[...] * eighth, k[...], v[...]
    keys, values = key_stack(ks, kl[...]), key_stack(vs, vl[...])
    keys_t = keys.T
    mask = near_mask(number, GROUP)
    ps, gs, dq_t, d_heads, q_heads = [], [], [], [], []
    for h in range(heads):
        s = dot(head_lanes(keys, h), qs, 1, 1)
        p = jnp.where(mask, jnp.exp(s - log[0, h : h + 1, :]), 0.0)
        gp = p * dot(head_lanes(values, h), d_tok, 1, 1)
        g = (gp - p * jnp.sum(gp, 0, keepdims=True)).astype(BF)
        dq_t.append(dot(keys_t[h * HEAD : (h + 1) * HEAD], g, 1, 0))
        ps.append(p.astype(BF))
        gs.append(g)
        d_heads.append(head_lanes(d_tok, h))
        q_heads.append(head_lanes(qs, h))
    dv = dot(jnp.concatenate(ps, 1), jnp.concatenate(d_heads, 0), 1, 0)
    dk = dot(jnp.concatenate(gs, 1), jnp.concatenate(q_heads, 0), 1, 0)
    dq = (jnp.concatenate(dq_t, 0).T * 0.125).astype(BF)
    pad = jnp.zeros((LAT, wide), F32)
    q8, o8 = ql[...] * 0.125, far[...].astype(F32)[0 : 2 * LAT]
    o8 = jnp.where(step % 2 == 0, o8[0:LAT], o8[LAT : 2 * LAT])
    lg = logs_far[...].astype(F32)
    lg = jnp.where(step % 2 == 0, lg[0:LAT], lg[LAT : 2 * LAT])
    q_rows, d_rows, log_col, del_col = [], [], [], []
    big = jnp.full((LAT, 1), 1e30, F32)
    zero = jnp.zeros((LAT, 1), F32)
    for h in range(heads):
        q_rows += [head_lanes(q8, h), pad]
        dh = head_lanes(d_lat, h)
        d_rows += [dh, pad]
        log_col += [lg[:, h : h + 1] + lg[:, heads + h : heads + h + 1] + lg[:, 2 * heads + h : 2 * heads + h + 1], big]
        del_col += [jnp.sum(dh * o8, 1, keepdims=True), zero]
    q_f, d_f = jnp.concatenate(q_rows, 0).astype(BF), jnp.concatenate(d_rows, 0).astype(BF)
    l_f, x_f = jnp.concatenate(log_col, 0), jnp.concatenate(del_col, 0)
    lane = lax.broadcasted_iota(jnp.int32, (2 * LAT * heads, GROUP), 1)
    p_f = jnp.where(lane < number, jnp.exp(dot(q_f, ks, 1, 1) - l_f), 0.0)
    g_f = (p_f * (dot(d_f, vs, 1, 1) - x_f)).astype(BF)
    dk_tok = (dk[0:GROUP] + dot(g_f, q_f, 0, 0)).astype(BF)
    dv_tok = (dv[0:GROUP] + dot(p_f.astype(BF), d_f, 0, 0)).astype(BF)
    dk_near[...] = dk[GROUP : GROUP + LAT]
    dv_near[...] = dv[GROUP : GROUP + LAT]
    dq_all = dot(g_f, ks, 1, 0)
    dq_lat = jnp.zeros((LAT, wide), F32)
    for h in range(heads):
        dq_lat += head_lanes(dq_all[2 * LAT * h : 2 * LAT * h + LAT], h)
    dq_far[...] = dq_lat
    rows = normed[...]

    @pl.when(step == 0)
    def _():
        grad_w[...] = jnp.zeros_like(grad_w)
        bias[...] = jnp.zeros_like(bias)

    total = dot(dq, w[0], 1, 0) + dot(dk_tok, w[1], 1, 0) + dot(dv_tok, w[2], 1, 0)
    part[...] = total.astype(BF)
    for i, g in enumerate((dq, dk_tok, dv_tok)):
        grad_w[i] += dot(g, rows, 0, 0)
    bias[0:1, :] += jnp.sum(dq.astype(F32), 0, keepdims=True)
    bias[1:2, :] += jnp.sum(dv_tok.astype(F32), 0, keepdims=True)


def backward_far(
    own_im, key_im, own_im_row, key_im_col, qa, ka, va, bundle, normed, dq_a, dq_b, dk_a, dk_b, dv_a, dv_b,
    w, gw_a, gw_b, bias_a, bias_b, part, grad_w, bias,
):
    own = normed.shape[0]
    wide = qa.shape[1]
    heads = wide // HEAD
    eighth = jnp.asarray(0.125, BF)
    q_all, k_all, v_all = qa[...] * eighth, ka[...], va[...]
    part_wide = 4 * HEAD
    d_all, o_all = bundle[:, 0:wide], bundle[:, part_wide : part_wide + wide]
    extra = bundle[:, 2 * part_wide : 2 * part_wide + 2 * HEAD].astype(F32)
    prod = d_all.astype(F32) * o_all.astype(F32)
    q_own, k_own, v_own, d_own = q_all[0:own], k_all[0:own], v_all[0:own], d_all[0:own]
    mask_q = own_im[...] == key_im[...]
    mask_k = key_im_col[...] == own_im_row[...]
    dq = jnp.concatenate([dq_a[...], dq_b[...]], 0)
    dk = jnp.concatenate([dk_a[...], dk_b[...]], 0)
    dv = jnp.concatenate([dv_a[...], dv_b[...]], 0)
    for h in range(heads):
        log = extra[:, h : h + 1] + extra[:, heads + h : heads + h + 1] + extra[:, 2 * heads + h : 2 * heads + h + 1]
        delta = jnp.sum(head_lanes(prod, h), 1, keepdims=True)
        s = dot(head_lanes(q_own, h), k_all, 1, 1)
        p = jnp.where(mask_q, jnp.exp(s - log[0:own]), 0.0)
        g = (p * (dot(head_lanes(d_own, h), v_all, 1, 1) - delta[0:own])).astype(BF)
        dq += head_lanes(dot(g, k_all, 1, 0), h)
        s = dot(q_all, head_lanes(k_own, h), 1, 1)
        p = jnp.where(mask_k, jnp.exp(s - log), 0.0)
        g = (p * (dot(d_all, head_lanes(v_own, h), 1, 1) - delta)).astype(BF)
        dk += head_lanes(dot(g, q_all, 0, 0), h)
        dv += head_lanes(dot(p.astype(BF), d_all, 0, 0), h)
    dq, dk, dv = (dq * 0.125).astype(BF), dk.astype(BF), dv.astype(BF)
    part[...] = (dot(dq, w[0], 1, 0) + dot(dk, w[1], 1, 0) + dot(dv, w[2], 1, 0)).astype(BF)
    rows = normed[...]
    for i, g in enumerate((dq, dk, dv)):
        grad_w[i] = (gw_a[i] + gw_b[i] + dot(g, rows, 0, 0)).astype(BF)
    bias[...] = bias_a[...] + bias_b[...]
    bias[0:1, :] += jnp.sum(dq.astype(F32), 0, keepdims=True)
    bias[1:2, :] += jnp.sum(dv.astype(F32), 0, keepdims=True)


def final_rows(where, tok, lat, a, b, c, grad_res, gain, out, stats):
    n, m = tok.shape[0], lat.shape[0]
    stats[...] = jnp.zeros_like(stats)
    for x, at in ((tok, slice(0, n)), (lat, slice(n, n + m))):
        grad = a[at, :].astype(F32) + b[at, :].astype(F32) + c[at, :].astype(F32)
        unit, inverse = norm_parts(x[...].astype(F32))
        out[at, :] = (grad_res[at, :] + norm_back(grad, unit, inverse, gain[...])).astype(BF)
        stats[0:1, :] += jnp.sum(grad * unit, 0, keepdims=True)
        stats[1:2, :] += jnp.sum(grad, 0, keepdims=True)


def place_rows(order, a, b, c, d, tok_out, lat_out):
    n = tok_out.shape[0]
    for i, ref in enumerate((a, b, c, d)):

        @pl.when(pl.program_id(0) == i)
        def _(ref=ref):
            tok_out[...] = ref[0:n, :]
            lat_out[...] = ref[n:, :]


def make(mesh):
    dp_size, mp_size = mesh.shape["dp"], mesh.shape["mp"]
    assert mp_size == 4
    dp_bits = [1 << i for i in range(dp_size.bit_length() - 1)]
    assert 1 << len(dp_bits) == dp_size

    def swap(v, dp_bit, mp_bit):
        pairs = [
            (d * mp_size + m, (d ^ dp_bit) * mp_size + (m ^ mp_bit))
            for d in range(dp_size)
            for m in range(mp_size)
        ]
        return lax.ppermute(v, ("dp", "mp"), pairs)

    def per_device(
        tokens,
        latents,
        image_of_group,
        token_valid,
        norm1_gain,
        norm1_shift,
        w_qkv,
        b_qv,
        w_out,
        b_out,
        norm2_gain,
        norm2_shift,
        w_up,
        b_up,
        w_down,
        b_down,
        cot_tokens,
        cot_latents,
    ):
        dp_at, mp_at = lax.axis_index("dp"), lax.axis_index("mp")
        tok_count, width = tokens.shape
        lat_count = latents.shape[0]
        groups = lat_count // LAT
        wide = w_qkv.shape[2]
        hidden = w_up.shape[1]
        tok_own, lat_own = tok_count // 4, lat_count // 4
        rows_own = tok_own + lat_own
        order = (mp_at ^ jnp.arange(4, dtype=jnp.int32)).astype(jnp.int32)
        where = jnp.reshape(mp_at, (1,)).astype(jnp.int32)
        all_lat = dp_size * lat_count

        def by_slot(v):
            return jnp.take(v.reshape((4, v.shape[0] // 4) + v.shape[1:]), order, axis=0)

        def row(v):
            return v.reshape(1, -1)

        lat_rel = by_slot(latents).reshape(lat_count, width)
        lat_all = lat_rel
        for bit in dp_bits:
            lat_all = jnp.concatenate([lat_all, swap(lat_all, bit, 0)], 0)
        bias_rows = jnp.stack(list(split3(b_up)) + [jnp.zeros((width,), BF)] * 13)
        o0 = jnp.concatenate([w_out, bias_rows], 0)
        o1 = swap(o0, 0, 1)
        o2 = swap(o0, 0, 2)
        o3 = swap(o2, 0, 1)
        pack = jnp.concatenate([w_up, w_down], 0)
        x_bit = dp_at & 1
        half = pack.shape[0] // 2
        got = swap(lax.dynamic_slice_in_dim(pack, x_bit * half, half), 0, 2)
        other = swap(got, 1, 0)
        p1 = swap(pack, 0, 1)
        p2 = jnp.where(x_bit == 0, jnp.concatenate([got, other], 0), jnp.concatenate([other, got], 0))
        p3 = swap(p2, 0, 1)

        image_abs = image_of_group.reshape(dp_size, 4, groups // 4)
        image_rel = image_abs[(dp_at ^ jnp.arange(dp_size))[:, None], order[None, :]].reshape(-1)
        key_im = jnp.repeat(image_rel, LAT)
        own_im = key_im[:lat_count]
        count = by_slot(jnp.sum(token_valid.reshape(groups, GROUP), 1)).reshape(groups).astype(jnp.int32)

        gain1, shift1, gain2, shift2 = (row(v) for v in (norm1_gain, norm1_shift, norm2_gain, norm2_shift))
        w_t = jnp.transpose(w_qkv, (0, 2, 1))
        group_rows = pl.BlockSpec((GROUP, wide), lambda i, *_: (i, 0))

        def slot_rows(s):
            return pl.BlockSpec((GROUP, wide), lambda i, *_: (jnp.clip(i - 2 * s, 0, 1), 0))

        normed, q, k, v, t0, t1, t2, t3, log, ql, kl, vl = call(
            forward_near,
            name="forward_near",
            grid=(groups,),
            scalars=2,
            ins=[
                pl.BlockSpec((GROUP, width), lambda i, order, _: (order[i // 2] * 2 + i % 2, 0)),
                kept((lat_count, width)),
                kept((1, width)),
                kept((1, width)),
                kept((3, wide, width)),
                kept((2, wide)),
            ],
            outs=[((tok_count, width), BF, pl.BlockSpec((GROUP, width), lambda i, *_: (i, 0)))]
            + [((tok_count, wide), BF, group_rows)] * 3
            + [((tok_own, wide), BF, slot_rows(s)) for s in range(4)]
            + [((groups, 8, GROUP), F32, pl.BlockSpec((1, 8, GROUP), lambda i, *_: (i, 0, 0)))]
            + [((lat_count, wide), F32, kept((lat_count, wide)))] * 3,
            flops=tok_count * (width * wide * 6 + GROUP * wide * 4),
            moved=8 << 20,
        )(order, count, tokens, lat_rel, gain1, shift1, w_t, b_qv)

        chunk = min(512, all_lat)
        normed_lat, qa, ka, va, l0, l1, l2, l3, far, far_logs = call(
            forward_far,
            name="forward_far",
            grid=(all_lat // chunk,),
            scalars=1,
            ins=[
                pl.BlockSpec((chunk, width), lambda i, *_: (i, 0)),
                kept((1, width)),
                kept((1, width)),
                whole((3, wide, width)),
                kept((2, wide)),
                kept((lat_count, 1)),
                kept((1, all_lat)),
                whole((tok_count, wide)),
                whole((tok_count, wide)),
            ],
            outs=[((lat_count, width), BF, kept((lat_count, width)))]
            + [((all_lat, wide), BF, whole((all_lat, wide)))] * 3
            + [((lat_own, wide), BF, kept((lat_own, wide)))] * 4
            + [((lat_count, wide), BF, kept((lat_count, wide)))]
            + [((lat_count, 2 * HEAD), BF, kept((lat_count, 2 * HEAD)))],
            flops=all_lat * width * wide * 6,
            moved=5 << 20,
        )(count, lat_all, gain1, shift1, w_t, b_qv, own_im[:, None], key_im[None, :], k, v)

        t1, t2, t3 = (swap(t, 0, i) for i, t in ((1, t1), (2, t2), (3, t3)))
        l1, l2, l3 = (swap(t, 0, i) for i, t in ((1, l1), (2, l2), (3, l3)))

        own_tok = pl.BlockSpec((tok_own, width), lambda i, where, _: (where[0], 0), pipeline_mode=pl.Buffered(1))
        own_lat = pl.BlockSpec((lat_own, width), lambda i, where, _: (where[0], 0), pipeline_mode=pl.Buffered(1))
        big = (rows_own, width)
        square = lambda at: pl.BlockSpec((width, hidden), lambda *_: (at, 0), pipeline_mode=pl.Buffered(1))

        def full(shape, kind):
            return (shape, kind, whole(shape))

        outs_shape = (wide + 16, width)
        residual, n2, branch, back, cot, stats1, bsum1, pack0, pack1 = call(
            middle_one,
            name="middle_one",
            grid=(1,),
            scalars=2,
            ins=[whole((tok_own, wide))] * 4
            + [whole((lat_own, wide))] * 4
            + [whole(outs_shape)] * 4
            + [own_tok, whole((lat_own, width)), own_tok, own_lat]
            + [whole((1, width))] * 3
            + [square(0), square(0), square(0), square(1)],
            outs=[
                full(big, F32),
                full(big, BF),
                full(big, F32),
                full(big, F32),
                full(big, BF),
                full((8, width), F32),
                full((2, hidden), F32),
                full((width + hidden, width), BF),
                full((width + hidden, width), BF),
            ],
            scratch=[pltpu.VMEM((rows_own, hidden), BF)] * 2,
            flops=rows_own * width * (wide * 8 + hidden * 24),
            moved=20 << 20,
        )(
            where, count, t0, t1, t2, t3, l0, l1, l2, l3, o0, o1, o2, o3, tokens, lat_rel, cot_tokens, cot_latents,
            row(b_out), gain2, shift2, w_up, w_down, p1, p1,
        )

        out_rows, grad_res, g0, g1, g2, g3, grad_attn, act2, grad2, act3, grad3, stats2, bsum2 = call(
            middle_two,
            name="middle_two",
            grid=(1,),
            scalars=1,
            ins=[whole(big)] * 5
            + [whole(outs_shape)] * 4
            + [whole((width + hidden, width))] * 2
            + [whole((1, width))] * 2,
            outs=[full(big, BF), full(big, F32)]
            + [full((rows_own, wide), BF)] * 4
            + [full(big, BF)]
            + [full((rows_own, hidden), BF)] * 4
            + [full((8, width), F32), full((2, hidden), F32)],
            scratch=[pltpu.VMEM(big, F32)] * 2,
            flops=rows_own * width * (wide * 8 + hidden * 16),
            moved=20 << 20,
        )(count, residual, n2, cot, branch, back, o0, o1, o2, o3, p2, p3, row(b_down), gain2)

        g1, g2, g3 = (swap(t, 0, i) for i, t in ((1, g1), (2, g2), (3, g3)))

        own_out, send_out, pair_out = call(
            middle_grads,
            name="middle_grads",
            grid=(1,),
            scalars=0,
            ins=[whole(big)] * 3
            + [whole((tok_own, wide))] * 4
            + [whole((lat_own, wide))] * 4
            + [whole((rows_own, hidden))] * 4,
            outs=[
                full((wide, width), BF),
                full((width + hidden + 2 * wide, width), BF),
                full((width + hidden + wide, width), BF),
            ],
            flops=rows_own * width * (wide * 8 + hidden * 8),
            moved=20 << 20,
        )(n2, cot, grad_attn, t0, t1, t2, t3, l0, l1, l2, l3, act2, grad2, act3, grad3)

        def add(a, b):
            return (a.astype(F32) + b.astype(F32)).astype(BF)

        def scatter(v, bits):
            for bit in bits:
                n = v.shape[0] // 2
                at = jnp.where((dp_at & bit) == 0, 0, 1)
                mine = lax.dynamic_slice_in_dim(v, at * n, n)
                sent = lax.dynamic_slice_in_dim(v, (1 - at) * n, n)
                v = add(mine, swap(sent, bit, 0))
            return v

        def gather(v, bits):
            for bit in bits:
                got = swap(v, bit, 0)
                v = jnp.where(
                    (dp_at & bit) == 0, jnp.concatenate([v, got], 0), jnp.concatenate([got, v], 0)
                )
            return v

        def dp_sum(v, bits):
            rows = v.shape[0]
            spare = -rows % dp_size
            if spare:
                v = jnp.concatenate([v, jnp.zeros((spare,) + v.shape[1:], v.dtype)], 0)
            return gather(scatter(v, bits), bits[::-1])[:rows]

        got1 = swap(pack1, 0, 1)
        got3 = swap(send_out, 0, 1)
        rows = width + hidden
        keep = jnp.concatenate([add(pack0, got1), add(own_out, got3[rows + wide :])], 0)
        send = add(pair_out, got3[: rows + wide])
        keep = add(keep, swap(send, 0, 2))
        cut = keep.shape[0] // 2
        part_a = dp_sum(keep[:cut], dp_bits)
        part_b = dp_sum(keep[cut:], dp_bits[1:] + dp_bits[:1])
        sums = jnp.concatenate([part_a, part_b], 0).astype(F32)
        grad_w_up, grad_w_down, grad_w_out = sums[:width], sums[width:rows], sums[rows:]

        zeros = jnp.zeros((lat_count, HEAD), BF)
        d_lat = jnp.concatenate([g[tok_own:] for g in (g0, g1, g2, g3)], 0)
        bundle = jnp.concatenate([d_lat, zeros, far, zeros, far_logs], 1)
        for bit in dp_bits:
            bundle = jnp.concatenate([bundle, swap(bundle, bit, 0)], 0)

        def near(at, da, db):
            four = 4 * at
            tok_block = lambda which: pl.BlockSpec(
                (GROUP, wide), lambda i, *_: (jnp.clip(i - 2 * which, 0, 1), 0)
            )
            lat_block = pl.BlockSpec((lat_own, wide), lambda *_: (tok_own // lat_own, 0))
            eight = pl.BlockSpec((LAT, wide), lambda i, *_: (i + four, 0))
            return call(
                backward_near,
                name="backward_near",
                grid=(4,),
                scalars=2,
                ins=[
                    pl.BlockSpec((GROUP, width), lambda i, *_: (i + four, 0)),
                    *[pl.BlockSpec((GROUP, wide), lambda i, *_: (i + four, 0))] * 3,
                    eight,
                    eight,
                    eight,
                    pl.BlockSpec((1, 8, GROUP), lambda i, *_: (i + four, 0, 0)),
                    pl.BlockSpec((2 * LAT, wide), lambda i, *_: ((i + four) // 2, 0)),
                    pl.BlockSpec((2 * LAT, 2 * HEAD), lambda i, *_: ((i + four) // 2, 0)),
                    tok_block(0),
                    tok_block(1),
                    lat_block,
                    lat_block,
                    kept((3, wide, width)),
                ],
                outs=[
                    ((4 * GROUP, width), BF, pl.BlockSpec((GROUP, width), lambda i, *_: (i, 0))),
                    ((3, wide, width), F32, kept((3, wide, width))),
                    ((8, wide), F32, kept((8, wide))),
                    *[((4 * LAT, wide), F32, pl.BlockSpec((LAT, wide), lambda i, *_: (i, 0)))] * 3,
                ],
                flops=4 * GROUP * (width * wide * 12 + GROUP * wide * 10),
                moved=10 << 20,
            )(order, count[four : four + 4], normed, q, k, v, ql, kl, vl, log, far, far_logs, da, db, da, db, w_t)

        part_a1, gw_a, bias_a, dq_a, dk_a, dv_a = near(0, g0, g1)
        part_b1, gw_b, bias_b, dq_b, dk_b, dv_b = near(1, g2, g3)
        part_lat, grad_w, bias = call(
            backward_far,
            name="backward_far",
            grid=(1,),
            scalars=0,
            ins=[
                whole((lat_count, 1)),
                whole((1, all_lat)),
                whole((1, lat_count)),
                whole((all_lat, 1)),
                *[whole((all_lat, wide))] * 3,
                whole((all_lat, 10 * HEAD)),
                whole((lat_count, width)),
                *[whole((lat_count // 2, wide))] * 6,
                whole((3, wide, width)),
                *[whole((3, wide, width))] * 2,
                *[whole((8, wide))] * 2,
            ],
            outs=[full((lat_count, width), BF), full((3, wide, width), BF), full((8, wide), F32)],
            flops=all_lat * lat_count * wide * 14,
            moved=10 << 20,
        )(
            own_im[:, None], key_im[None, :], own_im[None, :], key_im[:, None], qa, ka, va, bundle, normed_lat,
            dq_a, dq_b, dk_a, dk_b, dv_a, dv_b, w_t, gw_a, gw_b, bias_a, bias_b,
        )

        grad_w = grad_w.reshape(3 * wide, width)
        cut = 3 * wide // 2
        gw = [dp_sum(grad_w[:cut], dp_bits), dp_sum(grad_w[cut:], dp_bits[1:] + dp_bits[:1])]
        grad_w_qkv = jnp.concatenate(gw, 0).astype(F32).reshape(3, wide, width).transpose(0, 2, 1)

        def slot_part(s):
            tok = (part_a1, part_b1)[s // 2][(s % 2) * tok_own : (s % 2 + 1) * tok_own]
            return jnp.concatenate([tok, part_lat[s * lat_own : (s + 1) * lat_own]], 0)

        got = swap(jnp.concatenate([slot_part(1), slot_part(3)], 0), 0, 1)
        there = add(slot_part(2), got[rows_own:])
        from_y = swap(there, 0, 2)
        grad_rows, stats3 = call(
            final_rows,
            name="final_rows",
            grid=(1,),
            scalars=1,
            ins=[
                pl.BlockSpec((tok_own, width), lambda i, where: (where[0], 0), pipeline_mode=pl.Buffered(1)),
                whole((lat_own, width)),
                *[whole(big)] * 4,
                whole((1, width)),
            ],
            outs=[full(big, BF), full((8, width), F32)],
            moved=8 << 20,
        )(where, tokens, lat_rel, slot_part(0), got[:rows_own], from_y, grad_res, gain1)

        def all_rows(v):
            v_y = swap(v, 0, 2)
            v_c = swap(v, 0, 1)
            v_yc = swap(v_y, 0, 1)
            return call(
                place_rows,
                name="place_rows",
                grid=(4,),
                scalars=1,
                ins=[kept(big)] * 4,
                outs=[
                    ((tok_count, width), BF, pl.BlockSpec((tok_own, width), lambda i, order: (order[i], 0))),
                    ((lat_count, width), BF, pl.BlockSpec((lat_own, width), lambda i, order: (order[i], 0))),
                ],
                moved=8 << 20,
            )(order, v, v_c, v_y, v_yc)

        out_tok, out_lat = all_rows(out_rows)
        grad_tok, grad_lat = all_rows(grad_rows)

        def place(v):
            return lax.dynamic_update_slice_in_dim(jnp.zeros((4 * wide,), F32), v, mp_at * wide, 0)

        bias_up = jnp.concatenate([bsum1, bsum2], 0)
        small = jnp.concatenate(
            [
                stats1[:1],
                stats2[:6],
                stats3[:2],
                place(bias[0])[None],
                place(bias[1])[None],
                jnp.take(bias_up, order, axis=0),
                jnp.full((1, width), 0.25 * jnp.sum(token_valid).astype(F32)),
            ],
            0,
        )
        for bit in (1, 2):
            small = small + swap(small, 0, bit)
        for bit in dp_bits:
            small = small + swap(small, bit, 0)
        squares = jnp.sum(jnp.stack([small[1], small[0], small[2]]), 1)
        root_means = jnp.sqrt(squares / (small[15, 0] * width))
        grad_b_qv = lax.dynamic_slice_in_dim(small[9:11], mp_at * wide, wide, 1)
        grad_b_up = lax.dynamic_index_in_dim(small[11:15], mp_at, 0, keepdims=False)
        return (
            out_tok,
            out_lat,
            grad_tok,
            grad_lat,
            small[7],
            small[8],
            grad_w_qkv,
            grad_b_qv,
            grad_w_out,
            small[5],
            small[3],
            small[4],
            grad_w_up,
            grad_b_up,
            grad_w_down,
            small[6],
            root_means,
        )

    return per_device


def solution(mesh):
    rows, whole = P("dp", None), P()
    return jax.shard_map(
        make(mesh),
        mesh=mesh,
        in_specs=(
            rows,
            rows,
            whole,
            P("dp"),
            whole,
            whole,
            P(None, None, "mp"),
            P(None, "mp"),
            P("mp", None),
            whole,
            whole,
            whole,
            P(None, "mp"),
            P("mp"),
            P("mp", None),
            whole,
            rows,
            rows,
        ),
        out_specs=(
            rows,
            rows,
            rows,
            rows,
            whole,
            whole,
            P(None, None, "mp"),
            P(None, "mp"),
            P("mp", None),
            whole,
            whole,
            whole,
            P(None, "mp"),
            P("mp"),
            P("mp", None),
            whole,
            whole,
        ),
        check_vma=False,
    )
```

```python
import jax
import jax.numpy as jnp
from jax import lax
from jax.experimental import pallas as pl
from jax.experimental.pallas import tpu as pltpu
from jax.sharding import PartitionSpec as P

HEAD = 64
LANES = 128
GROUP = 256
LAT = 8
BF = jnp.bfloat16
F32 = jnp.float32
FAR = -1e30
MIB = 1 << 20
GAIN1, SHIFT1, B_OUT, GAIN2, SHIFT2, B_DOWN, B_UP = range(7)


def dot(a, b, ca, cb):
    return lax.dot_general(a, b, (((ca,), (cb,)), ((), ())), preferred_element_type=F32)


def norm_parts(values):
    center = values - jnp.mean(values, axis=-1, keepdims=True)
    spread = jnp.mean(center * center, axis=-1, keepdims=True)
    inverse = lax.rsqrt(spread + 1e-06)
    return center * inverse, inverse


def norm_back(grad, unit, inverse, gain):
    scaled = grad * gain
    inner = jnp.mean(scaled * unit, axis=-1, keepdims=True)
    return inverse * (scaled - jnp.mean(scaled, axis=-1, keepdims=True) - unit * inner)


def gelu_both(values):
    square = values * values
    inner = jnp.tanh(values * (0.7978845608028654 + 0.035677408136300125 * square))
    half = 0.5 + 0.5 * inner
    slope = values * (0.3989422804014327 + 0.05351611220494518 * square)
    return values * half, half + (1.0 - inner * inner) * slope


def split3(v):
    hi = v.astype(BF)
    mid = (v - hi.astype(F32)).astype(BF)
    low = (v - hi.astype(F32) - mid.astype(F32)).astype(BF)
    return hi, mid, low


def head_lanes(v, h):
    lane = lax.broadcasted_iota(jnp.int32, v.shape, v.ndim - 1)
    return jnp.where((lane >= h * HEAD) & (lane < (h + 1) * HEAD), v, jnp.zeros_like(v))


def kept(shape):
    return pl.BlockSpec(shape, lambda *_: (0,) * len(shape))


def whole(shape):
    return pl.BlockSpec(shape, lambda *_: (0,) * len(shape), pipeline_mode=pl.Buffered(1))


ANY = pl.BlockSpec(memory_space=pl.ANY)
OWN, SENT = (0, 1, 2, 3), (0, 2, 1, 3)


def call(body, *, name, scalars, ins, outs, grid=(1,), scratch=(), deps=(), us=1.0):
    first, extra = scalars + len(ins), len(deps)

    def wrapped(*refs):
        body(*refs[:first], *refs[first + extra :])

    def run(*args):
        return pl.pallas_call(
            wrapped,
            name=name,
            out_shape=[jax.ShapeDtypeStruct(s, d) for s, d, _ in outs],
            grid_spec=pltpu.PrefetchScalarGridSpec(
                num_scalar_prefetch=scalars,
                grid=grid,
                in_specs=list(ins) + [ANY] * extra,
                out_specs=[spec for _, _, spec in outs],
                scratch_shapes=list(scratch),
            ),
            compiler_params=pltpu.CompilerParams(
                dimension_semantics=("arbitrary",) * len(grid), vmem_limit_bytes=56 * MIB
            ),
            cost_estimate=pl.CostEstimate(
                flops=int(us * 1.0e10), bytes_accessed=1 << 16, transcendentals=0
            ),
        )(*args, *deps)

    return run


def mover(sems):
    used = []

    def start(src, dst):
        copy = pltpu.make_async_copy(src, dst, sems.at[len(used)])
        used.append(copy)
        copy.start()
        return copy

    return start


def sides(meta):
    return meta[0] & 1, (meta[0] >> 1) & 1


def combine(name, meta, arrays, outs, deps=(), us=1.0):
    def body(meta, *refs):
        x, z = sides(meta)

        def rows_at(at, n):
            return pl.ds(pl.multiple_of(at(x, z), 16), n) if callable(at) else slice(at, at + n)

        for ref, (_, kind, segments) in zip(refs[len(arrays) :], outs):
            for to, n, terms in segments:
                parts = [refs[i][rows_at(at, n), :] for i, at in terms]
                value = parts[0]
                if len(parts) > 1:
                    value = parts[0].astype(F32)
                    for part in parts[1:]:
                        value = value + part.astype(F32)
                ref[rows_at(to, n), :] = value.astype(kind)

    width = arrays[0].shape[1]
    return call(
        body,
        name=name,
        scalars=1,
        ins=[whole(a.shape) for a in arrays],
        outs=[((rows, width), kind, whole((rows, width))) for rows, kind, _ in outs],
        deps=deps,
        us=us,
    )(meta, *arrays)


def group_at(meta, count, slot, i):
    return count[(meta[1] ^ slot) * 2 + i]


def image_list(meta, image, devices, per_device, slots):
    each = per_device // 4
    return [
        image[(meta[0] ^ j) * per_device + (meta[1] ^ s) * each + i]
        for j in range(devices)
        for s in slots
        for i in range(each)
    ]


def image_column(images):
    return jnp.concatenate([jnp.full((LAT, 1), im, jnp.int32) for im in images], 0)


def image_row(images):
    group = lax.broadcasted_iota(jnp.int32, (1, len(images) * LAT), 1) // LAT
    out = jnp.zeros(group.shape, jnp.int32)
    for g, im in enumerate(images):
        out = jnp.where(group == g, im, out)
    return out


def key_stack(tok, lat8):
    pad = jnp.concatenate([lat8, jnp.zeros_like(lat8)], 0).astype(BF)
    return jnp.concatenate([tok, pad], 0)


def near_mask(count, columns):
    row = lax.broadcasted_iota(jnp.int32, (GROUP + 2 * LAT, columns), 0)
    return (row < count) | ((row >= GROUP) & (row < GROUP + LAT))


def param(params, i):
    return params[i : i + 1, :]


def project(rows, params, w, bias):
    unit, _ = norm_parts(rows.astype(F32))
    rows = (unit * param(params, GAIN1) + param(params, SHIFT1)).astype(BF)
    return (
        rows,
        (dot(rows, w[0], 1, 1) + bias[0:1]).astype(BF),
        dot(rows, w[1], 1, 1).astype(BF),
        (dot(rows, w[2], 1, 1) + bias[1:2]).astype(BF),
    )


def prepare(meta, lat, w_out, g1, s1, bo, g2, s2, bd, bu, up, down, lat_rel, lat_half, out_pack, part, params):
    n = lat.shape[0] // 4
    for s in range(4):
        rows = lat[pl.ds(pl.multiple_of((meta[1] ^ s) * n, 16), n), :]
        lat_rel[s * n : (s + 1) * n, :] = rows
        if s % 2 == 0:
            lat_half[s // 2 * n : (s // 2 + 1) * n, :] = rows
    for i, ref in enumerate((g1, s1, bo, g2, s2, bd, bu)):
        params[i : i + 1, :] = ref[...].reshape(1, ref.shape[0])
    params[7:8, :] = jnp.zeros_like(params[7:8, :])
    wide = w_out.shape[0]
    out_pack[0:wide, :] = w_out[...]
    bias = param(params, B_UP)
    rows = [v.astype(F32) for v in split3(bias)]
    out_pack[wide : wide + 16, :] = jnp.concatenate(rows + [jnp.zeros((13, bias.shape[1]), F32)], 0).astype(BF)
    n = up.shape[0]
    part[0:n, :], part[n : 2 * n, :] = up[...], down[...]


def latent_rows(lat, params, w, bias, normed, ql, kl, vl):
    normed[...], a, b, c = project(lat[...], params, w, bias)
    ql[...], kl[...], vl[...] = a.astype(F32), b.astype(F32), c.astype(F32)


def forward_near(base, meta, count, tok, kl, vl, params, w, bias, normed, q, k, v, mixed_out, log):
    step = pl.program_id(0)
    wide = w.shape[1]
    rows, qs, ks, vs = project(tok[...], params, w, bias)
    normed[...], q[...], k[...], v[...] = rows, qs, ks, vs
    qs = qs * jnp.asarray(0.125, BF)
    for i in range(tok.shape[0] // GROUP):
        here = slice(i * LAT, (i + 1) * LAT)
        at = slice(i * GROUP, (i + 1) * GROUP)
        keys = key_stack(ks[at], kl[here, :])
        values = key_stack(vs[at], vl[here, :]).T
        mask = near_mask(group_at(meta, count, step + base, i), GROUP)
        logs, outs = [], []
        for h in range(wide // HEAD):
            s = jnp.where(mask, dot(head_lanes(keys, h), qs[at], 1, 1), FAR)
            top = jnp.max(s, 0, keepdims=True)
            e = jnp.exp(s - top)
            total = jnp.sum(e, 0, keepdims=True)
            logs.append(top + jnp.log(total))
            outs.append(dot(values[h * HEAD : (h + 1) * HEAD], e.astype(BF), 1, 0) * (1.0 / total))
        log[i] = jnp.concatenate(logs + [jnp.zeros((8 - len(logs), GROUP), F32)], 0)
        mixed_out[:, at] = jnp.concatenate(outs, 0).astype(BF)


def forward_far(meta, count, image, lat, params, w, bias, k_near, k_away, v_near, v_away, ql, qa, ka, va, m_near, m_away, far, logs_out):
    step = pl.program_id(0)
    wide = w.shape[1]
    rows_step = lat.shape[0]
    own = ql.shape[0]
    groups = own // LAT

    def rows_of(near, away, g):
        half = groups // 2
        ref, at = (near, g) if g < half else (away, g - half)
        return ref[at * GROUP : (at + 1) * GROUP, :]

    _, a, b, c = project(lat[...], params, w, bias)
    here = pl.ds(pl.multiple_of(step * rows_step, rows_step), rows_step)
    qa[here, :], ka[here, :], va[here, :] = a, b, c

    @pl.when(step == pl.num_programs(0) - 1)
    def _():
        q32 = ql[...] * 0.125
        images = image_list(meta, image, qa.shape[0] // own, groups, SENT)
        mask = image_column(image_list(meta, image, 1, groups, OWN)) == image_row(images)
        lane = lax.broadcasted_iota(jnp.int32, (LAT, GROUP), 1)
        full = jnp.zeros((own, wide), F32)
        logs = []
        for h in range(wide // HEAD):
            qh = head_lanes(q32, h)
            s_lat = jnp.where(mask, dot(qh.astype(BF), ka[...], 1, 1), FAR)
            s_tok = jnp.concatenate(
                [
                    jnp.where(
                        lane < group_at(meta, count, g // 2, g % 2),
                        dot(qh[g * LAT : (g + 1) * LAT].astype(BF), rows_of(k_near, k_away, g), 1, 1),
                        FAR,
                    )
                    for g in range(groups)
                ],
                0,
            )
            top = jnp.maximum(jnp.max(s_lat, 1, keepdims=True), jnp.max(s_tok, 1, keepdims=True))
            e_lat, e_tok = jnp.exp(s_lat - top), jnp.exp(s_tok - top)
            total = jnp.sum(e_lat, 1, keepdims=True) + jnp.sum(e_tok, 1, keepdims=True)
            logs.append(top + jnp.log(total))
            near = jnp.concatenate(
                [
                    dot(e_tok[g * LAT : (g + 1) * LAT].astype(BF), rows_of(v_near, v_away, g), 1, 0)
                    for g in range(groups)
                ],
                0,
            )
            full = full + head_lanes((dot(e_lat.astype(BF), va[...], 1, 0) + near) * (1.0 / total), h)
        mixed = full.astype(BF)
        m_near[...], m_away[...] = mixed[: own // 2], mixed[own // 2 :]
        parts = [split3(x) for x in logs]
        cols = [p[i] for i in range(3) for p in parts]
        lane = lax.broadcasted_iota(jnp.int32, (own, 2 * HEAD), 1)
        extra = jnp.zeros((own, 2 * HEAD), F32)
        for i, c in enumerate(cols):
            extra = jnp.where(lane == i, c.astype(F32), extra)
        far[...] = mixed
        logs_out[...] = extra.astype(BF)


def valid_rows(meta, count, rows):
    row = lax.broadcasted_iota(jnp.int32, (rows, 1), 0)
    first = (row < GROUP) & (row < group_at(meta, count, 0, 0))
    return first | ((row >= GROUP) & (row < GROUP + group_at(meta, count, 0, 1)))


def slot_block(meta, ref, slot):
    n = ref.shape[0] // 4
    return ref.at[pl.ds(pl.multiple_of((meta[1] ^ slot) * n, 16), n)]


def project_out(t_near, t_far, l_near, l_far, o0, o2, out):
    wide, n = t_near.shape
    value = dot(t_near[...], o0[0:wide, :], 0, 0) + dot(t_far[...], o2[0:wide, :], 0, 0)
    out[0:n, :] = value.astype(out.dtype)
    value = dot(l_near[...], o0[0:wide, :], 1, 0) + dot(l_far[...], o2[0:wide, :], 1, 0)
    out[n:, :] = value.astype(out.dtype)


def cot_back(meta, cot_tok, cot_lat, down_w, out):
    n = cot_tok.shape[0]
    out[0:n, :] = dot(cot_tok[...], down_w[...], 1, 1).astype(BF)
    out[n:, :] = dot(cot_lat[...], down_w[...], 1, 1).astype(BF)


def add_norm(meta, count, params, own, got, tok, lat, residual, n2, stats):
    n, m = tok.shape[0], lat.shape[0]
    stats[...] = jnp.zeros_like(stats)
    for at, size, x in ((0, n, tok), (n, m, lat)):
        rows = slice(at, at + size)
        attn = own[rows, :] + got[rows, :].astype(F32) + param(params, B_OUT)
        if at == 0:
            real = valid_rows(meta, count, n)
            stats[0:1, :] = jnp.sum(jnp.where(real, attn * attn, 0.0), 0, keepdims=True)
        res = x[...].astype(F32) + attn
        residual[rows, :] = res
        unit, _ = norm_parts(res)
        n2[rows, :] = (unit * param(params, GAIN2) + param(params, SHIFT2)).astype(BF)


def hidden_part(n2, cot, up_w, down_w, bias, act_out, grad_out):
    cut = 256
    sums = []
    for at in range(0, up_w.shape[1], cut):
        cols = slice(at, at + cut)
        up = dot(n2, up_w[:, cols], 1, 0) + bias[:, cols]
        active, slope = gelu_both(up)
        grad_up = (dot(cot, down_w[cols, :], 1, 1) * slope).astype(BF)
        act_out[:, cols] = active.astype(BF)
        grad_out[:, cols] = grad_up
        sums.append(jnp.sum(grad_up.astype(F32), 0, keepdims=True))
    return jnp.concatenate(sums, 1)


def two_halves(meta, fetch, n2_own, n2_sib, cot_tok, cot_lat, vn2, vcot):
    rows = n2_own.shape[0]
    n = cot_tok.shape[0] // 4
    copies = [fetch(n2_own, vn2.at[0:rows]), fetch(n2_sib, vn2.at[rows:])]
    for s in (0, 1):
        at = s * rows
        copies.append(fetch(slot_block(meta, cot_tok, s), vcot.at[at : at + n]))
        copies.append(fetch(slot_block(meta, cot_lat, s), vcot.at[at + n : at + rows]))
    return copies


def send_parts(meta, flush, pack, parts):
    x, z = sides(meta)
    n = parts[0].shape[0] // 2
    copies = []
    for ref, (dx, dz) in zip(parts, ((0, 0), (1, 0), (0, 1), (1, 1))):
        q = (x ^ dx) * 2 + (z ^ dz)
        for i in (0, 1):
            src = pack.at[pl.ds(pl.multiple_of(i * 4 * n + q * n, 16), n)]
            copies.append(flush(src, ref.at[i * n : (i + 1) * n]))
    return copies


def hidden_rows(n2, up_w, bias, got, act_out, grad_out, sums):
    cut = 256
    for at in range(0, up_w.shape[1], cut):
        cols = slice(at, at + cut)
        active, slope = gelu_both(dot(n2, up_w[:, cols], 1, 0) + bias[:, cols])
        grad_up = (got[:, cols].astype(F32) * slope).astype(BF)
        act_out[:, cols] = active.astype(BF)
        grad_out[:, cols] = grad_up
        sums[0:1, cols] = jnp.sum(grad_up.astype(F32), 0, keepdims=True)


def hidden_first(params, n2, up_w, got, act, grad, stats):
    stats[...] = jnp.zeros_like(stats)
    hidden_rows(n2[...], up_w, param(params, B_UP), got, act, grad, stats)


def hidden_own(
    meta, params, n2_own, n2_sib, cot_tok, cot_lat, up_w, down_w, got_in, act_in, grad_in,
    branch_out, back_out, p0, p1, p2, p3, stats,
    vn2, vcot, vw, branch, back, act, grad, got, vpack, in_sems, out_sems,
):
    width, hidden = vw.shape[1], vw.shape[2]
    rows = got.shape[0]
    fetch, flush = mover(in_sems), mover(out_sems)
    first = [fetch(n2_sib, vn2.at[rows:]), fetch(up_w, vw.at[0]), fetch(got_in, got)]
    copies = [fetch(grad_in, grad.at[0:rows]), fetch(act_in, act.at[0:rows]), fetch(down_w, vw.at[1])]
    copies.append(fetch(n2_own, vn2.at[0:rows]))
    n = cot_tok.shape[0] // 4
    for s in (0, 1):
        at = s * rows
        copies.append(fetch(slot_block(meta, cot_tok, s), vcot.at[at : at + n]))
        copies.append(fetch(slot_block(meta, cot_lat, s), vcot.at[at + n : at + rows]))
    for copy in first:
        copy.wait()
    stats[...] = jnp.zeros_like(stats)
    hidden_rows(vn2[rows:, :], vw.at[0], param(params, B_UP), got, act.at[rows:], grad.at[rows:], stats)
    for copy in copies:
        copy.wait()
    back[...] = dot(grad[...], vw[0], 1, 1)
    outs = [flush(back, back_out)]
    branch[...] = dot(act[...], vw[1], 1, 0)
    outs.append(flush(branch, branch_out))
    vpack[0:width, :] = dot(vn2[...], grad[...], 0, 0).astype(BF)
    vpack[width : width + hidden, :] = dot(act[...], vcot[...], 0, 0).astype(BF)
    outs += send_parts(meta, flush, vpack, (p0, p1, p2, p3))
    for copy in outs:
        copy.wait()


def hidden_away(
    meta, o2, n2_own, n2_sib, cot_tok, cot_lat, w0, w1, w2, w3, branch_in, back_in,
    branch_own, back_own, send, act_out, grad_out, stats,
    vn2, vcot, vw, branch, back, act, grad, vsend, in_sems, out_sems,
):
    rows, width = n2_own.shape
    x, z = sides(meta)
    quarter = w0.shape[0] // 2
    fetch, flush = mover(in_sems), mover(out_sems)
    copies = two_halves(meta, fetch, n2_own, n2_sib, cot_tok, cot_lat, vn2, vcot)
    for ref, (dx, dz) in zip((w0, w1, w2, w3), ((0, 0), (1, 0), (0, 1), (1, 1))):
        q = pl.multiple_of(((x ^ dx) * 2 + (z ^ dz)) * quarter, 16)
        for i in (0, 1):
            copies.append(fetch(ref.at[i * quarter : (i + 1) * quarter], vw.at[i, pl.ds(q, quarter)]))
    late = [fetch(back_in, back), fetch(branch_in, branch)]
    for copy in copies:
        copy.wait()
    base = o2.shape[0] - 16
    bias = o2[base : base + 16, :].astype(F32)
    bias = bias[0:1] + bias[1:2] + bias[2:3]
    n2, ct = vn2[...], vcot[...]
    stats[...] = jnp.zeros_like(stats)
    stats[0:1, :] = hidden_part(n2, ct, vw.at[0], vw.at[1], bias, act, grad)
    outs = [flush(act, act_out), flush(grad, grad_out)]
    for i, (ref, src, w, turn, own) in enumerate(
        ((back, grad, vw.at[0], 1, back_own), (branch, act, vw.at[1], 0, branch_own))
    ):
        late[i].wait()
        ref[...] += dot(src[...], w[...], 1, turn)
        vsend[i * rows : (i + 1) * rows, :] = ref[rows:, :].astype(BF)
        outs.append(flush(ref.at[0:rows], own))
        outs.append(flush(vsend.at[i * rows : (i + 1) * rows], send.at[i * rows : (i + 1) * rows]))
    for copy in outs:
        copy.wait()


def away_grads(
    meta, n2_own, n2_sib, cot_tok, cot_lat, act_in, grad_in, p0, p1, p2, p3,
    vn2, vcot, act, grad, vpack, in_sems, out_sems,
):
    width, hidden = vn2.shape[1], act.shape[1]
    fetch, flush = mover(in_sems), mover(out_sems)
    copies = [fetch(grad_in, grad)] + two_halves(meta, fetch, n2_own, n2_sib, cot_tok, cot_lat, vn2, vcot)
    last = fetch(act_in, act)
    for copy in copies:
        copy.wait()
    vpack[0:width, :] = dot(vn2[...], grad[...], 0, 0).astype(BF)
    last.wait()
    vpack[width : width + hidden, :] = dot(act[...], vcot[...], 0, 0).astype(BF)
    for copy in send_parts(meta, flush, vpack, (p0, p1, p2, p3)):
        copy.wait()


def middle_rows(meta, count, params, residual, branch, back, got, cot_tok, cot_lat, out_rows, grad_res, grad_attn, stats):
    n, m = cot_tok.shape[0], cot_lat.shape[0]
    rows_own = n + m
    stats[...] = jnp.zeros_like(stats)
    for at, size, cot in ((0, n, cot_tok), (n, m, cot_lat)):
        rows = slice(at, at + size)
        bk = back[rows, :] + got[rows, :].astype(F32)
        br = branch[rows, :] + got[rows_own + at : rows_own + at + size, :].astype(F32) + param(params, B_DOWN)
        res = residual[rows, :]
        out = res + br
        out_rows[rows, :] = out.astype(BF)
        if at == 0:
            real = valid_rows(meta, count, n)
            stats[0:1, :] = jnp.sum(jnp.where(real, out * out, 0.0), 0, keepdims=True)
            stats[1:2, :] = jnp.sum(jnp.where(real, br * br, 0.0), 0, keepdims=True)
        unit, inverse = norm_parts(res)
        stats[2:3, :] += jnp.sum(bk * unit, 0, keepdims=True)
        stats[3:4, :] += jnp.sum(bk, 0, keepdims=True)
        cot32 = cot[...].astype(F32)
        gr = cot32 + norm_back(bk, unit, inverse, param(params, GAIN2))
        grad_res[rows, :] = gr
        ga = gr.astype(BF)
        grad_attn[rows, :] = ga
        stats[4:5, :] += jnp.sum(ga.astype(F32), 0, keepdims=True)
        stats[5:6, :] += jnp.sum(cot32, 0, keepdims=True)


def back_out(ga_own, ga_sib, o0, o2, t_near, t_far, l_near, l_far, g0, g2, d0, d2, w0, w2):
    wide, n = t_near.shape[0], t_near.shape[1] // 2
    m = l_near.shape[0] // 2
    for o, g, d in ((o2, g2, d2), (o0, g0, d0)):
        for i, ga in enumerate((ga_own, ga_sib)):
            g[:, i * n : (i + 1) * n] = dot(o[0:wide, :], ga[0:n, :], 1, 1).astype(BF)
            d[i * m : (i + 1) * m, :] = dot(ga[n : n + m, :], o[0:wide, :], 1, 1).astype(BF)
    for t, l, w in ((t_far, l_far, w2), (t_near, l_near, w0)):
        total = jnp.zeros(w.shape, F32)
        for i, ga in enumerate((ga_own, ga_sib)):
            total += dot(t[:, i * n : (i + 1) * n], ga[0:n, :], 1, 0)
            total += dot(l[i * m : (i + 1) * m, :], ga[n : n + m, :], 0, 0)
        w[...] = total.astype(BF)


def near_slot(
    slot, meta, count, normed, q, k, v, ql, kl, vl, log, far, logs_far, d_in, d_lat_in, w, grad_w, bias,
    dq_far, dk_near, dv_near,
):
    wide = q.shape[1]
    heads = wide // HEAD
    rows = normed[...]
    slot_rows = rows.shape[0]
    d_lat = d_lat_in[...].astype(F32)
    eighth = jnp.asarray(0.125, BF)
    q_all, k_all, v_all = q[...] * eighth, k[...], v[...]
    far32 = far[...].astype(F32)
    far_log = logs_far[...].astype(F32)
    dqs, dks, dvs = [], [], []
    for i in range(slot_rows // GROUP):
        at, lat_at = slice(i * GROUP, (i + 1) * GROUP), slice(i * LAT, (i + 1) * LAT)
        number = group_at(meta, count, slot, i)
        d_cols = d_in[:, at]
        d_tok, qs, ks, vs = d_cols.T, q_all[at], k_all[at], v_all[at]
        keys, values = key_stack(ks, kl[lat_at, :]), key_stack(vs, vl[lat_at, :])
        keys_t = keys.T
        mask = near_mask(number, GROUP)
        ps, gs, dq_t, d_heads, q_heads = [], [], [], [], []
        for h in range(heads):
            s = dot(head_lanes(keys, h), qs, 1, 1)
            p = jnp.where(mask, jnp.exp(s - log[i, h : h + 1, :]), 0.0)
            gp = p * dot(head_lanes(values, h), d_cols, 1, 0)
            g = (gp - p * jnp.sum(gp, 0, keepdims=True)).astype(BF)
            dq_t.append(dot(keys_t[h * HEAD : (h + 1) * HEAD], g, 1, 0))
            ps.append(p.astype(BF))
            gs.append(g)
            d_heads.append(head_lanes(d_tok, h))
            q_heads.append(head_lanes(qs, h))
        dv = dot(jnp.concatenate(ps, 1), jnp.concatenate(d_heads, 0), 1, 0)
        dk = dot(jnp.concatenate(gs, 1), jnp.concatenate(q_heads, 0), 1, 0)
        dqs.append((jnp.concatenate(dq_t, 0).T * 0.125).astype(BF))
        pad = jnp.zeros((LAT, wide), F32)
        q8, o8, d8, lg = ql[lat_at, :] * 0.125, far32[lat_at], d_lat[lat_at], far_log[lat_at]
        q_rows, do_rows, log_col, del_col = [], [], [], []
        big = jnp.full((LAT, 1), 1e30, F32)
        zero = jnp.zeros((LAT, 1), F32)
        for h in range(heads):
            q_rows += [head_lanes(q8, h), pad]
            dh = head_lanes(d8, h)
            do_rows += [dh, pad]
            col = lg[:, h : h + 1] + lg[:, heads + h : heads + h + 1] + lg[:, 2 * heads + h : 2 * heads + h + 1]
            log_col += [col, big]
            del_col += [jnp.sum(dh * o8, 1, keepdims=True), zero]
        q_f, d_f = jnp.concatenate(q_rows, 0).astype(BF), jnp.concatenate(do_rows, 0).astype(BF)
        l_f, x_f = jnp.concatenate(log_col, 0), jnp.concatenate(del_col, 0)
        lane = lax.broadcasted_iota(jnp.int32, (2 * LAT * heads, GROUP), 1)
        p_f = jnp.where(lane < number, jnp.exp(dot(q_f, ks, 1, 1) - l_f), 0.0)
        g_f = (p_f * (dot(d_f, vs, 1, 1) - x_f)).astype(BF)
        dks.append((dk[0:GROUP] + dot(g_f, q_f, 0, 0)).astype(BF))
        dvs.append((dv[0:GROUP] + dot(p_f.astype(BF), d_f, 0, 0)).astype(BF))
        dk_near[lat_at, :] = dk[GROUP : GROUP + LAT]
        dv_near[lat_at, :] = dv[GROUP : GROUP + LAT]
        dq_all = dot(g_f, ks, 1, 0)
        dq_lat = jnp.zeros((LAT, wide), F32)
        for h in range(heads):
            dq_lat += head_lanes(dq_all[2 * LAT * h : 2 * LAT * h + LAT], h)
        dq_far[lat_at, :] = dq_lat

    dq, dk, dv = (jnp.concatenate(v, 0) for v in (dqs, dks, dvs))
    total = dot(dq, w[0], 1, 0) + dot(dk, w[1], 1, 0) + dot(dv, w[2], 1, 0)
    for i, g in enumerate((dq, dk, dv)):
        grad_w[i] += dot(g, rows, 0, 0)
    bias[0:1, :] += jnp.sum(dq.astype(F32), 0, keepdims=True)
    bias[1:2, :] += jnp.sum(dv.astype(F32), 0, keepdims=True)
    bias[2:3, :] += jnp.sum(dk.astype(F32), 0, keepdims=True)
    return total.astype(BF)


def backward_rows(
    first, begin, meta, count, normed, q, k, v, ql, kl, vl, log, far, logs_far, d_in, d_lat, w, gw_in, bias_in, *outs,
):
    step = pl.program_id(0)
    parts, (grad_w, bias, dq_far, dk_near, dv_near) = outs[:-5], outs[-5:]

    @pl.when(step == 0)
    def _():
        grad_w[...] = jnp.zeros_like(grad_w) if begin else gw_in[...]
        bias[...] = jnp.zeros_like(bias) if begin else bias_in[...]

    total = near_slot(
        step + first, meta, count, normed, q, k, v, ql, kl, vl, log, far, logs_far, d_in, d_lat, w, grad_w, bias,
        dq_far, dk_near, dv_near,
    )
    for slot, ref in enumerate(parts):

        @pl.when(step == slot)
        def _(ref=ref):
            ref[...] = total


def latent_bundle(d_near, d_far, far, logs_far, own, sent):
    count, wide = far.shape
    heads = wide // HEAD
    n = count // 4
    d32 = jnp.concatenate([d_near[...], d_far[...]], 0).astype(F32)
    prod = d32 * far[...].astype(F32)
    lg = logs_far[...].astype(F32)
    deltas = [split3(jnp.sum(head_lanes(prod, h), 1, keepdims=True)) for h in range(heads)]
    cols = [lg[:, i : i + 1] for i in range(3 * heads)] + [p[i].astype(F32) for i in (0, 1) for p in deltas]
    lane = lax.broadcasted_iota(jnp.int32, (count, 4 * HEAD), 1)
    value = jnp.concatenate([d32, jnp.zeros((count, HEAD), F32)], 1)
    for i, c in enumerate(cols):
        value = jnp.where(lane == wide + i, c, value)
    value = value.astype(BF)
    own[...] = value
    for i, s in enumerate(SENT):
        sent[i * n : (i + 1) * n, :] = value[s * n : (s + 1) * n]


def backward_far(
    meta, tokens_real, image, qa, ka, va, ql, kl, vl, own, bundle, normed, w, gw, bias_in, wo_a, wo_b,
    params, stats1, stats2, hid_first, hid_near, hid_away, *refs,
):
    near, (lat_keep, lat_send, p0, p1, p2, p3, small, pack, out_sems) = refs[:-9], refs[-9:]
    count, wide = ql.shape
    heads = wide // HEAD
    groups = count // LAT
    q_all, k_all, v_all = qa[...] * jnp.asarray(0.125, BF), ka[...], va[...]
    q_own, k_own, v_own = (ql[...] * 0.125).astype(BF), kl[...].astype(BF), vl[...].astype(BF)
    d_own, d_all = own[:, 0:wide], bundle[:, 0:wide]

    def stats(ref, h):
        x = ref[...].astype(F32)
        col = [x[:, wide + i : wide + i + 1] for i in range(5 * heads)]
        return col[h] + col[heads + h] + col[2 * heads + h], col[3 * heads + h] + col[4 * heads + h]

    mine = image_list(meta, image, 1, groups, OWN)
    images = image_list(meta, image, qa.shape[0] // count, groups, SENT)
    mask_q = image_column(mine) == image_row(images)
    mask_k = image_column(images) == image_row(mine)
    each = len(near) // 3
    dq, dk, dv = (jnp.concatenate([ref[...] for ref in near[i * each : (i + 1) * each]], 0) for i in range(3))
    for h in range(heads):
        log, delta = stats(own, h)
        s = dot(head_lanes(q_own, h), k_all, 1, 1)
        p = jnp.where(mask_q, jnp.exp(s - log), 0.0)
        g = (p * (dot(head_lanes(d_own, h), v_all, 1, 1) - delta)).astype(BF)
        dq += head_lanes(dot(g, k_all, 1, 0), h)
        log, delta = stats(bundle, h)
        s = dot(q_all, head_lanes(k_own, h), 1, 1)
        p = jnp.where(mask_k, jnp.exp(s - log), 0.0)
        g = (p * (dot(d_all, head_lanes(v_own, h), 1, 1) - delta)).astype(BF)
        dk += head_lanes(dot(g, q_all, 0, 0), h)
        dv += head_lanes(dot(p.astype(BF), d_all, 0, 0), h)
    dq, dk, dv = (dq * 0.125).astype(BF), dk.astype(BF), dv.astype(BF)
    lat_rows = normed[...]
    sums = [bias_in[i : i + 1, :] for i in (0, 2, 1)]
    sums = [b + jnp.sum(g.astype(F32), 0, keepdims=True) for b, g in zip(sums, (dq, dk, dv))]
    columns = jnp.concatenate(sums + [jnp.zeros((5, wide), F32)], 0).T
    first_gain = jnp.zeros((1, pack.shape[1]), F32)
    first_shift = first_gain
    for i, g in enumerate((dq, dk, dv)):
        total = gw[i] + dot(g, lat_rows, 0, 0)
        pack[i * wide : (i + 1) * wide, :] = total.astype(BF)
        col, weight = columns[:, i : i + 1], w[i].astype(F32)
        first_shift += jnp.sum(weight * col, 0, keepdims=True)
        first_gain += jnp.sum(weight * (total - col * param(params, SHIFT1)), 0, keepdims=True)
    first_gain = first_gain / param(params, GAIN1)
    pack[3 * wide :, :] = (wo_a[...].astype(F32) + wo_b[...].astype(F32)).astype(BF)
    x, z = sides(meta)
    flush = mover(out_sems)
    copies = []
    for ref, (dx, dz) in zip((p0, p1, p2, p3), ((0, 0), (1, 0), (0, 1), (1, 1))):
        part = (x ^ dx) * 2 + (z ^ dz)
        at = 0
        for base, size in ((0, 3 * wide // 4), (3 * wide, wide // 4)):
            src = pack.at[pl.ds(pl.multiple_of(base + part * size, 16), size)]
            copies.append(flush(src, ref.at[at : at + size]))
            at += size
    rows = (dot(dq, w[0], 1, 0) + dot(dk, w[1], 1, 0) + dot(dv, w[2], 1, 0)).astype(BF)
    n = count // 4
    lat_keep[0:n, :], lat_keep[n : 2 * n, :] = rows[0:n], rows[2 * n : 3 * n]
    lat_send[0:n, :], lat_send[n : 2 * n, :] = rows[n : 2 * n], rows[3 * n :]
    small[...] = jnp.zeros_like(small)
    small[0:1, :] = stats1[0:1, :]
    small[1:7, :] = stats2[0:6, :]
    small[7:8, :], small[8:9, :] = first_gain, first_shift
    real = tokens_real[0]
    for i in range(1, tokens_real.shape[0]):
        real = real + tokens_real[i]
    for at, part in ((9, real - real % 64), (22, real % 64)):
        small[at : at + 1, :] = jnp.full((1, small.shape[1]), 0.25, F32) * part.astype(F32)
    for s, row in ((0, hid_first[0:1, :] + hid_near[0:1, :]), (2, hid_away[0:1, :])):
        small[pl.ds(10 + (meta[1] ^ s), 1), :] = row
    small[pl.ds(14 + meta[1], 1), 0:wide] = sums[0]
    small[pl.ds(18 + meta[1], 1), 0:wide] = sums[2]
    for copy in copies:
        copy.wait()


def final_rows(meta, tok, lat, a, b, c, la, lb, grad_res, params, out):
    n, m = tok.shape[0], lat.shape[0]
    for x, at, terms in ((tok, slice(0, n), (a, b)), (lat, slice(n, n + m), (la, lb))):
        grad = c[at, :].astype(F32)
        for term in terms:
            grad += term[0 : x.shape[0], :].astype(F32)
        unit, inverse = norm_parts(x[...].astype(F32))
        out[at, :] = (grad_res[at, :] + norm_back(grad, unit, inverse, param(params, GAIN1))).astype(BF)


def place_rows(meta, a, b, c, d, tok_out, lat_out):
    n = tok_out.shape[0]
    for i, ref in enumerate((a, b, c, d)):

        @pl.when(pl.program_id(0) == i)
        def _(ref=ref):
            tok_out[...] = ref[0:n, :]
            lat_out[...] = ref[n:, :]


def after(v, *deps):
    return lax.optimization_barrier((v,) + deps)[0]


def make(mesh):
    dp_size, mp_size = mesh.shape["dp"], mesh.shape["mp"]
    assert mp_size == 4 and dp_size >= 4
    dp_bits = [1 << i for i in range(dp_size.bit_length() - 1)]
    assert 1 << len(dp_bits) == dp_size
    x_bit, z_bit, rest_bits = dp_bits[0], dp_bits[1], dp_bits[2:]

    def swap(v, dp_bit, mp_bit):
        pairs = [
            (d * mp_size + m, (d ^ dp_bit) * mp_size + (m ^ mp_bit))
            for d in range(dp_size)
            for m in range(mp_size)
        ]
        return lax.ppermute(v, ("dp", "mp"), pairs)

    def per_device(
        tokens,
        latents,
        image_of_group,
        token_valid,
        norm1_gain,
        norm1_shift,
        w_qkv,
        b_qv,
        w_out,
        b_out,
        norm2_gain,
        norm2_shift,
        w_up,
        b_up,
        w_down,
        b_down,
        cot_tokens,
        cot_latents,
    ):
        dp_at, mp_at = lax.axis_index("dp"), lax.axis_index("mp")
        tok_count, width = tokens.shape
        lat_count = latents.shape[0]
        groups = lat_count // LAT
        wide = w_qkv.shape[2]
        hidden = w_up.shape[1]
        tok_own, lat_own = tok_count // 4, lat_count // 4
        rows_own = tok_own + lat_own
        all_lat = dp_size * lat_count
        meta = jnp.stack([dp_at, mp_at]).astype(jnp.int32)
        count = jnp.sum(token_valid.reshape(groups, GROUP), 1).astype(jnp.int32)
        par = whole((8, width))
        w_t = jnp.transpose(w_qkv, (0, 2, 1))
        w_all = (3, wide, width)
        quarter, small = width // 4, wide // 4
        half = 2 * quarter
        big = (rows_own, width)
        chip_rows, chip_tok, chip_lat = 2 * rows_own, 2 * tok_own, 2 * lat_own
        vec = pl.BlockSpec((width,), lambda *_: (0,))

        def out(shape, kind=BF):
            return (shape, kind, whole(shape))

        def kept_out(shape, kind=BF):
            return (shape, kind, kept(shape))

        def any_out(shape, kind=BF):
            return (shape, kind, ANY)

        def dma(n):
            return pltpu.SemaphoreType.DMA((n,))

        def cube(v, vx=None, vz=None, vxz=None):
            vx, vz, vxz = (v if w is None else w for w in (vx, vz, vxz))
            return swap(vx, x_bit, 0), swap(vz, z_bit, 0), swap(vxz, x_bit | z_bit, 0)

        def all_latents(v):
            v = jnp.concatenate((v,) + cube(v), 0)
            for bit in rest_bits:
                v = jnp.concatenate([v, swap(v, bit, 0)], 0)
            return v

        part_block = pl.BlockSpec((quarter, width), lambda i, meta: ((meta[0] & 1) * 2 + ((meta[0] >> 1) & 1), 0))
        lat_rel, lat_half, o0, weight_part, params = call(
            prepare,
            name="prepare",
            scalars=1,
            ins=[whole((lat_count, width)), whole((wide, width))] + [vec] * 7 + [part_block, part_block],
            outs=[out((lat_count, width)), out((chip_lat, width)), out((wide + 16, width)), out((half, width)), out((8, width), F32)],
            us=2,
        )(meta, latents, w_out, norm1_gain, norm1_shift, b_out, norm2_gain, norm2_shift, b_down, b_up, w_up, w_down)
        lat_four = jnp.concatenate((lat_half,) + cube(lat_half), 0)
        w_own = swap(weight_part, 0, 2)
        o2 = swap(o0, 0, 2)

        normed_lat, ql, kl, vl = call(
            latent_rows,
            name="latent_rows",
            scalars=0,
            ins=[whole((lat_count, width)), par, whole(w_all), whole((2, wide))],
            outs=[out((lat_count, width))] + [out((lat_count, wide), F32)] * 3,
            us=2,
        )(lat_rel, params, w_t, b_qv)

        def cot_through(slot, meta):
            return call(
                cot_back,
                name="cot_back",
                scalars=1,
                ins=[
                    pl.BlockSpec((tok_own, width), lambda i, meta: (meta[1] ^ slot, 0), pipeline_mode=pl.Buffered(1)),
                    pl.BlockSpec((lat_own, width), lambda i, meta: (meta[1] ^ slot, 0), pipeline_mode=pl.Buffered(1)),
                    whole((hidden, width)),
                ],
                outs=[out((rows_own, hidden))],
                us=4,
            )(meta, cot_tokens, cot_latents, w_down)[0]

        cot_own = cot_through(0, after(meta, kl))
        lat_here = lat_four = after(lat_four, cot_own)
        for bit in rest_bits:
            lat_here = jnp.concatenate([lat_here, swap(lat_here, bit, 0)], 0)

        def near_forward(base, *deps):
            def run(*args):
                return forward_near(base, *args)

            rows = lambda wide_here: pl.BlockSpec((tok_own, wide_here), lambda i, *_: (i, 0))
            lat_block = pl.BlockSpec((lat_own, wide), lambda i, *_: (i + base, 0))
            each = groups // 4
            return call(
                run,
                name="forward_near",
                grid=(2,),
                scalars=2,
                ins=[
                    pl.BlockSpec((tok_own, width), lambda i, meta, _: (meta[1] ^ (i + base), 0)),
                    lat_block,
                    lat_block,
                    par,
                    whole(w_all),
                    whole((2, wide)),
                ],
                outs=[((chip_tok, width), BF, rows(width))]
                + [((chip_tok, wide), BF, rows(wide))] * 3
                + [((wide, chip_tok), BF, pl.BlockSpec((wide, tok_own), lambda i, *_: (0, i)))]
                + [((2 * each, 8, GROUP), F32, pl.BlockSpec((each, 8, GROUP), lambda i, *_: (i, 0, 0)))],
                us=8,
            )(meta, count, tokens, after(kl, *deps), vl, params, w_t, b_qv)

        normed_b, q_b, k_b, v_b, t_b, log_b = near_forward(2, lat_four)
        t_far = swap(t_b, 0, 2)
        lat_here = after(lat_here, t_b)
        normed_a, q_a, k_a, v_a, t_near, log_a = near_forward(0, lat_here)
        w_x, w_z, w_xz = cube(after(w_own, t_near))
        lat_all = [v.reshape(dp_size, chip_lat, width) for v in (lat_here, swap(lat_here, 0, 1))]
        lat_all = jnp.concatenate(lat_all, 1).reshape(all_lat, width)
        lat_all = after(lat_all, t_near)

        chunk = min(512, all_lat)
        qa, ka, va, l_near, l_b, far, far_logs = call(
            forward_far,
            name="forward_far",
            grid=(all_lat // chunk,),
            scalars=3,
            ins=[pl.BlockSpec((chunk, width), lambda i, *_: (i, 0)), par, whole(w_all), whole((2, wide))]
            + [whole((chip_tok, wide))] * 4
            + [whole((lat_count, wide))],
            outs=[out((all_lat, wide))] * 3
            + [kept_out((chip_lat, wide))] * 2
            + [kept_out((lat_count, wide)), kept_out((lat_count, 2 * HEAD))],
            us=6,
        )(meta, count, image_of_group, lat_all, params, w_t, b_qv, k_a, k_b, v_a, v_b, ql)
        l_far = swap(l_b, 0, 2)

        out_pack = whole((wide + 16, width))
        mixed_specs = [whole((wide, chip_tok))] * 2 + [whole((chip_lat, wide))] * 2
        cot_sib = cot_through(1, after(meta, far))

        def out_rows_of(slot, kind, o0):
            return call(
                project_out,
                name="project_out",
                scalars=0,
                ins=[pl.BlockSpec((wide, tok_own), lambda *_: (0, slot), pipeline_mode=pl.Buffered(1))] * 2
                + [pl.BlockSpec((lat_own, wide), lambda *_: (slot, 0), pipeline_mode=pl.Buffered(1))] * 2
                + [out_pack] * 2,
                outs=[out(big, kind)],
                us=3,
            )(t_near, t_far, l_near, l_far, o0, o2)[0]

        attn_send = out_rows_of(1, BF, after(o0, cot_sib))
        attn_own = out_rows_of(0, F32, after(o0, attn_send))
        attn_got = swap(attn_send, 0, 1)
        own_tok = pl.BlockSpec((tok_own, width), lambda i, meta, _: (meta[1], 0), pipeline_mode=pl.Buffered(1))
        own_lat = pl.BlockSpec((lat_own, width), lambda i, meta, _: (meta[1], 0), pipeline_mode=pl.Buffered(1))
        residual, n2, stats1 = call(
            add_norm,
            name="add_norm",
            scalars=2,
            ins=[par, whole(big), whole(big), own_tok, whole((lat_own, width))],
            outs=[out(big, F32), out(big), out((8, width), F32)],
            us=3,
        )(meta, count, params, attn_own, attn_got, tokens, lat_rel)
        n2_sib = swap(n2, 0, 1)

        chip = (chip_rows, width)
        piece = (half, width)
        vm = pltpu.VMEM
        act_first, grad_first, bias_first = call(
            hidden_first,
            name="hidden_first",
            scalars=0,
            ins=[par, whole(big), whole((width, hidden)), whole((rows_own, hidden))],
            outs=[out((rows_own, hidden))] * 2 + [out((8, hidden), F32)],
            us=4,
        )(params, n2, w_up, cot_own)
        branch, back, a0, a1, a2, a3, bias_near = call(
            hidden_own,
            name="hidden_own",
            scalars=1,
            ins=[par] + [ANY] * 9,
            outs=[any_out(chip, F32), any_out(chip, F32)] + [any_out(piece)] * 4 + [out((8, hidden), F32)],
            scratch=[
                vm(chip, BF),
                vm(chip, BF),
                vm((2, width, hidden), BF),
                vm(chip, F32),
                vm(chip, F32),
                vm((chip_rows, hidden), BF),
                vm((chip_rows, hidden), BF),
                vm((rows_own, hidden), BF),
                vm((width + hidden, width), BF),
                dma(11),
                dma(10),
            ],
            us=12,
        )(meta, params, n2, n2_sib, cot_tokens, cot_latents, w_up, w_down, cot_sib, act_first, grad_first)
        near_parts = (a0,) + cube(None, a1, a2, a3)

        branch, back, middle_send, act, grad, bias_away = call(
            hidden_away,
            name="hidden_away",
            scalars=1,
            ins=[out_pack] + [ANY] * 10,
            outs=[any_out(big, F32), any_out(big, F32), any_out(chip), any_out((chip_rows, hidden)), any_out((chip_rows, hidden))]
            + [out((8, hidden), F32)],
            scratch=[
                vm(chip, BF),
                vm(chip, BF),
                vm((2, width, hidden), BF),
                vm(chip, F32),
                vm(chip, F32),
                vm((chip_rows, hidden), BF),
                vm((chip_rows, hidden), BF),
                vm(chip, BF),
                dma(16),
                dma(6),
            ],
            us=10,
        )(meta, o2, n2, n2_sib, cot_tokens, cot_latents, w_own, w_x, w_z, w_xz, branch, back)
        middle_got = swap(middle_send, 0, 1)

        b0, b1, b2, b3 = call(
            away_grads,
            name="away_grads",
            scalars=1,
            ins=[ANY] * 6,
            outs=[any_out(piece)] * 4,
            scratch=[
                vm(chip, BF),
                vm(chip, BF),
                vm((chip_rows, hidden), BF),
                vm((chip_rows, hidden), BF),
                vm((width + hidden, width), BF),
                dma(8),
                dma(8),
            ],
            us=6,
        )(meta, n2, n2_sib, cot_tokens, cot_latents, act, grad)

        out_rows, grad_res, grad_attn, stats2 = call(
            middle_rows,
            name="middle_rows",
            scalars=2,
            ins=[par, whole(big), whole(big), whole(big), whole(chip), own_tok, own_lat],
            outs=[out(big), out(big, F32), out(big), out((8, width), F32)],
            us=5,
            deps=(b0,),
        )(meta, count, params, residual, branch, back, middle_got, cot_tokens, cot_latents)
        grad_attn_sib = swap(grad_attn, 0, 1)

        def terms(n, at=0):
            return [(i, at) for i in range(n)]

        sides4 = ((0, 0), (1, 0), (0, 1), (1, 1))

        def at(d, size, base=0):
            return lambda x, z: base + ((x ^ d[0]) * 2 + (z ^ d[1])) * size


        (near_sum,) = combine("near_sum", meta, near_parts, [(half, BF, [(0, half, terms(4))])], us=2)
        away_parts = (b0,) + cube(None, *(after(v, near_sum) for v in (b1, b2, b3)))

        g_near, g_send, d_near, d_send, out_grad, out_grad_send = call(
            back_out,
            name="back_out",
            scalars=0,
            ins=[whole(big), whole(big), out_pack, out_pack] + mixed_specs,
            outs=[out((wide, chip_tok))] * 2 + [out((chip_lat, wide))] * 2 + [out((wide, width))] * 2,
            us=4,
            deps=(near_sum,),
        )(grad_attn, grad_attn_sib, o0, o2, t_near, t_far, l_near, l_far)
        d_far = swap(d_send, 0, 2)
        g_far = swap(g_send, 0, 2)
        out_grad_got = swap(after(out_grad_send, g_far), 0, 2)

        zero_w, zero_b = jnp.zeros((8, LANES), F32), jnp.zeros((8, LANES), F32)

        def rows_backward(first, steps, half_in, g, d, gw, bias, *deps):
            normed, q, k, v, log = half_in
            base = first % 2

            def rows(n, wide_here, shift):
                return pl.BlockSpec((n, wide_here), lambda i, *_: (i + shift, 0))

            def run(*args):
                return backward_rows(first, gw is None, *args)

            init = (zero_w, zero_b) if gw is None else (gw, bias)
            return call(
                run,
                name="backward_rows",
                grid=(steps,),
                scalars=2,
                ins=[
                    rows(tok_own, width, base),
                    *[rows(tok_own, wide, base)] * 3,
                    *[rows(lat_own, wide, first)] * 3,
                    pl.BlockSpec((groups // 4, 8, GROUP), lambda i, *_: (i + base, 0, 0)),
                    rows(lat_own, wide, first),
                    rows(lat_own, 2 * HEAD, first),
                    pl.BlockSpec((wide, tok_own), lambda i, *_: (0, i + base)),
                    rows(lat_own, wide, base),
                    whole(w_all),
                    whole(init[0].shape),
                    whole(init[1].shape),
                ],
                outs=[kept_out((tok_own, width))] * steps
                + [kept_out(w_all, F32), kept_out((8, wide), F32)]
                + [((steps * lat_own, wide), F32, rows(lat_own, wide, 0))] * 3,
                us=7 * steps,
                deps=deps,
            )(meta, count, normed, q, k, v, ql, kl, vl, log, far, far_logs, g, d, w_t, *init)

        half_a, half_b = (normed_a, q_a, k_a, v_a, log_a), (normed_b, q_b, k_b, v_b, log_b)
        part0, gw, bias, *near_0 = rows_backward(0, 1, half_a, g_near, d_near, None, None)
        bundle_own, bundle = call(
            latent_bundle,
            name="latent_bundle",
            scalars=0,
            ins=[whole((chip_lat, wide))] * 2 + [whole((lat_count, wide)), whole((lat_count, 2 * HEAD))],
            outs=[out((lat_count, 4 * HEAD))] * 2,
            us=2,
            deps=(part0,),
        )(d_near, d_far, far, far_logs)
        steps = [bundle]

        def spread(bit):
            got = swap(steps[0], bit, 0)
            return lambda done: steps.__setitem__(0, jnp.concatenate([after(steps[0], done), got], 0))

        join = spread(x_bit)
        part1, gw, bias, *near_1 = rows_backward(1, 1, half_a, g_near, d_near, gw, bias, bundle_own)
        got1 = swap(part1, 0, 1)
        join(part1)
        join = spread(z_bit)
        part3, gw, bias, *near_3 = rows_backward(3, 1, half_b, g_far, d_far, gw, bias)
        join(part3)
        for bit in rest_bits[:-1]:
            spread(bit)(part3)
        join = spread(rest_bits[-1]) if rest_bits else None
        (away_sum,) = combine("away_sum", meta, away_parts, [(half, BF, [(0, half, terms(4))])], us=2, deps=(part3,))
        away_got = swap(away_sum, 0, 2)
        got3 = swap(part3, 0, 1)
        part2, gw, bias, *near_2 = rows_backward(2, 1, half_b, g_far, d_far, gw, bias, away_sum)
        if rest_bits:
            join(part2)
        bundle = steps[0]
        near_all = [v for three in zip(near_0, near_1, near_2, near_3) for v in three]
        shard = (small * 4, width)
        lat_keep, lat_send, c0, c1, c2, c3, small_rows = call(
            backward_far,
            name="backward_far",
            scalars=3,
            ins=[whole((all_lat, wide))] * 3
            + [whole((lat_count, wide))] * 3
            + [whole((lat_count, 4 * HEAD)), whole((all_lat, 4 * HEAD)), whole((lat_count, width)), whole(w_all), whole(w_all)]
            + [whole((8, wide))]
            + [whole((wide, width))] * 2
            + [par]
            + [whole((8, width))] * 5
            + [whole(v.shape) for v in near_all],
            outs=[out((chip_lat, width))] * 2 + [any_out(shard)] * 4 + [out((32, width), F32)],
            scratch=[vm((4 * wide, width), BF), dma(8)],
            us=8,
        )(
            meta, count, image_of_group, qa, ka, va, ql, kl, vl, bundle_own, bundle, normed_lat, w_t, gw, bias, out_grad,
            out_grad_got, params, stats1, stats2, bias_first, bias_near, bias_away, *near_all,
        )

        lat_got = swap(lat_send, 0, 1)
        (total,) = combine(
            "weights_sum", meta, [near_sum, away_got], [(half, BF, [(0, half, terms(2))])], us=20, deps=(lat_keep,)
        )
        (there,) = combine(
            "rows_sum", meta, [part2, got3, lat_keep, lat_got],
            [(rows_own, BF, [(0, tok_own, terms(2)), (tok_own, lat_own, [(2, lat_own), (3, lat_own)])])],
            us=2, deps=(total,),
        )
        from_y = swap(there, 0, 2)
        small_rows = small_rows + swap(small_rows, 0, 1)
        small_got = swap(small_rows, 0, 2)
        rows4 = 4 * small
        qkv_parts = (c0,) + cube(None, c1, c2, c3)
        (qkv,) = combine(
            "qkv_sum", meta, qkv_parts + (small_rows, small_got),
            [(rows4 + 32, BF, [(0, rows4, terms(4)), (rows4, 32, [(4, 0), (5, 0)])])],
            us=2, deps=(there,),
        )
        (grad_rows,) = call(
            final_rows,
            name="final_rows",
            scalars=1,
            ins=[
                pl.BlockSpec((tok_own, width), lambda i, meta: (meta[1], 0), pipeline_mode=pl.Buffered(1)),
                whole((lat_own, width)),
                *[whole((tok_own, width))] * 2,
                whole(big),
                *[whole((chip_lat, width))] * 2,
                whole(big),
                par,
            ],
            outs=[out(big)],
            us=4,
            deps=(qkv,),
        )(meta, tokens, lat_rel, part0, got1, from_y, lat_keep, lat_got, grad_res, params)

        out_y = swap(after(out_rows, there), 0, 2)
        grad_y = swap(grad_rows, 0, 2)
        for bit in rest_bits:
            (total,) = combine(
                "rest_sum", meta, [total, swap(total, bit, 0)], [(half, BF, [(0, half, terms(2))])], us=2,
                deps=(grad_rows,),
            )
        four = (total,) + cube(total)
        grad_w_up, grad_w_down = combine(
            "weights_out", meta, four,
            [
                (4 * quarter, F32, [(at(d, quarter), quarter, [(i, r * quarter)]) for i, d in enumerate(sides4)])
                for r in (0, 1)
            ]
            ,
            us=5,
            deps=(grad_y, qkv,),
        )
        for bit in rest_bits:
            (qkv,) = combine("qkv_rest", meta, [qkv, swap(qkv, bit, 0)], [(rows4 + 32, BF, [(0, rows4 + 32, terms(2))])], us=2, deps=(total, total))
        four = (qkv,) + cube(after(qkv, *four[1:]))
        grad_w_qkv, grad_w_out, small_rows = combine(
            "qkv_out", meta, four,
            [
                (3 * wide, F32, [(at(d, 3 * small), 3 * small, [(i, 0)]) for i, d in enumerate(sides4)]),
                (wide, F32, [(at(d, small), small, [(i, 3 * small)]) for i, d in enumerate(sides4)]),
                (32, F32, [(0, 32, terms(4, rows4))]),
            ],
            us=3,
        )
        grad_w_qkv = grad_w_qkv.reshape(3, wide, width).transpose(0, 2, 1)

        def all_rows(v, v_y):
            v_c, v_yc = swap(v, 0, 1), swap(v_y, 0, 1)
            place = lambda n: pl.BlockSpec((n, width), lambda i, meta: (meta[1] ^ i, 0))
            return call(
                place_rows,
                name="place_rows",
                grid=(4,),
                scalars=1,
                ins=[whole(big)] * 4,
                outs=[((tok_count, width), BF, place(tok_own)), ((lat_count, width), BF, place(lat_own))],
                us=4,
            )(meta, v, v_c, v_y, v_yc)

        grad_tok, grad_lat = all_rows(grad_rows, grad_y)
        out_tok, out_lat = all_rows(out_rows, out_y)

        squares = jnp.sum(jnp.stack([small_rows[1], small_rows[0], small_rows[2]]), 1)
        root_means = jnp.sqrt(squares / ((small_rows[9, 0] + small_rows[22, 0]) * width))
        grad_b_qv = jnp.stack([small_rows[14 + 4 * i : 18 + 4 * i, :wide] for i in (0, 1)])
        grad_b_qv = lax.dynamic_index_in_dim(grad_b_qv, mp_at, 1, keepdims=False)
        grad_b_up = lax.dynamic_index_in_dim(small_rows[10:14], mp_at, 0, keepdims=False)
        return (
            out_tok,
            out_lat,
            grad_tok,
            grad_lat,
            small_rows[7],
            small_rows[8],
            grad_w_qkv,
            grad_b_qv,
            grad_w_out,
            small_rows[5],
            small_rows[3],
            small_rows[4],
            grad_w_up,
            grad_b_up,
            grad_w_down,
            small_rows[6],
            root_means,
        )

    return per_device


def solution(mesh):
    rows, whole = P("dp", None), P()
    return jax.shard_map(
        make(mesh),
        mesh=mesh,
        in_specs=(
            rows,
            rows,
            whole,
            P("dp"),
            whole,
            whole,
            P(None, None, "mp"),
            P(None, "mp"),
            P("mp", None),
            whole,
            whole,
            whole,
            P(None, "mp"),
            P("mp"),
            P("mp", None),
            whole,
            rows,
            rows,
        ),
        out_specs=(
            rows,
            rows,
            rows,
            rows,
            whole,
            whole,
            P(None, None, "mp"),
            P(None, "mp"),
            P("mp", None),
            whole,
            whole,
            whole,
            P(None, "mp"),
            P("mp"),
            P("mp", None),
            whole,
            whole,
        ),
        check_vma=False,
    )
```

```python
import jax
import jax.numpy as jnp
from jax import lax
from jax.experimental import pallas as pl
from jax.experimental.pallas import tpu as pltpu
from jax.sharding import PartitionSpec as P

HEAD = 64
LANES = 128
GROUP = 256
LAT = 8
BF = jnp.bfloat16
F32 = jnp.float32
FAR = -1e30
MIB = 1 << 20
GAIN1, SHIFT1, B_OUT, GAIN2, SHIFT2, B_DOWN, B_UP = range(7)


def dot(a, b, ca, cb):
    return lax.dot_general(a, b, (((ca,), (cb,)), ((), ())), preferred_element_type=F32)


def norm_parts(values):
    center = values - jnp.mean(values, axis=-1, keepdims=True)
    spread = jnp.mean(center * center, axis=-1, keepdims=True)
    inverse = lax.rsqrt(spread + 1e-06)
    return center * inverse, inverse


def norm_back(grad, unit, inverse, gain):
    scaled = grad * gain
    inner = jnp.mean(scaled * unit, axis=-1, keepdims=True)
    return inverse * (scaled - jnp.mean(scaled, axis=-1, keepdims=True) - unit * inner)


def gelu_both(values):
    square = values * values
    inner = jnp.tanh(values * (0.7978845608028654 + 0.035677408136300125 * square))
    half = 0.5 + 0.5 * inner
    slope = values * (0.3989422804014327 + 0.05351611220494518 * square)
    return values * half, half + (1.0 - inner * inner) * slope


def split3(v):
    hi = v.astype(BF)
    mid = (v - hi.astype(F32)).astype(BF)
    low = (v - hi.astype(F32) - mid.astype(F32)).astype(BF)
    return hi, mid, low


def head_lanes(v, h):
    lane = lax.broadcasted_iota(jnp.int32, v.shape, v.ndim - 1)
    return jnp.where((lane >= h * HEAD) & (lane < (h + 1) * HEAD), v, jnp.zeros_like(v))


def kept(shape):
    return pl.BlockSpec(shape, lambda *_: (0,) * len(shape))


def whole(shape):
    return pl.BlockSpec(shape, lambda *_: (0,) * len(shape), pipeline_mode=pl.Buffered(1))


ANY = pl.BlockSpec(memory_space=pl.ANY)
OWN, SENT = (0, 1, 2, 3), (0, 2, 1, 3)


def block_bytes(shape, kind, copies):
    size = jnp.dtype(kind).itemsize
    dims = [1, 1] + list(shape)
    rows, lanes = 32 // size, LANES
    dims[-1] = -(-dims[-1] // lanes) * lanes
    dims[-2] = -(-dims[-2] // rows) * rows
    total = size * copies
    for d in dims:
        total *= d
    return total


def spec_bytes(spec, kind):
    if spec.block_shape is None:
        return 0
    return block_bytes(spec.block_shape, kind, 1 if spec.pipeline_mode is not None else 2)


def call(body, *, name, scalars, ins, outs, grid=(1,), scratch=(), deps=(), us=1.0, room=3):
    first, extra = scalars + len(ins), len(deps)

    def wrapped(*refs):
        body(*refs[:first], *refs[first + extra :])

    def run(*args):
        need = room * MIB + sum(spec_bytes(spec, kind) for _, kind, spec in outs)
        need += sum(spec_bytes(spec, a.dtype) for spec, a in zip(ins, args[scalars:]))
        need += sum(block_bytes(s.shape, s.dtype, 1) for s in scratch if s.shape and len(s.shape) > 1)
        return pl.pallas_call(
            wrapped,
            name=name,
            out_shape=[jax.ShapeDtypeStruct(s, d) for s, d, _ in outs],
            grid_spec=pltpu.PrefetchScalarGridSpec(
                num_scalar_prefetch=scalars,
                grid=grid,
                in_specs=list(ins) + [ANY] * extra,
                out_specs=[spec for _, _, spec in outs],
                scratch_shapes=list(scratch),
            ),
            compiler_params=pltpu.CompilerParams(
                dimension_semantics=("arbitrary",) * len(grid), vmem_limit_bytes=max(need, 20 * MIB)
            ),
            cost_estimate=pl.CostEstimate(
                flops=int(us * 1.0e10), bytes_accessed=1 << 16, transcendentals=0
            ),
        )(*args, *deps)

    return run


def mover(sems):
    used = []

    def start(src, dst):
        copy = pltpu.make_async_copy(src, dst, sems.at[len(used)])
        used.append(copy)
        copy.start()
        return copy

    return start


def sides(meta):
    return meta[0] & 1, (meta[0] >> 1) & 1


def combine(name, meta, arrays, outs, deps=(), us=1.0):
    def body(meta, *refs):
        x, z = sides(meta)

        def rows_at(at, n):
            return pl.ds(pl.multiple_of(at(x, z), 16), n) if callable(at) else slice(at, at + n)

        for ref, (_, kind, segments) in zip(refs[len(arrays) :], outs):
            for to, n, terms in segments:
                parts = [refs[i][rows_at(at, n), :] for i, at in terms]
                value = parts[0]
                if len(parts) > 1:
                    value = parts[0].astype(F32)
                    for part in parts[1:]:
                        value = value + part.astype(F32)
                ref[rows_at(to, n), :] = value.astype(kind)

    width = arrays[0].shape[1]
    return call(
        body,
        name=name,
        scalars=1,
        ins=[whole(a.shape) for a in arrays],
        outs=[((rows, width), kind, whole((rows, width))) for rows, kind, _ in outs],
        deps=deps,
        us=us,
    )(meta, *arrays)


def group_at(meta, count, slot, i):
    return count[(meta[1] ^ slot) * 2 + i]


def image_list(meta, image, devices, per_device, slots):
    each = per_device // 4
    return [
        image[(meta[0] ^ j) * per_device + (meta[1] ^ s) * each + i]
        for j in range(devices)
        for s in slots
        for i in range(each)
    ]


def image_column(images):
    return jnp.concatenate([jnp.full((LAT, 1), im, jnp.int32) for im in images], 0)


def image_row(images):
    group = lax.broadcasted_iota(jnp.int32, (1, len(images) * LAT), 1) // LAT
    out = jnp.zeros(group.shape, jnp.int32)
    for g, im in enumerate(images):
        out = jnp.where(group == g, im, out)
    return out


def key_stack(tok, lat8):
    pad = jnp.concatenate([lat8, jnp.zeros_like(lat8)], 0).astype(BF)
    return jnp.concatenate([tok, pad], 0)


def near_mask(count, columns):
    row = lax.broadcasted_iota(jnp.int32, (GROUP + 2 * LAT, columns), 0)
    return (row < count) | ((row >= GROUP) & (row < GROUP + LAT))


def param(params, i):
    return params[i : i + 1, :]


def project(rows, params, w, bias):
    unit, _ = norm_parts(rows.astype(F32))
    rows = (unit * param(params, GAIN1) + param(params, SHIFT1)).astype(BF)
    return (
        rows,
        (dot(rows, w[0], 1, 1) + bias[0:1]).astype(BF),
        dot(rows, w[1], 1, 1).astype(BF),
        (dot(rows, w[2], 1, 1) + bias[1:2]).astype(BF),
    )


def prepare(
    meta, lat, w_out, g1, s1, bo, g2, s2, bd, bu, up, down, lat_rel, lat_half, out_pack, part, params,
    vlat, vout, sems, *vecs,
):
    fetch = mover(sems)
    lat_copy = fetch(lat, vlat)
    copies = [fetch(ref, dst) for ref, dst in zip((g1, s1, bo, g2, s2, bd, bu), vecs)]
    x, z = sides(meta)
    n = part.shape[0] // 2
    here = pl.ds(pl.multiple_of((x * 2 + z) * n, 16), n)
    parts = [fetch(up.at[here], part.at[0:n]), fetch(down.at[here], part.at[n:])]
    wide = w_out.shape[0]
    parts.append(fetch(w_out, vout))
    lat_copy.wait()
    n = lat.shape[0] // 4
    for s in range(4):
        rows = vlat[pl.ds(pl.multiple_of((meta[1] ^ s) * n, 16), n), :]
        lat_rel[s * n : (s + 1) * n, :] = rows
        if s % 2 == 0:
            lat_half[s // 2 * n : (s // 2 + 1) * n, :] = rows
    for copy in copies:
        copy.wait()
    for i in range(7):
        params[i : i + 1, :] = vecs[i][...].reshape(1, params.shape[1])
    params[7:8, :] = jnp.zeros_like(params[7:8, :])
    bias = param(params, B_UP)
    rows = [v.astype(F32) for v in split3(bias)]
    out_pack[wide : wide + 16, :] = jnp.concatenate(rows + [jnp.zeros((13, bias.shape[1]), F32)], 0).astype(BF)
    for copy in parts:
        copy.wait()
    out_pack[0:wide, :] = vout[...]


def latent_rows(lat, params, w, bias, normed, ql, kl, vl):
    normed[...], a, b, c = project(lat[...], params, w, bias)
    ql[...], kl[...], vl[...] = a.astype(F32), b.astype(F32), c.astype(F32)


def forward_near(base, meta, count, tok, kl, vl, params, w, bias, normed, q, k, v, mixed_out, log):
    step = pl.program_id(0)
    wide = w.shape[1]
    rows, qs, ks, vs = project(tok[...], params, w, bias)
    normed[...], q[...], k[...], v[...] = rows, qs, ks, vs
    qs = qs * jnp.asarray(0.125, BF)
    for i in range(tok.shape[0] // GROUP):
        here = slice(i * LAT, (i + 1) * LAT)
        at = slice(i * GROUP, (i + 1) * GROUP)
        keys = key_stack(ks[at], kl[here, :])
        values = key_stack(vs[at], vl[here, :]).T
        mask = near_mask(group_at(meta, count, step + base, i), GROUP)
        logs, outs = [], []
        for h in range(wide // HEAD):
            s = jnp.where(mask, dot(head_lanes(keys, h), qs[at], 1, 1), FAR)
            top = jnp.max(s, 0, keepdims=True)
            e = jnp.exp(s - top)
            total = jnp.sum(e, 0, keepdims=True)
            logs.append(top + jnp.log(total))
            outs.append(dot(values[h * HEAD : (h + 1) * HEAD], e.astype(BF), 1, 0) * (1.0 / total))
        log[i] = jnp.concatenate(logs + [jnp.zeros((8 - len(logs), GROUP), F32)], 0)
        mixed_out[:, at] = jnp.concatenate(outs, 0).astype(BF)


def forward_far(meta, count, image, lat, params, w, bias, k_near, k_away, v_near, v_away, ql, qa, ka, va, m_near, m_away, far, logs_out):
    step = pl.program_id(0)
    wide = w.shape[1]
    rows_step = lat.shape[0]
    own = ql.shape[0]
    groups = own // LAT

    def rows_of(near, away, g):
        half = groups // 2
        ref, at = (near, g) if g < half else (away, g - half)
        return ref[at * GROUP : (at + 1) * GROUP, :]

    _, a, b, c = project(lat[...], params, w, bias)
    here = pl.ds(pl.multiple_of(step * rows_step, rows_step), rows_step)
    qa[here, :], ka[here, :], va[here, :] = a, b, c

    @pl.when(step == pl.num_programs(0) - 1)
    def _():
        q32 = ql[...] * 0.125
        images = image_list(meta, image, qa.shape[0] // own, groups, SENT)
        mask = image_column(image_list(meta, image, 1, groups, OWN)) == image_row(images)
        lane = lax.broadcasted_iota(jnp.int32, (LAT, GROUP), 1)
        full = jnp.zeros((own, wide), F32)
        logs = []
        for h in range(wide // HEAD):
            qh = head_lanes(q32, h)
            s_lat = jnp.where(mask, dot(qh.astype(BF), ka[...], 1, 1), FAR)
            s_tok = jnp.concatenate(
                [
                    jnp.where(
                        lane < group_at(meta, count, g // 2, g % 2),
                        dot(qh[g * LAT : (g + 1) * LAT].astype(BF), rows_of(k_near, k_away, g), 1, 1),
                        FAR,
                    )
                    for g in range(groups)
                ],
                0,
            )
            top = jnp.maximum(jnp.max(s_lat, 1, keepdims=True), jnp.max(s_tok, 1, keepdims=True))
            e_lat, e_tok = jnp.exp(s_lat - top), jnp.exp(s_tok - top)
            total = jnp.sum(e_lat, 1, keepdims=True) + jnp.sum(e_tok, 1, keepdims=True)
            logs.append(top + jnp.log(total))
            near = jnp.concatenate(
                [
                    dot(e_tok[g * LAT : (g + 1) * LAT].astype(BF), rows_of(v_near, v_away, g), 1, 0)
                    for g in range(groups)
                ],
                0,
            )
            full = full + head_lanes((dot(e_lat.astype(BF), va[...], 1, 0) + near) * (1.0 / total), h)
        mixed = full.astype(BF)
        m_near[...], m_away[...] = mixed[: own // 2], mixed[own // 2 :]
        parts = [split3(x) for x in logs]
        cols = [p[i] for i in range(3) for p in parts]
        lane = lax.broadcasted_iota(jnp.int32, (own, 2 * HEAD), 1)
        extra = jnp.zeros((own, 2 * HEAD), F32)
        for i, c in enumerate(cols):
            extra = jnp.where(lane == i, c.astype(F32), extra)
        far[...] = mixed
        logs_out[...] = extra.astype(BF)


def valid_rows(meta, count, rows):
    row = lax.broadcasted_iota(jnp.int32, (rows, 1), 0)
    first = (row < GROUP) & (row < group_at(meta, count, 0, 0))
    return first | ((row >= GROUP) & (row < GROUP + group_at(meta, count, 0, 1)))


def slot_block(meta, ref, slot):
    n = ref.shape[0] // 4
    return ref.at[pl.ds(pl.multiple_of((meta[1] ^ slot) * n, 16), n)]


def project_out(t_near, t_far, l_near, l_far, o0, o2, out):
    wide, n = t_near.shape
    value = dot(t_near[...], o0[0:wide, :], 0, 0) + dot(t_far[...], o2[0:wide, :], 0, 0)
    out[0:n, :] = value.astype(out.dtype)
    value = dot(l_near[...], o0[0:wide, :], 1, 0) + dot(l_far[...], o2[0:wide, :], 1, 0)
    out[n:, :] = value.astype(out.dtype)


def cot_back(meta, cot_tok, cot_lat, down_w, out):
    n = cot_tok.shape[0]
    out[0:n, :] = dot(cot_tok[...], down_w[...], 1, 1).astype(BF)
    out[n:, :] = dot(cot_lat[...], down_w[...], 1, 1).astype(BF)


def add_norm(meta, count, params, own, got, tok, lat, residual, n2, stats):
    n, m = tok.shape[0], lat.shape[0]
    stats[...] = jnp.zeros_like(stats)
    for at, size, x in ((0, n, tok), (n, m, lat)):
        rows = slice(at, at + size)
        attn = own[rows, :] + got[rows, :].astype(F32) + param(params, B_OUT)
        if at == 0:
            real = valid_rows(meta, count, n)
            stats[0:1, :] = jnp.sum(jnp.where(real, attn * attn, 0.0), 0, keepdims=True)
        res = x[...].astype(F32) + attn
        residual[rows, :] = res
        unit, _ = norm_parts(res)
        n2[rows, :] = (unit * param(params, GAIN2) + param(params, SHIFT2)).astype(BF)


def hidden_part(n2, cot, up_w, down_w, bias, act_out, grad_out):
    cut = 256
    sums = []
    for at in range(0, up_w.shape[1], cut):
        cols = slice(at, at + cut)
        up = dot(n2, up_w[:, cols], 1, 0) + bias[:, cols]
        active, slope = gelu_both(up)
        grad_up = (dot(cot, down_w[cols, :], 1, 1) * slope).astype(BF)
        act_out[:, cols] = active.astype(BF)
        grad_out[:, cols] = grad_up
        sums.append(jnp.sum(grad_up.astype(F32), 0, keepdims=True))
    return jnp.concatenate(sums, 1)


def two_halves(meta, fetch, n2_own, n2_sib, cot_tok, cot_lat, vn2, vcot):
    rows = n2_own.shape[0]
    n = cot_tok.shape[0] // 4
    copies = [fetch(n2_own, vn2.at[0:rows]), fetch(n2_sib, vn2.at[rows:])]
    for s in (0, 1):
        at = s * rows
        copies.append(fetch(slot_block(meta, cot_tok, s), vcot.at[at : at + n]))
        copies.append(fetch(slot_block(meta, cot_lat, s), vcot.at[at + n : at + rows]))
    return copies


def send_parts(meta, flush, pack, parts):
    x, z = sides(meta)
    n = parts[0].shape[0] // 2
    copies = []
    for ref, (dx, dz) in zip(parts, ((0, 0), (1, 0), (0, 1), (1, 1))):
        q = (x ^ dx) * 2 + (z ^ dz)
        for i in (0, 1):
            src = pack.at[pl.ds(pl.multiple_of(i * 4 * n + q * n, 16), n)]
            copies.append(flush(src, ref.at[i * n : (i + 1) * n]))
    return copies


def hidden_rows(n2, up_w, bias, got, act_out, grad_out, sums):
    cut = 256
    for at in range(0, up_w.shape[1], cut):
        cols = slice(at, at + cut)
        active, slope = gelu_both(dot(n2, up_w[:, cols], 1, 0) + bias[:, cols])
        grad_up = (got[:, cols].astype(F32) * slope).astype(BF)
        act_out[:, cols] = active.astype(BF)
        grad_out[:, cols] = grad_up
        sums[0:1, cols] = jnp.sum(grad_up.astype(F32), 0, keepdims=True)


def hidden_first(params, n2, up_w, got, act, grad, stats):
    stats[...] = jnp.zeros_like(stats)
    hidden_rows(n2[...], up_w, param(params, B_UP), got, act, grad, stats)


def hidden_own(
    meta, params, n2_own, n2_sib, cot_tok, cot_lat, up_w, got_in, act_in, grad_in,
    act_out, grad_out, p0, p1, p2, p3, stats,
    vn2, vcot, vw, act, grad, got, vpack, in_sems, out_sems,
):
    width, hidden = vw.shape
    rows = got.shape[0]
    fetch, flush = mover(in_sems), mover(out_sems)
    first = [fetch(n2_sib, vn2.at[rows:]), fetch(up_w, vw), fetch(got_in, got)]
    copies = [fetch(grad_in, grad.at[0:rows]), fetch(act_in, act.at[0:rows]), fetch(n2_own, vn2.at[0:rows])]
    n = cot_tok.shape[0] // 4
    for s in (0, 1):
        at = s * rows
        copies.append(fetch(slot_block(meta, cot_tok, s), vcot.at[at : at + n]))
        copies.append(fetch(slot_block(meta, cot_lat, s), vcot.at[at + n : at + rows]))
    for copy in first:
        copy.wait()
    stats[...] = jnp.zeros_like(stats)
    hidden_rows(vn2[rows:, :], vw, param(params, B_UP), got, act.at[rows:], grad.at[rows:], stats)
    for copy in copies:
        copy.wait()
    outs = [flush(act, act_out), flush(grad, grad_out)]
    vpack[0:width, :] = dot(vn2[...], grad[...], 0, 0).astype(BF)
    vpack[width : width + hidden, :] = dot(act[...], vcot[...], 0, 0).astype(BF)
    outs += send_parts(meta, flush, vpack, (p0, p1, p2, p3))
    for copy in outs:
        copy.wait()


def hidden_away(
    meta, o2, n2_own, n2_sib, cot_tok, cot_lat, w0, w1, w2, w3, act_in, grad_in, up_w, down_w,
    branch_own, back_own, send, act_out, grad_out, stats,
    vn2, vcot, vw, vnear, act0, grad0, branch, back, act, grad, vsend, in_sems, out_sems,
):
    rows, width = n2_own.shape
    x, z = sides(meta)
    quarter = w0.shape[0] // 2
    fetch, flush = mover(in_sems), mover(out_sems)
    copies = two_halves(meta, fetch, n2_own, n2_sib, cot_tok, cot_lat, vn2, vcot)
    for ref, (dx, dz) in zip((w0, w1, w2, w3), ((0, 0), (1, 0), (0, 1), (1, 1))):
        q = pl.multiple_of(((x ^ dx) * 2 + (z ^ dz)) * quarter, 16)
        for i in (0, 1):
            copies.append(fetch(ref.at[i * quarter : (i + 1) * quarter], vw.at[i, pl.ds(q, quarter)]))
    late = [(fetch(grad_in, grad0), fetch(up_w, vnear.at[0])), (fetch(act_in, act0), fetch(down_w, vnear.at[1]))]
    for copy in copies:
        copy.wait()
    base = o2.shape[0] - 16
    bias = o2[base : base + 16, :].astype(F32)
    bias = bias[0:1] + bias[1:2] + bias[2:3]
    n2, ct = vn2[...], vcot[...]
    stats[...] = jnp.zeros_like(stats)
    stats[0:1, :] = hidden_part(n2, ct, vw.at[0], vw.at[1], bias, act, grad)
    outs = [flush(act, act_out), flush(grad, grad_out)]
    for i, (ref, near, src, turn, own) in enumerate(
        ((back, grad0, grad, 1, back_own), (branch, act0, act, 0, branch_own))
    ):
        for copy in late[i]:
            copy.wait()
        ref[...] = dot(near[...], vnear[i], 1, turn) + dot(src[...], vw[i], 1, turn)
        vsend[i * rows : (i + 1) * rows, :] = ref[rows:, :].astype(BF)
        outs.append(flush(ref.at[0:rows], own))
        outs.append(flush(vsend.at[i * rows : (i + 1) * rows], send.at[i * rows : (i + 1) * rows]))
    for copy in outs:
        copy.wait()


def away_grads(
    meta, n2_own, n2_sib, cot_tok, cot_lat, act_in, grad_in, p0, p1, p2, p3,
    vn2, vcot, act, grad, vpack, in_sems, out_sems,
):
    width, hidden = vn2.shape[1], act.shape[1]
    fetch, flush = mover(in_sems), mover(out_sems)
    copies = [fetch(grad_in, grad)] + two_halves(meta, fetch, n2_own, n2_sib, cot_tok, cot_lat, vn2, vcot)
    last = fetch(act_in, act)
    for copy in copies:
        copy.wait()
    vpack[0:width, :] = dot(vn2[...], grad[...], 0, 0).astype(BF)
    last.wait()
    vpack[width : width + hidden, :] = dot(act[...], vcot[...], 0, 0).astype(BF)
    for copy in send_parts(meta, flush, vpack, (p0, p1, p2, p3)):
        copy.wait()


def middle_rows(meta, count, params, residual, branch, back, got, cot_tok, cot_lat, out_rows, grad_res, grad_attn, stats):
    n, m = cot_tok.shape[0], cot_lat.shape[0]
    rows_own = n + m
    stats[...] = jnp.zeros_like(stats)
    for at, size, cot in ((0, n, cot_tok), (n, m, cot_lat)):
        rows = slice(at, at + size)
        bk = back[rows, :] + got[rows, :].astype(F32)
        br = branch[rows, :] + got[rows_own + at : rows_own + at + size, :].astype(F32) + param(params, B_DOWN)
        res = residual[rows, :]
        out = res + br
        out_rows[rows, :] = out.astype(BF)
        if at == 0:
            real = valid_rows(meta, count, n)
            stats[0:1, :] = jnp.sum(jnp.where(real, out * out, 0.0), 0, keepdims=True)
            stats[1:2, :] = jnp.sum(jnp.where(real, br * br, 0.0), 0, keepdims=True)
        unit, inverse = norm_parts(res)
        stats[2:3, :] += jnp.sum(bk * unit, 0, keepdims=True)
        stats[3:4, :] += jnp.sum(bk, 0, keepdims=True)
        cot32 = cot[...].astype(F32)
        gr = cot32 + norm_back(bk, unit, inverse, param(params, GAIN2))
        grad_res[rows, :] = gr
        ga = gr.astype(BF)
        grad_attn[rows, :] = ga
        stats[4:5, :] += jnp.sum(ga.astype(F32), 0, keepdims=True)
        stats[5:6, :] += jnp.sum(cot32, 0, keepdims=True)


def back_out(ga_own, ga_sib, o0, o2, t_near, t_far, l_near, l_far, g0, g2, d0, w0, sent):
    wide, n = t_near.shape[0], t_near.shape[1] // 2
    m = l_near.shape[0] // 2
    sent[wide:, :] = jnp.zeros_like(sent[wide:, :])
    for o, g, d, at in ((o2, g2, sent, wide), (o0, g0, d0, 0)):
        for i, ga in enumerate((ga_own, ga_sib)):
            g[:, i * n : (i + 1) * n] = dot(o[0:wide, :], ga[0:n, :], 1, 1).astype(BF)
            rows = dot(ga[n : n + m, :], o[0:wide, :], 1, 1).astype(BF)
            d[at + i * m : at + (i + 1) * m, 0:wide] = rows
    for t, l, w in ((t_far, l_far, sent.at[0:wide]), (t_near, l_near, w0)):
        total = jnp.zeros(w0.shape, F32)
        for i, ga in enumerate((ga_own, ga_sib)):
            total += dot(t[:, i * n : (i + 1) * n], ga[0:n, :], 1, 0)
            total += dot(l[i * m : (i + 1) * m, :], ga[n : n + m, :], 0, 0)
        w[...] = total.astype(BF)


def near_slot(
    slot, meta, count, normed, q, k, v, ql, kl, vl, log, far, logs_far, d_in, d_lat_in, w, grad_w, bias,
    dq_far, dk_near, dv_near,
):
    wide = q.shape[1]
    heads = wide // HEAD
    rows = normed[...]
    slot_rows = rows.shape[0]
    d_lat = d_lat_in[:, 0 : q.shape[1]].astype(F32)
    eighth = jnp.asarray(0.125, BF)
    q_all, k_all, v_all = q[...] * eighth, k[...], v[...]
    far32 = far[...].astype(F32)
    far_log = logs_far[...].astype(F32)
    dqs, dks, dvs = [], [], []
    for i in range(slot_rows // GROUP):
        at, lat_at = slice(i * GROUP, (i + 1) * GROUP), slice(i * LAT, (i + 1) * LAT)
        number = group_at(meta, count, slot, i)
        d_cols = d_in[:, at]
        d_tok, qs, ks, vs = d_cols.T, q_all[at], k_all[at], v_all[at]
        keys, values = key_stack(ks, kl[lat_at, :]), key_stack(vs, vl[lat_at, :])
        keys_t = keys.T
        mask = near_mask(number, GROUP)
        ps, gs, dq_t, d_heads, q_heads = [], [], [], [], []
        for h in range(heads):
            s = dot(head_lanes(keys, h), qs, 1, 1)
            p = jnp.where(mask, jnp.exp(s - log[i, h : h + 1, :]), 0.0)
            gp = p * dot(head_lanes(values, h), d_cols, 1, 0)
            g = (gp - p * jnp.sum(gp, 0, keepdims=True)).astype(BF)
            dq_t.append(dot(keys_t[h * HEAD : (h + 1) * HEAD], g, 1, 0))
            ps.append(p.astype(BF))
            gs.append(g)
            d_heads.append(head_lanes(d_tok, h))
            q_heads.append(head_lanes(qs, h))
        dv = dot(jnp.concatenate(ps, 1), jnp.concatenate(d_heads, 0), 1, 0)
        dk = dot(jnp.concatenate(gs, 1), jnp.concatenate(q_heads, 0), 1, 0)
        dqs.append((jnp.concatenate(dq_t, 0).T * 0.125).astype(BF))
        pad = jnp.zeros((LAT, wide), F32)
        q8, o8, d8, lg = ql[lat_at, :] * 0.125, far32[lat_at], d_lat[lat_at], far_log[lat_at]
        q_rows, do_rows, log_col, del_col = [], [], [], []
        big = jnp.full((LAT, 1), 1e30, F32)
        zero = jnp.zeros((LAT, 1), F32)
        for h in range(heads):
            q_rows += [head_lanes(q8, h), pad]
            dh = head_lanes(d8, h)
            do_rows += [dh, pad]
            col = lg[:, h : h + 1] + lg[:, heads + h : heads + h + 1] + lg[:, 2 * heads + h : 2 * heads + h + 1]
            log_col += [col, big]
            del_col += [jnp.sum(dh * o8, 1, keepdims=True), zero]
        q_f, d_f = jnp.concatenate(q_rows, 0).astype(BF), jnp.concatenate(do_rows, 0).astype(BF)
        l_f, x_f = jnp.concatenate(log_col, 0), jnp.concatenate(del_col, 0)
        lane = lax.broadcasted_iota(jnp.int32, (2 * LAT * heads, GROUP), 1)
        p_f = jnp.where(lane < number, jnp.exp(dot(q_f, ks, 1, 1) - l_f), 0.0)
        g_f = (p_f * (dot(d_f, vs, 1, 1) - x_f)).astype(BF)
        dks.append((dk[0:GROUP] + dot(g_f, q_f, 0, 0)).astype(BF))
        dvs.append((dv[0:GROUP] + dot(p_f.astype(BF), d_f, 0, 0)).astype(BF))
        dk_near[lat_at, :] = dk[GROUP : GROUP + LAT]
        dv_near[lat_at, :] = dv[GROUP : GROUP + LAT]
        dq_all = dot(g_f, ks, 1, 0)
        dq_lat = jnp.zeros((LAT, wide), F32)
        for h in range(heads):
            dq_lat += head_lanes(dq_all[2 * LAT * h : 2 * LAT * h + LAT], h)
        dq_far[lat_at, :] = dq_lat

    dq, dk, dv = (jnp.concatenate(v, 0) for v in (dqs, dks, dvs))
    total = dot(dq, w[0], 1, 0) + dot(dk, w[1], 1, 0) + dot(dv, w[2], 1, 0)
    for i, g in enumerate((dq, dk, dv)):
        grad_w[i] += dot(g, rows, 0, 0)
    bias[0:1, :] += jnp.sum(dq.astype(F32), 0, keepdims=True)
    bias[1:2, :] += jnp.sum(dv.astype(F32), 0, keepdims=True)
    bias[2:3, :] += jnp.sum(dk.astype(F32), 0, keepdims=True)
    return total.astype(BF)


def backward_rows(
    first, begin, meta, count, normed, q, k, v, ql, kl, vl, log, far, logs_far, d_in, d_lat, w, gw_in, bias_in, *outs,
):
    step = pl.program_id(0)
    parts, (grad_w, bias, dq_far, dk_near, dv_near) = outs[:-5], outs[-5:]

    @pl.when(step == 0)
    def _():
        grad_w[...] = jnp.zeros_like(grad_w) if begin else gw_in[...]
        bias[...] = jnp.zeros_like(bias) if begin else bias_in[...]

    total = near_slot(
        step + first, meta, count, normed, q, k, v, ql, kl, vl, log, far, logs_far, d_in, d_lat, w, grad_w, bias,
        dq_far, dk_near, dv_near,
    )
    for slot, ref in enumerate(parts):

        @pl.when(step == slot)
        def _(ref=ref):
            ref[...] = total


def latent_bundle(d_near, d_far, far, logs_far, own, sent):
    count, wide = far.shape
    heads = wide // HEAD
    n = count // 4
    d32 = jnp.concatenate([d_near[...], d_far[:, 0:wide]], 0).astype(F32)
    prod = d32 * far[...].astype(F32)
    lg = logs_far[...].astype(F32)
    deltas = [split3(jnp.sum(head_lanes(prod, h), 1, keepdims=True)) for h in range(heads)]
    cols = [lg[:, i : i + 1] for i in range(3 * heads)] + [p[i].astype(F32) for i in (0, 1) for p in deltas]
    lane = lax.broadcasted_iota(jnp.int32, (count, 4 * HEAD), 1)
    value = jnp.concatenate([d32, jnp.zeros((count, HEAD), F32)], 1)
    for i, c in enumerate(cols):
        value = jnp.where(lane == wide + i, c, value)
    value = value.astype(BF)
    own[...] = value
    for i, s in enumerate(SENT):
        sent[i * n : (i + 1) * n, :] = value[s * n : (s + 1) * n]


def backward_far(
    meta, tokens_real, image, qa, ka, va, ql, kl, vl, own, bundle, normed, w, gw, bias_in, wo_a, wo_b,
    params, stats1, stats2, hid_first, hid_near, hid_away, *refs,
):
    near, (lat_keep, lat_send, p0, p1, p2, p3, small, pack, out_sems) = refs[:-9], refs[-9:]
    count, wide = ql.shape
    heads = wide // HEAD
    groups = count // LAT
    q_all, k_all, v_all = qa[...] * jnp.asarray(0.125, BF), ka[...], va[...]
    q_own, k_own, v_own = (ql[...] * 0.125).astype(BF), kl[...].astype(BF), vl[...].astype(BF)
    d_own, d_all = own[:, 0:wide], bundle[:, 0:wide]

    def stats(ref, h):
        x = ref[...].astype(F32)
        col = [x[:, wide + i : wide + i + 1] for i in range(5 * heads)]
        return col[h] + col[heads + h] + col[2 * heads + h], col[3 * heads + h] + col[4 * heads + h]

    mine = image_list(meta, image, 1, groups, OWN)
    images = image_list(meta, image, qa.shape[0] // count, groups, SENT)
    mask_q = image_column(mine) == image_row(images)
    mask_k = image_column(images) == image_row(mine)
    each = len(near) // 3
    dq, dk, dv = (jnp.concatenate([ref[...] for ref in near[i * each : (i + 1) * each]], 0) for i in range(3))
    for h in range(heads):
        log, delta = stats(own, h)
        s = dot(head_lanes(q_own, h), k_all, 1, 1)
        p = jnp.where(mask_q, jnp.exp(s - log), 0.0)
        g = (p * (dot(head_lanes(d_own, h), v_all, 1, 1) - delta)).astype(BF)
        dq += head_lanes(dot(g, k_all, 1, 0), h)
        log, delta = stats(bundle, h)
        s = dot(q_all, head_lanes(k_own, h), 1, 1)
        p = jnp.where(mask_k, jnp.exp(s - log), 0.0)
        g = (p * (dot(d_all, head_lanes(v_own, h), 1, 1) - delta)).astype(BF)
        dk += head_lanes(dot(g, q_all, 0, 0), h)
        dv += head_lanes(dot(p.astype(BF), d_all, 0, 0), h)
    dq, dk, dv = (dq * 0.125).astype(BF), dk.astype(BF), dv.astype(BF)
    lat_rows = normed[...]
    sums = [bias_in[i : i + 1, :] for i in (0, 2, 1)]
    sums = [b + jnp.sum(g.astype(F32), 0, keepdims=True) for b, g in zip(sums, (dq, dk, dv))]
    columns = jnp.concatenate(sums + [jnp.zeros((5, wide), F32)], 0).T
    first_gain = jnp.zeros((1, pack.shape[1]), F32)
    first_shift = first_gain
    for i, g in enumerate((dq, dk, dv)):
        total = gw[i] + dot(g, lat_rows, 0, 0)
        pack[i * wide : (i + 1) * wide, :] = total.astype(BF)
        col, weight = columns[:, i : i + 1], w[i].astype(F32)
        first_shift += jnp.sum(weight * col, 0, keepdims=True)
        first_gain += jnp.sum(weight * (total - col * param(params, SHIFT1)), 0, keepdims=True)
    first_gain = first_gain / param(params, GAIN1)
    pack[3 * wide :, :] = (wo_a[...].astype(F32) + wo_b[...].astype(F32)).astype(BF)
    x, z = sides(meta)
    flush = mover(out_sems)
    copies = []
    for ref, (dx, dz) in zip((p0, p1, p2, p3), ((0, 0), (1, 0), (0, 1), (1, 1))):
        part = (x ^ dx) * 2 + (z ^ dz)
        at = 0
        for base, size in ((0, 3 * wide // 4), (3 * wide, wide // 4)):
            src = pack.at[pl.ds(pl.multiple_of(base + part * size, 16), size)]
            copies.append(flush(src, ref.at[at : at + size]))
            at += size
    rows = (dot(dq, w[0], 1, 0) + dot(dk, w[1], 1, 0) + dot(dv, w[2], 1, 0)).astype(BF)
    n = count // 4
    lat_keep[0:n, :], lat_keep[n : 2 * n, :] = rows[0:n], rows[2 * n : 3 * n]
    lat_send[0:n, :], lat_send[n : 2 * n, :] = rows[n : 2 * n], rows[3 * n :]
    small[...] = jnp.zeros_like(small)
    small[0:1, :] = stats1[0:1, :]
    small[1:7, :] = stats2[0:6, :]
    small[7:8, :], small[8:9, :] = first_gain, first_shift
    real = tokens_real[0]
    for i in range(1, tokens_real.shape[0]):
        real = real + tokens_real[i]
    for at, part in ((9, real - real % 64), (22, real % 64)):
        small[at : at + 1, :] = jnp.full((1, small.shape[1]), 0.25, F32) * part.astype(F32)
    for s, row in ((0, hid_first[0:1, :] + hid_near[0:1, :]), (2, hid_away[0:1, :])):
        small[pl.ds(10 + (meta[1] ^ s), 1), :] = row
    small[pl.ds(14 + meta[1], 1), 0:wide] = sums[0]
    small[pl.ds(18 + meta[1], 1), 0:wide] = sums[2]
    for copy in copies:
        copy.wait()


def final_rows(meta, tok, lat, a, b, c, la, lb, grad_res, params, out):
    n, m = tok.shape[0], lat.shape[0]
    for x, at, terms in ((tok, slice(0, n), (a, b)), (lat, slice(n, n + m), (la, lb))):
        grad = c[at, :].astype(F32)
        for term in terms:
            grad += term[0 : x.shape[0], :].astype(F32)
        unit, inverse = norm_parts(x[...].astype(F32))
        out[at, :] = (grad_res[at, :] + norm_back(grad, unit, inverse, param(params, GAIN1))).astype(BF)


def place_rows(meta, a, b, c, d, tok_out, lat_out):
    n = tok_out.shape[0]
    for i, ref in enumerate((a, b, c, d)):

        @pl.when(pl.program_id(0) == i)
        def _(ref=ref):
            tok_out[...] = ref[0:n, :]
            lat_out[...] = ref[n:, :]


def projections_out(meta, f0, f1, f2, f3, grad_w, grad_o, gain1, shift1, b_out, gain2, shift2, b_down, b_up, b_qv, roots):
    x, z = sides(meta)
    wide = grad_o.shape[0]
    four = (f0, f1, f2, f3)
    for ref, (dx, dz) in zip(four, ((0, 0), (1, 0), (0, 1), (1, 1))):
        part = (x ^ dx) * 2 + (z ^ dz)
        at = 0
        for dst, size in ((grad_w, 3 * wide // 4), (grad_o, wide // 4)):
            dst[pl.ds(pl.multiple_of(part * size, 16), size), :] = ref[at : at + size, :].astype(F32)
            at += size
    small = four[0][wide : wide + 32, :].astype(F32)
    for ref in four[1:]:
        small += ref[wide : wide + 32, :].astype(F32)
    for ref, row in ((gain1, 7), (shift1, 8), (b_out, 5), (gain2, 3), (shift2, 4), (b_down, 6)):
        ref[...] = small[row, :]

    def of_mp(first):
        value = small[first : first + 1]
        for m in (1, 2, 3):
            value = jnp.where(meta[1] == m, small[first + m : first + m + 1], value)
        return value

    b_up[...] = of_mp(10)[0]
    b_qv[...] = jnp.concatenate([of_mp(14)[:, 0:wide], of_mp(18)[:, 0:wide]], 0)
    real = (small[9:10, 0:1] + small[22:23, 0:1]) * small.shape[1]
    lane = lax.broadcasted_iota(jnp.int32, roots.shape, 1)
    value = jnp.zeros(roots.shape, F32)
    for i, row in enumerate((1, 0, 2)):
        root = jnp.sqrt(jnp.sum(small[row : row + 1], 1, keepdims=True) / real)
        value = jnp.where(lane == i, root, value)
    roots[...] = value


def after(v, *deps):
    return lax.optimization_barrier((v,) + deps)[0]


def make(mesh):
    dp_size, mp_size = mesh.shape["dp"], mesh.shape["mp"]
    assert mp_size == 4 and dp_size >= 4
    dp_bits = [1 << i for i in range(dp_size.bit_length() - 1)]
    assert 1 << len(dp_bits) == dp_size
    x_bit, z_bit, rest_bits = dp_bits[0], dp_bits[1], dp_bits[2:]

    def swap(v, dp_bit, mp_bit):
        pairs = [
            (d * mp_size + m, (d ^ dp_bit) * mp_size + (m ^ mp_bit))
            for d in range(dp_size)
            for m in range(mp_size)
        ]
        return lax.ppermute(v, ("dp", "mp"), pairs)

    def per_device(
        tokens,
        latents,
        image_of_group,
        token_valid,
        norm1_gain,
        norm1_shift,
        w_qkv,
        b_qv,
        w_out,
        b_out,
        norm2_gain,
        norm2_shift,
        w_up,
        b_up,
        w_down,
        b_down,
        cot_tokens,
        cot_latents,
    ):
        dp_at, mp_at = lax.axis_index("dp"), lax.axis_index("mp")
        tok_count, width = tokens.shape
        lat_count = latents.shape[0]
        groups = lat_count // LAT
        wide = w_qkv.shape[2]
        hidden = w_up.shape[1]
        tok_own, lat_own = tok_count // 4, lat_count // 4
        rows_own = tok_own + lat_own
        all_lat = dp_size * lat_count
        meta = jnp.stack([dp_at, mp_at]).astype(jnp.int32)
        count = jnp.sum(token_valid.reshape(groups, GROUP), 1).astype(jnp.int32)
        par = whole((8, width))
        w_t = jnp.transpose(w_qkv, (0, 2, 1))
        w_all = (3, wide, width)
        quarter, small = width // 4, wide // 4
        half = 2 * quarter
        big = (rows_own, width)
        chip_rows, chip_tok, chip_lat = 2 * rows_own, 2 * tok_own, 2 * lat_own
        vec = pl.BlockSpec((width,), lambda *_: (0,))

        def out(shape, kind=BF):
            return (shape, kind, whole(shape))

        def kept_out(shape, kind=BF):
            return (shape, kind, kept(shape))

        vm = pltpu.VMEM

        def any_out(shape, kind=BF):
            return (shape, kind, ANY)

        def dma(n):
            return pltpu.SemaphoreType.DMA((n,))

        def cube(v, vx=None, vz=None, vxz=None):
            vx, vz, vxz = (v if w is None else w for w in (vx, vz, vxz))
            return swap(vx, x_bit, 0), swap(vz, z_bit, 0), swap(vxz, x_bit | z_bit, 0)

        def all_latents(v):
            v = jnp.concatenate((v,) + cube(v), 0)
            for bit in rest_bits:
                v = jnp.concatenate([v, swap(v, bit, 0)], 0)
            return v

        part_block = pl.BlockSpec((quarter, width), lambda i, meta: ((meta[0] & 1) * 2 + ((meta[0] >> 1) & 1), 0))
        lat_rel, lat_half, o0, weight_part, params = call(
            prepare,
            name="prepare",
            room=62,
            scalars=1,
            ins=[pl.BlockSpec(memory_space=pltpu.HBM)] * 11,
            outs=[out((lat_count, width)), out((chip_lat, width)), out((wide + 16, width)), out((half, width)), out((8, width), F32)],
            scratch=[vm((lat_count, width), BF), vm((wide, width), BF), dma(11)] + [vm((width,), F32)] * 7,
            us=2,
        )(meta, latents, w_out, norm1_gain, norm1_shift, b_out, norm2_gain, norm2_shift, b_down, b_up, w_up, w_down)
        lat_four = jnp.concatenate((lat_half,) + cube(lat_half), 0)
        w_own = swap(weight_part, 0, 2)
        o2 = swap(o0, 0, 2)

        normed_lat, ql, kl, vl = call(
            latent_rows,
            name="latent_rows",
            room=3,
            scalars=0,
            ins=[whole((lat_count, width)), par, whole(w_all), whole((2, wide))],
            outs=[out((lat_count, width))] + [out((lat_count, wide), F32)] * 3,
            us=2,
        )(lat_rel, params, w_t, b_qv)

        def cot_through(slot, meta):
            return call(
                cot_back,
                name="cot_back",
            room=4,
                scalars=1,
                ins=[
                    pl.BlockSpec((tok_own, width), lambda i, meta: (meta[1] ^ slot, 0), pipeline_mode=pl.Buffered(1)),
                    pl.BlockSpec((lat_own, width), lambda i, meta: (meta[1] ^ slot, 0), pipeline_mode=pl.Buffered(1)),
                    whole((hidden, width)),
                ],
                outs=[out((rows_own, hidden))],
                us=4,
            )(meta, cot_tokens, cot_latents, w_down)[0]

        cot_own = cot_through(0, after(meta, kl))
        lat_here = lat_four = after(lat_four, cot_own)
        for bit in rest_bits:
            lat_here = jnp.concatenate([lat_here, swap(lat_here, bit, 0)], 0)

        def near_forward(base, *deps):
            def run(*args):
                return forward_near(base, *args)

            rows = lambda wide_here: pl.BlockSpec((tok_own, wide_here), lambda i, *_: (i, 0))
            lat_block = pl.BlockSpec((lat_own, wide), lambda i, *_: (i + base, 0))
            each = groups // 4
            return call(
                run,
                name="forward_near",
            room=8,
                grid=(2,),
                scalars=2,
                ins=[
                    pl.BlockSpec((tok_own, width), lambda i, meta, _: (meta[1] ^ (i + base), 0)),
                    lat_block,
                    lat_block,
                    par,
                    whole(w_all),
                    whole((2, wide)),
                ],
                outs=[((chip_tok, width), BF, rows(width))]
                + [((chip_tok, wide), BF, rows(wide))] * 3
                + [((wide, chip_tok), BF, pl.BlockSpec((wide, tok_own), lambda i, *_: (0, i)))]
                + [((2 * each, 8, GROUP), F32, pl.BlockSpec((each, 8, GROUP), lambda i, *_: (i, 0, 0)))],
                us=8,
            )(meta, count, tokens, after(kl, *deps), vl, params, w_t, b_qv)

        normed_b, q_b, k_b, v_b, t_b, log_b = near_forward(2, lat_four)
        t_far = swap(t_b, 0, 2)
        lat_here = after(lat_here, t_b)
        normed_a, q_a, k_a, v_a, t_near, log_a = near_forward(0, lat_here)
        w_x, w_z, w_xz = cube(after(w_own, t_near))
        lat_all = [v.reshape(dp_size, chip_lat, width) for v in (lat_here, swap(lat_here, 0, 1))]
        lat_all = jnp.concatenate(lat_all, 1).reshape(all_lat, width)
        lat_all = after(lat_all, t_near)

        chunk = min(512, all_lat)
        qa, ka, va, l_near, l_b, far, far_logs = call(
            forward_far,
            name="forward_far",
            room=6,
            grid=(all_lat // chunk,),
            scalars=3,
            ins=[pl.BlockSpec((chunk, width), lambda i, *_: (i, 0)), par, whole(w_all), whole((2, wide))]
            + [whole((chip_tok, wide))] * 4
            + [whole((lat_count, wide))],
            outs=[out((all_lat, wide))] * 3
            + [kept_out((chip_lat, wide))] * 2
            + [kept_out((lat_count, wide)), kept_out((lat_count, 2 * HEAD))],
            us=6,
        )(meta, count, image_of_group, lat_all, params, w_t, b_qv, k_a, k_b, v_a, v_b, ql)
        l_far = swap(l_b, 0, 2)

        out_pack = whole((wide + 16, width))
        mixed_specs = [whole((wide, chip_tok))] * 2 + [whole((chip_lat, wide))] * 2
        cot_sib = cot_through(1, after(meta, far))

        def out_rows_of(slot, kind, o0):
            return call(
                project_out,
                name="project_out",
            room=4,
                scalars=0,
                ins=[pl.BlockSpec((wide, tok_own), lambda *_: (0, slot), pipeline_mode=pl.Buffered(1))] * 2
                + [pl.BlockSpec((lat_own, wide), lambda *_: (slot, 0), pipeline_mode=pl.Buffered(1))] * 2
                + [out_pack] * 2,
                outs=[out(big, kind)],
                us=3,
            )(t_near, t_far, l_near, l_far, o0, o2)[0]

        attn_send = out_rows_of(1, BF, after(o0, cot_sib))
        attn_own = out_rows_of(0, F32, after(o0, attn_send))
        attn_got = swap(attn_send, 0, 1)
        own_tok = pl.BlockSpec((tok_own, width), lambda i, meta, _: (meta[1], 0), pipeline_mode=pl.Buffered(1))
        own_lat = pl.BlockSpec((lat_own, width), lambda i, meta, _: (meta[1], 0), pipeline_mode=pl.Buffered(1))
        residual, n2, stats1 = call(
            add_norm,
            name="add_norm",
            room=6,
            scalars=2,
            ins=[par, whole(big), whole(big), own_tok, whole((lat_own, width))],
            outs=[out(big, F32), out(big), out((8, width), F32)],
            us=3,
        )(meta, count, params, attn_own, attn_got, tokens, lat_rel)
        n2_sib = swap(n2, 0, 1)

        chip = (chip_rows, width)
        piece = (half, width)
        act_first, grad_first, bias_first = call(
            hidden_first,
            name="hidden_first",
            room=6,
            scalars=0,
            ins=[par, whole(big), whole((width, hidden)), whole((rows_own, hidden))],
            outs=[out((rows_own, hidden))] * 2 + [out((8, hidden), F32)],
            us=4,
        )(params, n2, w_up, cot_own)
        act_near, grad_near, a0, a1, a2, a3, bias_near = call(
            hidden_own,
            name="hidden_own",
            room=12,
            scalars=1,
            ins=[par] + [ANY] * 8,
            outs=[any_out((chip_rows, hidden))] * 2 + [any_out(piece)] * 4 + [out((8, hidden), F32)],
            scratch=[
                vm(chip, BF),
                vm(chip, BF),
                vm((width, hidden), BF),
                vm((chip_rows, hidden), BF),
                vm((chip_rows, hidden), BF),
                vm((rows_own, hidden), BF),
                vm((width + hidden, width), BF),
                dma(10),
                dma(10),
            ],
            us=9,
        )(meta, params, n2, n2_sib, cot_tokens, cot_latents, w_up, cot_sib, act_first, grad_first)
        near_parts = (a0,) + cube(None, a1, a2, a3)

        branch, back, middle_send, act, grad, bias_away = call(
            hidden_away,
            name="hidden_away",
            room=14,
            scalars=1,
            ins=[out_pack] + [ANY] * 12,
            outs=[any_out(big, F32), any_out(big, F32), any_out(chip), any_out((chip_rows, hidden)), any_out((chip_rows, hidden))]
            + [out((8, hidden), F32)],
            scratch=[
                vm(chip, BF),
                vm(chip, BF),
                vm((2, width, hidden), BF),
                vm((2, width, hidden), BF),
                vm((chip_rows, hidden), BF),
                vm((chip_rows, hidden), BF),
                vm(chip, F32),
                vm(chip, F32),
                vm((chip_rows, hidden), BF),
                vm((chip_rows, hidden), BF),
                vm(chip, BF),
                dma(18),
                dma(6),
            ],
            us=10,
        )(meta, o2, n2, n2_sib, cot_tokens, cot_latents, w_own, w_x, w_z, w_xz, act_near, grad_near, w_up, w_down)
        middle_got = swap(middle_send, 0, 1)

        b0, b1, b2, b3 = call(
            away_grads,
            name="away_grads",
            room=12,
            scalars=1,
            ins=[ANY] * 6,
            outs=[any_out(piece)] * 4,
            scratch=[
                vm(chip, BF),
                vm(chip, BF),
                vm((chip_rows, hidden), BF),
                vm((chip_rows, hidden), BF),
                vm((width + hidden, width), BF),
                dma(8),
                dma(8),
            ],
            us=6,
        )(meta, n2, n2_sib, cot_tokens, cot_latents, act, grad)

        out_rows, grad_res, grad_attn, stats2 = call(
            middle_rows,
            name="middle_rows",
            room=8,
            scalars=2,
            ins=[par, whole(big), whole(big), whole(big), whole(chip), own_tok, own_lat],
            outs=[out(big), out(big, F32), out(big), out((8, width), F32)],
            us=5,
            deps=(b0,),
        )(meta, count, params, residual, branch, back, middle_got, cot_tokens, cot_latents)
        grad_attn_sib = swap(grad_attn, 0, 1)

        def terms(n, at=0):
            return [(i, at) for i in range(n)]

        sides4 = ((0, 0), (1, 0), (0, 1), (1, 1))

        def at(d, size, base=0):
            return lambda x, z: base + ((x ^ d[0]) * 2 + (z ^ d[1])) * size


        (near_sum,) = combine("near_sum", meta, near_parts, [(half, BF, [(0, half, terms(4))])], us=2)
        away_parts = (b0,) + cube(None, *(after(v, near_sum) for v in (b1, b2, b3)))

        g_near, g_send, d_near, out_grad, out_send = call(
            back_out,
            name="back_out",
            room=6,
            scalars=0,
            ins=[whole(big), whole(big), out_pack, out_pack] + mixed_specs,
            outs=[out((wide, chip_tok))] * 2 + [out((chip_lat, wide)), out((wide, width)), out((wide + chip_lat, width))],
            us=4,
            deps=(near_sum,),
        )(grad_attn, grad_attn_sib, o0, o2, t_near, t_far, l_near, l_far)
        out_got = swap(out_send, 0, 2)
        g_far = swap(g_send, 0, 2)

        zero_w, zero_b = jnp.zeros((8, LANES), F32), jnp.zeros((8, LANES), F32)

        def rows_backward(first, steps, half_in, g, d, gw, bias, *deps):
            normed, q, k, v, log = half_in
            base = first % 2

            def rows(n, wide_here, shift):
                return pl.BlockSpec((n, wide_here), lambda i, *_: (i + shift, 0))

            def run(*args):
                return backward_rows(first, gw is None, *args)

            init = (zero_w, zero_b) if gw is None else (gw, bias)
            return call(
                run,
                name="backward_rows",
            room=8,
                grid=(steps,),
                scalars=2,
                ins=[
                    rows(tok_own, width, base),
                    *[rows(tok_own, wide, base)] * 3,
                    *[rows(lat_own, wide, first)] * 3,
                    pl.BlockSpec((groups // 4, 8, GROUP), lambda i, *_: (i + base, 0, 0)),
                    rows(lat_own, wide, first),
                    rows(lat_own, 2 * HEAD, first),
                    pl.BlockSpec((wide, tok_own), lambda i, *_: (0, i + base)),
                    rows(lat_own, d.shape[1], base + (wide // lat_own if d.shape[1] != wide else 0)),
                    whole(w_all),
                    whole(init[0].shape),
                    whole(init[1].shape),
                ],
                outs=[kept_out((tok_own, width))] * steps
                + [kept_out(w_all, F32), kept_out((8, wide), F32)]
                + [((steps * lat_own, wide), F32, rows(lat_own, wide, 0))] * 3,
                us=7 * steps,
                deps=deps,
            )(meta, count, normed, q, k, v, ql, kl, vl, log, far, far_logs, g, d, w_t, *init)

        half_a, half_b = (normed_a, q_a, k_a, v_a, log_a), (normed_b, q_b, k_b, v_b, log_b)
        part0, gw, bias, *near_0 = rows_backward(0, 1, half_a, g_near, d_near, None, None)
        bundle_own, bundle = call(
            latent_bundle,
            name="latent_bundle",
            scalars=0,
            ins=[whole((chip_lat, wide)), pl.BlockSpec((chip_lat, width), lambda *_: (wide // chip_lat, 0))]
            + [whole((lat_count, wide)), whole((lat_count, 2 * HEAD))],
            outs=[out((lat_count, 4 * HEAD))] * 2,
            us=2,
            deps=(part0,),
        )(d_near, out_got, far, far_logs)
        steps = [bundle]

        def spread(bit):
            got = swap(steps[0], bit, 0)
            return lambda done: steps.__setitem__(0, jnp.concatenate([after(steps[0], done), got], 0))

        join = spread(x_bit)
        part1, gw, bias, *near_1 = rows_backward(1, 1, half_a, g_near, d_near, gw, bias, bundle_own)
        got1 = swap(part1, 0, 1)
        join(part1)
        join = spread(z_bit)
        part3, gw, bias, *near_3 = rows_backward(3, 1, half_b, g_far, out_got, gw, bias)
        join(part3)
        for bit in rest_bits[:-1]:
            spread(bit)(part3)
        join = spread(rest_bits[-1]) if rest_bits else None
        (away_sum,) = combine("away_sum", meta, away_parts, [(half, BF, [(0, half, terms(4))])], us=2, deps=(part3,))
        away_got = swap(away_sum, 0, 2)
        got3 = swap(part3, 0, 1)
        part2, gw, bias, *near_2 = rows_backward(2, 1, half_b, g_far, out_got, gw, bias, away_sum, got1, got3)
        if rest_bits:
            join(part2)
        bundle = steps[0]
        near_all = [v for three in zip(near_0, near_1, near_2, near_3) for v in three]
        shard = (small * 4, width)
        lat_keep, lat_send, c0, c1, c2, c3, small_rows = call(
            backward_far,
            name="backward_far",
            room=6,
            scalars=3,
            ins=[whole((all_lat, wide))] * 3
            + [whole((lat_count, wide))] * 3
            + [whole((lat_count, 4 * HEAD)), whole((all_lat, 4 * HEAD)), whole((lat_count, width)), whole(w_all), whole(w_all)]
            + [whole((8, wide))]
            + [whole((wide, width)), pl.BlockSpec((wide, width), lambda *_: (0, 0), pipeline_mode=pl.Buffered(1))]
            + [par]
            + [whole((8, width))] * 5
            + [whole(v.shape) for v in near_all],
            outs=[out((chip_lat, width))] * 2 + [any_out(shard)] * 4 + [out((32, width), F32)],
            scratch=[vm((4 * wide, width), BF), dma(8)],
            us=8,
        )(
            meta, count, image_of_group, qa, ka, va, ql, kl, vl, bundle_own, bundle, normed_lat, w_t, gw, bias, out_grad,
            out_got, params, stats1, stats2, bias_first, bias_near, bias_away, *near_all,
        )

        lat_got = swap(lat_send, 0, 1)
        (total,) = combine(
            "weights_sum", meta, [near_sum, away_got], [(half, BF, [(0, half, terms(2))])], us=20, deps=(lat_keep,)
        )
        (there,) = combine(
            "rows_sum", meta, [part2, got3, lat_keep, lat_got],
            [(rows_own, BF, [(0, tok_own, terms(2)), (tok_own, lat_own, [(2, lat_own), (3, lat_own)])])],
            us=2, deps=(total,),
        )
        from_y = swap(there, 0, 2)
        small_rows = small_rows + swap(small_rows, 0, 1)
        small_got = swap(small_rows, 0, 2)
        rows4 = 4 * small
        qkv_parts = (c0,) + cube(None, *(after(v, total) for v in (c1, c2, c3)))
        (qkv,) = combine(
            "qkv_sum", meta, qkv_parts + (small_rows, small_got),
            [(rows4 + 32, BF, [(0, rows4, terms(4)), (rows4, 32, [(4, 0), (5, 0)])])],
            us=2, deps=(there,),
        )
        (grad_rows,) = call(
            final_rows,
            name="final_rows",
            room=6,
            scalars=1,
            ins=[
                pl.BlockSpec((tok_own, width), lambda i, meta: (meta[1], 0), pipeline_mode=pl.Buffered(1)),
                whole((lat_own, width)),
                *[whole((tok_own, width))] * 2,
                whole(big),
                *[whole((chip_lat, width))] * 2,
                whole(big),
                par,
            ],
            outs=[out(big)],
            us=4,
            deps=(qkv,),
        )(meta, tokens, lat_rel, part0, got1, from_y, lat_keep, lat_got, grad_res, params)

        grad_y = swap(grad_rows, 0, 2)
        grad_c = swap(after(grad_rows, grad_y), 0, 1)
        out_y = swap(after(out_rows, qkv), 0, 2)
        for bit in rest_bits:
            (total,) = combine(
                "rest_sum", meta, [total, swap(total, bit, 0)], [(half, BF, [(0, half, terms(2))])], us=2,
                deps=(grad_rows,),
            )
        def all_rows(v, v_y, v_c):
            v_yc = swap(v_y, 0, 1)
            place = lambda n: pl.BlockSpec((n, width), lambda i, meta: (meta[1] ^ i, 0))
            return call(
                place_rows,
                name="place_rows",
                grid=(4,),
                scalars=1,
                ins=[whole(big)] * 4,
                outs=[((tok_count, width), BF, place(tok_own)), ((lat_count, width), BF, place(lat_own))],
                us=4,
            )(meta, v, v_c, v_y, v_yc)

        grad_tok, grad_lat = all_rows(grad_rows, grad_y, grad_c)
        out_tok, out_lat = all_rows(out_rows, out_y, swap(after(out_rows, out_y), 0, 1))
        four = (total,) + cube(total)
        grad_w_up, grad_w_down = combine(
            "weights_out", meta, four,
            [
                (4 * quarter, F32, [(at(d, quarter), quarter, [(i, r * quarter)]) for i, d in enumerate(sides4)])
                for r in (0, 1)
            ]
            ,
            us=5,
            deps=(qkv, out_y, grad_tok),
        )
        for bit in rest_bits:
            (qkv,) = combine("qkv_rest", meta, [qkv, swap(qkv, bit, 0)], [(rows4 + 32, BF, [(0, rows4 + 32, terms(2))])], us=2, deps=(total, total, grad_y))
        four = (qkv,) + tuple(
            swap(after(qkv, v), bit, 0) for v, bit in zip(four[1:], (x_bit, z_bit, x_bit | z_bit))
        )
        grad_w_qkv, grad_w_out, *vectors, grad_b_qv, roots = call(
            projections_out,
            name="qkv_out",
            scalars=1,
            ins=[whole((rows4 + 32, width))] * 4,
            outs=[out((3 * wide, width), F32), out((wide, width), F32)]
            + [((width,), F32, vec)] * 7
            + [out((2, wide), F32), out((8, LANES), F32)],
            us=3,
            deps=(out_tok, grad_w_up),
        )(meta, *four)
        grad_w_qkv = grad_w_qkv.reshape(3, wide, width).transpose(0, 2, 1)


        root_means = roots[0, :3]
        gain1, shift1, b_out_grad, gain2, shift2, b_down_grad, grad_b_up = vectors
        return (
            out_tok,
            out_lat,
            grad_tok,
            grad_lat,
            gain1,
            shift1,
            grad_w_qkv,
            grad_b_qv,
            grad_w_out,
            b_out_grad,
            gain2,
            shift2,
            grad_w_up,
            grad_b_up,
            grad_w_down,
            b_down_grad,
            root_means,
        )

    return per_device


def solution(mesh):
    rows, whole = P("dp", None), P()
    return jax.shard_map(
        make(mesh),
        mesh=mesh,
        in_specs=(
            rows,
            rows,
            whole,
            P("dp"),
            whole,
            whole,
            P(None, None, "mp"),
            P(None, "mp"),
            P("mp", None),
            whole,
            whole,
            whole,
            P(None, "mp"),
            P("mp"),
            P("mp", None),
            whole,
            rows,
            rows,
        ),
        out_specs=(
            rows,
            rows,
            rows,
            rows,
            whole,
            whole,
            P(None, None, "mp"),
            P(None, "mp"),
            P("mp", None),
            whole,
            whole,
            whole,
            P(None, "mp"),
            P("mp"),
            P("mp", None),
            whole,
            whole,
        ),
        check_vma=False,
    )
```

```python
import jax
import jax.numpy as jnp
from jax import lax
from jax.experimental import pallas as pl
from jax.experimental.pallas import tpu as pltpu
from jax.sharding import PartitionSpec as P

HEAD = 64
LANES = 128
GROUP = 256
LAT = 8
BF = jnp.bfloat16
F32 = jnp.float32
FAR = -1e30
MIB = 1 << 20
GAIN1, SHIFT1, B_OUT, GAIN2, SHIFT2, B_DOWN, B_UP = range(7)


def dot(a, b, ca, cb):
    return lax.dot_general(a, b, (((ca,), (cb,)), ((), ())), preferred_element_type=F32)


def norm_parts(values):
    center = values - jnp.mean(values, axis=-1, keepdims=True)
    spread = jnp.mean(center * center, axis=-1, keepdims=True)
    inverse = lax.rsqrt(spread + 1e-06)
    return center * inverse, inverse


def norm_back(grad, unit, inverse, gain):
    scaled = grad * gain
    inner = jnp.mean(scaled * unit, axis=-1, keepdims=True)
    return inverse * (scaled - jnp.mean(scaled, axis=-1, keepdims=True) - unit * inner)


def gelu_both(values):
    square = values * values
    inner = jnp.tanh(values * (0.7978845608028654 + 0.035677408136300125 * square))
    half = 0.5 + 0.5 * inner
    slope = values * (0.3989422804014327 + 0.05351611220494518 * square)
    return values * half, half + (1.0 - inner * inner) * slope


def split3(v):
    hi = v.astype(BF)
    mid = (v - hi.astype(F32)).astype(BF)
    low = (v - hi.astype(F32) - mid.astype(F32)).astype(BF)
    return hi, mid, low


def head_lanes(v, h):
    lane = lax.broadcasted_iota(jnp.int32, v.shape, v.ndim - 1)
    return jnp.where((lane >= h * HEAD) & (lane < (h + 1) * HEAD), v, jnp.zeros_like(v))


def kept(shape):
    return pl.BlockSpec(shape, lambda *_: (0,) * len(shape))


def whole(shape):
    return pl.BlockSpec(shape, lambda *_: (0,) * len(shape), pipeline_mode=pl.Buffered(1))


ANY = pl.BlockSpec(memory_space=pl.ANY)
OWN, SENT = (0, 1, 2, 3), (0, 2, 1, 3)


def block_bytes(shape, kind, copies):
    size = jnp.dtype(kind).itemsize
    dims = [1, 1] + list(shape)
    rows, lanes = 32 // size, LANES
    dims[-1] = -(-dims[-1] // lanes) * lanes
    dims[-2] = -(-dims[-2] // rows) * rows
    total = size * copies
    for d in dims:
        total *= d
    return total


def spec_bytes(spec, kind):
    if spec.block_shape is None:
        return 0
    return block_bytes(spec.block_shape, kind, 1 if spec.pipeline_mode is not None else 2)


def after(v, *deps):
    return lax.optimization_barrier((v,) + deps)[0]


def call(body, *, name, scalars, ins, outs, grid=(1,), scratch=(), deps=(), us=1.0, room=3):
    def run(*args):
        if deps:
            args = (after(args[0], *deps),) + args[1:]
        need = room * MIB + sum(spec_bytes(spec, kind) for _, kind, spec in outs)
        need += sum(spec_bytes(spec, a.dtype) for spec, a in zip(ins, args[scalars:]))
        need += sum(block_bytes(s.shape, s.dtype, 1) for s in scratch if s.shape and len(s.shape) > 1)
        return pl.pallas_call(
            body,
            name=name,
            out_shape=[jax.ShapeDtypeStruct(s, d) for s, d, _ in outs],
            grid_spec=pltpu.PrefetchScalarGridSpec(
                num_scalar_prefetch=scalars,
                grid=grid,
                in_specs=list(ins),
                out_specs=[spec for _, _, spec in outs],
                scratch_shapes=list(scratch),
            ),
            compiler_params=pltpu.CompilerParams(
                dimension_semantics=("arbitrary",) * len(grid), vmem_limit_bytes=need
            ),
            cost_estimate=pl.CostEstimate(
                flops=int(us * 1.0e10), bytes_accessed=1 << 16, transcendentals=0
            ),
        )(*args)

    return run


def mover(sems):
    used = []

    def start(src, dst):
        copy = pltpu.make_async_copy(src, dst, sems.at[len(used)])
        used.append(copy)
        copy.start()
        return copy

    return start


def sides(meta):
    return meta[0] & 1, (meta[0] >> 1) & 1


def combine(name, meta, arrays, outs, deps=(), us=1.0):
    def body(meta, *refs):
        x, z = sides(meta)

        def rows_at(at, n):
            return pl.ds(pl.multiple_of(at(x, z), 16), n) if callable(at) else slice(at, at + n)

        for ref, (_, kind, segments) in zip(refs[len(arrays) :], outs):
            for to, n, terms in segments:
                parts = [refs[i][rows_at(at, n), :] for i, at in terms]
                value = parts[0]
                if len(parts) > 1:
                    value = parts[0].astype(F32)
                    for part in parts[1:]:
                        value = value + part.astype(F32)
                ref[rows_at(to, n), :] = value.astype(kind)

    width = arrays[0].shape[1]
    return call(
        body,
        name=name,
        scalars=1,
        ins=[whole(a.shape) for a in arrays],
        outs=[((rows, width), kind, whole((rows, width))) for rows, kind, _ in outs],
        deps=deps,
        us=us,
    )(meta, *arrays)


def group_at(meta, count, slot, i):
    return count[(meta[1] ^ slot) * 2 + i]


def image_list(meta, image, devices, per_device, slots):
    each = per_device // 4
    return [
        image[(meta[0] ^ j) * per_device + (meta[1] ^ s) * each + i]
        for j in range(devices)
        for s in slots
        for i in range(each)
    ]


def image_column(images):
    return jnp.concatenate([jnp.full((LAT, 1), im, jnp.int32) for im in images], 0)


def image_row(images):
    group = lax.broadcasted_iota(jnp.int32, (1, len(images) * LAT), 1) // LAT
    out = jnp.zeros(group.shape, jnp.int32)
    for g, im in enumerate(images):
        out = jnp.where(group == g, im, out)
    return out


def key_stack(tok, lat8):
    pad = jnp.concatenate([lat8, jnp.zeros_like(lat8)], 0).astype(BF)
    return jnp.concatenate([tok, pad], 0)


def near_mask(count, columns):
    row = lax.broadcasted_iota(jnp.int32, (GROUP + 2 * LAT, columns), 0)
    return (row < count) | ((row >= GROUP) & (row < GROUP + LAT))


def param(params, i):
    return params[i : i + 1, :]


def project(rows, params, w, bias):
    unit, _ = norm_parts(rows.astype(F32))
    rows = (unit * param(params, GAIN1) + param(params, SHIFT1)).astype(BF)
    return (
        rows,
        (dot(rows, w[0], 1, 1) + bias[0:1]).astype(BF),
        dot(rows, w[1], 1, 1).astype(BF),
        (dot(rows, w[2], 1, 1) + bias[1:2]).astype(BF),
    )


def prepare(
    meta, lat, w_out, g1, s1, bo, g2, s2, bd, bu, up, down, lat_rel, lat_half, out_pack, part, params,
    vlat, vout, sems, *vecs,
):
    fetch = mover(sems)
    lat_copy = fetch(lat, vlat)
    copies = [fetch(ref, dst) for ref, dst in zip((g1, s1, bo, g2, s2, bd, bu), vecs)]
    x, z = sides(meta)
    n = part.shape[0] // 2
    here = pl.ds(pl.multiple_of((x * 2 + z) * n, 16), n)
    parts = [fetch(up.at[here], part.at[0:n]), fetch(down.at[here], part.at[n:])]
    wide = w_out.shape[0]
    parts.append(fetch(w_out, vout))
    lat_copy.wait()
    n = lat.shape[0] // 4
    for s in range(4):
        rows = vlat[pl.ds(pl.multiple_of((meta[1] ^ s) * n, 16), n), :]
        lat_rel[s * n : (s + 1) * n, :] = rows
        if s % 2 == 0:
            lat_half[s // 2 * n : (s // 2 + 1) * n, :] = rows
    for copy in copies:
        copy.wait()
    for i in range(7):
        params[i : i + 1, :] = vecs[i][...].reshape(1, params.shape[1])
    params[7:8, :] = jnp.zeros_like(params[7:8, :])
    bias = param(params, B_UP)
    rows = [v.astype(F32) for v in split3(bias)]
    out_pack[wide : wide + 16, :] = jnp.concatenate(rows + [jnp.zeros((13, bias.shape[1]), F32)], 0).astype(BF)
    for copy in parts:
        copy.wait()
    out_pack[0:wide, :] = vout[...]


def latent_rows(lat, params, w, bias, normed, ql, kl, vl):
    normed[...], a, b, c = project(lat[...], params, w, bias)
    ql[...], kl[...], vl[...] = a.astype(F32), b.astype(F32), c.astype(F32)


def forward_near(base, meta, count, tok, kl, vl, params, w, bias, normed, q, k, v, mixed_out, log):
    step = pl.program_id(0)
    wide = w.shape[1]
    rows, qs, ks, vs = project(tok[...], params, w, bias)
    normed[...], q[...], k[...], v[...] = rows, qs, ks, vs
    qs = qs * jnp.asarray(0.125, BF)
    for i in range(tok.shape[0] // GROUP):
        here = slice(i * LAT, (i + 1) * LAT)
        at = slice(i * GROUP, (i + 1) * GROUP)
        keys = key_stack(ks[at], kl[here, :])
        values = key_stack(vs[at], vl[here, :]).T
        mask = near_mask(group_at(meta, count, step + base, i), GROUP)
        logs, outs = [], []
        for h in range(wide // HEAD):
            s = jnp.where(mask, dot(head_lanes(keys, h), qs[at], 1, 1), FAR)
            top = jnp.max(s, 0, keepdims=True)
            e = jnp.exp(s - top)
            total = jnp.sum(e, 0, keepdims=True)
            logs.append(top + jnp.log(total))
            outs.append(dot(values[h * HEAD : (h + 1) * HEAD], e.astype(BF), 1, 0) * (1.0 / total))
        log[i] = jnp.concatenate(logs + [jnp.zeros((8 - len(logs), GROUP), F32)], 0)
        mixed_out[:, at] = jnp.concatenate(outs, 0).astype(BF)


def forward_far(meta, count, image, lat, params, w, bias, k_near, k_away, v_near, v_away, ql, qa, ka, va, m_near, m_away, far, logs_out):
    step = pl.program_id(0)
    wide = w.shape[1]
    rows_step = lat.shape[0]
    own = ql.shape[0]
    groups = own // LAT

    def rows_of(near, away, g):
        half = groups // 2
        ref, at = (near, g) if g < half else (away, g - half)
        return ref[at * GROUP : (at + 1) * GROUP, :]

    _, a, b, c = project(lat[...], params, w, bias)
    here = pl.ds(pl.multiple_of(step * rows_step, rows_step), rows_step)
    qa[here, :], ka[here, :], va[here, :] = a, b, c

    @pl.when(step == pl.num_programs(0) - 1)
    def _():
        q32 = ql[...] * 0.125
        images = image_list(meta, image, qa.shape[0] // own, groups, SENT)
        mask = image_column(image_list(meta, image, 1, groups, OWN)) == image_row(images)
        lane = lax.broadcasted_iota(jnp.int32, (LAT, GROUP), 1)
        full = jnp.zeros((own, wide), F32)
        logs = []
        for h in range(wide // HEAD):
            qh = head_lanes(q32, h)
            s_lat = jnp.where(mask, dot(qh.astype(BF), ka[...], 1, 1), FAR)
            s_tok = jnp.concatenate(
                [
                    jnp.where(
                        lane < group_at(meta, count, g // 2, g % 2),
                        dot(qh[g * LAT : (g + 1) * LAT].astype(BF), rows_of(k_near, k_away, g), 1, 1),
                        FAR,
                    )
                    for g in range(groups)
                ],
                0,
            )
            top = jnp.maximum(jnp.max(s_lat, 1, keepdims=True), jnp.max(s_tok, 1, keepdims=True))
            e_lat, e_tok = jnp.exp(s_lat - top), jnp.exp(s_tok - top)
            total = jnp.sum(e_lat, 1, keepdims=True) + jnp.sum(e_tok, 1, keepdims=True)
            logs.append(top + jnp.log(total))
            near = jnp.concatenate(
                [
                    dot(e_tok[g * LAT : (g + 1) * LAT].astype(BF), rows_of(v_near, v_away, g), 1, 0)
                    for g in range(groups)
                ],
                0,
            )
            full = full + head_lanes((dot(e_lat.astype(BF), va[...], 1, 0) + near) * (1.0 / total), h)
        mixed = full.astype(BF)
        m_near[...], m_away[...] = mixed[: own // 2], mixed[own // 2 :]
        parts = [split3(x) for x in logs]
        cols = [p[i] for i in range(3) for p in parts]
        lane = lax.broadcasted_iota(jnp.int32, (own, 2 * HEAD), 1)
        extra = jnp.zeros((own, 2 * HEAD), F32)
        for i, c in enumerate(cols):
            extra = jnp.where(lane == i, c.astype(F32), extra)
        far[...] = mixed
        logs_out[...] = extra.astype(BF)


def valid_rows(meta, count, rows):
    row = lax.broadcasted_iota(jnp.int32, (rows, 1), 0)
    first = (row < GROUP) & (row < group_at(meta, count, 0, 0))
    return first | ((row >= GROUP) & (row < GROUP + group_at(meta, count, 0, 1)))


def slot_block(meta, ref, slot):
    n = ref.shape[0] // 4
    return ref.at[pl.ds(pl.multiple_of((meta[1] ^ slot) * n, 16), n)]


def project_out(t_near, t_far, l_near, l_far, o0, o2, out):
    wide, n = t_near.shape
    value = dot(t_near[...], o0[0:wide, :], 0, 0) + dot(t_far[...], o2[0:wide, :], 0, 0)
    out[0:n, :] = value.astype(out.dtype)
    value = dot(l_near[...], o0[0:wide, :], 1, 0) + dot(l_far[...], o2[0:wide, :], 1, 0)
    out[n:, :] = value.astype(out.dtype)


def cot_back(meta, cot_tok, cot_lat, down_w, out):
    n = cot_tok.shape[0]
    out[0:n, :] = dot(cot_tok[...], down_w[...], 1, 1).astype(BF)
    out[n:, :] = dot(cot_lat[...], down_w[...], 1, 1).astype(BF)


def add_norm(meta, count, params, own, got, tok, lat, residual, n2, stats):
    n, m = tok.shape[0], lat.shape[0]
    stats[...] = jnp.zeros_like(stats)
    for at, size, x in ((0, n, tok), (n, m, lat)):
        rows = slice(at, at + size)
        attn = own[rows, :] + got[rows, :].astype(F32) + param(params, B_OUT)
        if at == 0:
            real = valid_rows(meta, count, n)
            stats[0:1, :] = jnp.sum(jnp.where(real, attn * attn, 0.0), 0, keepdims=True)
        res = x[...].astype(F32) + attn
        residual[rows, :] = res
        unit, _ = norm_parts(res)
        n2[rows, :] = (unit * param(params, GAIN2) + param(params, SHIFT2)).astype(BF)


def hidden_part(n2, cot, up_w, down_w, bias, act_out, grad_out):
    cut = 256
    sums = []
    for at in range(0, up_w.shape[1], cut):
        cols = slice(at, at + cut)
        up = dot(n2, up_w[:, cols], 1, 0) + bias[:, cols]
        active, slope = gelu_both(up)
        grad_up = (dot(cot, down_w[cols, :], 1, 1) * slope).astype(BF)
        act_out[:, cols] = active.astype(BF)
        grad_out[:, cols] = grad_up
        sums.append(jnp.sum(grad_up.astype(F32), 0, keepdims=True))
    return jnp.concatenate(sums, 1)


def two_halves(meta, fetch, n2_own, n2_sib, cot_tok, cot_lat, vn2, vcot):
    rows = n2_own.shape[0]
    n = cot_tok.shape[0] // 4
    copies = [fetch(n2_own, vn2.at[0:rows]), fetch(n2_sib, vn2.at[rows:])]
    for s in (0, 1):
        at = s * rows
        copies.append(fetch(slot_block(meta, cot_tok, s), vcot.at[at : at + n]))
        copies.append(fetch(slot_block(meta, cot_lat, s), vcot.at[at + n : at + rows]))
    return copies


def send_parts(meta, flush, pack, parts):
    x, z = sides(meta)
    n = parts[0].shape[0] // 2
    copies = []
    for ref, (dx, dz) in zip(parts, ((0, 0), (1, 0), (0, 1), (1, 1))):
        q = (x ^ dx) * 2 + (z ^ dz)
        for i in (0, 1):
            src = pack.at[pl.ds(pl.multiple_of(i * 4 * n + q * n, 16), n)]
            copies.append(flush(src, ref.at[i * n : (i + 1) * n]))
    return copies


def hidden_rows(n2, up_w, bias, got, act_out, grad_out, sums):
    cut = 256
    for at in range(0, up_w.shape[1], cut):
        cols = slice(at, at + cut)
        active, slope = gelu_both(dot(n2, up_w[:, cols], 1, 0) + bias[:, cols])
        grad_up = (got[:, cols].astype(F32) * slope).astype(BF)
        act_out[:, cols] = active.astype(BF)
        grad_out[:, cols] = grad_up
        sums[0:1, cols] = jnp.sum(grad_up.astype(F32), 0, keepdims=True)


def hidden_first(params, n2, up_w, got, act, grad, stats):
    stats[...] = jnp.zeros_like(stats)
    hidden_rows(n2[...], up_w, param(params, B_UP), got, act, grad, stats)


def hidden_own(
    meta, params, n2_own, n2_sib, cot_tok, cot_lat, up_w, got_in, act_in, grad_in,
    act_out, grad_out, p0, p1, p2, p3, stats,
    vn2, vcot, vw, act, grad, got, vpack, in_sems, out_sems,
):
    width, hidden = vw.shape
    rows = got.shape[0]
    fetch, flush = mover(in_sems), mover(out_sems)
    first = [fetch(n2_sib, vn2.at[rows:]), fetch(up_w, vw), fetch(got_in, got)]
    copies = [fetch(grad_in, grad.at[0:rows]), fetch(act_in, act.at[0:rows]), fetch(n2_own, vn2.at[0:rows])]
    n = cot_tok.shape[0] // 4
    for s in (0, 1):
        at = s * rows
        copies.append(fetch(slot_block(meta, cot_tok, s), vcot.at[at : at + n]))
        copies.append(fetch(slot_block(meta, cot_lat, s), vcot.at[at + n : at + rows]))
    for copy in first:
        copy.wait()
    stats[...] = jnp.zeros_like(stats)
    hidden_rows(vn2[rows:, :], vw, param(params, B_UP), got, act.at[rows:], grad.at[rows:], stats)
    for copy in copies:
        copy.wait()
    outs = [flush(act, act_out), flush(grad, grad_out)]
    vpack[0:width, :] = dot(vn2[...], grad[...], 0, 0).astype(BF)
    vpack[width : width + hidden, :] = dot(act[...], vcot[...], 0, 0).astype(BF)
    outs += send_parts(meta, flush, vpack, (p0, p1, p2, p3))
    for copy in outs:
        copy.wait()


def hidden_away(
    meta, o2, n2_own, n2_sib, cot_tok, cot_lat, w0, w1, w2, w3, act_in, grad_in, up_w, down_w,
    branch_own, back_own, send, act_out, grad_out, stats,
    vn2, vcot, vw, vnear, act0, grad0, branch, back, act, grad, vsend, in_sems, out_sems,
):
    rows, width = n2_own.shape
    x, z = sides(meta)
    quarter = w0.shape[0] // 2
    fetch, flush = mover(in_sems), mover(out_sems)
    copies = two_halves(meta, fetch, n2_own, n2_sib, cot_tok, cot_lat, vn2, vcot)
    for ref, (dx, dz) in zip((w0, w1, w2, w3), ((0, 0), (1, 0), (0, 1), (1, 1))):
        q = pl.multiple_of(((x ^ dx) * 2 + (z ^ dz)) * quarter, 16)
        for i in (0, 1):
            copies.append(fetch(ref.at[i * quarter : (i + 1) * quarter], vw.at[i, pl.ds(q, quarter)]))
    late = [(fetch(grad_in, grad0), fetch(up_w, vnear.at[0])), (fetch(act_in, act0), fetch(down_w, vnear.at[1]))]
    for copy in copies:
        copy.wait()
    base = o2.shape[0] - 16
    bias = o2[base : base + 16, :].astype(F32)
    bias = bias[0:1] + bias[1:2] + bias[2:3]
    n2, ct = vn2[...], vcot[...]
    stats[...] = jnp.zeros_like(stats)
    stats[0:1, :] = hidden_part(n2, ct, vw.at[0], vw.at[1], bias, act, grad)
    outs = [flush(act, act_out), flush(grad, grad_out)]
    for i, (ref, near, src, turn, own) in enumerate(
        ((back, grad0, grad, 1, back_own), (branch, act0, act, 0, branch_own))
    ):
        for copy in late[i]:
            copy.wait()
        ref[...] = dot(near[...], vnear[i], 1, turn) + dot(src[...], vw[i], 1, turn)
        vsend[i * rows : (i + 1) * rows, :] = ref[rows:, :].astype(BF)
        outs.append(flush(ref.at[0:rows], own))
        outs.append(flush(vsend.at[i * rows : (i + 1) * rows], send.at[i * rows : (i + 1) * rows]))
    for copy in outs:
        copy.wait()


def away_grads(
    meta, n2_own, n2_sib, cot_tok, cot_lat, act_in, grad_in, p0, p1, p2, p3,
    vn2, vcot, act, grad, vpack, in_sems, out_sems,
):
    width, hidden = vn2.shape[1], act.shape[1]
    fetch, flush = mover(in_sems), mover(out_sems)
    copies = [fetch(grad_in, grad)] + two_halves(meta, fetch, n2_own, n2_sib, cot_tok, cot_lat, vn2, vcot)
    last = fetch(act_in, act)
    for copy in copies:
        copy.wait()
    vpack[0:width, :] = dot(vn2[...], grad[...], 0, 0).astype(BF)
    last.wait()
    vpack[width : width + hidden, :] = dot(act[...], vcot[...], 0, 0).astype(BF)
    for copy in send_parts(meta, flush, vpack, (p0, p1, p2, p3)):
        copy.wait()


def middle_rows(meta, count, params, residual, branch, back, got, cot_tok, cot_lat, out_rows, grad_res, grad_attn, stats):
    n, m = cot_tok.shape[0], cot_lat.shape[0]
    rows_own = n + m
    stats[...] = jnp.zeros_like(stats)
    for at, size, cot in ((0, n, cot_tok), (n, m, cot_lat)):
        rows = slice(at, at + size)
        bk = back[rows, :] + got[rows, :].astype(F32)
        br = branch[rows, :] + got[rows_own + at : rows_own + at + size, :].astype(F32) + param(params, B_DOWN)
        res = residual[rows, :]
        out = res + br
        out_rows[rows, :] = out.astype(BF)
        if at == 0:
            real = valid_rows(meta, count, n)
            stats[0:1, :] = jnp.sum(jnp.where(real, out * out, 0.0), 0, keepdims=True)
            stats[1:2, :] = jnp.sum(jnp.where(real, br * br, 0.0), 0, keepdims=True)
        unit, inverse = norm_parts(res)
        stats[2:3, :] += jnp.sum(bk * unit, 0, keepdims=True)
        stats[3:4, :] += jnp.sum(bk, 0, keepdims=True)
        cot32 = cot[...].astype(F32)
        gr = cot32 + norm_back(bk, unit, inverse, param(params, GAIN2))
        grad_res[rows, :] = gr
        ga = gr.astype(BF)
        grad_attn[rows, :] = ga
        stats[4:5, :] += jnp.sum(ga.astype(F32), 0, keepdims=True)
        stats[5:6, :] += jnp.sum(cot32, 0, keepdims=True)


def back_out(meta, ga_own, ga_sib, o0, o2, t_near, t_far, l_near, l_far, g0, g2, d0, w0, sent):
    wide, n = t_near.shape[0], t_near.shape[1] // 2
    m = l_near.shape[0] // 2
    sent[wide:, :] = jnp.zeros_like(sent[wide:, :])
    for o, g, d, at in ((o2, g2, sent, wide), (o0, g0, d0, 0)):
        for i, ga in enumerate((ga_own, ga_sib)):
            g[:, i * n : (i + 1) * n] = dot(o[0:wide, :], ga[0:n, :], 1, 1).astype(BF)
            rows = dot(ga[n : n + m, :], o[0:wide, :], 1, 1).astype(BF)
            d[at + i * m : at + (i + 1) * m, 0:wide] = rows
    for t, l, w in ((t_far, l_far, sent.at[0:wide]), (t_near, l_near, w0)):
        total = jnp.zeros(w0.shape, F32)
        for i, ga in enumerate((ga_own, ga_sib)):
            total += dot(t[:, i * n : (i + 1) * n], ga[0:n, :], 1, 0)
            total += dot(l[i * m : (i + 1) * m, :], ga[n : n + m, :], 0, 0)
        w[...] = total.astype(BF)


def near_slot(
    slot, meta, count, normed, q, k, v, ql, kl, vl, log, far, logs_far, d_in, d_lat_in, w, grad_w, bias,
    dq_far, dk_near, dv_near,
):
    wide = q.shape[1]
    heads = wide // HEAD
    rows = normed[...]
    slot_rows = rows.shape[0]
    d_lat = d_lat_in[:, 0 : q.shape[1]].astype(F32)
    eighth = jnp.asarray(0.125, BF)
    q_all, k_all, v_all = q[...] * eighth, k[...], v[...]
    far32 = far[...].astype(F32)
    far_log = logs_far[...].astype(F32)
    dqs, dks, dvs = [], [], []
    for i in range(slot_rows // GROUP):
        at, lat_at = slice(i * GROUP, (i + 1) * GROUP), slice(i * LAT, (i + 1) * LAT)
        number = group_at(meta, count, slot, i)
        d_cols = d_in[:, at]
        d_tok, qs, ks, vs = d_cols.T, q_all[at], k_all[at], v_all[at]
        keys, values = key_stack(ks, kl[lat_at, :]), key_stack(vs, vl[lat_at, :])
        keys_t = keys.T
        mask = near_mask(number, GROUP)
        ps, gs, dq_t, d_heads, q_heads = [], [], [], [], []
        for h in range(heads):
            s = dot(head_lanes(keys, h), qs, 1, 1)
            p = jnp.where(mask, jnp.exp(s - log[i, h : h + 1, :]), 0.0)
            gp = p * dot(head_lanes(values, h), d_cols, 1, 0)
            g = (gp - p * jnp.sum(gp, 0, keepdims=True)).astype(BF)
            dq_t.append(dot(keys_t[h * HEAD : (h + 1) * HEAD], g, 1, 0))
            ps.append(p.astype(BF))
            gs.append(g)
            d_heads.append(head_lanes(d_tok, h))
            q_heads.append(head_lanes(qs, h))
        dv = dot(jnp.concatenate(ps, 1), jnp.concatenate(d_heads, 0), 1, 0)
        dk = dot(jnp.concatenate(gs, 1), jnp.concatenate(q_heads, 0), 1, 0)
        dqs.append((jnp.concatenate(dq_t, 0).T * 0.125).astype(BF))
        pad = jnp.zeros((LAT, wide), F32)
        q8, o8, d8, lg = ql[lat_at, :] * 0.125, far32[lat_at], d_lat[lat_at], far_log[lat_at]
        q_rows, do_rows, log_col, del_col = [], [], [], []
        big = jnp.full((LAT, 1), 1e30, F32)
        zero = jnp.zeros((LAT, 1), F32)
        for h in range(heads):
            q_rows += [head_lanes(q8, h), pad]
            dh = head_lanes(d8, h)
            do_rows += [dh, pad]
            col = lg[:, h : h + 1] + lg[:, heads + h : heads + h + 1] + lg[:, 2 * heads + h : 2 * heads + h + 1]
            log_col += [col, big]
            del_col += [jnp.sum(dh * o8, 1, keepdims=True), zero]
        q_f, d_f = jnp.concatenate(q_rows, 0).astype(BF), jnp.concatenate(do_rows, 0).astype(BF)
        l_f, x_f = jnp.concatenate(log_col, 0), jnp.concatenate(del_col, 0)
        lane = lax.broadcasted_iota(jnp.int32, (2 * LAT * heads, GROUP), 1)
        p_f = jnp.where(lane < number, jnp.exp(dot(q_f, ks, 1, 1) - l_f), 0.0)
        g_f = (p_f * (dot(d_f, vs, 1, 1) - x_f)).astype(BF)
        dks.append((dk[0:GROUP] + dot(g_f, q_f, 0, 0)).astype(BF))
        dvs.append((dv[0:GROUP] + dot(p_f.astype(BF), d_f, 0, 0)).astype(BF))
        dk_near[lat_at, :] = dk[GROUP : GROUP + LAT]
        dv_near[lat_at, :] = dv[GROUP : GROUP + LAT]
        dq_all = dot(g_f, ks, 1, 0)
        dq_lat = jnp.zeros((LAT, wide), F32)
        for h in range(heads):
            dq_lat += head_lanes(dq_all[2 * LAT * h : 2 * LAT * h + LAT], h)
        dq_far[lat_at, :] = dq_lat

    dq, dk, dv = (jnp.concatenate(v, 0) for v in (dqs, dks, dvs))
    total = dot(dq, w[0], 1, 0) + dot(dk, w[1], 1, 0) + dot(dv, w[2], 1, 0)
    for i, g in enumerate((dq, dk, dv)):
        grad_w[i] += dot(g, rows, 0, 0)
    bias[0:1, :] += jnp.sum(dq.astype(F32), 0, keepdims=True)
    bias[1:2, :] += jnp.sum(dv.astype(F32), 0, keepdims=True)
    bias[2:3, :] += jnp.sum(dk.astype(F32), 0, keepdims=True)
    return total.astype(BF)


def backward_rows(
    first, begin, meta, count, normed, q, k, v, ql, kl, vl, log, far, logs_far, d_in, d_lat, w, gw_in, bias_in, *outs,
):
    step = pl.program_id(0)
    parts, (grad_w, bias, dq_far, dk_near, dv_near) = outs[:-5], outs[-5:]

    @pl.when(step == 0)
    def _():
        grad_w[...] = jnp.zeros_like(grad_w) if begin else gw_in[...]
        bias[...] = jnp.zeros_like(bias) if begin else bias_in[...]

    total = near_slot(
        step + first, meta, count, normed, q, k, v, ql, kl, vl, log, far, logs_far, d_in, d_lat, w, grad_w, bias,
        dq_far, dk_near, dv_near,
    )
    for slot, ref in enumerate(parts):

        @pl.when(step == slot)
        def _(ref=ref):
            ref[...] = total


def latent_bundle(meta, d_near, d_far, far, logs_far, own, sent):
    count, wide = far.shape
    heads = wide // HEAD
    n = count // 4
    d32 = jnp.concatenate([d_near[...], d_far[:, 0:wide]], 0).astype(F32)
    prod = d32 * far[...].astype(F32)
    lg = logs_far[...].astype(F32)
    deltas = [split3(jnp.sum(head_lanes(prod, h), 1, keepdims=True)) for h in range(heads)]
    cols = [lg[:, i : i + 1] for i in range(3 * heads)] + [p[i].astype(F32) for i in (0, 1) for p in deltas]
    lane = lax.broadcasted_iota(jnp.int32, (count, 4 * HEAD), 1)
    value = jnp.concatenate([d32, jnp.zeros((count, HEAD), F32)], 1)
    for i, c in enumerate(cols):
        value = jnp.where(lane == wide + i, c, value)
    value = value.astype(BF)
    own[...] = value
    for i, s in enumerate(SENT):
        sent[i * n : (i + 1) * n, :] = value[s * n : (s + 1) * n]


def backward_far(
    meta, tokens_real, image, qa, ka, va, ql, kl, vl, own, bundle, normed, w, gw, bias_in, wo_a, wo_b,
    params, stats1, stats2, hid_first, hid_near, hid_away, *refs,
):
    near, (lat_keep, lat_send, p0, p1, p2, p3, small, pack, out_sems) = refs[:-9], refs[-9:]
    count, wide = ql.shape
    heads = wide // HEAD
    groups = count // LAT
    q_all, k_all, v_all = qa[...] * jnp.asarray(0.125, BF), ka[...], va[...]
    q_own, k_own, v_own = (ql[...] * 0.125).astype(BF), kl[...].astype(BF), vl[...].astype(BF)
    d_own, d_all = own[:, 0:wide], bundle[:, 0:wide]

    def stats(ref, h):
        x = ref[...].astype(F32)
        col = [x[:, wide + i : wide + i + 1] for i in range(5 * heads)]
        return col[h] + col[heads + h] + col[2 * heads + h], col[3 * heads + h] + col[4 * heads + h]

    mine = image_list(meta, image, 1, groups, OWN)
    images = image_list(meta, image, qa.shape[0] // count, groups, SENT)
    mask_q = image_column(mine) == image_row(images)
    mask_k = image_column(images) == image_row(mine)
    each = len(near) // 3
    dq, dk, dv = (jnp.concatenate([ref[...] for ref in near[i * each : (i + 1) * each]], 0) for i in range(3))
    for h in range(heads):
        log, delta = stats(own, h)
        s = dot(head_lanes(q_own, h), k_all, 1, 1)
        p = jnp.where(mask_q, jnp.exp(s - log), 0.0)
        g = (p * (dot(head_lanes(d_own, h), v_all, 1, 1) - delta)).astype(BF)
        dq += head_lanes(dot(g, k_all, 1, 0), h)
        log, delta = stats(bundle, h)
        s = dot(q_all, head_lanes(k_own, h), 1, 1)
        p = jnp.where(mask_k, jnp.exp(s - log), 0.0)
        g = (p * (dot(d_all, head_lanes(v_own, h), 1, 1) - delta)).astype(BF)
        dk += head_lanes(dot(g, q_all, 0, 0), h)
        dv += head_lanes(dot(p.astype(BF), d_all, 0, 0), h)
    dq, dk, dv = (dq * 0.125).astype(BF), dk.astype(BF), dv.astype(BF)
    lat_rows = normed[...]
    sums = [bias_in[i : i + 1, :] for i in (0, 2, 1)]
    sums = [b + jnp.sum(g.astype(F32), 0, keepdims=True) for b, g in zip(sums, (dq, dk, dv))]
    columns = jnp.concatenate(sums + [jnp.zeros((5, wide), F32)], 0).T
    first_gain = jnp.zeros((1, pack.shape[1]), F32)
    first_shift = first_gain
    for i, g in enumerate((dq, dk, dv)):
        total = gw[i] + dot(g, lat_rows, 0, 0)
        pack[i * wide : (i + 1) * wide, :] = total.astype(BF)
        col, weight = columns[:, i : i + 1], w[i].astype(F32)
        first_shift += jnp.sum(weight * col, 0, keepdims=True)
        first_gain += jnp.sum(weight * (total - col * param(params, SHIFT1)), 0, keepdims=True)
    first_gain = first_gain / param(params, GAIN1)
    pack[3 * wide :, :] = (wo_a[...].astype(F32) + wo_b[...].astype(F32)).astype(BF)
    x, z = sides(meta)
    flush = mover(out_sems)
    copies = []
    for ref, (dx, dz) in zip((p0, p1, p2, p3), ((0, 0), (1, 0), (0, 1), (1, 1))):
        part = (x ^ dx) * 2 + (z ^ dz)
        at = 0
        for base, size in ((0, 3 * wide // 4), (3 * wide, wide // 4)):
            src = pack.at[pl.ds(pl.multiple_of(base + part * size, 16), size)]
            copies.append(flush(src, ref.at[at : at + size]))
            at += size
    rows = (dot(dq, w[0], 1, 0) + dot(dk, w[1], 1, 0) + dot(dv, w[2], 1, 0)).astype(BF)
    n = count // 4
    lat_keep[0:n, :], lat_keep[n : 2 * n, :] = rows[0:n], rows[2 * n : 3 * n]
    lat_send[0:n, :], lat_send[n : 2 * n, :] = rows[n : 2 * n], rows[3 * n :]
    small[...] = jnp.zeros_like(small)
    small[0:1, :] = stats1[0:1, :]
    small[1:7, :] = stats2[0:6, :]
    small[7:8, :], small[8:9, :] = first_gain, first_shift
    real = tokens_real[0]
    for i in range(1, tokens_real.shape[0]):
        real = real + tokens_real[i]
    for at, part in ((9, real - real % 64), (22, real % 64)):
        small[at : at + 1, :] = jnp.full((1, small.shape[1]), 0.25, F32) * part.astype(F32)
    for s, row in ((0, hid_first[0:1, :] + hid_near[0:1, :]), (2, hid_away[0:1, :])):
        small[pl.ds(10 + (meta[1] ^ s), 1), :] = row
    small[pl.ds(14 + meta[1], 1), 0:wide] = sums[0]
    small[pl.ds(18 + meta[1], 1), 0:wide] = sums[2]
    for copy in copies:
        copy.wait()


def final_rows(meta, tok, lat, a, b, c, la, lb, grad_res, params, out):
    n, m = tok.shape[0], lat.shape[0]
    for x, at, terms in ((tok, slice(0, n), (a, b)), (lat, slice(n, n + m), (la, lb))):
        grad = c[at, :].astype(F32)
        for term in terms:
            grad += term[0 : x.shape[0], :].astype(F32)
        unit, inverse = norm_parts(x[...].astype(F32))
        out[at, :] = (grad_res[at, :] + norm_back(grad, unit, inverse, param(params, GAIN1))).astype(BF)


def place_rows(meta, a, b, c, d, tok_out, lat_out):
    n = tok_out.shape[0]
    for i, ref in enumerate((a, b, c, d)):

        @pl.when(pl.program_id(0) == i)
        def _(ref=ref):
            tok_out[...] = ref[0:n, :]
            lat_out[...] = ref[n:, :]


def projections_out(meta, f0, f1, f2, f3, grad_w, grad_o, gain1, shift1, b_out, gain2, shift2, b_down, b_up, b_qv, roots):
    x, z = sides(meta)
    wide = grad_o.shape[0]
    four = (f0, f1, f2, f3)
    for ref, (dx, dz) in zip(four, ((0, 0), (1, 0), (0, 1), (1, 1))):
        part = (x ^ dx) * 2 + (z ^ dz)
        at = 0
        for dst, size in ((grad_w, 3 * wide // 4), (grad_o, wide // 4)):
            dst[pl.ds(pl.multiple_of(part * size, 16), size), :] = ref[at : at + size, :].astype(F32)
            at += size
    small = four[0][wide : wide + 32, :].astype(F32)
    for ref in four[1:]:
        small += ref[wide : wide + 32, :].astype(F32)
    for ref, row in ((gain1, 7), (shift1, 8), (b_out, 5), (gain2, 3), (shift2, 4), (b_down, 6)):
        ref[...] = small[row, :]

    def of_mp(first):
        value = small[first : first + 1]
        for m in (1, 2, 3):
            value = jnp.where(meta[1] == m, small[first + m : first + m + 1], value)
        return value

    b_up[...] = of_mp(10)[0]
    b_qv[...] = jnp.concatenate([of_mp(14)[:, 0:wide], of_mp(18)[:, 0:wide]], 0)
    real = (small[9:10, 0:1] + small[22:23, 0:1]) * small.shape[1]
    lane = lax.broadcasted_iota(jnp.int32, roots.shape, 1)
    value = jnp.zeros(roots.shape, F32)
    for i, row in enumerate((1, 0, 2)):
        root = jnp.sqrt(jnp.sum(small[row : row + 1], 1, keepdims=True) / real)
        value = jnp.where(lane == i, root, value)
    roots[...] = value


def make(mesh):
    dp_size, mp_size = mesh.shape["dp"], mesh.shape["mp"]
    assert mp_size == 4 and dp_size >= 4
    dp_bits = [1 << i for i in range(dp_size.bit_length() - 1)]
    assert 1 << len(dp_bits) == dp_size
    x_bit, z_bit, rest_bits = dp_bits[0], dp_bits[1], dp_bits[2:]

    def swap(v, dp_bit, mp_bit):
        pairs = [
            (d * mp_size + m, (d ^ dp_bit) * mp_size + (m ^ mp_bit))
            for d in range(dp_size)
            for m in range(mp_size)
        ]
        return lax.ppermute(v, ("dp", "mp"), pairs)

    def per_device(
        tokens,
        latents,
        image_of_group,
        token_valid,
        norm1_gain,
        norm1_shift,
        w_qkv,
        b_qv,
        w_out,
        b_out,
        norm2_gain,
        norm2_shift,
        w_up,
        b_up,
        w_down,
        b_down,
        cot_tokens,
        cot_latents,
    ):
        dp_at, mp_at = lax.axis_index("dp"), lax.axis_index("mp")
        tok_count, width = tokens.shape
        lat_count = latents.shape[0]
        groups = lat_count // LAT
        wide = w_qkv.shape[2]
        hidden = w_up.shape[1]
        tok_own, lat_own = tok_count // 4, lat_count // 4
        rows_own = tok_own + lat_own
        all_lat = dp_size * lat_count
        meta = jnp.stack([dp_at, mp_at]).astype(jnp.int32)
        count = jnp.sum(token_valid.reshape(groups, GROUP), 1).astype(jnp.int32)
        par = whole((8, width))
        w_t = jnp.transpose(w_qkv, (0, 2, 1))
        w_all = (3, wide, width)
        quarter, small = width // 4, wide // 4
        half = 2 * quarter
        big = (rows_own, width)
        chip_rows, chip_tok, chip_lat = 2 * rows_own, 2 * tok_own, 2 * lat_own
        vec = pl.BlockSpec((width,), lambda *_: (0,))

        def out(shape, kind=BF):
            return (shape, kind, whole(shape))

        def kept_out(shape, kind=BF):
            return (shape, kind, kept(shape))

        vm = pltpu.VMEM

        def any_out(shape, kind=BF):
            return (shape, kind, ANY)

        def dma(n):
            return pltpu.SemaphoreType.DMA((n,))

        def cube(v, vx=None, vz=None, vxz=None):
            vx, vz, vxz = (v if w is None else w for w in (vx, vz, vxz))
            return swap(vx, x_bit, 0), swap(vz, z_bit, 0), swap(vxz, x_bit | z_bit, 0)

        def all_latents(v):
            v = jnp.concatenate((v,) + cube(v), 0)
            for bit in rest_bits:
                v = jnp.concatenate([v, swap(v, bit, 0)], 0)
            return v

        part_block = pl.BlockSpec((quarter, width), lambda i, meta: ((meta[0] & 1) * 2 + ((meta[0] >> 1) & 1), 0))
        lat_rel, lat_half, o0, weight_part, params = call(
            prepare,
            name="prepare",
            room=62,
            scalars=1,
            ins=[pl.BlockSpec(memory_space=pltpu.HBM)] * 11,
            outs=[out((lat_count, width)), out((chip_lat, width)), out((wide + 16, width)), out((half, width)), out((8, width), F32)],
            scratch=[vm((lat_count, width), BF), vm((wide, width), BF), dma(11)] + [vm((width,), F32)] * 7,
            us=2,
        )(meta, latents, w_out, norm1_gain, norm1_shift, b_out, norm2_gain, norm2_shift, b_down, b_up, w_up, w_down)
        lat_four = jnp.concatenate((lat_half,) + cube(lat_half), 0)
        w_own = swap(weight_part, 0, 2)
        o2 = swap(o0, 0, 2)

        normed_lat, ql, kl, vl = call(
            latent_rows,
            name="latent_rows",
            room=3,
            scalars=0,
            ins=[whole((lat_count, width)), par, whole(w_all), whole((2, wide))],
            outs=[out((lat_count, width))] + [out((lat_count, wide), F32)] * 3,
            us=2,
        )(lat_rel, params, w_t, b_qv)

        def cot_through(slot, meta):
            return call(
                cot_back,
                name="cot_back",
            room=4,
                scalars=1,
                ins=[
                    pl.BlockSpec((tok_own, width), lambda i, meta: (meta[1] ^ slot, 0), pipeline_mode=pl.Buffered(1)),
                    pl.BlockSpec((lat_own, width), lambda i, meta: (meta[1] ^ slot, 0), pipeline_mode=pl.Buffered(1)),
                    whole((hidden, width)),
                ],
                outs=[out((rows_own, hidden))],
                us=4,
            )(meta, cot_tokens, cot_latents, w_down)[0]

        cot_own = cot_through(0, after(meta, kl))
        lat_here = lat_four = after(lat_four, cot_own)
        for bit in rest_bits:
            lat_here = jnp.concatenate([lat_here, swap(lat_here, bit, 0)], 0)

        def near_forward(base, *deps):
            def run(*args):
                return forward_near(base, *args)

            rows = lambda wide_here: pl.BlockSpec((tok_own, wide_here), lambda i, *_: (i, 0))
            lat_block = pl.BlockSpec((lat_own, wide), lambda i, *_: (i + base, 0))
            each = groups // 4
            return call(
                run,
                name="forward_near",
            room=46,
                grid=(2,),
                scalars=2,
                ins=[
                    pl.BlockSpec((tok_own, width), lambda i, meta, _: (meta[1] ^ (i + base), 0)),
                    lat_block,
                    lat_block,
                    par,
                    whole(w_all),
                    whole((2, wide)),
                ],
                outs=[((chip_tok, width), BF, rows(width))]
                + [((chip_tok, wide), BF, rows(wide))] * 3
                + [((wide, chip_tok), BF, pl.BlockSpec((wide, tok_own), lambda i, *_: (0, i)))]
                + [((2 * each, 8, GROUP), F32, pl.BlockSpec((each, 8, GROUP), lambda i, *_: (i, 0, 0)))],
                us=8,
            )(meta, count, tokens, after(kl, *deps), vl, params, w_t, b_qv)

        normed_b, q_b, k_b, v_b, t_b, log_b = near_forward(2, lat_four)
        t_far = swap(t_b, 0, 2)
        lat_here = after(lat_here, t_b)
        normed_a, q_a, k_a, v_a, t_near, log_a = near_forward(0, lat_here)
        w_x, w_z, w_xz = cube(after(w_own, t_near))
        lat_all = [v.reshape(dp_size, chip_lat, width) for v in (lat_here, swap(lat_here, 0, 1))]
        lat_all = jnp.concatenate(lat_all, 1).reshape(all_lat, width)
        lat_all = after(lat_all, t_near)

        chunk = min(512, all_lat)
        qa, ka, va, l_near, l_b, far, far_logs = call(
            forward_far,
            name="forward_far",
            room=6,
            grid=(all_lat // chunk,),
            scalars=3,
            ins=[pl.BlockSpec((chunk, width), lambda i, *_: (i, 0)), par, whole(w_all), whole((2, wide))]
            + [whole((chip_tok, wide))] * 4
            + [whole((lat_count, wide))],
            outs=[out((all_lat, wide))] * 3
            + [kept_out((chip_lat, wide))] * 2
            + [kept_out((lat_count, wide)), kept_out((lat_count, 2 * HEAD))],
            us=6,
        )(meta, count, image_of_group, lat_all, params, w_t, b_qv, k_a, k_b, v_a, v_b, ql)
        l_far = swap(l_b, 0, 2)

        out_pack = whole((wide + 16, width))
        mixed_specs = [whole((wide, chip_tok))] * 2 + [whole((chip_lat, wide))] * 2
        cot_sib = cot_through(1, after(meta, far))

        def out_rows_of(slot, kind, o0):
            return call(
                project_out,
                name="project_out",
            room=4,
                scalars=0,
                ins=[pl.BlockSpec((wide, tok_own), lambda *_: (0, slot), pipeline_mode=pl.Buffered(1))] * 2
                + [pl.BlockSpec((lat_own, wide), lambda *_: (slot, 0), pipeline_mode=pl.Buffered(1))] * 2
                + [out_pack] * 2,
                outs=[out(big, kind)],
                us=3,
            )(t_near, t_far, l_near, l_far, o0, o2)[0]

        attn_send = out_rows_of(1, BF, after(o0, cot_sib))
        attn_own = out_rows_of(0, F32, after(o0, attn_send))
        attn_got = swap(attn_send, 0, 1)
        own_tok = pl.BlockSpec((tok_own, width), lambda i, meta, _: (meta[1], 0), pipeline_mode=pl.Buffered(1))
        own_lat = pl.BlockSpec((lat_own, width), lambda i, meta, _: (meta[1], 0), pipeline_mode=pl.Buffered(1))
        residual, n2, stats1 = call(
            add_norm,
            name="add_norm",
            room=6,
            scalars=2,
            ins=[par, whole(big), whole(big), own_tok, whole((lat_own, width))],
            outs=[out(big, F32), out(big), out((8, width), F32)],
            us=3,
        )(meta, count, params, attn_own, attn_got, tokens, lat_rel)
        n2_sib = swap(n2, 0, 1)

        chip = (chip_rows, width)
        piece = (half, width)
        act_first, grad_first, bias_first = call(
            hidden_first,
            name="hidden_first",
            room=6,
            scalars=0,
            ins=[par, whole(big), whole((width, hidden)), whole((rows_own, hidden))],
            outs=[out((rows_own, hidden))] * 2 + [out((8, hidden), F32)],
            us=4,
        )(params, n2, w_up, cot_own)
        act_near, grad_near, a0, a1, a2, a3, bias_near = call(
            hidden_own,
            name="hidden_own",
            room=7,
            scalars=1,
            ins=[par] + [ANY] * 8,
            outs=[any_out((chip_rows, hidden))] * 2 + [any_out(piece)] * 4 + [out((8, hidden), F32)],
            scratch=[
                vm(chip, BF),
                vm(chip, BF),
                vm((width, hidden), BF),
                vm((chip_rows, hidden), BF),
                vm((chip_rows, hidden), BF),
                vm((rows_own, hidden), BF),
                vm((width + hidden, width), BF),
                dma(10),
                dma(10),
            ],
            us=9,
        )(meta, params, n2, n2_sib, cot_tokens, cot_latents, w_up, cot_sib, act_first, grad_first)
        near_parts = (a0,) + cube(None, a1, a2, a3)

        branch, back, middle_send, act, grad, bias_away = call(
            hidden_away,
            name="hidden_away",
            room=8,
            scalars=1,
            ins=[out_pack] + [ANY] * 12,
            outs=[any_out(big, F32), any_out(big, F32), any_out(chip), any_out((chip_rows, hidden)), any_out((chip_rows, hidden))]
            + [out((8, hidden), F32)],
            scratch=[
                vm(chip, BF),
                vm(chip, BF),
                vm((2, width, hidden), BF),
                vm((2, width, hidden), BF),
                vm((chip_rows, hidden), BF),
                vm((chip_rows, hidden), BF),
                vm(chip, F32),
                vm(chip, F32),
                vm((chip_rows, hidden), BF),
                vm((chip_rows, hidden), BF),
                vm(chip, BF),
                dma(18),
                dma(6),
            ],
            us=10,
        )(meta, o2, n2, n2_sib, cot_tokens, cot_latents, w_own, w_x, w_z, w_xz, act_near, grad_near, w_up, w_down)
        middle_got = swap(middle_send, 0, 1)

        b0, b1, b2, b3 = call(
            away_grads,
            name="away_grads",
            room=7,
            scalars=1,
            ins=[ANY] * 6,
            outs=[any_out(piece)] * 4,
            scratch=[
                vm(chip, BF),
                vm(chip, BF),
                vm((chip_rows, hidden), BF),
                vm((chip_rows, hidden), BF),
                vm((width + hidden, width), BF),
                dma(8),
                dma(8),
            ],
            us=6,
        )(meta, n2, n2_sib, cot_tokens, cot_latents, act, grad)

        out_rows, grad_res, grad_attn, stats2 = call(
            middle_rows,
            name="middle_rows",
            room=8,
            scalars=2,
            ins=[par, whole(big), whole(big), whole(big), whole(chip), own_tok, own_lat],
            outs=[out(big), out(big, F32), out(big), out((8, width), F32)],
            us=5,
            deps=(b0,),
        )(meta, count, params, residual, branch, back, middle_got, cot_tokens, cot_latents)
        grad_attn_sib = swap(grad_attn, 0, 1)

        def terms(n, at=0):
            return [(i, at) for i in range(n)]

        sides4 = ((0, 0), (1, 0), (0, 1), (1, 1))

        def at(d, size, base=0):
            return lambda x, z: base + ((x ^ d[0]) * 2 + (z ^ d[1])) * size


        (near_sum,) = combine("near_sum", meta, near_parts, [(half, BF, [(0, half, terms(4))])], us=2)
        away_parts = (b0,) + cube(None, *(after(v, near_parts[1], near_parts[2]) for v in (b1, b2, b3)))

        g_near, g_send, d_near, out_grad, out_send = call(
            back_out,
            name="back_out",
            room=6,
            scalars=1,
            ins=[whole(big), whole(big), out_pack, out_pack] + mixed_specs,
            outs=[out((wide, chip_tok))] * 2 + [out((chip_lat, wide)), out((wide, width)), out((wide + chip_lat, width))],
            us=4,
            deps=(near_sum,),
        )(meta, grad_attn, grad_attn_sib, o0, o2, t_near, t_far, l_near, l_far)
        out_got = swap(out_send, 0, 2)
        g_far = swap(g_send, 0, 2)

        zero_w, zero_b = jnp.zeros((8, LANES), F32), jnp.zeros((8, LANES), F32)

        def rows_backward(first, steps, half_in, g, d, gw, bias, *deps):
            normed, q, k, v, log = half_in
            base = first % 2

            def rows(n, wide_here, shift):
                return pl.BlockSpec((n, wide_here), lambda i, *_: (i + shift, 0))

            def run(*args):
                return backward_rows(first, gw is None, *args)

            init = (zero_w, zero_b) if gw is None else (gw, bias)
            return call(
                run,
                name="backward_rows",
            room=8,
                grid=(steps,),
                scalars=2,
                ins=[
                    rows(tok_own, width, base),
                    *[rows(tok_own, wide, base)] * 3,
                    *[rows(lat_own, wide, first)] * 3,
                    pl.BlockSpec((groups // 4, 8, GROUP), lambda i, *_: (i + base, 0, 0)),
                    rows(lat_own, wide, first),
                    rows(lat_own, 2 * HEAD, first),
                    pl.BlockSpec((wide, tok_own), lambda i, *_: (0, i + base)),
                    rows(lat_own, d.shape[1], base + (wide // lat_own if d.shape[1] != wide else 0)),
                    whole(w_all),
                    whole(init[0].shape),
                    whole(init[1].shape),
                ],
                outs=[kept_out((tok_own, width))] * steps
                + [kept_out(w_all, F32), kept_out((8, wide), F32)]
                + [((steps * lat_own, wide), F32, rows(lat_own, wide, 0))] * 3,
                us=7 * steps,
                deps=deps,
            )(meta, count, normed, q, k, v, ql, kl, vl, log, far, far_logs, g, d, w_t, *init)

        half_a, half_b = (normed_a, q_a, k_a, v_a, log_a), (normed_b, q_b, k_b, v_b, log_b)
        part0, gw, bias, *near_0 = rows_backward(0, 1, half_a, g_near, d_near, None, None)
        bundle_own, bundle = call(
            latent_bundle,
            name="latent_bundle",
            scalars=1,
            ins=[whole((chip_lat, wide)), pl.BlockSpec((chip_lat, width), lambda *_: (wide // chip_lat, 0))]
            + [whole((lat_count, wide)), whole((lat_count, 2 * HEAD))],
            outs=[out((lat_count, 4 * HEAD))] * 2,
            us=2,
            deps=(part0,),
        )(meta, d_near, out_got, far, far_logs)
        steps = [bundle]

        def spread(bit):
            got = swap(steps[0], bit, 0)
            return lambda done: steps.__setitem__(0, jnp.concatenate([after(steps[0], done), got], 0))

        join = spread(x_bit)
        part1, gw, bias, *near_1 = rows_backward(1, 1, half_a, g_near, d_near, gw, bias, bundle_own)
        join(part1)
        join = spread(z_bit)
        (away_sum,) = combine("away_sum", meta, away_parts, [(half, BF, [(0, half, terms(4))])], us=2, deps=(part1,))
        away_got = swap(away_sum, 0, 2)
        part3, gw, bias, *near_3 = rows_backward(3, 1, half_b, g_far, out_got, gw, bias, away_sum, steps[0])
        join(part3)
        for bit in rest_bits[:-1]:
            spread(bit)(part3)
        join = spread(rest_bits[-1]) if rest_bits else None
        got3 = swap(part3, 0, 1)
        got1 = swap(after(part1, part3), 0, 1)
        part2, gw, bias, *near_2 = rows_backward(2, 1, half_b, g_far, out_got, gw, bias)
        if rest_bits:
            join(part2)
        bundle = steps[0]
        (total,) = combine(
            "weights_sum", meta, [near_sum, away_got], [(half, BF, [(0, half, terms(2))])], us=20, deps=(part2,)
        )
        near_all = [v for three in zip(near_0, near_1, near_2, near_3) for v in three]
        shard = (small * 4, width)
        lat_keep, lat_send, c0, c1, c2, c3, small_rows = call(
            backward_far,
            name="backward_far",
            room=6,
            scalars=3,
            ins=[whole((all_lat, wide))] * 3
            + [whole((lat_count, wide))] * 3
            + [whole((lat_count, 4 * HEAD)), whole((all_lat, 4 * HEAD)), whole((lat_count, width)), whole(w_all), whole(w_all)]
            + [whole((8, wide))]
            + [whole((wide, width)), pl.BlockSpec((wide, width), lambda *_: (0, 0), pipeline_mode=pl.Buffered(1))]
            + [par]
            + [whole((8, width))] * 5
            + [whole(v.shape) for v in near_all],
            outs=[out((chip_lat, width))] * 2 + [any_out(shard)] * 4 + [out((32, width), F32)],
            scratch=[vm((4 * wide, width), BF), dma(8)],
            us=8,
            deps=(total, got1, got3),
        )(
            meta, count, image_of_group, qa, ka, va, ql, kl, vl, bundle_own, bundle, normed_lat, w_t, gw, bias, out_grad,
            out_got, params, stats1, stats2, bias_first, bias_near, bias_away, *near_all,
        )

        lat_got = swap(lat_send, 0, 1)
        (there,) = combine(
            "rows_sum", meta, [part2, got3, lat_keep, lat_got],
            [(rows_own, BF, [(0, tok_own, terms(2)), (tok_own, lat_own, [(2, lat_own), (3, lat_own)])])],
            us=2, deps=(total,),
        )
        from_y = swap(there, 0, 2)
        small_rows = small_rows + swap(small_rows, 0, 1)
        small_got = swap(small_rows, 0, 2)
        rows4 = 4 * small
        qkv_parts = (c0,) + cube(None, *(after(v, total) for v in (c1, c2, c3)))
        (qkv,) = combine(
            "qkv_sum", meta, qkv_parts + (small_rows, small_got),
            [(rows4 + 32, BF, [(0, rows4, terms(4)), (rows4, 32, [(4, 0), (5, 0)])])],
            us=2, deps=(there,),
        )
        (grad_rows,) = call(
            final_rows,
            name="final_rows",
            room=6,
            scalars=1,
            ins=[
                pl.BlockSpec((tok_own, width), lambda i, meta: (meta[1], 0), pipeline_mode=pl.Buffered(1)),
                whole((lat_own, width)),
                *[whole((tok_own, width))] * 2,
                whole(big),
                *[whole((chip_lat, width))] * 2,
                whole(big),
                par,
            ],
            outs=[out(big)],
            us=4,
            deps=(qkv,),
        )(meta, tokens, lat_rel, part0, got1, from_y, lat_keep, lat_got, grad_res, params)

        grad_y = swap(grad_rows, 0, 2)
        grad_c = swap(after(grad_rows, grad_y), 0, 1)
        out_y = swap(after(out_rows, qkv), 0, 2)
        for bit in rest_bits:
            (total,) = combine(
                "rest_sum", meta, [total, swap(total, bit, 0)], [(half, BF, [(0, half, terms(2))])], us=2,
                deps=(grad_rows,),
            )
        def all_rows(v, v_y, v_c):
            v_yc = swap(v_y, 0, 1)
            place = lambda n: pl.BlockSpec((n, width), lambda i, meta: (meta[1] ^ i, 0))
            return call(
                place_rows,
                name="place_rows",
                grid=(4,),
                scalars=1,
                ins=[whole(big)] * 4,
                outs=[((tok_count, width), BF, place(tok_own)), ((lat_count, width), BF, place(lat_own))],
                us=4,
            )(meta, v, v_c, v_y, v_yc)

        grad_tok, grad_lat = all_rows(grad_rows, grad_y, grad_c)
        out_tok, out_lat = all_rows(out_rows, out_y, swap(after(out_rows, out_y), 0, 1))
        four = (total,) + cube(total)
        grad_w_up, grad_w_down = combine(
            "weights_out", meta, four,
            [
                (4 * quarter, F32, [(at(d, quarter), quarter, [(i, r * quarter)]) for i, d in enumerate(sides4)])
                for r in (0, 1)
            ]
            ,
            us=5,
            deps=(qkv, out_y, grad_tok),
        )
        for bit in rest_bits:
            (qkv,) = combine("qkv_rest", meta, [qkv, swap(qkv, bit, 0)], [(rows4 + 32, BF, [(0, rows4 + 32, terms(2))])], us=2, deps=(total, total, grad_y))
        four = (qkv,) + tuple(
            swap(after(qkv, v), bit, 0) for v, bit in zip(four[1:], (x_bit, z_bit, x_bit | z_bit))
        )
        grad_w_qkv, grad_w_out, *vectors, grad_b_qv, roots = call(
            projections_out,
            name="qkv_out",
            scalars=1,
            ins=[whole((rows4 + 32, width))] * 4,
            outs=[out((3 * wide, width), F32), out((wide, width), F32)]
            + [((width,), F32, vec)] * 7
            + [out((2, wide), F32), out((8, LANES), F32)],
            us=3,
            deps=(out_tok, grad_w_up),
        )(meta, *four)
        grad_w_qkv = grad_w_qkv.reshape(3, wide, width).transpose(0, 2, 1)


        root_means = roots[0, :3]
        gain1, shift1, b_out_grad, gain2, shift2, b_down_grad, grad_b_up = vectors
        return (
            out_tok,
            out_lat,
            grad_tok,
            grad_lat,
            gain1,
            shift1,
            grad_w_qkv,
            grad_b_qv,
            grad_w_out,
            b_out_grad,
            gain2,
            shift2,
            grad_w_up,
            grad_b_up,
            grad_w_down,
            b_down_grad,
            root_means,
        )

    return per_device


def solution(mesh):
    rows, whole = P("dp", None), P()
    return jax.shard_map(
        make(mesh),
        mesh=mesh,
        in_specs=(
            rows,
            rows,
            whole,
            P("dp"),
            whole,
            whole,
            P(None, None, "mp"),
            P(None, "mp"),
            P("mp", None),
            whole,
            whole,
            whole,
            P(None, "mp"),
            P("mp"),
            P("mp", None),
            whole,
            rows,
            rows,
        ),
        out_specs=(
            rows,
            rows,
            rows,
            rows,
            whole,
            whole,
            P(None, None, "mp"),
            P(None, "mp"),
            P("mp", None),
            whole,
            whole,
            whole,
            P(None, "mp"),
            P("mp"),
            P("mp", None),
            whole,
            whole,
        ),
        check_vma=False,
    )
```

```python
import jax
import jax.numpy as jnp
from jax import lax
from jax.experimental import pallas as pl
from jax.experimental.pallas import tpu as pltpu
from jax.sharding import PartitionSpec as P

HEAD = 64
LANES = 128
GROUP = 256
LAT = 8
BF = jnp.bfloat16
F32 = jnp.float32
FAR = -1e30
MIB = 1 << 20
GAIN1, SHIFT1, B_OUT, GAIN2, SHIFT2, B_DOWN, B_UP = range(7)


def dot(a, b, ca, cb):
    return lax.dot_general(a, b, (((ca,), (cb,)), ((), ())), preferred_element_type=F32)


def norm_parts(values):
    center = values - jnp.mean(values, axis=-1, keepdims=True)
    spread = jnp.mean(center * center, axis=-1, keepdims=True)
    inverse = lax.rsqrt(spread + 1e-06)
    return center * inverse, inverse


def norm_back(grad, unit, inverse, gain):
    scaled = grad * gain
    inner = jnp.mean(scaled * unit, axis=-1, keepdims=True)
    return inverse * (scaled - jnp.mean(scaled, axis=-1, keepdims=True) - unit * inner)


def gelu_both(values):
    square = values * values
    inner = jnp.tanh(values * (0.7978845608028654 + 0.035677408136300125 * square))
    half = 0.5 + 0.5 * inner
    slope = values * (0.3989422804014327 + 0.05351611220494518 * square)
    return values * half, half + (1.0 - inner * inner) * slope


def split3(v):
    hi = v.astype(BF)
    mid = (v - hi.astype(F32)).astype(BF)
    low = (v - hi.astype(F32) - mid.astype(F32)).astype(BF)
    return hi, mid, low


def head_lanes(v, h):
    lane = lax.broadcasted_iota(jnp.int32, v.shape, v.ndim - 1)
    return jnp.where((lane >= h * HEAD) & (lane < (h + 1) * HEAD), v, jnp.zeros_like(v))


def kept(shape):
    return pl.BlockSpec(shape, lambda *_: (0,) * len(shape))


def whole(shape):
    return pl.BlockSpec(shape, lambda *_: (0,) * len(shape), pipeline_mode=pl.Buffered(1))


ANY = pl.BlockSpec(memory_space=pl.ANY)
OWN, SENT = (0, 1, 2, 3), (0, 2, 1, 3)


def block_bytes(shape, kind, copies):
    size = jnp.dtype(kind).itemsize
    dims = [1, 1] + list(shape)
    rows, lanes = 32 // size, LANES
    dims[-1] = -(-dims[-1] // lanes) * lanes
    dims[-2] = -(-dims[-2] // rows) * rows
    total = size * copies
    for d in dims:
        total *= d
    return total


def spec_bytes(spec, kind):
    if spec.block_shape is None:
        return 0
    return block_bytes(spec.block_shape, kind, 1 if spec.pipeline_mode is not None else 2)


def after(v, *deps):
    return lax.optimization_barrier((v,) + deps)[0]


def call(body, *, name, scalars, ins, outs, grid=(1,), scratch=(), deps=(), us=1.0, room=3):
    def run(*args):
        if deps:
            args = (after(args[0], *deps),) + args[1:]
        need = room * MIB + sum(spec_bytes(spec, kind) for _, kind, spec in outs)
        need += sum(spec_bytes(spec, a.dtype) for spec, a in zip(ins, args[scalars:]))
        need += sum(block_bytes(s.shape, s.dtype, 1) for s in scratch if s.shape and len(s.shape) > 1)
        return pl.pallas_call(
            body,
            name=name,
            out_shape=[jax.ShapeDtypeStruct(s, d) for s, d, _ in outs],
            grid_spec=pltpu.PrefetchScalarGridSpec(
                num_scalar_prefetch=scalars,
                grid=grid,
                in_specs=list(ins),
                out_specs=[spec for _, _, spec in outs],
                scratch_shapes=list(scratch),
            ),
            compiler_params=pltpu.CompilerParams(
                dimension_semantics=("arbitrary",) * len(grid), vmem_limit_bytes=need
            ),
            cost_estimate=pl.CostEstimate(
                flops=int(us * 1.0e10), bytes_accessed=1 << 16, transcendentals=0
            ),
        )(*args)

    return run


def mover(sems):
    used = []

    def start(src, dst):
        copy = pltpu.make_async_copy(src, dst, sems.at[len(used)])
        used.append(copy)
        copy.start()
        return copy

    return start


def sides(meta):
    return meta[0] & 1, (meta[0] >> 1) & 1


def combine(name, meta, arrays, outs, deps=(), us=1.0):
    def body(meta, *refs):
        x, z = sides(meta)

        def rows_at(at, n):
            return pl.ds(pl.multiple_of(at(x, z), 16), n) if callable(at) else slice(at, at + n)

        for ref, (_, kind, segments) in zip(refs[len(arrays) :], outs):
            for to, n, terms in segments:
                parts = [refs[i][rows_at(at, n), :] for i, at in terms]
                value = parts[0]
                if len(parts) > 1:
                    value = parts[0].astype(F32)
                    for part in parts[1:]:
                        value = value + part.astype(F32)
                ref[rows_at(to, n), :] = value.astype(kind)

    width = arrays[0].shape[1]
    return call(
        body,
        name=name,
        scalars=1,
        ins=[whole(a.shape) for a in arrays],
        outs=[((rows, width), kind, whole((rows, width))) for rows, kind, _ in outs],
        deps=deps,
        us=us,
    )(meta, *arrays)


def group_at(meta, count, slot, i):
    return count[(meta[1] ^ slot) * 2 + i]


def image_list(meta, image, devices, per_device, slots):
    each = per_device // 4
    return [
        image[(meta[0] ^ j) * per_device + (meta[1] ^ s) * each + i]
        for j in range(devices)
        for s in slots
        for i in range(each)
    ]


def image_column(images):
    return jnp.concatenate([jnp.full((LAT, 1), im, jnp.int32) for im in images], 0)


def image_row(images):
    group = lax.broadcasted_iota(jnp.int32, (1, len(images) * LAT), 1) // LAT
    out = jnp.zeros(group.shape, jnp.int32)
    for g, im in enumerate(images):
        out = jnp.where(group == g, im, out)
    return out


def key_stack(tok, lat8):
    pad = jnp.concatenate([lat8, jnp.zeros_like(lat8)], 0).astype(BF)
    return jnp.concatenate([tok, pad], 0)


def near_mask(count, columns):
    row = lax.broadcasted_iota(jnp.int32, (GROUP + 2 * LAT, columns), 0)
    return (row < count) | ((row >= GROUP) & (row < GROUP + LAT))


def param(params, i):
    return params[i : i + 1, :]


def project(rows, params, w, bias):
    unit, _ = norm_parts(rows.astype(F32))
    rows = (unit * param(params, GAIN1) + param(params, SHIFT1)).astype(BF)
    return (
        rows,
        (dot(rows, w[0], 1, 1) + bias[0:1]).astype(BF),
        dot(rows, w[1], 1, 1).astype(BF),
        (dot(rows, w[2], 1, 1) + bias[1:2]).astype(BF),
    )


def prepare(
    meta, lat, w_out, g1, s1, bo, g2, s2, bd, bu, up, down, lat_rel, lat_half, out_pack, part, params,
    vlat, vout, sems, *vecs,
):
    fetch = mover(sems)
    lat_copy = fetch(lat, vlat)
    copies = [fetch(ref, dst) for ref, dst in zip((g1, s1, bo, g2, s2, bd, bu), vecs)]
    x, z = sides(meta)
    n = part.shape[0] // 2
    here = pl.ds(pl.multiple_of((x * 2 + z) * n, 16), n)
    parts = [fetch(up.at[here], part.at[0:n]), fetch(down.at[here], part.at[n:])]
    wide = w_out.shape[0]
    parts.append(fetch(w_out, vout))
    lat_copy.wait()
    n = lat.shape[0] // 4
    for s in range(4):
        rows = vlat[pl.ds(pl.multiple_of((meta[1] ^ s) * n, 16), n), :]
        lat_rel[s * n : (s + 1) * n, :] = rows
        if s % 2 == 0:
            lat_half[s // 2 * n : (s // 2 + 1) * n, :] = rows
    for copy in copies:
        copy.wait()
    for i in range(7):
        params[i : i + 1, :] = vecs[i][...].reshape(1, params.shape[1])
    params[7:8, :] = jnp.zeros_like(params[7:8, :])
    bias = param(params, B_UP)
    rows = [v.astype(F32) for v in split3(bias)]
    out_pack[wide : wide + 16, :] = jnp.concatenate(rows + [jnp.zeros((13, bias.shape[1]), F32)], 0).astype(BF)
    for copy in parts:
        copy.wait()
    out_pack[0:wide, :] = vout[...]


def latent_rows(lat, params, w, bias, normed, ql, kl, vl):
    normed[...], a, b, c = project(lat[...], params, w, bias)
    ql[...], kl[...], vl[...] = a.astype(F32), b.astype(F32), c.astype(F32)


def forward_near(base, meta, count, tok, kl, vl, params, w, bias, normed, q, k, v, mixed_out, log):
    step = pl.program_id(0)
    wide = w.shape[1]
    rows, qs, ks, vs = project(tok[...], params, w, bias)
    normed[...], q[...], k[...], v[...] = rows, qs, ks, vs
    qs = qs * jnp.asarray(0.125, BF)
    for i in range(tok.shape[0] // GROUP):
        here = slice(i * LAT, (i + 1) * LAT)
        at = slice(i * GROUP, (i + 1) * GROUP)
        keys = key_stack(ks[at], kl[here, :])
        values = key_stack(vs[at], vl[here, :]).T
        mask = near_mask(group_at(meta, count, step + base, i), GROUP)
        logs, outs = [], []
        for h in range(wide // HEAD):
            s = jnp.where(mask, dot(head_lanes(keys, h), qs[at], 1, 1), FAR)
            top = jnp.max(s, 0, keepdims=True)
            e = jnp.exp(s - top)
            total = jnp.sum(e, 0, keepdims=True)
            logs.append(top + jnp.log(total))
            outs.append(dot(values[h * HEAD : (h + 1) * HEAD], e.astype(BF), 1, 0) * (1.0 / total))
        log[i] = jnp.concatenate(logs + [jnp.zeros((8 - len(logs), GROUP), F32)], 0)
        mixed_out[:, at] = jnp.concatenate(outs, 0).astype(BF)


def forward_far(meta, count, image, lat, params, w, bias, k_near, k_away, v_near, v_away, ql, qa, ka, va, m_near, m_away, far, logs_out):
    step = pl.program_id(0)
    wide = w.shape[1]
    rows_step = lat.shape[0]
    own = ql.shape[0]
    groups = own // LAT

    def rows_of(near, away, g):
        half = groups // 2
        ref, at = (near, g) if g < half else (away, g - half)
        return ref[at * GROUP : (at + 1) * GROUP, :]

    _, a, b, c = project(lat[...], params, w, bias)
    here = pl.ds(pl.multiple_of(step * rows_step, rows_step), rows_step)
    qa[here, :], ka[here, :], va[here, :] = a, b, c

    @pl.when(step == pl.num_programs(0) - 1)
    def _():
        q32 = ql[...] * 0.125
        images = image_list(meta, image, qa.shape[0] // own, groups, SENT)
        mask = image_column(image_list(meta, image, 1, groups, OWN)) == image_row(images)
        lane = lax.broadcasted_iota(jnp.int32, (LAT, GROUP), 1)
        full = jnp.zeros((own, wide), F32)
        logs = []
        for h in range(wide // HEAD):
            qh = head_lanes(q32, h)
            s_lat = jnp.where(mask, dot(qh.astype(BF), ka[...], 1, 1), FAR)
            s_tok = jnp.concatenate(
                [
                    jnp.where(
                        lane < group_at(meta, count, g // 2, g % 2),
                        dot(qh[g * LAT : (g + 1) * LAT].astype(BF), rows_of(k_near, k_away, g), 1, 1),
                        FAR,
                    )
                    for g in range(groups)
                ],
                0,
            )
            top = jnp.maximum(jnp.max(s_lat, 1, keepdims=True), jnp.max(s_tok, 1, keepdims=True))
            e_lat, e_tok = jnp.exp(s_lat - top), jnp.exp(s_tok - top)
            total = jnp.sum(e_lat, 1, keepdims=True) + jnp.sum(e_tok, 1, keepdims=True)
            logs.append(top + jnp.log(total))
            near = jnp.concatenate(
                [
                    dot(e_tok[g * LAT : (g + 1) * LAT].astype(BF), rows_of(v_near, v_away, g), 1, 0)
                    for g in range(groups)
                ],
                0,
            )
            full = full + head_lanes((dot(e_lat.astype(BF), va[...], 1, 0) + near) * (1.0 / total), h)
        mixed = full.astype(BF)
        m_near[...], m_away[...] = mixed[: own // 2], mixed[own // 2 :]
        parts = [split3(x) for x in logs]
        cols = [p[i] for i in range(3) for p in parts]
        lane = lax.broadcasted_iota(jnp.int32, (own, 2 * HEAD), 1)
        extra = jnp.zeros((own, 2 * HEAD), F32)
        for i, c in enumerate(cols):
            extra = jnp.where(lane == i, c.astype(F32), extra)
        far[...] = mixed
        logs_out[...] = extra.astype(BF)


def valid_rows(meta, count, rows):
    row = lax.broadcasted_iota(jnp.int32, (rows, 1), 0)
    first = (row < GROUP) & (row < group_at(meta, count, 0, 0))
    return first | ((row >= GROUP) & (row < GROUP + group_at(meta, count, 0, 1)))


def slot_block(meta, ref, slot):
    n = ref.shape[0] // 4
    return ref.at[pl.ds(pl.multiple_of((meta[1] ^ slot) * n, 16), n)]


def project_out(t_near, t_far, l_near, l_far, o0, o2, out):
    wide, n = t_near.shape
    value = dot(t_near[...], o0[0:wide, :], 0, 0) + dot(t_far[...], o2[0:wide, :], 0, 0)
    out[0:n, :] = value.astype(out.dtype)
    value = dot(l_near[...], o0[0:wide, :], 1, 0) + dot(l_far[...], o2[0:wide, :], 1, 0)
    out[n:, :] = value.astype(out.dtype)


def cot_back(meta, cot_tok, cot_lat, down_w, out):
    n = cot_tok.shape[0]
    out[0:n, :] = dot(cot_tok[...], down_w[...], 1, 1).astype(BF)
    out[n:, :] = dot(cot_lat[...], down_w[...], 1, 1).astype(BF)


def add_norm(meta, count, params, own, got, tok, lat, residual, n2, stats):
    n, m = tok.shape[0], lat.shape[0]
    stats[...] = jnp.zeros_like(stats)
    for at, size, x in ((0, n, tok), (n, m, lat)):
        rows = slice(at, at + size)
        attn = own[rows, :] + got[rows, :].astype(F32) + param(params, B_OUT)
        if at == 0:
            real = valid_rows(meta, count, n)
            stats[0:1, :] = jnp.sum(jnp.where(real, attn * attn, 0.0), 0, keepdims=True)
        res = x[...].astype(F32) + attn
        residual[rows, :] = res
        unit, _ = norm_parts(res)
        n2[rows, :] = (unit * param(params, GAIN2) + param(params, SHIFT2)).astype(BF)


def hidden_part(n2, cot, up_w, down_w, bias, act_out, grad_out):
    cut = 256
    sums = []
    for at in range(0, up_w.shape[1], cut):
        cols = slice(at, at + cut)
        up = dot(n2, up_w[:, cols], 1, 0) + bias[:, cols]
        active, slope = gelu_both(up)
        grad_up = (dot(cot, down_w[cols, :], 1, 1) * slope).astype(BF)
        act_out[:, cols] = active.astype(BF)
        grad_out[:, cols] = grad_up
        sums.append(jnp.sum(grad_up.astype(F32), 0, keepdims=True))
    return jnp.concatenate(sums, 1)


def two_halves(meta, fetch, n2_own, n2_sib, cot_tok, cot_lat, vn2, vcot):
    rows = n2_own.shape[0]
    n = cot_tok.shape[0] // 4
    copies = [fetch(n2_own, vn2.at[0:rows]), fetch(n2_sib, vn2.at[rows:])]
    for s in (0, 1):
        at = s * rows
        copies.append(fetch(slot_block(meta, cot_tok, s), vcot.at[at : at + n]))
        copies.append(fetch(slot_block(meta, cot_lat, s), vcot.at[at + n : at + rows]))
    return copies


def send_parts(meta, flush, pack, parts):
    x, z = sides(meta)
    n = parts[0].shape[0] // 2
    copies = []
    for ref, (dx, dz) in zip(parts, ((0, 0), (1, 0), (0, 1), (1, 1))):
        q = (x ^ dx) * 2 + (z ^ dz)
        for i in (0, 1):
            src = pack.at[pl.ds(pl.multiple_of(i * 4 * n + q * n, 16), n)]
            copies.append(flush(src, ref.at[i * n : (i + 1) * n]))
    return copies


def hidden_rows(n2, up_w, bias, got, act_out, grad_out, sums):
    cut = 256
    for at in range(0, up_w.shape[1], cut):
        cols = slice(at, at + cut)
        active, slope = gelu_both(dot(n2, up_w[:, cols], 1, 0) + bias[:, cols])
        grad_up = (got[:, cols].astype(F32) * slope).astype(BF)
        act_out[:, cols] = active.astype(BF)
        grad_out[:, cols] = grad_up
        sums[0:1, cols] = jnp.sum(grad_up.astype(F32), 0, keepdims=True)


def hidden_first(params, n2, up_w, got, act, grad, stats):
    stats[...] = jnp.zeros_like(stats)
    hidden_rows(n2[...], up_w, param(params, B_UP), got, act, grad, stats)


def hidden_own(
    meta, params, n2_own, n2_sib, cot_tok, cot_lat, up_w, got_in, act_in, grad_in,
    act_out, grad_out, p0, p1, p2, p3, stats,
    vn2, vcot, vw, act, grad, got, vpack, in_sems, out_sems,
):
    width, hidden = vw.shape
    rows = got.shape[0]
    fetch, flush = mover(in_sems), mover(out_sems)
    first = [fetch(n2_sib, vn2.at[rows:]), fetch(up_w, vw), fetch(got_in, got)]
    copies = [fetch(grad_in, grad.at[0:rows]), fetch(act_in, act.at[0:rows]), fetch(n2_own, vn2.at[0:rows])]
    n = cot_tok.shape[0] // 4
    for s in (0, 1):
        at = s * rows
        copies.append(fetch(slot_block(meta, cot_tok, s), vcot.at[at : at + n]))
        copies.append(fetch(slot_block(meta, cot_lat, s), vcot.at[at + n : at + rows]))
    for copy in first:
        copy.wait()
    stats[...] = jnp.zeros_like(stats)
    hidden_rows(vn2[rows:, :], vw, param(params, B_UP), got, act.at[rows:], grad.at[rows:], stats)
    for copy in copies:
        copy.wait()
    outs = [flush(act, act_out), flush(grad, grad_out)]
    vpack[0:width, :] = dot(vn2[...], grad[...], 0, 0).astype(BF)
    vpack[width : width + hidden, :] = dot(act[...], vcot[...], 0, 0).astype(BF)
    outs += send_parts(meta, flush, vpack, (p0, p1, p2, p3))
    for copy in outs:
        copy.wait()


def hidden_away(
    meta, o2, n2_own, n2_sib, cot_tok, cot_lat, w0, w1, w2, w3, act_in, grad_in, up_w, down_w,
    branch_own, back_own, send, act_out, grad_out, stats,
    vn2, vcot, vw, vnear, act0, grad0, branch, back, act, grad, vsend, in_sems, out_sems,
):
    rows, width = n2_own.shape
    x, z = sides(meta)
    quarter = w0.shape[0] // 2
    fetch, flush = mover(in_sems), mover(out_sems)
    copies = two_halves(meta, fetch, n2_own, n2_sib, cot_tok, cot_lat, vn2, vcot)
    for ref, (dx, dz) in zip((w0, w1, w2, w3), ((0, 0), (1, 0), (0, 1), (1, 1))):
        q = pl.multiple_of(((x ^ dx) * 2 + (z ^ dz)) * quarter, 16)
        for i in (0, 1):
            copies.append(fetch(ref.at[i * quarter : (i + 1) * quarter], vw.at[i, pl.ds(q, quarter)]))
    late = [(fetch(grad_in, grad0), fetch(up_w, vnear.at[0])), (fetch(act_in, act0), fetch(down_w, vnear.at[1]))]
    for copy in copies:
        copy.wait()
    base = o2.shape[0] - 16
    bias = o2[base : base + 16, :].astype(F32)
    bias = bias[0:1] + bias[1:2] + bias[2:3]
    n2, ct = vn2[...], vcot[...]
    stats[...] = jnp.zeros_like(stats)
    stats[0:1, :] = hidden_part(n2, ct, vw.at[0], vw.at[1], bias, act, grad)
    outs = [flush(act, act_out), flush(grad, grad_out)]
    for i, (ref, near, src, turn, own) in enumerate(
        ((back, grad0, grad, 1, back_own), (branch, act0, act, 0, branch_own))
    ):
        for copy in late[i]:
            copy.wait()
        ref[...] = dot(near[...], vnear[i], 1, turn) + dot(src[...], vw[i], 1, turn)
        vsend[i * rows : (i + 1) * rows, :] = ref[rows:, :].astype(BF)
        outs.append(flush(ref.at[0:rows], own))
        outs.append(flush(vsend.at[i * rows : (i + 1) * rows], send.at[i * rows : (i + 1) * rows]))
    for copy in outs:
        copy.wait()


def away_grads(
    meta, n2_own, n2_sib, cot_tok, cot_lat, act_in, grad_in, p0, p1, p2, p3,
    vn2, vcot, act, grad, vpack, in_sems, out_sems,
):
    width, hidden = vn2.shape[1], act.shape[1]
    fetch, flush = mover(in_sems), mover(out_sems)
    copies = [fetch(grad_in, grad)] + two_halves(meta, fetch, n2_own, n2_sib, cot_tok, cot_lat, vn2, vcot)
    last = fetch(act_in, act)
    for copy in copies:
        copy.wait()
    vpack[0:width, :] = dot(vn2[...], grad[...], 0, 0).astype(BF)
    last.wait()
    vpack[width : width + hidden, :] = dot(act[...], vcot[...], 0, 0).astype(BF)
    for copy in send_parts(meta, flush, vpack, (p0, p1, p2, p3)):
        copy.wait()


def middle_rows(meta, count, params, residual, branch, back, got, cot_tok, cot_lat, out_rows, grad_res, grad_attn, stats):
    n, m = cot_tok.shape[0], cot_lat.shape[0]
    rows_own = n + m
    stats[...] = jnp.zeros_like(stats)
    for at, size, cot in ((0, n, cot_tok), (n, m, cot_lat)):
        rows = slice(at, at + size)
        bk = back[rows, :] + got[rows, :].astype(F32)
        br = branch[rows, :] + got[rows_own + at : rows_own + at + size, :].astype(F32) + param(params, B_DOWN)
        res = residual[rows, :]
        out = res + br
        out_rows[rows, :] = out.astype(BF)
        if at == 0:
            real = valid_rows(meta, count, n)
            stats[0:1, :] = jnp.sum(jnp.where(real, out * out, 0.0), 0, keepdims=True)
            stats[1:2, :] = jnp.sum(jnp.where(real, br * br, 0.0), 0, keepdims=True)
        unit, inverse = norm_parts(res)
        stats[2:3, :] += jnp.sum(bk * unit, 0, keepdims=True)
        stats[3:4, :] += jnp.sum(bk, 0, keepdims=True)
        cot32 = cot[...].astype(F32)
        gr = cot32 + norm_back(bk, unit, inverse, param(params, GAIN2))
        grad_res[rows, :] = gr
        ga = gr.astype(BF)
        grad_attn[rows, :] = ga
        stats[4:5, :] += jnp.sum(ga.astype(F32), 0, keepdims=True)
        stats[5:6, :] += jnp.sum(cot32, 0, keepdims=True)


def back_out(meta, ga_own, ga_sib, o0, o2, t_near, t_far, l_near, l_far, g0, g2, d0, w0, sent):
    wide, n = t_near.shape[0], t_near.shape[1] // 2
    m = l_near.shape[0] // 2
    sent[wide:, :] = jnp.zeros_like(sent[wide:, :])
    for o, g, d, at in ((o2, g2, sent, wide), (o0, g0, d0, 0)):
        for i, ga in enumerate((ga_own, ga_sib)):
            g[:, i * n : (i + 1) * n] = dot(o[0:wide, :], ga[0:n, :], 1, 1).astype(BF)
            rows = dot(ga[n : n + m, :], o[0:wide, :], 1, 1).astype(BF)
            d[at + i * m : at + (i + 1) * m, 0:wide] = rows
    for t, l, w in ((t_far, l_far, sent.at[0:wide]), (t_near, l_near, w0)):
        total = jnp.zeros(w0.shape, F32)
        for i, ga in enumerate((ga_own, ga_sib)):
            total += dot(t[:, i * n : (i + 1) * n], ga[0:n, :], 1, 0)
            total += dot(l[i * m : (i + 1) * m, :], ga[n : n + m, :], 0, 0)
        w[...] = total.astype(BF)


def near_slot(
    slot, meta, count, normed, q, k, v, ql, kl, vl, log, far, logs_far, d_in, d_lat_in, w, grad_w, bias,
    dq_far, dk_near, dv_near,
):
    wide = q.shape[1]
    heads = wide // HEAD
    rows = normed[...]
    slot_rows = rows.shape[0]
    d_lat = d_lat_in[:, 0 : q.shape[1]].astype(F32)
    eighth = jnp.asarray(0.125, BF)
    q_all, k_all, v_all = q[...] * eighth, k[...], v[...]
    far32 = far[...].astype(F32)
    far_log = logs_far[...].astype(F32)
    dqs, dks, dvs = [], [], []
    for i in range(slot_rows // GROUP):
        at, lat_at = slice(i * GROUP, (i + 1) * GROUP), slice(i * LAT, (i + 1) * LAT)
        number = group_at(meta, count, slot, i)
        d_cols = d_in[:, at]
        d_tok, qs, ks, vs = d_cols.T, q_all[at], k_all[at], v_all[at]
        keys, values = key_stack(ks, kl[lat_at, :]), key_stack(vs, vl[lat_at, :])
        keys_t = keys.T
        mask = near_mask(number, GROUP)
        ps, gs, dq_t, d_heads, q_heads = [], [], [], [], []
        for h in range(heads):
            s = dot(head_lanes(keys, h), qs, 1, 1)
            p = jnp.where(mask, jnp.exp(s - log[i, h : h + 1, :]), 0.0)
            gp = p * dot(head_lanes(values, h), d_cols, 1, 0)
            g = (gp - p * jnp.sum(gp, 0, keepdims=True)).astype(BF)
            dq_t.append(dot(keys_t[h * HEAD : (h + 1) * HEAD], g, 1, 0))
            ps.append(p.astype(BF))
            gs.append(g)
            d_heads.append(head_lanes(d_tok, h))
            q_heads.append(head_lanes(qs, h))
        dv = dot(jnp.concatenate(ps, 1), jnp.concatenate(d_heads, 0), 1, 0)
        dk = dot(jnp.concatenate(gs, 1), jnp.concatenate(q_heads, 0), 1, 0)
        dqs.append((jnp.concatenate(dq_t, 0).T * 0.125).astype(BF))
        pad = jnp.zeros((LAT, wide), F32)
        q8, o8, d8, lg = ql[lat_at, :] * 0.125, far32[lat_at], d_lat[lat_at], far_log[lat_at]
        q_rows, do_rows, log_col, del_col = [], [], [], []
        big = jnp.full((LAT, 1), 1e30, F32)
        zero = jnp.zeros((LAT, 1), F32)
        for h in range(heads):
            q_rows += [head_lanes(q8, h), pad]
            dh = head_lanes(d8, h)
            do_rows += [dh, pad]
            col = lg[:, h : h + 1] + lg[:, heads + h : heads + h + 1] + lg[:, 2 * heads + h : 2 * heads + h + 1]
            log_col += [col, big]
            del_col += [jnp.sum(dh * o8, 1, keepdims=True), zero]
        q_f, d_f = jnp.concatenate(q_rows, 0).astype(BF), jnp.concatenate(do_rows, 0).astype(BF)
        l_f, x_f = jnp.concatenate(log_col, 0), jnp.concatenate(del_col, 0)
        lane = lax.broadcasted_iota(jnp.int32, (2 * LAT * heads, GROUP), 1)
        p_f = jnp.where(lane < number, jnp.exp(dot(q_f, ks, 1, 1) - l_f), 0.0)
        g_f = (p_f * (dot(d_f, vs, 1, 1) - x_f)).astype(BF)
        dks.append((dk[0:GROUP] + dot(g_f, q_f, 0, 0)).astype(BF))
        dvs.append((dv[0:GROUP] + dot(p_f.astype(BF), d_f, 0, 0)).astype(BF))
        dk_near[lat_at, :] = dk[GROUP : GROUP + LAT]
        dv_near[lat_at, :] = dv[GROUP : GROUP + LAT]
        dq_all = dot(g_f, ks, 1, 0)
        dq_lat = jnp.zeros((LAT, wide), F32)
        for h in range(heads):
            dq_lat += head_lanes(dq_all[2 * LAT * h : 2 * LAT * h + LAT], h)
        dq_far[lat_at, :] = dq_lat

    dq, dk, dv = (jnp.concatenate(v, 0) for v in (dqs, dks, dvs))
    total = dot(dq, w[0], 1, 0) + dot(dk, w[1], 1, 0) + dot(dv, w[2], 1, 0)
    for i, g in enumerate((dq, dk, dv)):
        grad_w[i] += dot(g, rows, 0, 0)
    bias[0:1, :] += jnp.sum(dq.astype(F32), 0, keepdims=True)
    bias[1:2, :] += jnp.sum(dv.astype(F32), 0, keepdims=True)
    bias[2:3, :] += jnp.sum(dk.astype(F32), 0, keepdims=True)
    return total.astype(BF)


def backward_rows(
    first, begin, meta, count, normed, q, k, v, ql, kl, vl, log, far, logs_far, d_in, d_lat, w, gw_in, bias_in, *outs,
):
    step = pl.program_id(0)
    parts, (grad_w, bias, dq_far, dk_near, dv_near) = outs[:-5], outs[-5:]

    @pl.when(step == 0)
    def _():
        grad_w[...] = jnp.zeros_like(grad_w) if begin else gw_in[...]
        bias[...] = jnp.zeros_like(bias) if begin else bias_in[...]

    total = near_slot(
        step + first, meta, count, normed, q, k, v, ql, kl, vl, log, far, logs_far, d_in, d_lat, w, grad_w, bias,
        dq_far, dk_near, dv_near,
    )
    for slot, ref in enumerate(parts):

        @pl.when(step == slot)
        def _(ref=ref):
            ref[...] = total


def latent_bundle(meta, d_near, d_far, far, logs_far, own, sent):
    count, wide = far.shape
    heads = wide // HEAD
    n = count // 4
    d32 = jnp.concatenate([d_near[...], d_far[:, 0:wide]], 0).astype(F32)
    prod = d32 * far[...].astype(F32)
    lg = logs_far[...].astype(F32)
    deltas = [split3(jnp.sum(head_lanes(prod, h), 1, keepdims=True)) for h in range(heads)]
    cols = [lg[:, i : i + 1] for i in range(3 * heads)] + [p[i].astype(F32) for i in (0, 1) for p in deltas]
    lane = lax.broadcasted_iota(jnp.int32, (count, 4 * HEAD), 1)
    value = jnp.concatenate([d32, jnp.zeros((count, HEAD), F32)], 1)
    for i, c in enumerate(cols):
        value = jnp.where(lane == wide + i, c, value)
    value = value.astype(BF)
    own[...] = value
    for i, s in enumerate(SENT):
        sent[i * n : (i + 1) * n, :] = value[s * n : (s + 1) * n]


def backward_far(
    meta, tokens_real, image, qa, ka, va, ql, kl, vl, own, bundle, normed, w, gw, bias_in, wo_a, wo_b,
    params, stats1, stats2, hid_first, hid_near, hid_away, *refs,
):
    near, (lat_keep, lat_send, p0, p1, p2, p3, small, pack, out_sems) = refs[:-9], refs[-9:]
    count, wide = ql.shape
    heads = wide // HEAD
    groups = count // LAT
    q_all, k_all, v_all = qa[...] * jnp.asarray(0.125, BF), ka[...], va[...]
    q_own, k_own, v_own = (ql[...] * 0.125).astype(BF), kl[...].astype(BF), vl[...].astype(BF)
    d_own, d_all = own[:, 0:wide], bundle[:, 0:wide]

    def stats(ref, h):
        x = ref[...].astype(F32)
        col = [x[:, wide + i : wide + i + 1] for i in range(5 * heads)]
        return col[h] + col[heads + h] + col[2 * heads + h], col[3 * heads + h] + col[4 * heads + h]

    mine = image_list(meta, image, 1, groups, OWN)
    images = image_list(meta, image, qa.shape[0] // count, groups, SENT)
    mask_q = image_column(mine) == image_row(images)
    mask_k = image_column(images) == image_row(mine)
    each = len(near) // 3
    dq, dk, dv = (jnp.concatenate([ref[...] for ref in near[i * each : (i + 1) * each]], 0) for i in range(3))
    for h in range(heads):
        log, delta = stats(own, h)
        s = dot(head_lanes(q_own, h), k_all, 1, 1)
        p = jnp.where(mask_q, jnp.exp(s - log), 0.0)
        g = (p * (dot(head_lanes(d_own, h), v_all, 1, 1) - delta)).astype(BF)
        dq += head_lanes(dot(g, k_all, 1, 0), h)
        log, delta = stats(bundle, h)
        s = dot(q_all, head_lanes(k_own, h), 1, 1)
        p = jnp.where(mask_k, jnp.exp(s - log), 0.0)
        g = (p * (dot(d_all, head_lanes(v_own, h), 1, 1) - delta)).astype(BF)
        dk += head_lanes(dot(g, q_all, 0, 0), h)
        dv += head_lanes(dot(p.astype(BF), d_all, 0, 0), h)
    dq, dk, dv = (dq * 0.125).astype(BF), dk.astype(BF), dv.astype(BF)
    lat_rows = normed[...]
    sums = [bias_in[i : i + 1, :] for i in (0, 2, 1)]
    sums = [b + jnp.sum(g.astype(F32), 0, keepdims=True) for b, g in zip(sums, (dq, dk, dv))]
    columns = jnp.concatenate(sums + [jnp.zeros((5, wide), F32)], 0).T
    first_gain = jnp.zeros((1, pack.shape[1]), F32)
    first_shift = first_gain
    for i, g in enumerate((dq, dk, dv)):
        total = gw[i] + dot(g, lat_rows, 0, 0)
        pack[i * wide : (i + 1) * wide, :] = total.astype(BF)
        col, weight = columns[:, i : i + 1], w[i].astype(F32)
        first_shift += jnp.sum(weight * col, 0, keepdims=True)
        first_gain += jnp.sum(weight * (total - col * param(params, SHIFT1)), 0, keepdims=True)
    first_gain = first_gain / param(params, GAIN1)
    pack[3 * wide :, :] = (wo_a[...].astype(F32) + wo_b[...].astype(F32)).astype(BF)
    x, z = sides(meta)
    flush = mover(out_sems)
    copies = []
    for ref, (dx, dz) in zip((p0, p1, p2, p3), ((0, 0), (1, 0), (0, 1), (1, 1))):
        part = (x ^ dx) * 2 + (z ^ dz)
        at = 0
        for base, size in ((0, 3 * wide // 4), (3 * wide, wide // 4)):
            src = pack.at[pl.ds(pl.multiple_of(base + part * size, 16), size)]
            copies.append(flush(src, ref.at[at : at + size]))
            at += size
    rows = (dot(dq, w[0], 1, 0) + dot(dk, w[1], 1, 0) + dot(dv, w[2], 1, 0)).astype(BF)
    n = count // 4
    lat_keep[0:n, :], lat_keep[n : 2 * n, :] = rows[0:n], rows[2 * n : 3 * n]
    lat_send[0:n, :], lat_send[n : 2 * n, :] = rows[n : 2 * n], rows[3 * n :]
    small[...] = jnp.zeros_like(small)
    small[0:1, :] = stats1[0:1, :]
    small[1:7, :] = stats2[0:6, :]
    small[7:8, :], small[8:9, :] = first_gain, first_shift
    real = tokens_real[0]
    for i in range(1, tokens_real.shape[0]):
        real = real + tokens_real[i]
    for at, part in ((9, real - real % 64), (22, real % 64)):
        small[at : at + 1, :] = jnp.full((1, small.shape[1]), 0.25, F32) * part.astype(F32)
    for s, row in ((0, hid_first[0:1, :] + hid_near[0:1, :]), (2, hid_away[0:1, :])):
        small[pl.ds(10 + (meta[1] ^ s), 1), :] = row
    small[pl.ds(14 + meta[1], 1), 0:wide] = sums[0]
    small[pl.ds(18 + meta[1], 1), 0:wide] = sums[2]
    for copy in copies:
        copy.wait()


def final_rows(meta, tok, lat, a, b, c, la, lb, grad_res, params, out):
    n, m = tok.shape[0], lat.shape[0]
    for x, at, terms in ((tok, slice(0, n), (a, b)), (lat, slice(n, n + m), (la, lb))):
        grad = c[at, :].astype(F32)
        for term in terms:
            grad += term[0 : x.shape[0], :].astype(F32)
        unit, inverse = norm_parts(x[...].astype(F32))
        out[at, :] = (grad_res[at, :] + norm_back(grad, unit, inverse, param(params, GAIN1))).astype(BF)


def place_rows(meta, a, b, c, d, tok_out, lat_out):
    n = tok_out.shape[0]
    for i, ref in enumerate((a, b, c, d)):

        @pl.when(pl.program_id(0) == i)
        def _(ref=ref):
            tok_out[...] = ref[0:n, :]
            lat_out[...] = ref[n:, :]


def projections_out(meta, f0, f1, f2, f3, grad_w, grad_o, gain1, shift1, b_out, gain2, shift2, b_down, b_up, b_qv, roots):
    x, z = sides(meta)
    wide = grad_o.shape[0]
    four = (f0, f1, f2, f3)
    for ref, (dx, dz) in zip(four, ((0, 0), (1, 0), (0, 1), (1, 1))):
        part = (x ^ dx) * 2 + (z ^ dz)
        at = 0
        for dst, size in ((grad_w, 3 * wide // 4), (grad_o, wide // 4)):
            dst[pl.ds(pl.multiple_of(part * size, 16), size), :] = ref[at : at + size, :].astype(F32)
            at += size
    small = four[0][wide : wide + 32, :].astype(F32)
    for ref in four[1:]:
        small += ref[wide : wide + 32, :].astype(F32)
    for ref, row in ((gain1, 7), (shift1, 8), (b_out, 5), (gain2, 3), (shift2, 4), (b_down, 6)):
        ref[...] = small[row, :]

    def of_mp(first):
        value = small[first : first + 1]
        for m in (1, 2, 3):
            value = jnp.where(meta[1] == m, small[first + m : first + m + 1], value)
        return value

    b_up[...] = of_mp(10)[0]
    b_qv[...] = jnp.concatenate([of_mp(14)[:, 0:wide], of_mp(18)[:, 0:wide]], 0)
    real = (small[9:10, 0:1] + small[22:23, 0:1]) * small.shape[1]
    lane = lax.broadcasted_iota(jnp.int32, roots.shape, 1)
    value = jnp.zeros(roots.shape, F32)
    for i, row in enumerate((1, 0, 2)):
        root = jnp.sqrt(jnp.sum(small[row : row + 1], 1, keepdims=True) / real)
        value = jnp.where(lane == i, root, value)
    roots[...] = value


def make(mesh):
    dp_size, mp_size = mesh.shape["dp"], mesh.shape["mp"]
    assert mp_size == 4 and dp_size >= 4
    dp_bits = [1 << i for i in range(dp_size.bit_length() - 1)]
    assert 1 << len(dp_bits) == dp_size
    x_bit, z_bit, rest_bits = dp_bits[0], dp_bits[1], dp_bits[2:]

    def swap(v, dp_bit, mp_bit):
        pairs = [
            (d * mp_size + m, (d ^ dp_bit) * mp_size + (m ^ mp_bit))
            for d in range(dp_size)
            for m in range(mp_size)
        ]
        return lax.ppermute(v, ("dp", "mp"), pairs)

    def per_device(
        tokens,
        latents,
        image_of_group,
        token_valid,
        norm1_gain,
        norm1_shift,
        w_qkv,
        b_qv,
        w_out,
        b_out,
        norm2_gain,
        norm2_shift,
        w_up,
        b_up,
        w_down,
        b_down,
        cot_tokens,
        cot_latents,
    ):
        dp_at, mp_at = lax.axis_index("dp"), lax.axis_index("mp")
        tok_count, width = tokens.shape
        lat_count = latents.shape[0]
        groups = lat_count // LAT
        wide = w_qkv.shape[2]
        hidden = w_up.shape[1]
        tok_own, lat_own = tok_count // 4, lat_count // 4
        rows_own = tok_own + lat_own
        all_lat = dp_size * lat_count
        meta = jnp.stack([dp_at, mp_at]).astype(jnp.int32)
        count = jnp.sum(token_valid.reshape(groups, GROUP), 1).astype(jnp.int32)
        par = whole((8, width))
        w_t = jnp.transpose(w_qkv, (0, 2, 1))
        w_all = (3, wide, width)
        quarter, small = width // 4, wide // 4
        half = 2 * quarter
        big = (rows_own, width)
        chip_rows, chip_tok, chip_lat = 2 * rows_own, 2 * tok_own, 2 * lat_own
        vec = pl.BlockSpec((width,), lambda *_: (0,))

        def out(shape, kind=BF):
            return (shape, kind, whole(shape))

        def kept_out(shape, kind=BF):
            return (shape, kind, kept(shape))

        vm = pltpu.VMEM

        def any_out(shape, kind=BF):
            return (shape, kind, ANY)

        def dma(n):
            return pltpu.SemaphoreType.DMA((n,))

        def cube(v, vx=None, vz=None, vxz=None):
            vx, vz, vxz = (v if w is None else w for w in (vx, vz, vxz))
            return swap(vx, x_bit, 0), swap(vz, z_bit, 0), swap(vxz, x_bit | z_bit, 0)

        def all_latents(v):
            v = jnp.concatenate((v,) + cube(v), 0)
            for bit in rest_bits:
                v = jnp.concatenate([v, swap(v, bit, 0)], 0)
            return v

        part_block = pl.BlockSpec((quarter, width), lambda i, meta: ((meta[0] & 1) * 2 + ((meta[0] >> 1) & 1), 0))
        lat_rel, lat_half, o0, weight_part, params = call(
            prepare,
            name="prepare",
            room=62,
            scalars=1,
            ins=[pl.BlockSpec(memory_space=pltpu.HBM)] * 11,
            outs=[out((lat_count, width)), out((chip_lat, width)), out((wide + 16, width)), out((half, width)), out((8, width), F32)],
            scratch=[vm((lat_count, width), BF), vm((wide, width), BF), dma(11)] + [vm((width,), F32)] * 7,
            us=2,
        )(meta, latents, w_out, norm1_gain, norm1_shift, b_out, norm2_gain, norm2_shift, b_down, b_up, w_up, w_down)
        lat_four = jnp.concatenate((lat_half,) + cube(lat_half), 0)
        w_own = swap(weight_part, 0, 2)
        o2 = swap(o0, 0, 2)

        normed_lat, ql, kl, vl = call(
            latent_rows,
            name="latent_rows",
            room=3,
            scalars=0,
            ins=[whole((lat_count, width)), par, whole(w_all), whole((2, wide))],
            outs=[out((lat_count, width))] + [out((lat_count, wide), F32)] * 3,
            us=2,
        )(lat_rel, params, w_t, b_qv)

        def cot_through(slot, meta):
            return call(
                cot_back,
                name="cot_back",
            room=4,
                scalars=1,
                ins=[
                    pl.BlockSpec((tok_own, width), lambda i, meta: (meta[1] ^ slot, 0), pipeline_mode=pl.Buffered(1)),
                    pl.BlockSpec((lat_own, width), lambda i, meta: (meta[1] ^ slot, 0), pipeline_mode=pl.Buffered(1)),
                    whole((hidden, width)),
                ],
                outs=[out((rows_own, hidden))],
                us=4,
            )(meta, cot_tokens, cot_latents, w_down)[0]

        cot_own = cot_through(0, after(meta, kl))
        lat_here = lat_four = after(lat_four, cot_own)
        for bit in rest_bits:
            lat_here = jnp.concatenate([lat_here, swap(lat_here, bit, 0)], 0)

        def near_forward(base, *deps):
            def run(*args):
                return forward_near(base, *args)

            rows = lambda wide_here: pl.BlockSpec((tok_own, wide_here), lambda i, *_: (i, 0))
            lat_block = pl.BlockSpec((lat_own, wide), lambda i, *_: (i + base, 0))
            each = groups // 4
            return call(
                run,
                name="forward_near",
            room=46,
                grid=(2,),
                scalars=2,
                ins=[
                    pl.BlockSpec((tok_own, width), lambda i, meta, _: (meta[1] ^ (i + base), 0)),
                    lat_block,
                    lat_block,
                    par,
                    whole(w_all),
                    whole((2, wide)),
                ],
                outs=[((chip_tok, width), BF, rows(width))]
                + [((chip_tok, wide), BF, rows(wide))] * 3
                + [((wide, chip_tok), BF, pl.BlockSpec((wide, tok_own), lambda i, *_: (0, i)))]
                + [((2 * each, 8, GROUP), F32, pl.BlockSpec((each, 8, GROUP), lambda i, *_: (i, 0, 0)))],
                us=8,
            )(meta, count, tokens, after(kl, *deps), vl, params, w_t, b_qv)

        normed_b, q_b, k_b, v_b, t_b, log_b = near_forward(2, lat_four)
        t_far = swap(t_b, 0, 2)
        lat_here = after(lat_here, t_b)
        normed_a, q_a, k_a, v_a, t_near, log_a = near_forward(0, lat_here)
        w_x, w_z, w_xz = cube(after(w_own, t_near))
        lat_all = [v.reshape(dp_size, chip_lat, width) for v in (lat_here, swap(lat_here, 0, 1))]
        lat_all = jnp.concatenate(lat_all, 1).reshape(all_lat, width)
        lat_all = after(lat_all, t_near)

        chunk = min(512, all_lat)
        qa, ka, va, l_near, l_b, far, far_logs = call(
            forward_far,
            name="forward_far",
            room=6,
            grid=(all_lat // chunk,),
            scalars=3,
            ins=[pl.BlockSpec((chunk, width), lambda i, *_: (i, 0)), par, whole(w_all), whole((2, wide))]
            + [whole((chip_tok, wide))] * 4
            + [whole((lat_count, wide))],
            outs=[out((all_lat, wide))] * 3
            + [kept_out((chip_lat, wide))] * 2
            + [kept_out((lat_count, wide)), kept_out((lat_count, 2 * HEAD))],
            us=6,
        )(meta, count, image_of_group, lat_all, params, w_t, b_qv, k_a, k_b, v_a, v_b, ql)
        l_far = swap(l_b, 0, 2)

        out_pack = whole((wide + 16, width))
        mixed_specs = [whole((wide, chip_tok))] * 2 + [whole((chip_lat, wide))] * 2
        cot_sib = cot_through(1, after(meta, far))

        def out_rows_of(slot, kind, o0):
            return call(
                project_out,
                name="project_out",
            room=4,
                scalars=0,
                ins=[pl.BlockSpec((wide, tok_own), lambda *_: (0, slot), pipeline_mode=pl.Buffered(1))] * 2
                + [pl.BlockSpec((lat_own, wide), lambda *_: (slot, 0), pipeline_mode=pl.Buffered(1))] * 2
                + [out_pack] * 2,
                outs=[out(big, kind)],
                us=3,
            )(t_near, t_far, l_near, l_far, o0, o2)[0]

        attn_send = out_rows_of(1, BF, after(o0, cot_sib))
        attn_own = out_rows_of(0, F32, after(o0, attn_send))
        attn_got = swap(attn_send, 0, 1)
        own_tok = pl.BlockSpec((tok_own, width), lambda i, meta, _: (meta[1], 0), pipeline_mode=pl.Buffered(1))
        own_lat = pl.BlockSpec((lat_own, width), lambda i, meta, _: (meta[1], 0), pipeline_mode=pl.Buffered(1))
        residual, n2, stats1 = call(
            add_norm,
            name="add_norm",
            room=6,
            scalars=2,
            ins=[par, whole(big), whole(big), own_tok, whole((lat_own, width))],
            outs=[out(big, F32), out(big), out((8, width), F32)],
            us=3,
        )(meta, count, params, attn_own, attn_got, tokens, lat_rel)
        n2_sib = swap(n2, 0, 1)

        chip = (chip_rows, width)
        piece = (half, width)
        act_first, grad_first, bias_first = call(
            hidden_first,
            name="hidden_first",
            room=6,
            scalars=0,
            ins=[par, whole(big), whole((width, hidden)), whole((rows_own, hidden))],
            outs=[out((rows_own, hidden))] * 2 + [out((8, hidden), F32)],
            us=4,
        )(params, n2, w_up, cot_own)
        act_near, grad_near, a0, a1, a2, a3, bias_near = call(
            hidden_own,
            name="hidden_own",
            room=7,
            scalars=1,
            ins=[par] + [ANY] * 8,
            outs=[any_out((chip_rows, hidden))] * 2 + [any_out(piece)] * 4 + [out((8, hidden), F32)],
            scratch=[
                vm(chip, BF),
                vm(chip, BF),
                vm((width, hidden), BF),
                vm((chip_rows, hidden), BF),
                vm((chip_rows, hidden), BF),
                vm((rows_own, hidden), BF),
                vm((width + hidden, width), BF),
                dma(10),
                dma(10),
            ],
            us=9,
        )(meta, params, n2, n2_sib, cot_tokens, cot_latents, w_up, cot_sib, act_first, grad_first)
        near_parts = (a0,) + cube(None, a1, a2, a3)

        branch, back, middle_send, act, grad, bias_away = call(
            hidden_away,
            name="hidden_away",
            room=8,
            scalars=1,
            ins=[out_pack] + [ANY] * 12,
            outs=[any_out(big, F32), any_out(big, F32), any_out(chip), any_out((chip_rows, hidden)), any_out((chip_rows, hidden))]
            + [out((8, hidden), F32)],
            scratch=[
                vm(chip, BF),
                vm(chip, BF),
                vm((2, width, hidden), BF),
                vm((2, width, hidden), BF),
                vm((chip_rows, hidden), BF),
                vm((chip_rows, hidden), BF),
                vm(chip, F32),
                vm(chip, F32),
                vm((chip_rows, hidden), BF),
                vm((chip_rows, hidden), BF),
                vm(chip, BF),
                dma(18),
                dma(6),
            ],
            us=10,
        )(meta, o2, n2, n2_sib, cot_tokens, cot_latents, w_own, w_x, w_z, w_xz, act_near, grad_near, w_up, w_down)
        middle_got = swap(middle_send, 0, 1)

        b0, b1, b2, b3 = call(
            away_grads,
            name="away_grads",
            room=7,
            scalars=1,
            ins=[ANY] * 6,
            outs=[any_out(piece)] * 4,
            scratch=[
                vm(chip, BF),
                vm(chip, BF),
                vm((chip_rows, hidden), BF),
                vm((chip_rows, hidden), BF),
                vm((width + hidden, width), BF),
                dma(8),
                dma(8),
            ],
            us=6,
        )(meta, n2, n2_sib, cot_tokens, cot_latents, act, grad)

        out_rows, grad_res, grad_attn, stats2 = call(
            middle_rows,
            name="middle_rows",
            room=8,
            scalars=2,
            ins=[par, whole(big), whole(big), whole(big), whole(chip), own_tok, own_lat],
            outs=[out(big), out(big, F32), out(big), out((8, width), F32)],
            us=5,
            deps=(b0,),
        )(meta, count, params, residual, branch, back, middle_got, cot_tokens, cot_latents)
        grad_attn_sib = swap(grad_attn, 0, 1)

        def terms(n, at=0):
            return [(i, at) for i in range(n)]

        sides4 = ((0, 0), (1, 0), (0, 1), (1, 1))

        def at(d, size, base=0):
            return lambda x, z: base + ((x ^ d[0]) * 2 + (z ^ d[1])) * size


        (near_sum,) = combine("near_sum", meta, near_parts, [(half, BF, [(0, half, terms(4))])], us=2)
        away_parts = (b0,) + cube(None, *(after(v, near_parts[1], near_parts[2]) for v in (b1, b2, b3)))

        g_near, g_send, d_near, out_grad, out_send = call(
            back_out,
            name="back_out",
            room=6,
            scalars=1,
            ins=[whole(big), whole(big), out_pack, out_pack] + mixed_specs,
            outs=[out((wide, chip_tok))] * 2 + [out((chip_lat, wide)), out((wide, width)), out((wide + chip_lat, width))],
            us=4,
            deps=(near_sum,),
        )(meta, grad_attn, grad_attn_sib, o0, o2, t_near, t_far, l_near, l_far)
        out_got = swap(out_send, 0, 2)
        g_far = swap(g_send, 0, 2)

        zero_w, zero_b = jnp.zeros((8, LANES), F32), jnp.zeros((8, LANES), F32)

        def rows_backward(first, steps, half_in, g, d, gw, bias, *deps):
            normed, q, k, v, log = half_in
            base = first % 2

            def rows(n, wide_here, shift):
                return pl.BlockSpec((n, wide_here), lambda i, *_: (i + shift, 0))

            def run(*args):
                return backward_rows(first, gw is None, *args)

            init = (zero_w, zero_b) if gw is None else (gw, bias)
            return call(
                run,
                name="backward_rows",
            room=8,
                grid=(steps,),
                scalars=2,
                ins=[
                    rows(tok_own, width, base),
                    *[rows(tok_own, wide, base)] * 3,
                    *[rows(lat_own, wide, first)] * 3,
                    pl.BlockSpec((groups // 4, 8, GROUP), lambda i, *_: (i + base, 0, 0)),
                    rows(lat_own, wide, first),
                    rows(lat_own, 2 * HEAD, first),
                    pl.BlockSpec((wide, tok_own), lambda i, *_: (0, i + base)),
                    rows(lat_own, d.shape[1], base + (wide // lat_own if d.shape[1] != wide else 0)),
                    whole(w_all),
                    whole(init[0].shape),
                    whole(init[1].shape),
                ],
                outs=[kept_out((tok_own, width))] * steps
                + [kept_out(w_all, F32), kept_out((8, wide), F32)]
                + [((steps * lat_own, wide), F32, rows(lat_own, wide, 0))] * 3,
                us=7 * steps,
                deps=deps,
            )(meta, count, normed, q, k, v, ql, kl, vl, log, far, far_logs, g, d, w_t, *init)

        half_a, half_b = (normed_a, q_a, k_a, v_a, log_a), (normed_b, q_b, k_b, v_b, log_b)
        part0, gw, bias, *near_0 = rows_backward(0, 1, half_a, g_near, d_near, None, None)
        bundle_own, bundle = call(
            latent_bundle,
            name="latent_bundle",
            scalars=1,
            ins=[whole((chip_lat, wide)), pl.BlockSpec((chip_lat, width), lambda *_: (wide // chip_lat, 0))]
            + [whole((lat_count, wide)), whole((lat_count, 2 * HEAD))],
            outs=[out((lat_count, 4 * HEAD))] * 2,
            us=2,
            deps=(part0,),
        )(meta, d_near, out_got, far, far_logs)
        steps = [bundle]

        def spread(bit):
            got = swap(steps[0], bit, 0)
            return lambda done: steps.__setitem__(0, jnp.concatenate([after(steps[0], done), got], 0))

        join = spread(x_bit)
        part1, gw, bias, *near_1 = rows_backward(1, 1, half_a, g_near, d_near, gw, bias, bundle_own)
        join(part1)
        join = spread(z_bit)
        (away_sum,) = combine("away_sum", meta, away_parts, [(half, BF, [(0, half, terms(4))])], us=2, deps=(part1,))
        away_got = swap(away_sum, 0, 2)
        part3, gw, bias, *near_3 = rows_backward(3, 1, half_b, g_far, out_got, gw, bias, away_sum, steps[0])
        join(part3)
        for bit in rest_bits[:-1]:
            spread(bit)(part3)
        join = spread(rest_bits[-1]) if rest_bits else None
        got3 = swap(part3, 0, 1)
        got1 = swap(after(part1, part3), 0, 1)
        part2, gw, bias, *near_2 = rows_backward(2, 1, half_b, g_far, out_got, gw, bias)
        if rest_bits:
            join(part2)
        bundle = steps[0]
        (total,) = combine(
            "weights_sum", meta, [near_sum, away_got], [(half, BF, [(0, half, terms(2))])], us=20, deps=(part2,)
        )
        near_all = [v for three in zip(near_0, near_1, near_2, near_3) for v in three]
        shard = (small * 4, width)
        lat_keep, lat_send, c0, c1, c2, c3, small_rows = call(
            backward_far,
            name="backward_far",
            room=6,
            scalars=3,
            ins=[whole((all_lat, wide))] * 3
            + [whole((lat_count, wide))] * 3
            + [whole((lat_count, 4 * HEAD)), whole((all_lat, 4 * HEAD)), whole((lat_count, width)), whole(w_all), whole(w_all)]
            + [whole((8, wide))]
            + [whole((wide, width)), pl.BlockSpec((wide, width), lambda *_: (0, 0), pipeline_mode=pl.Buffered(1))]
            + [par]
            + [whole((8, width))] * 5
            + [whole(v.shape) for v in near_all],
            outs=[out((chip_lat, width))] * 2 + [any_out(shard)] * 4 + [out((32, width), F32)],
            scratch=[vm((4 * wide, width), BF), dma(8)],
            us=8,
            deps=(total, got1, got3),
        )(
            meta, count, image_of_group, qa, ka, va, ql, kl, vl, bundle_own, bundle, normed_lat, w_t, gw, bias, out_grad,
            out_got, params, stats1, stats2, bias_first, bias_near, bias_away, *near_all,
        )

        lat_got = swap(lat_send, 0, 1)
        (there,) = combine(
            "rows_sum", meta, [part2, got3, lat_keep, lat_got],
            [(rows_own, BF, [(0, tok_own, terms(2)), (tok_own, lat_own, [(2, lat_own), (3, lat_own)])])],
            us=2, deps=(total,),
        )
        from_y = swap(there, 0, 2)
        small_rows = small_rows + swap(small_rows, 0, 1)
        small_got = swap(small_rows, 0, 2)
        rows4 = 4 * small
        qkv_parts = (c0,) + cube(None, *(after(v, total) for v in (c1, c2, c3)))
        (qkv,) = combine(
            "qkv_sum", meta, qkv_parts + (small_rows, small_got),
            [(rows4 + 32, BF, [(0, rows4, terms(4)), (rows4, 32, [(4, 0), (5, 0)])])],
            us=2, deps=(there,),
        )
        (grad_rows,) = call(
            final_rows,
            name="final_rows",
            room=6,
            scalars=1,
            ins=[
                pl.BlockSpec((tok_own, width), lambda i, meta: (meta[1], 0), pipeline_mode=pl.Buffered(1)),
                whole((lat_own, width)),
                *[whole((tok_own, width))] * 2,
                whole(big),
                *[whole((chip_lat, width))] * 2,
                whole(big),
                par,
            ],
            outs=[out(big)],
            us=4,
            deps=(qkv,),
        )(meta, tokens, lat_rel, part0, got1, from_y, lat_keep, lat_got, grad_res, params)

        grad_y = swap(grad_rows, 0, 2)
        grad_c = swap(after(grad_rows, grad_y), 0, 1)
        out_y = swap(after(out_rows, qkv), 0, 2)
        for bit in rest_bits:
            (total,) = combine(
                "rest_sum", meta, [total, swap(total, bit, 0)], [(half, BF, [(0, half, terms(2))])], us=2,
                deps=(grad_rows,),
            )
        def all_rows(v, v_y, v_c):
            v_yc = swap(v_y, 0, 1)
            place = lambda n: pl.BlockSpec((n, width), lambda i, meta: (meta[1] ^ i, 0))
            return call(
                place_rows,
                name="place_rows",
                grid=(4,),
                scalars=1,
                ins=[whole(big)] * 4,
                outs=[((tok_count, width), BF, place(tok_own)), ((lat_count, width), BF, place(lat_own))],
                us=4,
            )(meta, v, v_c, v_y, v_yc)

        grad_tok, grad_lat = all_rows(grad_rows, grad_y, grad_c)
        out_tok, out_lat = all_rows(out_rows, out_y, swap(after(out_rows, out_y), 0, 1))
        four = (total,) + cube(total)
        grad_w_up, grad_w_down = combine(
            "weights_out", meta, four,
            [
                (4 * quarter, F32, [(at(d, quarter), quarter, [(i, r * quarter)]) for i, d in enumerate(sides4)])
                for r in (0, 1)
            ]
            ,
            us=5,
            deps=(qkv, out_y, grad_tok),
        )
        for bit in rest_bits:
            (qkv,) = combine("qkv_rest", meta, [qkv, swap(qkv, bit, 0)], [(rows4 + 32, BF, [(0, rows4 + 32, terms(2))])], us=2, deps=(total,))
        four = (qkv,) + tuple(
            swap(after(qkv, v), bit, 0) for v, bit in zip(four[1:], (x_bit, z_bit, x_bit | z_bit))
        )
        grad_w_qkv, grad_w_out, *vectors, grad_b_qv, roots = call(
            projections_out,
            name="qkv_out",
            scalars=1,
            ins=[whole((rows4 + 32, width))] * 4,
            outs=[out((3 * wide, width), F32), out((wide, width), F32)]
            + [((width,), F32, vec)] * 7
            + [out((2, wide), F32), out((8, LANES), F32)],
            us=3,
            deps=(out_tok, grad_w_up),
        )(meta, *four)
        grad_w_qkv = grad_w_qkv.reshape(3, wide, width).transpose(0, 2, 1)


        root_means = roots[0, :3]
        gain1, shift1, b_out_grad, gain2, shift2, b_down_grad, grad_b_up = vectors
        return (
            out_tok,
            out_lat,
            grad_tok,
            grad_lat,
            gain1,
            shift1,
            grad_w_qkv,
            grad_b_qv,
            grad_w_out,
            b_out_grad,
            gain2,
            shift2,
            grad_w_up,
            grad_b_up,
            grad_w_down,
            b_down_grad,
            root_means,
        )

    return per_device


def solution(mesh):
    rows, whole = P("dp", None), P()
    return jax.shard_map(
        make(mesh),
        mesh=mesh,
        in_specs=(
            rows,
            rows,
            whole,
            P("dp"),
            whole,
            whole,
            P(None, None, "mp"),
            P(None, "mp"),
            P("mp", None),
            whole,
            whole,
            whole,
            P(None, "mp"),
            P("mp"),
            P("mp", None),
            whole,
            rows,
            rows,
        ),
        out_specs=(
            rows,
            rows,
            rows,
            rows,
            whole,
            whole,
            P(None, None, "mp"),
            P(None, "mp"),
            P("mp", None),
            whole,
            whole,
            whole,
            P(None, "mp"),
            P("mp"),
            P("mp", None),
            whole,
            whole,
        ),
        check_vma=False,
    )
```

```python
import jax
import jax.numpy as jnp
from jax import lax
from jax.experimental import pallas as pl
from jax.experimental.pallas import tpu as pltpu
from jax.sharding import PartitionSpec as P

HEAD = 64
LANES = 128
GROUP = 256
LAT = 8
BF = jnp.bfloat16
F32 = jnp.float32
FAR = -1e30
MIB = 1 << 20
GAIN1, SHIFT1, B_OUT, GAIN2, SHIFT2, B_DOWN, B_UP = range(7)


def dot(a, b, ca, cb):
    return lax.dot_general(a, b, (((ca,), (cb,)), ((), ())), preferred_element_type=F32)


def norm_parts(values):
    center = values - jnp.mean(values, axis=-1, keepdims=True)
    spread = jnp.mean(center * center, axis=-1, keepdims=True)
    inverse = lax.rsqrt(spread + 1e-06)
    return center * inverse, inverse


def norm_back(grad, unit, inverse, gain):
    scaled = grad * gain
    inner = jnp.mean(scaled * unit, axis=-1, keepdims=True)
    return inverse * (scaled - jnp.mean(scaled, axis=-1, keepdims=True) - unit * inner)


def gelu_both(values):
    square = values * values
    inner = jnp.tanh(values * (0.7978845608028654 + 0.035677408136300125 * square))
    half = 0.5 + 0.5 * inner
    slope = values * (0.3989422804014327 + 0.05351611220494518 * square)
    return values * half, half + (1.0 - inner * inner) * slope


def split3(v):
    hi = v.astype(BF)
    mid = (v - hi.astype(F32)).astype(BF)
    low = (v - hi.astype(F32) - mid.astype(F32)).astype(BF)
    return hi, mid, low


def head_lanes(v, h):
    lane = lax.broadcasted_iota(jnp.int32, v.shape, v.ndim - 1)
    return jnp.where((lane >= h * HEAD) & (lane < (h + 1) * HEAD), v, jnp.zeros_like(v))


def kept(shape):
    return pl.BlockSpec(shape, lambda *_: (0,) * len(shape))


def whole(shape):
    return pl.BlockSpec(shape, lambda *_: (0,) * len(shape), pipeline_mode=pl.Buffered(1))


ANY = pl.BlockSpec(memory_space=pl.ANY)
OWN, SENT = (0, 1, 2, 3), (0, 2, 1, 3)


def block_bytes(shape, kind, copies):
    size = jnp.dtype(kind).itemsize
    dims = [1, 1] + list(shape)
    rows, lanes = 32 // size, LANES
    dims[-1] = -(-dims[-1] // lanes) * lanes
    dims[-2] = -(-dims[-2] // rows) * rows
    total = size * copies
    for d in dims:
        total *= d
    return total


def spec_bytes(spec, kind):
    if spec.block_shape is None:
        return 0
    return block_bytes(spec.block_shape, kind, 1 if spec.pipeline_mode is not None else 2)


def after(v, *deps):
    return lax.optimization_barrier((v,) + deps)[0]


def call(body, *, name, scalars, ins, outs, grid=(1,), scratch=(), deps=(), us=1.0, room=3):
    def run(*args):
        if deps:
            args = (after(args[0], *deps),) + args[1:]
        need = room * MIB + sum(spec_bytes(spec, kind) for _, kind, spec in outs)
        need += sum(spec_bytes(spec, a.dtype) for spec, a in zip(ins, args[scalars:]))
        need += sum(block_bytes(s.shape, s.dtype, 1) for s in scratch if s.shape and len(s.shape) > 1)
        return pl.pallas_call(
            body,
            name=name,
            out_shape=[jax.ShapeDtypeStruct(s, d) for s, d, _ in outs],
            grid_spec=pltpu.PrefetchScalarGridSpec(
                num_scalar_prefetch=scalars,
                grid=grid,
                in_specs=list(ins),
                out_specs=[spec for _, _, spec in outs],
                scratch_shapes=list(scratch),
            ),
            compiler_params=pltpu.CompilerParams(
                dimension_semantics=("arbitrary",) * len(grid), vmem_limit_bytes=need
            ),
            cost_estimate=pl.CostEstimate(
                flops=int(us * 1.0e10), bytes_accessed=1 << 16, transcendentals=0
            ),
        )(*args)

    return run


def mover(sems):
    used = []

    def start(src, dst):
        copy = pltpu.make_async_copy(src, dst, sems.at[len(used)])
        used.append(copy)
        copy.start()
        return copy

    return start


def sides(meta):
    return meta[0] & 1, (meta[0] >> 1) & 1


def combine(name, meta, arrays, outs, deps=(), us=1.0):
    def body(meta, *refs):
        x, z = sides(meta)

        def rows_at(at, n):
            return pl.ds(pl.multiple_of(at(x, z), 16), n) if callable(at) else slice(at, at + n)

        for ref, (_, kind, segments) in zip(refs[len(arrays) :], outs):
            for to, n, terms in segments:
                parts = [refs[i][rows_at(at, n), :] for i, at in terms]
                value = parts[0]
                if len(parts) > 1:
                    value = parts[0].astype(F32)
                    for part in parts[1:]:
                        value = value + part.astype(F32)
                ref[rows_at(to, n), :] = value.astype(kind)

    width = arrays[0].shape[1]
    return call(
        body,
        name=name,
        scalars=1,
        ins=[whole(a.shape) for a in arrays],
        outs=[((rows, width), kind, whole((rows, width))) for rows, kind, _ in outs],
        deps=deps,
        us=us,
    )(meta, *arrays)


def group_at(meta, count, slot, i):
    return count[(meta[1] ^ slot) * 2 + i]


def image_list(meta, image, devices, per_device, slots):
    each = per_device // 4
    return [
        image[(meta[0] ^ j) * per_device + (meta[1] ^ s) * each + i]
        for j in range(devices)
        for s in slots
        for i in range(each)
    ]


def image_column(images):
    return jnp.concatenate([jnp.full((LAT, 1), im, jnp.int32) for im in images], 0)


def image_row(images):
    group = lax.broadcasted_iota(jnp.int32, (1, len(images) * LAT), 1) // LAT
    out = jnp.zeros(group.shape, jnp.int32)
    for g, im in enumerate(images):
        out = jnp.where(group == g, im, out)
    return out


def key_stack(tok, lat8):
    pad = jnp.concatenate([lat8, jnp.zeros_like(lat8)], 0).astype(BF)
    return jnp.concatenate([tok, pad], 0)


def near_mask(count, columns):
    row = lax.broadcasted_iota(jnp.int32, (GROUP + 2 * LAT, columns), 0)
    return (row < count) | ((row >= GROUP) & (row < GROUP + LAT))


def param(params, i):
    return params[i : i + 1, :]


def project(rows, params, w, bias):
    unit, _ = norm_parts(rows.astype(F32))
    rows = (unit * param(params, GAIN1) + param(params, SHIFT1)).astype(BF)
    return (
        rows,
        (dot(rows, w[0], 1, 1) + bias[0:1]).astype(BF),
        dot(rows, w[1], 1, 1).astype(BF),
        (dot(rows, w[2], 1, 1) + bias[1:2]).astype(BF),
    )


def prepare(
    meta, lat, w_out, g1, s1, bo, g2, s2, bd, bu, up, down, lat_rel, lat_half, out_pack, part, params,
    vlat, vout, sems, *vecs,
):
    fetch = mover(sems)
    lat_copy = fetch(lat, vlat)
    copies = [fetch(ref, dst) for ref, dst in zip((g1, s1, bo, g2, s2, bd, bu), vecs)]
    x, z = sides(meta)
    n = part.shape[0] // 2
    here = pl.ds(pl.multiple_of((x * 2 + z) * n, 16), n)
    parts = [fetch(up.at[here], part.at[0:n]), fetch(down.at[here], part.at[n:])]
    wide = w_out.shape[0]
    parts.append(fetch(w_out, vout))
    lat_copy.wait()
    n = lat.shape[0] // 4
    for s in range(4):
        rows = vlat[pl.ds(pl.multiple_of((meta[1] ^ s) * n, 16), n), :]
        lat_rel[s * n : (s + 1) * n, :] = rows
        if s % 2 == 0:
            lat_half[s // 2 * n : (s // 2 + 1) * n, :] = rows
    for copy in copies:
        copy.wait()
    for i in range(7):
        params[i : i + 1, :] = vecs[i][...].reshape(1, params.shape[1])
    params[7:8, :] = jnp.zeros_like(params[7:8, :])
    bias = param(params, B_UP)
    rows = [v.astype(F32) for v in split3(bias)]
    out_pack[wide : wide + 16, :] = jnp.concatenate(rows + [jnp.zeros((13, bias.shape[1]), F32)], 0).astype(BF)
    for copy in parts:
        copy.wait()
    out_pack[0:wide, :] = vout[...]


def latent_rows(lat, params, w, bias, normed, ql, kl, vl):
    normed[...], a, b, c = project(lat[...], params, w, bias)
    ql[...], kl[...], vl[...] = a.astype(F32), b.astype(F32), c.astype(F32)


def forward_near(base, meta, count, tok, kl, vl, params, w, bias, normed, q, k, v, mixed_out, log):
    step = pl.program_id(0)
    wide = w.shape[1]
    rows, qs, ks, vs = project(tok[...], params, w, bias)
    normed[...], q[...], k[...], v[...] = rows, qs, ks, vs
    qs = qs * jnp.asarray(0.125, BF)
    for i in range(tok.shape[0] // GROUP):
        here = slice(i * LAT, (i + 1) * LAT)
        at = slice(i * GROUP, (i + 1) * GROUP)
        keys = key_stack(ks[at], kl[here, :])
        values = key_stack(vs[at], vl[here, :]).T
        mask = near_mask(group_at(meta, count, step + base, i), GROUP)
        logs, outs = [], []
        for h in range(wide // HEAD):
            s = jnp.where(mask, dot(head_lanes(keys, h), qs[at], 1, 1), FAR)
            top = jnp.max(s, 0, keepdims=True)
            e = jnp.exp(s - top)
            total = jnp.sum(e, 0, keepdims=True)
            logs.append(top + jnp.log(total))
            outs.append(dot(values[h * HEAD : (h + 1) * HEAD], e.astype(BF), 1, 0) * (1.0 / total))
        log[i] = jnp.concatenate(logs + [jnp.zeros((8 - len(logs), GROUP), F32)], 0)
        mixed_out[:, at] = jnp.concatenate(outs, 0).astype(BF)


def forward_far(meta, count, image, lat, params, w, bias, k_near, k_away, v_near, v_away, ql, qa, ka, va, m_near, m_away, far, logs_out):
    step = pl.program_id(0)
    wide = w.shape[1]
    rows_step = lat.shape[0]
    own = ql.shape[0]
    groups = own // LAT

    def rows_of(near, away, g):
        half = groups // 2
        ref, at = (near, g) if g < half else (away, g - half)
        return ref[at * GROUP : (at + 1) * GROUP, :]

    _, a, b, c = project(lat[...], params, w, bias)
    here = pl.ds(pl.multiple_of(step * rows_step, rows_step), rows_step)
    qa[here, :], ka[here, :], va[here, :] = a, b, c

    @pl.when(step == pl.num_programs(0) - 1)
    def _():
        q32 = ql[...] * 0.125
        images = image_list(meta, image, qa.shape[0] // own, groups, SENT)
        mask = image_column(image_list(meta, image, 1, groups, OWN)) == image_row(images)
        lane = lax.broadcasted_iota(jnp.int32, (LAT, GROUP), 1)
        full = jnp.zeros((own, wide), F32)
        logs = []
        for h in range(wide // HEAD):
            qh = head_lanes(q32, h)
            s_lat = jnp.where(mask, dot(qh.astype(BF), ka[...], 1, 1), FAR)
            s_tok = jnp.concatenate(
                [
                    jnp.where(
                        lane < group_at(meta, count, g // 2, g % 2),
                        dot(qh[g * LAT : (g + 1) * LAT].astype(BF), rows_of(k_near, k_away, g), 1, 1),
                        FAR,
                    )
                    for g in range(groups)
                ],
                0,
            )
            top = jnp.maximum(jnp.max(s_lat, 1, keepdims=True), jnp.max(s_tok, 1, keepdims=True))
            e_lat, e_tok = jnp.exp(s_lat - top), jnp.exp(s_tok - top)
            total = jnp.sum(e_lat, 1, keepdims=True) + jnp.sum(e_tok, 1, keepdims=True)
            logs.append(top + jnp.log(total))
            near = jnp.concatenate(
                [
                    dot(e_tok[g * LAT : (g + 1) * LAT].astype(BF), rows_of(v_near, v_away, g), 1, 0)
                    for g in range(groups)
                ],
                0,
            )
            full = full + head_lanes((dot(e_lat.astype(BF), va[...], 1, 0) + near) * (1.0 / total), h)
        mixed = full.astype(BF)
        m_near[...], m_away[...] = mixed[: own // 2], mixed[own // 2 :]
        parts = [split3(x) for x in logs]
        cols = [p[i] for i in range(3) for p in parts]
        lane = lax.broadcasted_iota(jnp.int32, (own, 2 * HEAD), 1)
        extra = jnp.zeros((own, 2 * HEAD), F32)
        for i, c in enumerate(cols):
            extra = jnp.where(lane == i, c.astype(F32), extra)
        far[...] = mixed
        logs_out[...] = extra.astype(BF)


def valid_rows(meta, count, rows):
    row = lax.broadcasted_iota(jnp.int32, (rows, 1), 0)
    first = (row < GROUP) & (row < group_at(meta, count, 0, 0))
    return first | ((row >= GROUP) & (row < GROUP + group_at(meta, count, 0, 1)))


def slot_block(meta, ref, slot):
    n = ref.shape[0] // 4
    return ref.at[pl.ds(pl.multiple_of((meta[1] ^ slot) * n, 16), n)]


def project_out(t_near, t_far, l_near, l_far, o0, o2, out):
    wide, n = t_near.shape
    value = dot(t_near[...], o0[0:wide, :], 0, 0) + dot(t_far[...], o2[0:wide, :], 0, 0)
    out[0:n, :] = value.astype(out.dtype)
    value = dot(l_near[...], o0[0:wide, :], 1, 0) + dot(l_far[...], o2[0:wide, :], 1, 0)
    out[n:, :] = value.astype(out.dtype)


def cot_back(meta, cot_tok, cot_lat, down_w, out):
    n = cot_tok.shape[0]
    out[0:n, :] = dot(cot_tok[...], down_w[...], 1, 1).astype(BF)
    out[n:, :] = dot(cot_lat[...], down_w[...], 1, 1).astype(BF)


def add_norm(meta, count, params, own, got, tok, lat, residual, n2, stats):
    n, m = tok.shape[0], lat.shape[0]
    stats[...] = jnp.zeros_like(stats)
    for at, size, x in ((0, n, tok), (n, m, lat)):
        rows = slice(at, at + size)
        attn = own[rows, :] + got[rows, :].astype(F32) + param(params, B_OUT)
        if at == 0:
            real = valid_rows(meta, count, n)
            stats[0:1, :] = jnp.sum(jnp.where(real, attn * attn, 0.0), 0, keepdims=True)
        res = x[...].astype(F32) + attn
        residual[rows, :] = res
        unit, _ = norm_parts(res)
        n2[rows, :] = (unit * param(params, GAIN2) + param(params, SHIFT2)).astype(BF)


def hidden_part(n2, cot, up_w, down_w, bias, act_out, grad_out):
    cut = 256
    sums = []
    for at in range(0, up_w.shape[1], cut):
        cols = slice(at, at + cut)
        up = dot(n2, up_w[:, cols], 1, 0) + bias[:, cols]
        active, slope = gelu_both(up)
        grad_up = (dot(cot, down_w[cols, :], 1, 1) * slope).astype(BF)
        act_out[:, cols] = active.astype(BF)
        grad_out[:, cols] = grad_up
        sums.append(jnp.sum(grad_up.astype(F32), 0, keepdims=True))
    return jnp.concatenate(sums, 1)


def two_halves(meta, fetch, n2_own, n2_sib, cot_tok, cot_lat, vn2, vcot):
    rows = n2_own.shape[0]
    n = cot_tok.shape[0] // 4
    copies = [fetch(n2_own, vn2.at[0:rows]), fetch(n2_sib, vn2.at[rows:])]
    for s in (0, 1):
        at = s * rows
        copies.append(fetch(slot_block(meta, cot_tok, s), vcot.at[at : at + n]))
        copies.append(fetch(slot_block(meta, cot_lat, s), vcot.at[at + n : at + rows]))
    return copies


def send_parts(meta, flush, pack, parts):
    x, z = sides(meta)
    n = parts[0].shape[0] // 2
    copies = []
    for ref, (dx, dz) in zip(parts, ((0, 0), (1, 0), (0, 1), (1, 1))):
        q = (x ^ dx) * 2 + (z ^ dz)
        for i in (0, 1):
            src = pack.at[pl.ds(pl.multiple_of(i * 4 * n + q * n, 16), n)]
            copies.append(flush(src, ref.at[i * n : (i + 1) * n]))
    return copies


def hidden_rows(n2, up_w, bias, got, act_out, grad_out, sums):
    cut = 256
    for at in range(0, up_w.shape[1], cut):
        cols = slice(at, at + cut)
        active, slope = gelu_both(dot(n2, up_w[:, cols], 1, 0) + bias[:, cols])
        grad_up = (got[:, cols].astype(F32) * slope).astype(BF)
        act_out[:, cols] = active.astype(BF)
        grad_out[:, cols] = grad_up
        sums[0:1, cols] = jnp.sum(grad_up.astype(F32), 0, keepdims=True)


def hidden_first(params, n2, up_w, got, act, grad, stats):
    stats[...] = jnp.zeros_like(stats)
    hidden_rows(n2[...], up_w, param(params, B_UP), got, act, grad, stats)


def hidden_own(
    meta, params, n2_own, n2_sib, cot_tok, cot_lat, up_w, got_in, act_in, grad_in,
    act_out, grad_out, p0, p1, p2, p3, stats,
    vn2, vcot, vw, act, grad, got, vpack, in_sems, out_sems,
):
    width, hidden = vw.shape
    rows = got.shape[0]
    fetch, flush = mover(in_sems), mover(out_sems)
    first = [fetch(n2_sib, vn2.at[rows:]), fetch(up_w, vw), fetch(got_in, got)]
    copies = [fetch(grad_in, grad.at[0:rows]), fetch(act_in, act.at[0:rows]), fetch(n2_own, vn2.at[0:rows])]
    n = cot_tok.shape[0] // 4
    for s in (0, 1):
        at = s * rows
        copies.append(fetch(slot_block(meta, cot_tok, s), vcot.at[at : at + n]))
        copies.append(fetch(slot_block(meta, cot_lat, s), vcot.at[at + n : at + rows]))
    for copy in first:
        copy.wait()
    stats[...] = jnp.zeros_like(stats)
    hidden_rows(vn2[rows:, :], vw, param(params, B_UP), got, act.at[rows:], grad.at[rows:], stats)
    for copy in copies:
        copy.wait()
    outs = [flush(act, act_out), flush(grad, grad_out)]
    vpack[0:width, :] = dot(vn2[...], grad[...], 0, 0).astype(BF)
    vpack[width : width + hidden, :] = dot(act[...], vcot[...], 0, 0).astype(BF)
    outs += send_parts(meta, flush, vpack, (p0, p1, p2, p3))
    for copy in outs:
        copy.wait()


def hidden_away(
    meta, o2, n2_own, n2_sib, cot_tok, cot_lat, w0, w1, w2, w3, act_in, grad_in, up_w, down_w,
    branch_own, back_own, send, act_out, grad_out, stats,
    vn2, vcot, vw, vnear, act0, grad0, branch, back, act, grad, vsend, in_sems, out_sems,
):
    rows, width = n2_own.shape
    x, z = sides(meta)
    quarter = w0.shape[0] // 2
    fetch, flush = mover(in_sems), mover(out_sems)
    copies = two_halves(meta, fetch, n2_own, n2_sib, cot_tok, cot_lat, vn2, vcot)
    for ref, (dx, dz) in zip((w0, w1, w2, w3), ((0, 0), (1, 0), (0, 1), (1, 1))):
        q = pl.multiple_of(((x ^ dx) * 2 + (z ^ dz)) * quarter, 16)
        for i in (0, 1):
            copies.append(fetch(ref.at[i * quarter : (i + 1) * quarter], vw.at[i, pl.ds(q, quarter)]))
    late = [(fetch(grad_in, grad0), fetch(up_w, vnear.at[0])), (fetch(act_in, act0), fetch(down_w, vnear.at[1]))]
    for copy in copies:
        copy.wait()
    base = o2.shape[0] - 16
    bias = o2[base : base + 16, :].astype(F32)
    bias = bias[0:1] + bias[1:2] + bias[2:3]
    n2, ct = vn2[...], vcot[...]
    stats[...] = jnp.zeros_like(stats)
    stats[0:1, :] = hidden_part(n2, ct, vw.at[0], vw.at[1], bias, act, grad)
    outs = [flush(act, act_out), flush(grad, grad_out)]
    for i, (ref, near, src, turn, own) in enumerate(
        ((back, grad0, grad, 1, back_own), (branch, act0, act, 0, branch_own))
    ):
        for copy in late[i]:
            copy.wait()
        ref[...] = dot(near[...], vnear[i], 1, turn) + dot(src[...], vw[i], 1, turn)
        vsend[i * rows : (i + 1) * rows, :] = ref[rows:, :].astype(BF)
        outs.append(flush(ref.at[0:rows], own))
        outs.append(flush(vsend.at[i * rows : (i + 1) * rows], send.at[i * rows : (i + 1) * rows]))
    for copy in outs:
        copy.wait()


def away_grads(
    meta, n2_own, n2_sib, cot_tok, cot_lat, act_in, grad_in, p0, p1, p2, p3,
    vn2, vcot, act, grad, vpack, in_sems, out_sems,
):
    width, hidden = vn2.shape[1], act.shape[1]
    fetch, flush = mover(in_sems), mover(out_sems)
    copies = [fetch(grad_in, grad)] + two_halves(meta, fetch, n2_own, n2_sib, cot_tok, cot_lat, vn2, vcot)
    last = fetch(act_in, act)
    for copy in copies:
        copy.wait()
    vpack[0:width, :] = dot(vn2[...], grad[...], 0, 0).astype(BF)
    last.wait()
    vpack[width : width + hidden, :] = dot(act[...], vcot[...], 0, 0).astype(BF)
    for copy in send_parts(meta, flush, vpack, (p0, p1, p2, p3)):
        copy.wait()


def middle_rows(meta, count, params, residual, branch, back, got, cot_tok, cot_lat, out_rows, grad_res, grad_attn, stats):
    n, m = cot_tok.shape[0], cot_lat.shape[0]
    rows_own = n + m
    stats[...] = jnp.zeros_like(stats)
    for at, size, cot in ((0, n, cot_tok), (n, m, cot_lat)):
        rows = slice(at, at + size)
        bk = back[rows, :] + got[rows, :].astype(F32)
        br = branch[rows, :] + got[rows_own + at : rows_own + at + size, :].astype(F32) + param(params, B_DOWN)
        res = residual[rows, :]
        out = res + br
        out_rows[rows, :] = out.astype(BF)
        if at == 0:
            real = valid_rows(meta, count, n)
            stats[0:1, :] = jnp.sum(jnp.where(real, out * out, 0.0), 0, keepdims=True)
            stats[1:2, :] = jnp.sum(jnp.where(real, br * br, 0.0), 0, keepdims=True)
        unit, inverse = norm_parts(res)
        stats[2:3, :] += jnp.sum(bk * unit, 0, keepdims=True)
        stats[3:4, :] += jnp.sum(bk, 0, keepdims=True)
        cot32 = cot[...].astype(F32)
        gr = cot32 + norm_back(bk, unit, inverse, param(params, GAIN2))
        grad_res[rows, :] = gr
        ga = gr.astype(BF)
        grad_attn[rows, :] = ga
        stats[4:5, :] += jnp.sum(ga.astype(F32), 0, keepdims=True)
        stats[5:6, :] += jnp.sum(cot32, 0, keepdims=True)


def back_out(meta, ga_own, ga_sib, o0, o2, t_near, t_far, l_near, l_far, g0, g2, d0, w0, sent):
    wide, n = t_near.shape[0], t_near.shape[1] // 2
    m = l_near.shape[0] // 2
    sent[wide:, :] = jnp.zeros_like(sent[wide:, :])
    for o, g, d, at in ((o2, g2, sent, wide), (o0, g0, d0, 0)):
        for i, ga in enumerate((ga_own, ga_sib)):
            g[:, i * n : (i + 1) * n] = dot(o[0:wide, :], ga[0:n, :], 1, 1).astype(BF)
            rows = dot(ga[n : n + m, :], o[0:wide, :], 1, 1).astype(BF)
            d[at + i * m : at + (i + 1) * m, 0:wide] = rows
    for t, l, w in ((t_far, l_far, sent.at[0:wide]), (t_near, l_near, w0)):
        total = jnp.zeros(w0.shape, F32)
        for i, ga in enumerate((ga_own, ga_sib)):
            total += dot(t[:, i * n : (i + 1) * n], ga[0:n, :], 1, 0)
            total += dot(l[i * m : (i + 1) * m, :], ga[n : n + m, :], 0, 0)
        w[...] = total.astype(BF)


def near_slot(
    slot, meta, count, normed, q, k, v, ql, kl, vl, log, far, logs_far, d_in, d_lat_in, w, grad_w, bias,
    dq_far, dk_near, dv_near,
):
    wide = q.shape[1]
    heads = wide // HEAD
    rows = normed[...]
    slot_rows = rows.shape[0]
    d_lat = d_lat_in[:, 0 : q.shape[1]].astype(F32)
    eighth = jnp.asarray(0.125, BF)
    q_all, k_all, v_all = q[...] * eighth, k[...], v[...]
    far32 = far[...].astype(F32)
    far_log = logs_far[...].astype(F32)
    dqs, dks, dvs = [], [], []
    for i in range(slot_rows // GROUP):
        at, lat_at = slice(i * GROUP, (i + 1) * GROUP), slice(i * LAT, (i + 1) * LAT)
        number = group_at(meta, count, slot, i)
        d_cols = d_in[:, at]
        d_tok, qs, ks, vs = d_cols.T, q_all[at], k_all[at], v_all[at]
        keys, values = key_stack(ks, kl[lat_at, :]), key_stack(vs, vl[lat_at, :])
        keys_t = keys.T
        mask = near_mask(number, GROUP)
        ps, gs, dq_t, d_heads, q_heads = [], [], [], [], []
        for h in range(heads):
            s = dot(head_lanes(keys, h), qs, 1, 1)
            p = jnp.where(mask, jnp.exp(s - log[i, h : h + 1, :]), 0.0)
            gp = p * dot(head_lanes(values, h), d_cols, 1, 0)
            g = (gp - p * jnp.sum(gp, 0, keepdims=True)).astype(BF)
            dq_t.append(dot(keys_t[h * HEAD : (h + 1) * HEAD], g, 1, 0))
            ps.append(p.astype(BF))
            gs.append(g)
            d_heads.append(head_lanes(d_tok, h))
            q_heads.append(head_lanes(qs, h))
        dv = dot(jnp.concatenate(ps, 1), jnp.concatenate(d_heads, 0), 1, 0)
        dk = dot(jnp.concatenate(gs, 1), jnp.concatenate(q_heads, 0), 1, 0)
        dqs.append((jnp.concatenate(dq_t, 0).T * 0.125).astype(BF))
        pad = jnp.zeros((LAT, wide), F32)
        q8, o8, d8, lg = ql[lat_at, :] * 0.125, far32[lat_at], d_lat[lat_at], far_log[lat_at]
        q_rows, do_rows, log_col, del_col = [], [], [], []
        big = jnp.full((LAT, 1), 1e30, F32)
        zero = jnp.zeros((LAT, 1), F32)
        for h in range(heads):
            q_rows += [head_lanes(q8, h), pad]
            dh = head_lanes(d8, h)
            do_rows += [dh, pad]
            col = lg[:, h : h + 1] + lg[:, heads + h : heads + h + 1] + lg[:, 2 * heads + h : 2 * heads + h + 1]
            log_col += [col, big]
            del_col += [jnp.sum(dh * o8, 1, keepdims=True), zero]
        q_f, d_f = jnp.concatenate(q_rows, 0).astype(BF), jnp.concatenate(do_rows, 0).astype(BF)
        l_f, x_f = jnp.concatenate(log_col, 0), jnp.concatenate(del_col, 0)
        lane = lax.broadcasted_iota(jnp.int32, (2 * LAT * heads, GROUP), 1)
        p_f = jnp.where(lane < number, jnp.exp(dot(q_f, ks, 1, 1) - l_f), 0.0)
        g_f = (p_f * (dot(d_f, vs, 1, 1) - x_f)).astype(BF)
        dks.append((dk[0:GROUP] + dot(g_f, q_f, 0, 0)).astype(BF))
        dvs.append((dv[0:GROUP] + dot(p_f.astype(BF), d_f, 0, 0)).astype(BF))
        dk_near[lat_at, :] = dk[GROUP : GROUP + LAT]
        dv_near[lat_at, :] = dv[GROUP : GROUP + LAT]
        dq_all = dot(g_f, ks, 1, 0)
        dq_lat = jnp.zeros((LAT, wide), F32)
        for h in range(heads):
            dq_lat += head_lanes(dq_all[2 * LAT * h : 2 * LAT * h + LAT], h)
        dq_far[lat_at, :] = dq_lat

    dq, dk, dv = (jnp.concatenate(v, 0) for v in (dqs, dks, dvs))
    total = dot(dq, w[0], 1, 0) + dot(dk, w[1], 1, 0) + dot(dv, w[2], 1, 0)
    for i, g in enumerate((dq, dk, dv)):
        grad_w[i] += dot(g, rows, 0, 0)
    bias[0:1, :] += jnp.sum(dq.astype(F32), 0, keepdims=True)
    bias[1:2, :] += jnp.sum(dv.astype(F32), 0, keepdims=True)
    bias[2:3, :] += jnp.sum(dk.astype(F32), 0, keepdims=True)
    return total.astype(BF)


def backward_rows(
    first, begin, meta, count, normed, q, k, v, ql, kl, vl, log, far, logs_far, d_in, d_lat, w, gw_in, bias_in, *outs,
):
    step = pl.program_id(0)
    parts, (grad_w, bias, dq_far, dk_near, dv_near) = outs[:-5], outs[-5:]

    @pl.when(step == 0)
    def _():
        grad_w[...] = jnp.zeros_like(grad_w) if begin else gw_in[...]
        bias[...] = jnp.zeros_like(bias) if begin else bias_in[...]

    total = near_slot(
        step + first, meta, count, normed, q, k, v, ql, kl, vl, log, far, logs_far, d_in, d_lat, w, grad_w, bias,
        dq_far, dk_near, dv_near,
    )
    for slot, ref in enumerate(parts):

        @pl.when(step == slot)
        def _(ref=ref):
            ref[...] = total


def latent_bundle(meta, d_near, d_far, far, logs_far, own, sent):
    count, wide = far.shape
    heads = wide // HEAD
    n = count // 4
    d32 = jnp.concatenate([d_near[...], d_far[:, 0:wide]], 0).astype(F32)
    prod = d32 * far[...].astype(F32)
    lg = logs_far[...].astype(F32)
    deltas = [split3(jnp.sum(head_lanes(prod, h), 1, keepdims=True)) for h in range(heads)]
    cols = [lg[:, i : i + 1] for i in range(3 * heads)] + [p[i].astype(F32) for i in (0, 1) for p in deltas]
    lane = lax.broadcasted_iota(jnp.int32, (count, 4 * HEAD), 1)
    value = jnp.concatenate([d32, jnp.zeros((count, HEAD), F32)], 1)
    for i, c in enumerate(cols):
        value = jnp.where(lane == wide + i, c, value)
    value = value.astype(BF)
    own[...] = value
    for i, s in enumerate(SENT):
        sent[i * n : (i + 1) * n, :] = value[s * n : (s + 1) * n]


def backward_far(
    meta, tokens_real, image, qa, ka, va, ql, kl, vl, own, bundle, normed, w, gw, bias_in, wo_a, wo_b,
    params, stats1, stats2, hid_first, hid_near, hid_away, *refs,
):
    near, (lat_keep, lat_send, p0, p1, p2, p3, small, pack, out_sems) = refs[:-9], refs[-9:]
    count, wide = ql.shape
    heads = wide // HEAD
    groups = count // LAT
    q_all, k_all, v_all = qa[...] * jnp.asarray(0.125, BF), ka[...], va[...]
    q_own, k_own, v_own = (ql[...] * 0.125).astype(BF), kl[...].astype(BF), vl[...].astype(BF)
    d_own, d_all = own[:, 0:wide], bundle[:, 0:wide]

    def stats(ref, h):
        x = ref[...].astype(F32)
        col = [x[:, wide + i : wide + i + 1] for i in range(5 * heads)]
        return col[h] + col[heads + h] + col[2 * heads + h], col[3 * heads + h] + col[4 * heads + h]

    mine = image_list(meta, image, 1, groups, OWN)
    images = image_list(meta, image, qa.shape[0] // count, groups, SENT)
    mask_q = image_column(mine) == image_row(images)
    mask_k = image_column(images) == image_row(mine)
    each = len(near) // 3
    dq, dk, dv = (jnp.concatenate([ref[...] for ref in near[i * each : (i + 1) * each]], 0) for i in range(3))
    for h in range(heads):
        log, delta = stats(own, h)
        s = dot(head_lanes(q_own, h), k_all, 1, 1)
        p = jnp.where(mask_q, jnp.exp(s - log), 0.0)
        g = (p * (dot(head_lanes(d_own, h), v_all, 1, 1) - delta)).astype(BF)
        dq += head_lanes(dot(g, k_all, 1, 0), h)
        log, delta = stats(bundle, h)
        s = dot(q_all, head_lanes(k_own, h), 1, 1)
        p = jnp.where(mask_k, jnp.exp(s - log), 0.0)
        g = (p * (dot(d_all, head_lanes(v_own, h), 1, 1) - delta)).astype(BF)
        dk += head_lanes(dot(g, q_all, 0, 0), h)
        dv += head_lanes(dot(p.astype(BF), d_all, 0, 0), h)
    dq, dk, dv = (dq * 0.125).astype(BF), dk.astype(BF), dv.astype(BF)
    lat_rows = normed[...]
    sums = [bias_in[i : i + 1, :] for i in (0, 2, 1)]
    sums = [b + jnp.sum(g.astype(F32), 0, keepdims=True) for b, g in zip(sums, (dq, dk, dv))]
    columns = jnp.concatenate(sums + [jnp.zeros((5, wide), F32)], 0).T
    first_gain = jnp.zeros((1, pack.shape[1]), F32)
    first_shift = first_gain
    for i, g in enumerate((dq, dk, dv)):
        total = gw[i] + dot(g, lat_rows, 0, 0)
        pack[i * wide : (i + 1) * wide, :] = total.astype(BF)
        col, weight = columns[:, i : i + 1], w[i].astype(F32)
        first_shift += jnp.sum(weight * col, 0, keepdims=True)
        first_gain += jnp.sum(weight * (total - col * param(params, SHIFT1)), 0, keepdims=True)
    first_gain = first_gain / param(params, GAIN1)
    pack[3 * wide :, :] = (wo_a[...].astype(F32) + wo_b[...].astype(F32)).astype(BF)
    x, z = sides(meta)
    flush = mover(out_sems)
    copies = []
    for ref, (dx, dz) in zip((p0, p1, p2, p3), ((0, 0), (1, 0), (0, 1), (1, 1))):
        part = (x ^ dx) * 2 + (z ^ dz)
        at = 0
        for base, size in ((0, 3 * wide // 4), (3 * wide, wide // 4)):
            src = pack.at[pl.ds(pl.multiple_of(base + part * size, 16), size)]
            copies.append(flush(src, ref.at[at : at + size]))
            at += size
    rows = (dot(dq, w[0], 1, 0) + dot(dk, w[1], 1, 0) + dot(dv, w[2], 1, 0)).astype(BF)
    n = count // 4
    lat_keep[0:n, :], lat_keep[n : 2 * n, :] = rows[0:n], rows[2 * n : 3 * n]
    lat_send[0:n, :], lat_send[n : 2 * n, :] = rows[n : 2 * n], rows[3 * n :]
    small[...] = jnp.zeros_like(small)
    small[0:1, :] = stats1[0:1, :]
    small[1:7, :] = stats2[0:6, :]
    small[7:8, :], small[8:9, :] = first_gain, first_shift
    real = tokens_real[0]
    for i in range(1, tokens_real.shape[0]):
        real = real + tokens_real[i]
    for at, part in ((9, real - real % 64), (22, real % 64)):
        small[at : at + 1, :] = jnp.full((1, small.shape[1]), 0.25, F32) * part.astype(F32)
    for s, row in ((0, hid_first[0:1, :] + hid_near[0:1, :]), (2, hid_away[0:1, :])):
        small[pl.ds(10 + (meta[1] ^ s), 1), :] = row
    small[pl.ds(14 + meta[1], 1), 0:wide] = sums[0]
    small[pl.ds(18 + meta[1], 1), 0:wide] = sums[2]
    for copy in copies:
        copy.wait()


def final_rows(meta, tok, lat, a, b, c, la, lb, grad_res, params, out):
    n, m = tok.shape[0], lat.shape[0]
    for x, at, terms in ((tok, slice(0, n), (a, b)), (lat, slice(n, n + m), (la, lb))):
        grad = c[at, :].astype(F32)
        for term in terms:
            grad += term[0 : x.shape[0], :].astype(F32)
        unit, inverse = norm_parts(x[...].astype(F32))
        out[at, :] = (grad_res[at, :] + norm_back(grad, unit, inverse, param(params, GAIN1))).astype(BF)


def place_rows(meta, a, b, c, d, tok_out, lat_out):
    n = tok_out.shape[0]
    for i, ref in enumerate((a, b, c, d)):

        @pl.when(pl.program_id(0) == i)
        def _(ref=ref):
            tok_out[...] = ref[0:n, :]
            lat_out[...] = ref[n:, :]


def projections_out(meta, f0, f1, f2, f3, grad_w, grad_o, gain1, shift1, b_out, gain2, shift2, b_down, b_up, b_qv, roots):
    x, z = sides(meta)
    wide = grad_o.shape[0]
    four = (f0, f1, f2, f3)
    for ref, (dx, dz) in zip(four, ((0, 0), (1, 0), (0, 1), (1, 1))):
        part = (x ^ dx) * 2 + (z ^ dz)
        at = 0
        for dst, size in ((grad_w, 3 * wide // 4), (grad_o, wide // 4)):
            dst[pl.ds(pl.multiple_of(part * size, 16), size), :] = ref[at : at + size, :].astype(F32)
            at += size
    small = four[0][wide : wide + 32, :].astype(F32)
    for ref in four[1:]:
        small += ref[wide : wide + 32, :].astype(F32)
    for ref, row in ((gain1, 7), (shift1, 8), (b_out, 5), (gain2, 3), (shift2, 4), (b_down, 6)):
        ref[...] = small[row, :]

    def of_mp(first):
        value = small[first : first + 1]
        for m in (1, 2, 3):
            value = jnp.where(meta[1] == m, small[first + m : first + m + 1], value)
        return value

    b_up[...] = of_mp(10)[0]
    b_qv[...] = jnp.concatenate([of_mp(14)[:, 0:wide], of_mp(18)[:, 0:wide]], 0)
    real = (small[9:10, 0:1] + small[22:23, 0:1]) * small.shape[1]
    lane = lax.broadcasted_iota(jnp.int32, roots.shape, 1)
    value = jnp.zeros(roots.shape, F32)
    for i, row in enumerate((1, 0, 2)):
        root = jnp.sqrt(jnp.sum(small[row : row + 1], 1, keepdims=True) / real)
        value = jnp.where(lane == i, root, value)
    roots[...] = value


def make(mesh):
    dp_size, mp_size = mesh.shape["dp"], mesh.shape["mp"]
    assert mp_size == 4 and dp_size >= 4
    dp_bits = [1 << i for i in range(dp_size.bit_length() - 1)]
    assert 1 << len(dp_bits) == dp_size
    x_bit, z_bit, rest_bits = dp_bits[0], dp_bits[1], dp_bits[2:]

    def swap(v, dp_bit, mp_bit):
        pairs = [
            (d * mp_size + m, (d ^ dp_bit) * mp_size + (m ^ mp_bit))
            for d in range(dp_size)
            for m in range(mp_size)
        ]
        return lax.ppermute(v, ("dp", "mp"), pairs)

    def per_device(
        tokens,
        latents,
        image_of_group,
        token_valid,
        norm1_gain,
        norm1_shift,
        w_qkv,
        b_qv,
        w_out,
        b_out,
        norm2_gain,
        norm2_shift,
        w_up,
        b_up,
        w_down,
        b_down,
        cot_tokens,
        cot_latents,
    ):
        dp_at, mp_at = lax.axis_index("dp"), lax.axis_index("mp")
        tok_count, width = tokens.shape
        lat_count = latents.shape[0]
        groups = lat_count // LAT
        wide = w_qkv.shape[2]
        hidden = w_up.shape[1]
        tok_own, lat_own = tok_count // 4, lat_count // 4
        rows_own = tok_own + lat_own
        all_lat = dp_size * lat_count
        meta = jnp.stack([dp_at, mp_at]).astype(jnp.int32)
        count = jnp.sum(token_valid.reshape(groups, GROUP), 1).astype(jnp.int32)
        par = whole((8, width))
        w_t = jnp.transpose(w_qkv, (0, 2, 1))
        w_all = (3, wide, width)
        quarter, small = width // 4, wide // 4
        half = 2 * quarter
        big = (rows_own, width)
        chip_rows, chip_tok, chip_lat = 2 * rows_own, 2 * tok_own, 2 * lat_own
        vec = pl.BlockSpec((width,), lambda *_: (0,))

        def out(shape, kind=BF):
            return (shape, kind, whole(shape))

        def kept_out(shape, kind=BF):
            return (shape, kind, kept(shape))

        vm = pltpu.VMEM

        def any_out(shape, kind=BF):
            return (shape, kind, ANY)

        def dma(n):
            return pltpu.SemaphoreType.DMA((n,))

        def cube(v, vx=None, vz=None, vxz=None):
            vx, vz, vxz = (v if w is None else w for w in (vx, vz, vxz))
            return swap(vx, x_bit, 0), swap(vz, z_bit, 0), swap(vxz, x_bit | z_bit, 0)

        def all_latents(v):
            v = jnp.concatenate((v,) + cube(v), 0)
            for bit in rest_bits:
                v = jnp.concatenate([v, swap(v, bit, 0)], 0)
            return v

        part_block = pl.BlockSpec((quarter, width), lambda i, meta: ((meta[0] & 1) * 2 + ((meta[0] >> 1) & 1), 0))
        lat_rel, lat_half, o0, weight_part, params = call(
            prepare,
            name="prepare",
            room=62,
            scalars=1,
            ins=[pl.BlockSpec(memory_space=pltpu.HBM)] * 11,
            outs=[out((lat_count, width)), out((chip_lat, width)), out((wide + 16, width)), out((half, width)), out((8, width), F32)],
            scratch=[vm((lat_count, width), BF), vm((wide, width), BF), dma(11)] + [vm((width,), F32)] * 7,
            us=2,
        )(meta, latents, w_out, norm1_gain, norm1_shift, b_out, norm2_gain, norm2_shift, b_down, b_up, w_up, w_down)
        lat_four = jnp.concatenate((lat_half,) + cube(lat_half), 0)
        w_own = swap(weight_part, 0, 2)
        o2 = swap(o0, 0, 2)

        normed_lat, ql, kl, vl = call(
            latent_rows,
            name="latent_rows",
            room=3,
            scalars=0,
            ins=[whole((lat_count, width)), par, whole(w_all), whole((2, wide))],
            outs=[out((lat_count, width))] + [out((lat_count, wide), F32)] * 3,
            us=2,
        )(lat_rel, params, w_t, b_qv)

        def cot_through(slot, meta):
            return call(
                cot_back,
                name="cot_back",
            room=4,
                scalars=1,
                ins=[
                    pl.BlockSpec((tok_own, width), lambda i, meta: (meta[1] ^ slot, 0), pipeline_mode=pl.Buffered(1)),
                    pl.BlockSpec((lat_own, width), lambda i, meta: (meta[1] ^ slot, 0), pipeline_mode=pl.Buffered(1)),
                    whole((hidden, width)),
                ],
                outs=[out((rows_own, hidden))],
                us=4,
            )(meta, cot_tokens, cot_latents, w_down)[0]

        cot_own = cot_through(0, after(meta, kl))
        lat_here = lat_four = after(lat_four, cot_own)
        for bit in rest_bits:
            lat_here = jnp.concatenate([lat_here, swap(lat_here, bit, 0)], 0)

        def near_forward(base, *deps):
            def run(*args):
                return forward_near(base, *args)

            rows = lambda wide_here: pl.BlockSpec((tok_own, wide_here), lambda i, *_: (i, 0))
            lat_block = pl.BlockSpec((lat_own, wide), lambda i, *_: (i + base, 0))
            each = groups // 4
            return call(
                run,
                name="forward_near",
            room=46,
                grid=(2,),
                scalars=2,
                ins=[
                    pl.BlockSpec((tok_own, width), lambda i, meta, _: (meta[1] ^ (i + base), 0)),
                    lat_block,
                    lat_block,
                    par,
                    whole(w_all),
                    whole((2, wide)),
                ],
                outs=[((chip_tok, width), BF, rows(width))]
                + [((chip_tok, wide), BF, rows(wide))] * 3
                + [((wide, chip_tok), BF, pl.BlockSpec((wide, tok_own), lambda i, *_: (0, i)))]
                + [((2 * each, 8, GROUP), F32, pl.BlockSpec((each, 8, GROUP), lambda i, *_: (i, 0, 0)))],
                us=8,
            )(meta, count, tokens, after(kl, *deps), vl, params, w_t, b_qv)

        normed_b, q_b, k_b, v_b, t_b, log_b = near_forward(2, lat_four)
        t_far = swap(t_b, 0, 2)
        lat_here = after(lat_here, t_b)
        normed_a, q_a, k_a, v_a, t_near, log_a = near_forward(0, lat_here)
        w_x, w_z, w_xz = cube(after(w_own, t_near))
        lat_all = [v.reshape(dp_size, chip_lat, width) for v in (lat_here, swap(lat_here, 0, 1))]
        lat_all = jnp.concatenate(lat_all, 1).reshape(all_lat, width)
        lat_all = after(lat_all, t_near)

        chunk = min(512, all_lat)
        qa, ka, va, l_near, l_b, far, far_logs = call(
            forward_far,
            name="forward_far",
            room=6,
            grid=(all_lat // chunk,),
            scalars=3,
            ins=[pl.BlockSpec((chunk, width), lambda i, *_: (i, 0)), par, whole(w_all), whole((2, wide))]
            + [whole((chip_tok, wide))] * 4
            + [whole((lat_count, wide))],
            outs=[out((all_lat, wide))] * 3
            + [kept_out((chip_lat, wide))] * 2
            + [kept_out((lat_count, wide)), kept_out((lat_count, 2 * HEAD))],
            us=6,
        )(meta, count, image_of_group, lat_all, params, w_t, b_qv, k_a, k_b, v_a, v_b, ql)
        l_far = swap(l_b, 0, 2)

        out_pack = whole((wide + 16, width))
        mixed_specs = [whole((wide, chip_tok))] * 2 + [whole((chip_lat, wide))] * 2
        cot_sib = cot_through(1, after(meta, far))

        def out_rows_of(slot, kind, o0):
            return call(
                project_out,
                name="project_out",
            room=4,
                scalars=0,
                ins=[pl.BlockSpec((wide, tok_own), lambda *_: (0, slot), pipeline_mode=pl.Buffered(1))] * 2
                + [pl.BlockSpec((lat_own, wide), lambda *_: (slot, 0), pipeline_mode=pl.Buffered(1))] * 2
                + [out_pack] * 2,
                outs=[out(big, kind)],
                us=3,
            )(t_near, t_far, l_near, l_far, o0, o2)[0]

        attn_send = out_rows_of(1, BF, after(o0, cot_sib))
        attn_own = out_rows_of(0, F32, after(o0, attn_send))
        attn_got = swap(attn_send, 0, 1)
        own_tok = pl.BlockSpec((tok_own, width), lambda i, meta, _: (meta[1], 0), pipeline_mode=pl.Buffered(1))
        own_lat = pl.BlockSpec((lat_own, width), lambda i, meta, _: (meta[1], 0), pipeline_mode=pl.Buffered(1))
        residual, n2, stats1 = call(
            add_norm,
            name="add_norm",
            room=6,
            scalars=2,
            ins=[par, whole(big), whole(big), own_tok, whole((lat_own, width))],
            outs=[out(big, F32), out(big), out((8, width), F32)],
            us=3,
        )(meta, count, params, attn_own, attn_got, tokens, lat_rel)
        n2_sib = swap(n2, 0, 1)

        chip = (chip_rows, width)
        piece = (half, width)
        act_first, grad_first, bias_first = call(
            hidden_first,
            name="hidden_first",
            room=6,
            scalars=0,
            ins=[par, whole(big), whole((width, hidden)), whole((rows_own, hidden))],
            outs=[out((rows_own, hidden))] * 2 + [out((8, hidden), F32)],
            us=4,
        )(params, n2, w_up, cot_own)
        act_near, grad_near, a0, a1, a2, a3, bias_near = call(
            hidden_own,
            name="hidden_own",
            room=7,
            scalars=1,
            ins=[par] + [ANY] * 8,
            outs=[any_out((chip_rows, hidden))] * 2 + [any_out(piece)] * 4 + [out((8, hidden), F32)],
            scratch=[
                vm(chip, BF),
                vm(chip, BF),
                vm((width, hidden), BF),
                vm((chip_rows, hidden), BF),
                vm((chip_rows, hidden), BF),
                vm((rows_own, hidden), BF),
                vm((width + hidden, width), BF),
                dma(10),
                dma(10),
            ],
            us=9,
        )(meta, params, n2, n2_sib, cot_tokens, cot_latents, w_up, cot_sib, act_first, grad_first)
        near_parts = (a0,) + cube(None, a1, a2, a3)

        branch, back, middle_send, act, grad, bias_away = call(
            hidden_away,
            name="hidden_away",
            room=8,
            scalars=1,
            ins=[out_pack] + [ANY] * 12,
            outs=[any_out(big, F32), any_out(big, F32), any_out(chip), any_out((chip_rows, hidden)), any_out((chip_rows, hidden))]
            + [out((8, hidden), F32)],
            scratch=[
                vm(chip, BF),
                vm(chip, BF),
                vm((2, width, hidden), BF),
                vm((2, width, hidden), BF),
                vm((chip_rows, hidden), BF),
                vm((chip_rows, hidden), BF),
                vm(chip, F32),
                vm(chip, F32),
                vm((chip_rows, hidden), BF),
                vm((chip_rows, hidden), BF),
                vm(chip, BF),
                dma(18),
                dma(6),
            ],
            us=10,
        )(meta, o2, n2, n2_sib, cot_tokens, cot_latents, w_own, w_x, w_z, w_xz, act_near, grad_near, w_up, w_down)
        middle_got = swap(middle_send, 0, 1)

        b0, b1, b2, b3 = call(
            away_grads,
            name="away_grads",
            room=7,
            scalars=1,
            ins=[ANY] * 6,
            outs=[any_out(piece)] * 4,
            scratch=[
                vm(chip, BF),
                vm(chip, BF),
                vm((chip_rows, hidden), BF),
                vm((chip_rows, hidden), BF),
                vm((width + hidden, width), BF),
                dma(8),
                dma(8),
            ],
            us=6,
        )(meta, n2, n2_sib, cot_tokens, cot_latents, act, grad)

        out_rows, grad_res, grad_attn, stats2 = call(
            middle_rows,
            name="middle_rows",
            room=8,
            scalars=2,
            ins=[par, whole(big), whole(big), whole(big), whole(chip), own_tok, own_lat],
            outs=[out(big), out(big, F32), out(big), out((8, width), F32)],
            us=5,
            deps=(b0,),
        )(meta, count, params, residual, branch, back, middle_got, cot_tokens, cot_latents)
        grad_attn_sib = swap(grad_attn, 0, 1)

        def terms(n, at=0):
            return [(i, at) for i in range(n)]

        sides4 = ((0, 0), (1, 0), (0, 1), (1, 1))

        def at(d, size, base=0):
            return lambda x, z: base + ((x ^ d[0]) * 2 + (z ^ d[1])) * size


        (near_sum,) = combine("near_sum", meta, near_parts, [(half, BF, [(0, half, terms(4))])], us=2)
        away_parts = (b0,) + cube(None, *(after(v, near_parts[1], near_parts[2]) for v in (b1, b2, b3)))

        g_near, g_send, d_near, out_grad, out_send = call(
            back_out,
            name="back_out",
            room=6,
            scalars=1,
            ins=[whole(big), whole(big), out_pack, out_pack] + mixed_specs,
            outs=[out((wide, chip_tok))] * 2 + [out((chip_lat, wide)), out((wide, width)), out((wide + chip_lat, width))],
            us=4,
            deps=(near_sum,),
        )(meta, grad_attn, grad_attn_sib, o0, o2, t_near, t_far, l_near, l_far)
        out_got = swap(out_send, 0, 2)
        g_far = swap(g_send, 0, 2)

        zero_w, zero_b = jnp.zeros((8, LANES), F32), jnp.zeros((8, LANES), F32)

        def rows_backward(first, steps, half_in, g, d, gw, bias, *deps):
            normed, q, k, v, log = half_in
            base = first % 2

            def rows(n, wide_here, shift):
                return pl.BlockSpec((n, wide_here), lambda i, *_: (i + shift, 0))

            def run(*args):
                return backward_rows(first, gw is None, *args)

            init = (zero_w, zero_b) if gw is None else (gw, bias)
            return call(
                run,
                name="backward_rows",
            room=8,
                grid=(steps,),
                scalars=2,
                ins=[
                    rows(tok_own, width, base),
                    *[rows(tok_own, wide, base)] * 3,
                    *[rows(lat_own, wide, first)] * 3,
                    pl.BlockSpec((groups // 4, 8, GROUP), lambda i, *_: (i + base, 0, 0)),
                    rows(lat_own, wide, first),
                    rows(lat_own, 2 * HEAD, first),
                    pl.BlockSpec((wide, tok_own), lambda i, *_: (0, i + base)),
                    rows(lat_own, d.shape[1], base + (wide // lat_own if d.shape[1] != wide else 0)),
                    whole(w_all),
                    whole(init[0].shape),
                    whole(init[1].shape),
                ],
                outs=[kept_out((tok_own, width))] * steps
                + [kept_out(w_all, F32), kept_out((8, wide), F32)]
                + [((steps * lat_own, wide), F32, rows(lat_own, wide, 0))] * 3,
                us=7 * steps,
                deps=deps,
            )(meta, count, normed, q, k, v, ql, kl, vl, log, far, far_logs, g, d, w_t, *init)

        half_a, half_b = (normed_a, q_a, k_a, v_a, log_a), (normed_b, q_b, k_b, v_b, log_b)
        part0, gw, bias, *near_0 = rows_backward(0, 1, half_a, g_near, d_near, None, None)
        bundle_own, bundle = call(
            latent_bundle,
            name="latent_bundle",
            scalars=1,
            ins=[whole((chip_lat, wide)), pl.BlockSpec((chip_lat, width), lambda *_: (wide // chip_lat, 0))]
            + [whole((lat_count, wide)), whole((lat_count, 2 * HEAD))],
            outs=[out((lat_count, 4 * HEAD))] * 2,
            us=2,
            deps=(part0,),
        )(meta, d_near, out_got, far, far_logs)
        steps = [bundle]

        def spread(bit):
            got = swap(steps[0], bit, 0)
            return lambda done: steps.__setitem__(0, jnp.concatenate([after(steps[0], done), got], 0))

        join = spread(x_bit)
        part1, gw, bias, *near_1 = rows_backward(1, 1, half_a, g_near, d_near, gw, bias, bundle_own)
        join(part1)
        join = spread(z_bit)
        (away_sum,) = combine("away_sum", meta, away_parts, [(half, BF, [(0, half, terms(4))])], us=2, deps=(part1,))
        away_got = swap(away_sum, 0, 2)
        part3, gw, bias, *near_3 = rows_backward(3, 1, half_b, g_far, out_got, gw, bias, away_sum, steps[0])
        join(part3)
        for bit in rest_bits[:-1]:
            spread(bit)(part3)
        join = spread(rest_bits[-1]) if rest_bits else None
        got3 = swap(part3, 0, 1)
        got1 = swap(after(part1, part3), 0, 1)
        part2, gw, bias, *near_2 = rows_backward(2, 1, half_b, g_far, out_got, gw, bias)
        if rest_bits:
            join(part2)
        bundle = steps[0]
        (total,) = combine(
            "weights_sum", meta, [near_sum, away_got], [(half, BF, [(0, half, terms(2))])], us=20, deps=(part2,)
        )
        near_all = [v for three in zip(near_0, near_1, near_2, near_3) for v in three]
        shard = (small * 4, width)
        lat_keep, lat_send, c0, c1, c2, c3, small_rows = call(
            backward_far,
            name="backward_far",
            room=6,
            scalars=3,
            ins=[whole((all_lat, wide))] * 3
            + [whole((lat_count, wide))] * 3
            + [whole((lat_count, 4 * HEAD)), whole((all_lat, 4 * HEAD)), whole((lat_count, width)), whole(w_all), whole(w_all)]
            + [whole((8, wide))]
            + [whole((wide, width)), pl.BlockSpec((wide, width), lambda *_: (0, 0), pipeline_mode=pl.Buffered(1))]
            + [par]
            + [whole((8, width))] * 5
            + [whole(v.shape) for v in near_all],
            outs=[out((chip_lat, width))] * 2 + [any_out(shard)] * 4 + [out((32, width), F32)],
            scratch=[vm((4 * wide, width), BF), dma(8)],
            us=8,
            deps=(total, got1, got3),
        )(
            meta, count, image_of_group, qa, ka, va, ql, kl, vl, bundle_own, bundle, normed_lat, w_t, gw, bias, out_grad,
            out_got, params, stats1, stats2, bias_first, bias_near, bias_away, *near_all,
        )

        lat_got = swap(lat_send, 0, 1)
        (there,) = combine(
            "rows_sum", meta, [part2, got3, lat_keep, lat_got],
            [(rows_own, BF, [(0, tok_own, terms(2)), (tok_own, lat_own, [(2, lat_own), (3, lat_own)])])],
            us=2, deps=(total,),
        )
        from_y = swap(there, 0, 2)
        small_rows = small_rows + swap(small_rows, 0, 1)
        small_got = swap(small_rows, 0, 2)
        rows4 = 4 * small
        qkv_parts = (c0,) + cube(None, *(after(v, total) for v in (c1, c2, c3)))
        (qkv,) = combine(
            "qkv_sum", meta, qkv_parts + (small_rows, small_got),
            [(rows4 + 32, BF, [(0, rows4, terms(4)), (rows4, 32, [(4, 0), (5, 0)])])],
            us=2, deps=(there,),
        )
        (grad_rows,) = call(
            final_rows,
            name="final_rows",
            room=6,
            scalars=1,
            ins=[
                pl.BlockSpec((tok_own, width), lambda i, meta: (meta[1], 0), pipeline_mode=pl.Buffered(1)),
                whole((lat_own, width)),
                *[whole((tok_own, width))] * 2,
                whole(big),
                *[whole((chip_lat, width))] * 2,
                whole(big),
                par,
            ],
            outs=[out(big)],
            us=4,
            deps=(qkv,),
        )(meta, tokens, lat_rel, part0, got1, from_y, lat_keep, lat_got, grad_res, params)

        grad_y = swap(grad_rows, 0, 2)
        grad_c = swap(after(grad_rows, grad_y), 0, 1)
        out_y = swap(after(out_rows, qkv), 0, 2)
        for bit in rest_bits:
            (total,) = combine(
                "rest_sum", meta, [total, swap(total, bit, 0)], [(half, BF, [(0, half, terms(2))])], us=2,
                deps=(there,),
            )
        def all_rows(v, v_y, v_c):
            v_yc = swap(v_y, 0, 1)
            place = lambda n: pl.BlockSpec((n, width), lambda i, meta: (meta[1] ^ i, 0))
            return call(
                place_rows,
                name="place_rows",
                grid=(4,),
                scalars=1,
                ins=[whole(big)] * 4,
                outs=[((tok_count, width), BF, place(tok_own)), ((lat_count, width), BF, place(lat_own))],
                us=4,
            )(meta, v, v_c, v_y, v_yc)

        grad_tok, grad_lat = all_rows(grad_rows, grad_y, grad_c)
        out_tok, out_lat = all_rows(out_rows, out_y, swap(after(out_rows, out_y), 0, 1))
        four = (total,) + cube(total)
        grad_w_up, grad_w_down = combine(
            "weights_out", meta, four,
            [
                (4 * quarter, F32, [(at(d, quarter), quarter, [(i, r * quarter)]) for i, d in enumerate(sides4)])
                for r in (0, 1)
            ]
            ,
            us=5,
            deps=(qkv, out_y, grad_tok),
        )
        for bit in rest_bits:
            (qkv,) = combine("qkv_rest", meta, [qkv, swap(qkv, bit, 0)], [(rows4 + 32, BF, [(0, rows4 + 32, terms(2))])], us=2, deps=(total,))
        four = (qkv,) + tuple(
            swap(after(qkv, v), bit, 0) for v, bit in zip(four[1:], (x_bit, z_bit, x_bit | z_bit))
        )
        grad_w_qkv, grad_w_out, *vectors, grad_b_qv, roots = call(
            projections_out,
            name="qkv_out",
            scalars=1,
            ins=[whole((rows4 + 32, width))] * 4,
            outs=[out((3 * wide, width), F32), out((wide, width), F32)]
            + [((width,), F32, vec)] * 7
            + [out((2, wide), F32), out((8, LANES), F32)],
            us=3,
            deps=(out_tok, grad_w_up),
        )(meta, *four)
        grad_w_qkv = grad_w_qkv.reshape(3, wide, width).transpose(0, 2, 1)


        root_means = roots[0, :3]
        gain1, shift1, b_out_grad, gain2, shift2, b_down_grad, grad_b_up = vectors
        return (
            out_tok,
            out_lat,
            grad_tok,
            grad_lat,
            gain1,
            shift1,
            grad_w_qkv,
            grad_b_qv,
            grad_w_out,
            b_out_grad,
            gain2,
            shift2,
            grad_w_up,
            grad_b_up,
            grad_w_down,
            b_down_grad,
            root_means,
        )

    return per_device


def solution(mesh):
    rows, whole = P("dp", None), P()
    return jax.shard_map(
        make(mesh),
        mesh=mesh,
        in_specs=(
            rows,
            rows,
            whole,
            P("dp"),
            whole,
            whole,
            P(None, None, "mp"),
            P(None, "mp"),
            P("mp", None),
            whole,
            whole,
            whole,
            P(None, "mp"),
            P("mp"),
            P("mp", None),
            whole,
            rows,
            rows,
        ),
        out_specs=(
            rows,
            rows,
            rows,
            rows,
            whole,
            whole,
            P(None, None, "mp"),
            P(None, "mp"),
            P("mp", None),
            whole,
            whole,
            whole,
            P(None, "mp"),
            P("mp"),
            P("mp", None),
            whole,
            whole,
        ),
        check_vma=False,
    )
```

```python
import jax
import jax.numpy as jnp
from jax import lax
from jax.experimental import pallas as pl
from jax.experimental.pallas import tpu as pltpu
from jax.sharding import PartitionSpec as P

HEAD = 64
LANES = 128
GROUP = 256
LAT = 8
BF = jnp.bfloat16
F32 = jnp.float32
FAR = -1e30
MIB = 1 << 20
GAIN1, SHIFT1, B_OUT, GAIN2, SHIFT2, B_DOWN, B_UP = range(7)


def dot(a, b, ca, cb):
    return lax.dot_general(a, b, (((ca,), (cb,)), ((), ())), preferred_element_type=F32)


def norm_parts(values):
    center = values - jnp.mean(values, axis=-1, keepdims=True)
    spread = jnp.mean(center * center, axis=-1, keepdims=True)
    inverse = lax.rsqrt(spread + 1e-06)
    return center * inverse, inverse


def norm_back(grad, unit, inverse, gain):
    scaled = grad * gain
    inner = jnp.mean(scaled * unit, axis=-1, keepdims=True)
    return inverse * (scaled - jnp.mean(scaled, axis=-1, keepdims=True) - unit * inner)


def gelu_both(values):
    square = values * values
    inner = jnp.tanh(values * (0.7978845608028654 + 0.035677408136300125 * square))
    half = 0.5 + 0.5 * inner
    slope = values * (0.3989422804014327 + 0.05351611220494518 * square)
    return values * half, half + (1.0 - inner * inner) * slope


def split3(v):
    hi = v.astype(BF)
    mid = (v - hi.astype(F32)).astype(BF)
    low = (v - hi.astype(F32) - mid.astype(F32)).astype(BF)
    return hi, mid, low


def head_lanes(v, h):
    lane = lax.broadcasted_iota(jnp.int32, v.shape, v.ndim - 1)
    return jnp.where((lane >= h * HEAD) & (lane < (h + 1) * HEAD), v, jnp.zeros_like(v))


def kept(shape):
    return pl.BlockSpec(shape, lambda *_: (0,) * len(shape))


def whole(shape):
    return pl.BlockSpec(shape, lambda *_: (0,) * len(shape), pipeline_mode=pl.Buffered(1))


ANY = pl.BlockSpec(memory_space=pl.ANY)
OWN, SENT = (0, 1, 2, 3), (0, 2, 1, 3)


def block_bytes(shape, kind, copies):
    size = jnp.dtype(kind).itemsize
    dims = [1, 1] + list(shape)
    rows, lanes = 32 // size, LANES
    dims[-1] = -(-dims[-1] // lanes) * lanes
    dims[-2] = -(-dims[-2] // rows) * rows
    total = size * copies
    for d in dims:
        total *= d
    return total


def spec_bytes(spec, kind):
    if spec.block_shape is None:
        return 0
    return block_bytes(spec.block_shape, kind, 1 if spec.pipeline_mode is not None else 2)


def after(v, *deps):
    return lax.optimization_barrier((v,) + deps)[0]


def call(body, *, name, scalars, ins, outs, grid=(1,), scratch=(), deps=(), us=1.0, room=3):
    def run(*args):
        if deps:
            args = (after(args[0], *deps),) + args[1:]
        need = room * MIB + sum(spec_bytes(spec, kind) for _, kind, spec in outs)
        need += sum(spec_bytes(spec, a.dtype) for spec, a in zip(ins, args[scalars:]))
        need += sum(block_bytes(s.shape, s.dtype, 1) for s in scratch if s.shape and len(s.shape) > 1)
        return pl.pallas_call(
            body,
            name=name,
            out_shape=[jax.ShapeDtypeStruct(s, d) for s, d, _ in outs],
            grid_spec=pltpu.PrefetchScalarGridSpec(
                num_scalar_prefetch=scalars,
                grid=grid,
                in_specs=list(ins),
                out_specs=[spec for _, _, spec in outs],
                scratch_shapes=list(scratch),
            ),
            compiler_params=pltpu.CompilerParams(
                dimension_semantics=("arbitrary",) * len(grid), vmem_limit_bytes=need
            ),
            cost_estimate=pl.CostEstimate(
                flops=int(us * 1.0e10), bytes_accessed=1 << 16, transcendentals=0
            ),
        )(*args)

    return run


def mover(sems):
    used = []

    def start(src, dst):
        copy = pltpu.make_async_copy(src, dst, sems.at[len(used)])
        used.append(copy)
        copy.start()
        return copy

    return start


def sides(meta):
    return meta[0] & 1, (meta[0] >> 1) & 1


def combine(name, meta, arrays, outs, deps=(), us=1.0):
    def body(meta, *refs):
        x, z = sides(meta)

        def rows_at(at, n):
            return pl.ds(pl.multiple_of(at(x, z), 16), n) if callable(at) else slice(at, at + n)

        for ref, (_, kind, segments) in zip(refs[len(arrays) :], outs):
            for to, n, terms in segments:
                parts = [refs[i][rows_at(at, n), :] for i, at in terms]
                value = parts[0]
                if len(parts) > 1:
                    value = parts[0].astype(F32)
                    for part in parts[1:]:
                        value = value + part.astype(F32)
                ref[rows_at(to, n), :] = value.astype(kind)

    width = arrays[0].shape[1]
    return call(
        body,
        name=name,
        scalars=1,
        ins=[whole(a.shape) for a in arrays],
        outs=[((rows, width), kind, whole((rows, width))) for rows, kind, _ in outs],
        deps=deps,
        us=us,
    )(meta, *arrays)


def group_at(meta, count, slot, i):
    return count[(meta[1] ^ slot) * 2 + i]


def image_list(meta, image, devices, per_device, slots):
    each = per_device // 4
    return [
        image[(meta[0] ^ j) * per_device + (meta[1] ^ s) * each + i]
        for j in range(devices)
        for s in slots
        for i in range(each)
    ]


def image_column(images):
    return jnp.concatenate([jnp.full((LAT, 1), im, jnp.int32) for im in images], 0)


def image_row(images):
    group = lax.broadcasted_iota(jnp.int32, (1, len(images) * LAT), 1) // LAT
    out = jnp.zeros(group.shape, jnp.int32)
    for g, im in enumerate(images):
        out = jnp.where(group == g, im, out)
    return out


def key_stack(tok, lat8):
    pad = jnp.concatenate([lat8, jnp.zeros_like(lat8)], 0).astype(BF)
    return jnp.concatenate([tok, pad], 0)


def near_mask(count, columns):
    row = lax.broadcasted_iota(jnp.int32, (GROUP + 2 * LAT, columns), 0)
    return (row < count) | ((row >= GROUP) & (row < GROUP + LAT))


def param(params, i):
    return params[i : i + 1, :]


def project(rows, params, w, bias):
    unit, _ = norm_parts(rows.astype(F32))
    rows = (unit * param(params, GAIN1) + param(params, SHIFT1)).astype(BF)
    return (
        rows,
        (dot(rows, w[0], 1, 1) + bias[0:1]).astype(BF),
        dot(rows, w[1], 1, 1).astype(BF),
        (dot(rows, w[2], 1, 1) + bias[1:2]).astype(BF),
    )


def prepare(
    meta, lat, w_out, g1, s1, bo, g2, s2, bd, bu, up, down, lat_rel, lat_half, out_pack, part, params,
    vlat, vout, sems, *vecs,
):
    fetch = mover(sems)
    lat_copy = fetch(lat, vlat)
    copies = [fetch(ref, dst) for ref, dst in zip((g1, s1, bo, g2, s2, bd, bu), vecs)]
    x, z = sides(meta)
    n = part.shape[0] // 2
    here = pl.ds(pl.multiple_of((x * 2 + z) * n, 16), n)
    parts = [fetch(up.at[here], part.at[0:n]), fetch(down.at[here], part.at[n:])]
    wide = w_out.shape[0]
    parts.append(fetch(w_out, vout))
    lat_copy.wait()
    n = lat.shape[0] // 4
    for s in range(4):
        rows = vlat[pl.ds(pl.multiple_of((meta[1] ^ s) * n, 16), n), :]
        lat_rel[s * n : (s + 1) * n, :] = rows
        if s % 2 == 0:
            lat_half[s // 2 * n : (s // 2 + 1) * n, :] = rows
    for copy in copies:
        copy.wait()
    for i in range(7):
        params[i : i + 1, :] = vecs[i][...].reshape(1, params.shape[1])
    params[7:8, :] = jnp.zeros_like(params[7:8, :])
    bias = param(params, B_UP)
    rows = [v.astype(F32) for v in split3(bias)]
    out_pack[wide : wide + 16, :] = jnp.concatenate(rows + [jnp.zeros((13, bias.shape[1]), F32)], 0).astype(BF)
    for copy in parts:
        copy.wait()
    out_pack[0:wide, :] = vout[...]


def latent_rows(lat, params, w, bias, normed, ql, kl, vl):
    normed[...], a, b, c = project(lat[...], params, w, bias)
    ql[...], kl[...], vl[...] = a.astype(F32), b.astype(F32), c.astype(F32)


def forward_near(base, meta, count, tok, kl, vl, params, w, bias, normed, q, k, v, mixed_out, log):
    step = pl.program_id(0)
    wide = w.shape[1]
    rows, qs, ks, vs = project(tok[...], params, w, bias)
    normed[...], q[...], k[...], v[...] = rows, qs, ks, vs
    qs = qs * jnp.asarray(0.125, BF)
    for i in range(tok.shape[0] // GROUP):
        here = slice(i * LAT, (i + 1) * LAT)
        at = slice(i * GROUP, (i + 1) * GROUP)
        keys = key_stack(ks[at], kl[here, :])
        values = key_stack(vs[at], vl[here, :]).T
        mask = near_mask(group_at(meta, count, step + base, i), GROUP)
        logs, outs = [], []
        for h in range(wide // HEAD):
            s = jnp.where(mask, dot(head_lanes(keys, h), qs[at], 1, 1), FAR)
            top = jnp.max(s, 0, keepdims=True)
            e = jnp.exp(s - top)
            total = jnp.sum(e, 0, keepdims=True)
            logs.append(top + jnp.log(total))
            outs.append(dot(values[h * HEAD : (h + 1) * HEAD], e.astype(BF), 1, 0) * (1.0 / total))
        log[i] = jnp.concatenate(logs + [jnp.zeros((8 - len(logs), GROUP), F32)], 0)
        mixed_out[:, at] = jnp.concatenate(outs, 0).astype(BF)


def forward_far(meta, count, image, lat, params, w, bias, k_near, k_away, v_near, v_away, ql, qa, ka, va, m_near, m_away, far, logs_out):
    step = pl.program_id(0)
    wide = w.shape[1]
    rows_step = lat.shape[0]
    own = ql.shape[0]
    groups = own // LAT

    def rows_of(near, away, g):
        half = groups // 2
        ref, at = (near, g) if g < half else (away, g - half)
        return ref[at * GROUP : (at + 1) * GROUP, :]

    _, a, b, c = project(lat[...], params, w, bias)
    here = pl.ds(pl.multiple_of(step * rows_step, rows_step), rows_step)
    qa[here, :], ka[here, :], va[here, :] = a, b, c

    @pl.when(step == pl.num_programs(0) - 1)
    def _():
        q32 = ql[...] * 0.125
        images = image_list(meta, image, qa.shape[0] // own, groups, SENT)
        mask = image_column(image_list(meta, image, 1, groups, OWN)) == image_row(images)
        lane = lax.broadcasted_iota(jnp.int32, (LAT, GROUP), 1)
        full = jnp.zeros((own, wide), F32)
        logs = []
        for h in range(wide // HEAD):
            qh = head_lanes(q32, h)
            s_lat = jnp.where(mask, dot(qh.astype(BF), ka[...], 1, 1), FAR)
            s_tok = jnp.concatenate(
                [
                    jnp.where(
                        lane < group_at(meta, count, g // 2, g % 2),
                        dot(qh[g * LAT : (g + 1) * LAT].astype(BF), rows_of(k_near, k_away, g), 1, 1),
                        FAR,
                    )
                    for g in range(groups)
                ],
                0,
            )
            top = jnp.maximum(jnp.max(s_lat, 1, keepdims=True), jnp.max(s_tok, 1, keepdims=True))
            e_lat, e_tok = jnp.exp(s_lat - top), jnp.exp(s_tok - top)
            total = jnp.sum(e_lat, 1, keepdims=True) + jnp.sum(e_tok, 1, keepdims=True)
            logs.append(top + jnp.log(total))
            near = jnp.concatenate(
                [
                    dot(e_tok[g * LAT : (g + 1) * LAT].astype(BF), rows_of(v_near, v_away, g), 1, 0)
                    for g in range(groups)
                ],
                0,
            )
            full = full + head_lanes((dot(e_lat.astype(BF), va[...], 1, 0) + near) * (1.0 / total), h)
        mixed = full.astype(BF)
        m_near[...], m_away[...] = mixed[: own // 2], mixed[own // 2 :]
        parts = [split3(x) for x in logs]
        cols = [p[i] for i in range(3) for p in parts]
        lane = lax.broadcasted_iota(jnp.int32, (own, 2 * HEAD), 1)
        extra = jnp.zeros((own, 2 * HEAD), F32)
        for i, c in enumerate(cols):
            extra = jnp.where(lane == i, c.astype(F32), extra)
        far[...] = mixed
        logs_out[...] = extra.astype(BF)


def valid_rows(meta, count, rows):
    row = lax.broadcasted_iota(jnp.int32, (rows, 1), 0)
    first = (row < GROUP) & (row < group_at(meta, count, 0, 0))
    return first | ((row >= GROUP) & (row < GROUP + group_at(meta, count, 0, 1)))


def slot_block(meta, ref, slot):
    n = ref.shape[0] // 4
    return ref.at[pl.ds(pl.multiple_of((meta[1] ^ slot) * n, 16), n)]


def project_out(t_near, t_far, l_near, l_far, o0, o2, out):
    wide, n = t_near.shape
    value = dot(t_near[...], o0[0:wide, :], 0, 0) + dot(t_far[...], o2[0:wide, :], 0, 0)
    out[0:n, :] = value.astype(out.dtype)
    value = dot(l_near[...], o0[0:wide, :], 1, 0) + dot(l_far[...], o2[0:wide, :], 1, 0)
    out[n:, :] = value.astype(out.dtype)


def cot_back(meta, cot_tok, cot_lat, down_w, out):
    n = cot_tok.shape[0]
    out[0:n, :] = dot(cot_tok[...], down_w[...], 1, 1).astype(BF)
    out[n:, :] = dot(cot_lat[...], down_w[...], 1, 1).astype(BF)


def add_norm(meta, count, params, own, got, tok, lat, residual, n2, stats):
    n, m = tok.shape[0], lat.shape[0]
    stats[...] = jnp.zeros_like(stats)
    for at, size, x in ((0, n, tok), (n, m, lat)):
        rows = slice(at, at + size)
        attn = own[rows, :] + got[rows, :].astype(F32) + param(params, B_OUT)
        if at == 0:
            real = valid_rows(meta, count, n)
            stats[0:1, :] = jnp.sum(jnp.where(real, attn * attn, 0.0), 0, keepdims=True)
        res = x[...].astype(F32) + attn
        residual[rows, :] = res
        unit, _ = norm_parts(res)
        n2[rows, :] = (unit * param(params, GAIN2) + param(params, SHIFT2)).astype(BF)


def hidden_part(n2, cot, up_w, down_w, bias, act_out, grad_out):
    cut = 256
    sums = []
    for at in range(0, up_w.shape[1], cut):
        cols = slice(at, at + cut)
        up = dot(n2, up_w[:, cols], 1, 0) + bias[:, cols]
        active, slope = gelu_both(up)
        grad_up = (dot(cot, down_w[cols, :], 1, 1) * slope).astype(BF)
        act_out[:, cols] = active.astype(BF)
        grad_out[:, cols] = grad_up
        sums.append(jnp.sum(grad_up.astype(F32), 0, keepdims=True))
    return jnp.concatenate(sums, 1)


def two_halves(meta, fetch, n2_own, n2_sib, cot_tok, cot_lat, vn2, vcot):
    rows = n2_own.shape[0]
    n = cot_tok.shape[0] // 4
    copies = [fetch(n2_own, vn2.at[0:rows]), fetch(n2_sib, vn2.at[rows:])]
    for s in (0, 1):
        at = s * rows
        copies.append(fetch(slot_block(meta, cot_tok, s), vcot.at[at : at + n]))
        copies.append(fetch(slot_block(meta, cot_lat, s), vcot.at[at + n : at + rows]))
    return copies


def send_parts(meta, flush, pack, parts):
    x, z = sides(meta)
    n = parts[0].shape[0] // 2
    copies = []
    for ref, (dx, dz) in zip(parts, ((0, 0), (1, 0), (0, 1), (1, 1))):
        q = (x ^ dx) * 2 + (z ^ dz)
        for i in (0, 1):
            src = pack.at[pl.ds(pl.multiple_of(i * 4 * n + q * n, 16), n)]
            copies.append(flush(src, ref.at[i * n : (i + 1) * n]))
    return copies


def hidden_rows(n2, up_w, bias, got, act_out, grad_out, sums):
    cut = 256
    for at in range(0, up_w.shape[1], cut):
        cols = slice(at, at + cut)
        active, slope = gelu_both(dot(n2, up_w[:, cols], 1, 0) + bias[:, cols])
        grad_up = (got[:, cols].astype(F32) * slope).astype(BF)
        act_out[:, cols] = active.astype(BF)
        grad_out[:, cols] = grad_up
        sums[0:1, cols] = jnp.sum(grad_up.astype(F32), 0, keepdims=True)


def hidden_first(params, n2, up_w, got, act, grad, stats):
    stats[...] = jnp.zeros_like(stats)
    hidden_rows(n2[...], up_w, param(params, B_UP), got, act, grad, stats)


def hidden_own(
    meta, params, n2_own, n2_sib, cot_tok, cot_lat, up_w, got_in, act_in, grad_in,
    act_out, grad_out, p0, p1, p2, p3, stats,
    vn2, vcot, vw, act, grad, got, vpack, in_sems, out_sems,
):
    width, hidden = vw.shape
    rows = got.shape[0]
    fetch, flush = mover(in_sems), mover(out_sems)
    first = [fetch(n2_sib, vn2.at[rows:]), fetch(up_w, vw), fetch(got_in, got)]
    copies = [fetch(grad_in, grad.at[0:rows]), fetch(act_in, act.at[0:rows]), fetch(n2_own, vn2.at[0:rows])]
    n = cot_tok.shape[0] // 4
    for s in (0, 1):
        at = s * rows
        copies.append(fetch(slot_block(meta, cot_tok, s), vcot.at[at : at + n]))
        copies.append(fetch(slot_block(meta, cot_lat, s), vcot.at[at + n : at + rows]))
    for copy in first:
        copy.wait()
    stats[...] = jnp.zeros_like(stats)
    hidden_rows(vn2[rows:, :], vw, param(params, B_UP), got, act.at[rows:], grad.at[rows:], stats)
    for copy in copies:
        copy.wait()
    outs = [flush(act, act_out), flush(grad, grad_out)]
    vpack[0:width, :] = dot(vn2[...], grad[...], 0, 0).astype(BF)
    vpack[width : width + hidden, :] = dot(act[...], vcot[...], 0, 0).astype(BF)
    outs += send_parts(meta, flush, vpack, (p0, p1, p2, p3))
    for copy in outs:
        copy.wait()


def hidden_away(
    meta, o2, n2_own, n2_sib, cot_tok, cot_lat, w0, w1, w2, w3, act_in, grad_in, up_w, down_w,
    branch_own, back_own, send, act_out, grad_out, stats,
    vn2, vcot, vw, vnear, act0, grad0, branch, back, act, grad, vsend, in_sems, out_sems,
):
    rows, width = n2_own.shape
    x, z = sides(meta)
    quarter = w0.shape[0] // 2
    fetch, flush = mover(in_sems), mover(out_sems)
    copies = two_halves(meta, fetch, n2_own, n2_sib, cot_tok, cot_lat, vn2, vcot)
    for ref, (dx, dz) in zip((w0, w1, w2, w3), ((0, 0), (1, 0), (0, 1), (1, 1))):
        q = pl.multiple_of(((x ^ dx) * 2 + (z ^ dz)) * quarter, 16)
        for i in (0, 1):
            copies.append(fetch(ref.at[i * quarter : (i + 1) * quarter], vw.at[i, pl.ds(q, quarter)]))
    late = [(fetch(grad_in, grad0), fetch(up_w, vnear.at[0])), (fetch(act_in, act0), fetch(down_w, vnear.at[1]))]
    for copy in copies:
        copy.wait()
    base = o2.shape[0] - 16
    bias = o2[base : base + 16, :].astype(F32)
    bias = bias[0:1] + bias[1:2] + bias[2:3]
    n2, ct = vn2[...], vcot[...]
    stats[...] = jnp.zeros_like(stats)
    stats[0:1, :] = hidden_part(n2, ct, vw.at[0], vw.at[1], bias, act, grad)
    outs = [flush(act, act_out), flush(grad, grad_out)]
    for i, (ref, near, src, turn, own) in enumerate(
        ((back, grad0, grad, 1, back_own), (branch, act0, act, 0, branch_own))
    ):
        for copy in late[i]:
            copy.wait()
        ref[...] = dot(near[...], vnear[i], 1, turn) + dot(src[...], vw[i], 1, turn)
        vsend[i * rows : (i + 1) * rows, :] = ref[rows:, :].astype(BF)
        outs.append(flush(ref.at[0:rows], own))
        outs.append(flush(vsend.at[i * rows : (i + 1) * rows], send.at[i * rows : (i + 1) * rows]))
    for copy in outs:
        copy.wait()


def away_grads(
    meta, n2_own, n2_sib, cot_tok, cot_lat, act_in, grad_in, p0, p1, p2, p3,
    vn2, vcot, act, grad, vpack, in_sems, out_sems,
):
    width, hidden = vn2.shape[1], act.shape[1]
    fetch, flush = mover(in_sems), mover(out_sems)
    copies = [fetch(grad_in, grad)] + two_halves(meta, fetch, n2_own, n2_sib, cot_tok, cot_lat, vn2, vcot)
    last = fetch(act_in, act)
    for copy in copies:
        copy.wait()
    vpack[0:width, :] = dot(vn2[...], grad[...], 0, 0).astype(BF)
    last.wait()
    vpack[width : width + hidden, :] = dot(act[...], vcot[...], 0, 0).astype(BF)
    for copy in send_parts(meta, flush, vpack, (p0, p1, p2, p3)):
        copy.wait()


def middle_rows(meta, count, params, residual, branch, back, got, cot_tok, cot_lat, out_rows, grad_attn, stats):
    n, m = cot_tok.shape[0], cot_lat.shape[0]
    rows_own = n + m
    stats[...] = jnp.zeros_like(stats)
    for at, size, cot in ((0, n, cot_tok), (n, m, cot_lat)):
        rows = slice(at, at + size)
        bk = back[rows, :] + got[rows, :].astype(F32)
        br = branch[rows, :] + got[rows_own + at : rows_own + at + size, :].astype(F32) + param(params, B_DOWN)
        res = residual[rows, :]
        out = res + br
        out_rows[rows, :] = out.astype(BF)
        if at == 0:
            real = valid_rows(meta, count, n)
            stats[0:1, :] = jnp.sum(jnp.where(real, out * out, 0.0), 0, keepdims=True)
            stats[1:2, :] = jnp.sum(jnp.where(real, br * br, 0.0), 0, keepdims=True)
        unit, inverse = norm_parts(res)
        stats[2:3, :] += jnp.sum(bk * unit, 0, keepdims=True)
        stats[3:4, :] += jnp.sum(bk, 0, keepdims=True)
        cot32 = cot[...].astype(F32)
        gr = cot32 + norm_back(bk, unit, inverse, param(params, GAIN2))
        ga = gr.astype(BF)
        grad_attn[rows, :] = ga
        stats[4:5, :] += jnp.sum(ga.astype(F32), 0, keepdims=True)
        stats[5:6, :] += jnp.sum(cot32, 0, keepdims=True)


def back_out(meta, ga_own, ga_sib, o0, o2, t_near, t_far, l_near, l_far, g0, g2, d0, w0, sent):
    wide, n = t_near.shape[0], t_near.shape[1] // 2
    m = l_near.shape[0] // 2
    sent[wide:, :] = jnp.zeros_like(sent[wide:, :])
    for o, g, d, at in ((o2, g2, sent, wide), (o0, g0, d0, 0)):
        for i, ga in enumerate((ga_own, ga_sib)):
            g[:, i * n : (i + 1) * n] = dot(o[0:wide, :], ga[0:n, :], 1, 1).astype(BF)
            rows = dot(ga[n : n + m, :], o[0:wide, :], 1, 1).astype(BF)
            d[at + i * m : at + (i + 1) * m, 0:wide] = rows
    for t, l, w in ((t_far, l_far, sent.at[0:wide]), (t_near, l_near, w0)):
        total = jnp.zeros(w0.shape, F32)
        for i, ga in enumerate((ga_own, ga_sib)):
            total += dot(t[:, i * n : (i + 1) * n], ga[0:n, :], 1, 0)
            total += dot(l[i * m : (i + 1) * m, :], ga[n : n + m, :], 0, 0)
        w[...] = total.astype(BF)


def near_slot(
    slot, meta, count, normed, q, k, v, ql, kl, vl, log, far, logs_far, d_in, d_lat_in, w, grad_w, bias,
    dq_far, dk_near, dv_near,
):
    wide = q.shape[1]
    heads = wide // HEAD
    rows = normed[...]
    slot_rows = rows.shape[0]
    d_lat = d_lat_in[:, 0 : q.shape[1]].astype(F32)
    eighth = jnp.asarray(0.125, BF)
    q_all, k_all, v_all = q[...] * eighth, k[...], v[...]
    far32 = far[...].astype(F32)
    far_log = logs_far[...].astype(F32)
    dqs, dks, dvs = [], [], []
    for i in range(slot_rows // GROUP):
        at, lat_at = slice(i * GROUP, (i + 1) * GROUP), slice(i * LAT, (i + 1) * LAT)
        number = group_at(meta, count, slot, i)
        d_cols = d_in[:, at]
        d_tok, qs, ks, vs = d_cols.T, q_all[at], k_all[at], v_all[at]
        keys, values = key_stack(ks, kl[lat_at, :]), key_stack(vs, vl[lat_at, :])
        keys_t = keys.T
        mask = near_mask(number, GROUP)
        ps, gs, dq_t, d_heads, q_heads = [], [], [], [], []
        for h in range(heads):
            s = dot(head_lanes(keys, h), qs, 1, 1)
            p = jnp.where(mask, jnp.exp(s - log[i, h : h + 1, :]), 0.0)
            gp = p * dot(head_lanes(values, h), d_cols, 1, 0)
            g = (gp - p * jnp.sum(gp, 0, keepdims=True)).astype(BF)
            dq_t.append(dot(keys_t[h * HEAD : (h + 1) * HEAD], g, 1, 0))
            ps.append(p.astype(BF))
            gs.append(g)
            d_heads.append(head_lanes(d_tok, h))
            q_heads.append(head_lanes(qs, h))
        dv = dot(jnp.concatenate(ps, 1), jnp.concatenate(d_heads, 0), 1, 0)
        dk = dot(jnp.concatenate(gs, 1), jnp.concatenate(q_heads, 0), 1, 0)
        dqs.append((jnp.concatenate(dq_t, 0).T * 0.125).astype(BF))
        pad = jnp.zeros((LAT, wide), F32)
        q8, o8, d8, lg = ql[lat_at, :] * 0.125, far32[lat_at], d_lat[lat_at], far_log[lat_at]
        q_rows, do_rows, log_col, del_col = [], [], [], []
        big = jnp.full((LAT, 1), 1e30, F32)
        zero = jnp.zeros((LAT, 1), F32)
        for h in range(heads):
            q_rows += [head_lanes(q8, h), pad]
            dh = head_lanes(d8, h)
            do_rows += [dh, pad]
            col = lg[:, h : h + 1] + lg[:, heads + h : heads + h + 1] + lg[:, 2 * heads + h : 2 * heads + h + 1]
            log_col += [col, big]
            del_col += [jnp.sum(dh * o8, 1, keepdims=True), zero]
        q_f, d_f = jnp.concatenate(q_rows, 0).astype(BF), jnp.concatenate(do_rows, 0).astype(BF)
        l_f, x_f = jnp.concatenate(log_col, 0), jnp.concatenate(del_col, 0)
        lane = lax.broadcasted_iota(jnp.int32, (2 * LAT * heads, GROUP), 1)
        p_f = jnp.where(lane < number, jnp.exp(dot(q_f, ks, 1, 1) - l_f), 0.0)
        g_f = (p_f * (dot(d_f, vs, 1, 1) - x_f)).astype(BF)
        dks.append((dk[0:GROUP] + dot(g_f, q_f, 0, 0)).astype(BF))
        dvs.append((dv[0:GROUP] + dot(p_f.astype(BF), d_f, 0, 0)).astype(BF))
        dk_near[lat_at, :] = dk[GROUP : GROUP + LAT]
        dv_near[lat_at, :] = dv[GROUP : GROUP + LAT]
        dq_all = dot(g_f, ks, 1, 0)
        dq_lat = jnp.zeros((LAT, wide), F32)
        for h in range(heads):
            dq_lat += head_lanes(dq_all[2 * LAT * h : 2 * LAT * h + LAT], h)
        dq_far[lat_at, :] = dq_lat

    dq, dk, dv = (jnp.concatenate(v, 0) for v in (dqs, dks, dvs))
    total = dot(dq, w[0], 1, 0) + dot(dk, w[1], 1, 0) + dot(dv, w[2], 1, 0)
    for i, g in enumerate((dq, dk, dv)):
        grad_w[i] += dot(g, rows, 0, 0)
    bias[0:1, :] += jnp.sum(dq.astype(F32), 0, keepdims=True)
    bias[1:2, :] += jnp.sum(dv.astype(F32), 0, keepdims=True)
    bias[2:3, :] += jnp.sum(dk.astype(F32), 0, keepdims=True)
    return total.astype(BF)


def backward_rows(
    first, begin, meta, count, normed, q, k, v, ql, kl, vl, log, far, logs_far, d_in, d_lat, w, gw_in, bias_in, *outs,
):
    step = pl.program_id(0)
    parts, (grad_w, bias, dq_far, dk_near, dv_near) = outs[:-5], outs[-5:]

    @pl.when(step == 0)
    def _():
        grad_w[...] = jnp.zeros_like(grad_w) if begin else gw_in[...]
        bias[...] = jnp.zeros_like(bias) if begin else bias_in[...]

    total = near_slot(
        step + first, meta, count, normed, q, k, v, ql, kl, vl, log, far, logs_far, d_in, d_lat, w, grad_w, bias,
        dq_far, dk_near, dv_near,
    )
    for slot, ref in enumerate(parts):

        @pl.when(step == slot)
        def _(ref=ref):
            ref[...] = total


def latent_bundle(meta, d_near, d_far, far, logs_far, own, sent):
    count, wide = far.shape
    heads = wide // HEAD
    n = count // 4
    d32 = jnp.concatenate([d_near[...], d_far[:, 0:wide]], 0).astype(F32)
    prod = d32 * far[...].astype(F32)
    lg = logs_far[...].astype(F32)
    deltas = [split3(jnp.sum(head_lanes(prod, h), 1, keepdims=True)) for h in range(heads)]
    cols = [lg[:, i : i + 1] for i in range(3 * heads)] + [p[i].astype(F32) for i in (0, 1) for p in deltas]
    lane = lax.broadcasted_iota(jnp.int32, (count, 4 * HEAD), 1)
    value = jnp.concatenate([d32, jnp.zeros((count, HEAD), F32)], 1)
    for i, c in enumerate(cols):
        value = jnp.where(lane == wide + i, c, value)
    value = value.astype(BF)
    own[...] = value
    for i, s in enumerate(SENT):
        sent[i * n : (i + 1) * n, :] = value[s * n : (s + 1) * n]


def backward_far(
    meta, tokens_real, image, qa, ka, va, ql, kl, vl, own, bundle, normed, w, gw, bias_in, wo_a, wo_b,
    params, stats1, stats2, hid_first, hid_near, hid_away, *refs,
):
    near, (lat_keep, lat_send, p0, p1, p2, p3, small, pack, out_sems) = refs[:-9], refs[-9:]
    count, wide = ql.shape
    heads = wide // HEAD
    groups = count // LAT
    q_all, k_all, v_all = qa[...] * jnp.asarray(0.125, BF), ka[...], va[...]
    q_own, k_own, v_own = (ql[...] * 0.125).astype(BF), kl[...].astype(BF), vl[...].astype(BF)
    d_own, d_all = own[:, 0:wide], bundle[:, 0:wide]

    def stats(ref, h):
        x = ref[...].astype(F32)
        col = [x[:, wide + i : wide + i + 1] for i in range(5 * heads)]
        return col[h] + col[heads + h] + col[2 * heads + h], col[3 * heads + h] + col[4 * heads + h]

    mine = image_list(meta, image, 1, groups, OWN)
    images = image_list(meta, image, qa.shape[0] // count, groups, SENT)
    mask_q = image_column(mine) == image_row(images)
    mask_k = image_column(images) == image_row(mine)
    each = len(near) // 3
    dq, dk, dv = (jnp.concatenate([ref[...] for ref in near[i * each : (i + 1) * each]], 0) for i in range(3))
    for h in range(heads):
        log, delta = stats(own, h)
        s = dot(head_lanes(q_own, h), k_all, 1, 1)
        p = jnp.where(mask_q, jnp.exp(s - log), 0.0)
        g = (p * (dot(head_lanes(d_own, h), v_all, 1, 1) - delta)).astype(BF)
        dq += head_lanes(dot(g, k_all, 1, 0), h)
        log, delta = stats(bundle, h)
        s = dot(q_all, head_lanes(k_own, h), 1, 1)
        p = jnp.where(mask_k, jnp.exp(s - log), 0.0)
        g = (p * (dot(d_all, head_lanes(v_own, h), 1, 1) - delta)).astype(BF)
        dk += head_lanes(dot(g, q_all, 0, 0), h)
        dv += head_lanes(dot(p.astype(BF), d_all, 0, 0), h)
    dq, dk, dv = (dq * 0.125).astype(BF), dk.astype(BF), dv.astype(BF)
    lat_rows = normed[...]
    sums = [bias_in[i : i + 1, :] for i in (0, 2, 1)]
    sums = [b + jnp.sum(g.astype(F32), 0, keepdims=True) for b, g in zip(sums, (dq, dk, dv))]
    columns = jnp.concatenate(sums + [jnp.zeros((5, wide), F32)], 0).T
    first_gain = jnp.zeros((1, pack.shape[1]), F32)
    first_shift = first_gain
    for i, g in enumerate((dq, dk, dv)):
        total = gw[i] + dot(g, lat_rows, 0, 0)
        pack[i * wide : (i + 1) * wide, :] = total.astype(BF)
        col, weight = columns[:, i : i + 1], w[i].astype(F32)
        first_shift += jnp.sum(weight * col, 0, keepdims=True)
        first_gain += jnp.sum(weight * (total - col * param(params, SHIFT1)), 0, keepdims=True)
    first_gain = first_gain / param(params, GAIN1)
    pack[3 * wide :, :] = (wo_a[...].astype(F32) + wo_b[...].astype(F32)).astype(BF)
    x, z = sides(meta)
    flush = mover(out_sems)
    copies = []
    for ref, (dx, dz) in zip((p0, p1, p2, p3), ((0, 0), (1, 0), (0, 1), (1, 1))):
        part = (x ^ dx) * 2 + (z ^ dz)
        at = 0
        for base, size in ((0, 3 * wide // 4), (3 * wide, wide // 4)):
            src = pack.at[pl.ds(pl.multiple_of(base + part * size, 16), size)]
            copies.append(flush(src, ref.at[at : at + size]))
            at += size
    rows = (dot(dq, w[0], 1, 0) + dot(dk, w[1], 1, 0) + dot(dv, w[2], 1, 0)).astype(BF)
    n = count // 4
    lat_keep[0:n, :], lat_keep[n : 2 * n, :] = rows[0:n], rows[2 * n : 3 * n]
    lat_send[0:n, :], lat_send[n : 2 * n, :] = rows[n : 2 * n], rows[3 * n :]
    small[...] = jnp.zeros_like(small)
    small[0:1, :] = stats1[0:1, :]
    small[1:7, :] = stats2[0:6, :]
    small[7:8, :], small[8:9, :] = first_gain, first_shift
    real = tokens_real[0]
    for i in range(1, tokens_real.shape[0]):
        real = real + tokens_real[i]
    for at, part in ((9, real - real % 64), (22, real % 64)):
        small[at : at + 1, :] = jnp.full((1, small.shape[1]), 0.25, F32) * part.astype(F32)
    for s, row in ((0, hid_first[0:1, :] + hid_near[0:1, :]), (2, hid_away[0:1, :])):
        small[pl.ds(10 + (meta[1] ^ s), 1), :] = row
    small[pl.ds(14 + meta[1], 1), 0:wide] = sums[0]
    small[pl.ds(18 + meta[1], 1), 0:wide] = sums[2]
    for copy in copies:
        copy.wait()


def final_rows(meta, tok, lat, a, b, c, la, lb, grad_res, params, out):
    n, m = tok.shape[0], lat.shape[0]
    for x, at, terms in ((tok, slice(0, n), (a, b)), (lat, slice(n, n + m), (la, lb))):
        grad = c[at, :].astype(F32)
        for term in terms:
            grad += term[0 : x.shape[0], :].astype(F32)
        unit, inverse = norm_parts(x[...].astype(F32))
        out[at, :] = (grad_res[at, :].astype(F32) + norm_back(grad, unit, inverse, param(params, GAIN1))).astype(BF)


def place_rows(meta, a, b, c, d, tok_out, lat_out):
    n = tok_out.shape[0]
    for i, ref in enumerate((a, b, c, d)):

        @pl.when(pl.program_id(0) == i)
        def _(ref=ref):
            tok_out[...] = ref[0:n, :]
            lat_out[...] = ref[n:, :]


def projections_out(meta, f0, f1, f2, f3, grad_w, grad_o, gain1, shift1, b_out, gain2, shift2, b_down, b_up, b_qv, roots):
    x, z = sides(meta)
    wide = grad_o.shape[0]
    four = (f0, f1, f2, f3)
    for ref, (dx, dz) in zip(four, ((0, 0), (1, 0), (0, 1), (1, 1))):
        part = (x ^ dx) * 2 + (z ^ dz)
        at = 0
        for dst, size in ((grad_w, 3 * wide // 4), (grad_o, wide // 4)):
            dst[pl.ds(pl.multiple_of(part * size, 16), size), :] = ref[at : at + size, :].astype(F32)
            at += size
    small = four[0][wide : wide + 32, :].astype(F32)
    for ref in four[1:]:
        small += ref[wide : wide + 32, :].astype(F32)
    for ref, row in ((gain1, 7), (shift1, 8), (b_out, 5), (gain2, 3), (shift2, 4), (b_down, 6)):
        ref[...] = small[row, :]

    def of_mp(first):
        value = small[first : first + 1]
        for m in (1, 2, 3):
            value = jnp.where(meta[1] == m, small[first + m : first + m + 1], value)
        return value

    b_up[...] = of_mp(10)[0]
    b_qv[...] = jnp.concatenate([of_mp(14)[:, 0:wide], of_mp(18)[:, 0:wide]], 0)
    real = (small[9:10, 0:1] + small[22:23, 0:1]) * small.shape[1]
    lane = lax.broadcasted_iota(jnp.int32, roots.shape, 1)
    value = jnp.zeros(roots.shape, F32)
    for i, row in enumerate((1, 0, 2)):
        root = jnp.sqrt(jnp.sum(small[row : row + 1], 1, keepdims=True) / real)
        value = jnp.where(lane == i, root, value)
    roots[...] = value


def make(mesh):
    dp_size, mp_size = mesh.shape["dp"], mesh.shape["mp"]
    assert mp_size == 4 and dp_size >= 4
    dp_bits = [1 << i for i in range(dp_size.bit_length() - 1)]
    assert 1 << len(dp_bits) == dp_size
    x_bit, z_bit, rest_bits = dp_bits[0], dp_bits[1], dp_bits[2:]

    def swap(v, dp_bit, mp_bit):
        pairs = [
            (d * mp_size + m, (d ^ dp_bit) * mp_size + (m ^ mp_bit))
            for d in range(dp_size)
            for m in range(mp_size)
        ]
        return lax.ppermute(v, ("dp", "mp"), pairs)

    def per_device(
        tokens,
        latents,
        image_of_group,
        token_valid,
        norm1_gain,
        norm1_shift,
        w_qkv,
        b_qv,
        w_out,
        b_out,
        norm2_gain,
        norm2_shift,
        w_up,
        b_up,
        w_down,
        b_down,
        cot_tokens,
        cot_latents,
    ):
        dp_at, mp_at = lax.axis_index("dp"), lax.axis_index("mp")
        tok_count, width = tokens.shape
        lat_count = latents.shape[0]
        groups = lat_count // LAT
        wide = w_qkv.shape[2]
        hidden = w_up.shape[1]
        tok_own, lat_own = tok_count // 4, lat_count // 4
        rows_own = tok_own + lat_own
        all_lat = dp_size * lat_count
        meta = jnp.stack([dp_at, mp_at]).astype(jnp.int32)
        count = jnp.sum(token_valid.reshape(groups, GROUP), 1).astype(jnp.int32)
        par = whole((8, width))
        w_t = jnp.transpose(w_qkv, (0, 2, 1))
        w_all = (3, wide, width)
        quarter, small = width // 4, wide // 4
        half = 2 * quarter
        big = (rows_own, width)
        chip_rows, chip_tok, chip_lat = 2 * rows_own, 2 * tok_own, 2 * lat_own
        vec = pl.BlockSpec((width,), lambda *_: (0,))

        def out(shape, kind=BF):
            return (shape, kind, whole(shape))

        def kept_out(shape, kind=BF):
            return (shape, kind, kept(shape))

        vm = pltpu.VMEM

        def any_out(shape, kind=BF):
            return (shape, kind, ANY)

        def dma(n):
            return pltpu.SemaphoreType.DMA((n,))

        def cube(v, vx=None, vz=None, vxz=None):
            vx, vz, vxz = (v if w is None else w for w in (vx, vz, vxz))
            return swap(vx, x_bit, 0), swap(vz, z_bit, 0), swap(vxz, x_bit | z_bit, 0)

        def all_latents(v):
            v = jnp.concatenate((v,) + cube(v), 0)
            for bit in rest_bits:
                v = jnp.concatenate([v, swap(v, bit, 0)], 0)
            return v

        part_block = pl.BlockSpec((quarter, width), lambda i, meta: ((meta[0] & 1) * 2 + ((meta[0] >> 1) & 1), 0))
        lat_rel, lat_half, o0, weight_part, params = call(
            prepare,
            name="prepare",
            room=62,
            scalars=1,
            ins=[pl.BlockSpec(memory_space=pltpu.HBM)] * 11,
            outs=[out((lat_count, width)), out((chip_lat, width)), out((wide + 16, width)), out((half, width)), out((8, width), F32)],
            scratch=[vm((lat_count, width), BF), vm((wide, width), BF), dma(11)] + [vm((width,), F32)] * 7,
            us=2,
        )(meta, latents, w_out, norm1_gain, norm1_shift, b_out, norm2_gain, norm2_shift, b_down, b_up, w_up, w_down)
        lat_four = jnp.concatenate((lat_half,) + cube(lat_half), 0)
        w_own = swap(weight_part, 0, 2)
        o2 = swap(o0, 0, 2)

        normed_lat, ql, kl, vl = call(
            latent_rows,
            name="latent_rows",
            room=3,
            scalars=0,
            ins=[whole((lat_count, width)), par, whole(w_all), whole((2, wide))],
            outs=[out((lat_count, width))] + [out((lat_count, wide), F32)] * 3,
            us=2,
        )(lat_rel, params, w_t, b_qv)

        def cot_through(slot, meta):
            return call(
                cot_back,
                name="cot_back",
            room=4,
                scalars=1,
                ins=[
                    pl.BlockSpec((tok_own, width), lambda i, meta: (meta[1] ^ slot, 0), pipeline_mode=pl.Buffered(1)),
                    pl.BlockSpec((lat_own, width), lambda i, meta: (meta[1] ^ slot, 0), pipeline_mode=pl.Buffered(1)),
                    whole((hidden, width)),
                ],
                outs=[out((rows_own, hidden))],
                us=4,
            )(meta, cot_tokens, cot_latents, w_down)[0]

        cot_own = cot_through(0, after(meta, kl))
        lat_here = lat_four = after(lat_four, cot_own)
        for bit in rest_bits:
            lat_here = jnp.concatenate([lat_here, swap(lat_here, bit, 0)], 0)

        def near_forward(base, *deps):
            def run(*args):
                return forward_near(base, *args)

            rows = lambda wide_here: pl.BlockSpec((tok_own, wide_here), lambda i, *_: (i, 0))
            lat_block = pl.BlockSpec((lat_own, wide), lambda i, *_: (i + base, 0))
            each = groups // 4
            return call(
                run,
                name="forward_near",
            room=46,
                grid=(2,),
                scalars=2,
                ins=[
                    pl.BlockSpec((tok_own, width), lambda i, meta, _: (meta[1] ^ (i + base), 0)),
                    lat_block,
                    lat_block,
                    par,
                    whole(w_all),
                    whole((2, wide)),
                ],
                outs=[((chip_tok, width), BF, rows(width))]
                + [((chip_tok, wide), BF, rows(wide))] * 3
                + [((wide, chip_tok), BF, pl.BlockSpec((wide, tok_own), lambda i, *_: (0, i)))]
                + [((2 * each, 8, GROUP), F32, pl.BlockSpec((each, 8, GROUP), lambda i, *_: (i, 0, 0)))],
                us=8,
            )(meta, count, tokens, after(kl, *deps), vl, params, w_t, b_qv)

        normed_b, q_b, k_b, v_b, t_b, log_b = near_forward(2, lat_four)
        t_far = swap(t_b, 0, 2)
        lat_here = after(lat_here, t_b)
        normed_a, q_a, k_a, v_a, t_near, log_a = near_forward(0, lat_here)
        w_x, w_z, w_xz = cube(after(w_own, t_near))
        lat_all = [v.reshape(dp_size, chip_lat, width) for v in (lat_here, swap(lat_here, 0, 1))]
        lat_all = jnp.concatenate(lat_all, 1).reshape(all_lat, width)
        lat_all = after(lat_all, t_near)

        chunk = min(512, all_lat)
        qa, ka, va, l_near, l_b, far, far_logs = call(
            forward_far,
            name="forward_far",
            room=6,
            grid=(all_lat // chunk,),
            scalars=3,
            ins=[pl.BlockSpec((chunk, width), lambda i, *_: (i, 0)), par, whole(w_all), whole((2, wide))]
            + [whole((chip_tok, wide))] * 4
            + [whole((lat_count, wide))],
            outs=[out((all_lat, wide))] * 3
            + [kept_out((chip_lat, wide))] * 2
            + [kept_out((lat_count, wide)), kept_out((lat_count, 2 * HEAD))],
            us=6,
        )(meta, count, image_of_group, lat_all, params, w_t, b_qv, k_a, k_b, v_a, v_b, ql)
        l_far = swap(l_b, 0, 2)

        out_pack = whole((wide + 16, width))
        mixed_specs = [whole((wide, chip_tok))] * 2 + [whole((chip_lat, wide))] * 2
        cot_sib = cot_through(1, after(meta, far))

        def out_rows_of(slot, kind, o0):
            return call(
                project_out,
                name="project_out",
            room=4,
                scalars=0,
                ins=[pl.BlockSpec((wide, tok_own), lambda *_: (0, slot), pipeline_mode=pl.Buffered(1))] * 2
                + [pl.BlockSpec((lat_own, wide), lambda *_: (slot, 0), pipeline_mode=pl.Buffered(1))] * 2
                + [out_pack] * 2,
                outs=[out(big, kind)],
                us=3,
            )(t_near, t_far, l_near, l_far, o0, o2)[0]

        attn_send = out_rows_of(1, BF, after(o0, cot_sib))
        attn_own = out_rows_of(0, F32, after(o0, attn_send))
        attn_got = swap(attn_send, 0, 1)
        own_tok = pl.BlockSpec((tok_own, width), lambda i, meta, _: (meta[1], 0), pipeline_mode=pl.Buffered(1))
        own_lat = pl.BlockSpec((lat_own, width), lambda i, meta, _: (meta[1], 0), pipeline_mode=pl.Buffered(1))
        residual, n2, stats1 = call(
            add_norm,
            name="add_norm",
            room=6,
            scalars=2,
            ins=[par, whole(big), whole(big), own_tok, whole((lat_own, width))],
            outs=[out(big, F32), out(big), out((8, width), F32)],
            us=3,
        )(meta, count, params, attn_own, attn_got, tokens, lat_rel)
        n2_sib = swap(n2, 0, 1)

        chip = (chip_rows, width)
        piece = (half, width)
        act_first, grad_first, bias_first = call(
            hidden_first,
            name="hidden_first",
            room=6,
            scalars=0,
            ins=[par, whole(big), whole((width, hidden)), whole((rows_own, hidden))],
            outs=[out((rows_own, hidden))] * 2 + [out((8, hidden), F32)],
            us=4,
        )(params, n2, w_up, cot_own)
        act_near, grad_near, a0, a1, a2, a3, bias_near = call(
            hidden_own,
            name="hidden_own",
            room=7,
            scalars=1,
            ins=[par] + [ANY] * 8,
            outs=[any_out((chip_rows, hidden))] * 2 + [any_out(piece)] * 4 + [out((8, hidden), F32)],
            scratch=[
                vm(chip, BF),
                vm(chip, BF),
                vm((width, hidden), BF),
                vm((chip_rows, hidden), BF),
                vm((chip_rows, hidden), BF),
                vm((rows_own, hidden), BF),
                vm((width + hidden, width), BF),
                dma(10),
                dma(10),
            ],
            us=9,
        )(meta, params, n2, n2_sib, cot_tokens, cot_latents, w_up, cot_sib, act_first, grad_first)
        near_parts = (a0,) + cube(None, a1, a2, a3)

        branch, back, middle_send, act, grad, bias_away = call(
            hidden_away,
            name="hidden_away",
            room=8,
            scalars=1,
            ins=[out_pack] + [ANY] * 12,
            outs=[any_out(big, F32), any_out(big, F32), any_out(chip), any_out((chip_rows, hidden)), any_out((chip_rows, hidden))]
            + [out((8, hidden), F32)],
            scratch=[
                vm(chip, BF),
                vm(chip, BF),
                vm((2, width, hidden), BF),
                vm((2, width, hidden), BF),
                vm((chip_rows, hidden), BF),
                vm((chip_rows, hidden), BF),
                vm(chip, F32),
                vm(chip, F32),
                vm((chip_rows, hidden), BF),
                vm((chip_rows, hidden), BF),
                vm(chip, BF),
                dma(18),
                dma(6),
            ],
            us=10,
        )(meta, o2, n2, n2_sib, cot_tokens, cot_latents, w_own, w_x, w_z, w_xz, act_near, grad_near, w_up, w_down)
        middle_got = swap(middle_send, 0, 1)

        b0, b1, b2, b3 = call(
            away_grads,
            name="away_grads",
            room=7,
            scalars=1,
            ins=[ANY] * 6,
            outs=[any_out(piece)] * 4,
            scratch=[
                vm(chip, BF),
                vm(chip, BF),
                vm((chip_rows, hidden), BF),
                vm((chip_rows, hidden), BF),
                vm((width + hidden, width), BF),
                dma(8),
                dma(8),
            ],
            us=6,
        )(meta, n2, n2_sib, cot_tokens, cot_latents, act, grad)

        out_rows, grad_attn, stats2 = call(
            middle_rows,
            name="middle_rows",
            room=8,
            scalars=2,
            ins=[par, whole(big), whole(big), whole(big), whole(chip), own_tok, own_lat],
            outs=[out(big), out(big), out((8, width), F32)],
            us=5,
            deps=(b0,),
        )(meta, count, params, residual, branch, back, middle_got, cot_tokens, cot_latents)
        grad_attn_sib = swap(grad_attn, 0, 1)

        def terms(n, at=0):
            return [(i, at) for i in range(n)]

        sides4 = ((0, 0), (1, 0), (0, 1), (1, 1))

        def at(d, size, base=0):
            return lambda x, z: base + ((x ^ d[0]) * 2 + (z ^ d[1])) * size


        (near_sum,) = combine("near_sum", meta, near_parts, [(half, BF, [(0, half, terms(4))])], us=2)
        away_parts = (b0,) + cube(None, *(after(v, near_parts[1], near_parts[2]) for v in (b1, b2, b3)))

        g_near, g_send, d_near, out_grad, out_send = call(
            back_out,
            name="back_out",
            room=6,
            scalars=1,
            ins=[whole(big), whole(big), out_pack, out_pack] + mixed_specs,
            outs=[out((wide, chip_tok))] * 2 + [out((chip_lat, wide)), out((wide, width)), out((wide + chip_lat, width))],
            us=4,
            deps=(near_sum,),
        )(meta, grad_attn, grad_attn_sib, o0, o2, t_near, t_far, l_near, l_far)
        out_got = swap(out_send, 0, 2)
        g_far = swap(g_send, 0, 2)

        zero_w, zero_b = jnp.zeros((8, LANES), F32), jnp.zeros((8, LANES), F32)

        def rows_backward(first, steps, half_in, g, d, gw, bias, *deps):
            normed, q, k, v, log = half_in
            base = first % 2

            def rows(n, wide_here, shift):
                return pl.BlockSpec((n, wide_here), lambda i, *_: (i + shift, 0))

            def run(*args):
                return backward_rows(first, gw is None, *args)

            init = (zero_w, zero_b) if gw is None else (gw, bias)
            return call(
                run,
                name="backward_rows",
            room=8,
                grid=(steps,),
                scalars=2,
                ins=[
                    rows(tok_own, width, base),
                    *[rows(tok_own, wide, base)] * 3,
                    *[rows(lat_own, wide, first)] * 3,
                    pl.BlockSpec((groups // 4, 8, GROUP), lambda i, *_: (i + base, 0, 0)),
                    rows(lat_own, wide, first),
                    rows(lat_own, 2 * HEAD, first),
                    pl.BlockSpec((wide, tok_own), lambda i, *_: (0, i + base)),
                    rows(lat_own, d.shape[1], base + (wide // lat_own if d.shape[1] != wide else 0)),
                    whole(w_all),
                    whole(init[0].shape),
                    whole(init[1].shape),
                ],
                outs=[kept_out((tok_own, width))] * steps
                + [kept_out(w_all, F32), kept_out((8, wide), F32)]
                + [((steps * lat_own, wide), F32, rows(lat_own, wide, 0))] * 3,
                us=7 * steps,
                deps=deps,
            )(meta, count, normed, q, k, v, ql, kl, vl, log, far, far_logs, g, d, w_t, *init)

        half_a, half_b = (normed_a, q_a, k_a, v_a, log_a), (normed_b, q_b, k_b, v_b, log_b)
        part0, gw, bias, *near_0 = rows_backward(0, 1, half_a, g_near, d_near, None, None)
        bundle_own, bundle = call(
            latent_bundle,
            name="latent_bundle",
            scalars=1,
            ins=[whole((chip_lat, wide)), pl.BlockSpec((chip_lat, width), lambda *_: (wide // chip_lat, 0))]
            + [whole((lat_count, wide)), whole((lat_count, 2 * HEAD))],
            outs=[out((lat_count, 4 * HEAD))] * 2,
            us=2,
            deps=(part0,),
        )(meta, d_near, out_got, far, far_logs)
        steps = [bundle]

        def spread(bit):
            got = swap(steps[0], bit, 0)
            return lambda done: steps.__setitem__(0, jnp.concatenate([after(steps[0], done), got], 0))

        join = spread(x_bit)
        part1, gw, bias, *near_1 = rows_backward(1, 1, half_a, g_near, d_near, gw, bias, bundle_own)
        join(part1)
        join = spread(z_bit)
        (away_sum,) = combine("away_sum", meta, away_parts, [(half, BF, [(0, half, terms(4))])], us=2, deps=(part1,))
        away_got = swap(away_sum, 0, 2)
        part3, gw, bias, *near_3 = rows_backward(3, 1, half_b, g_far, out_got, gw, bias, away_sum, steps[0])
        join(part3)
        for bit in rest_bits[:-1]:
            spread(bit)(part3)
        join = spread(rest_bits[-1]) if rest_bits else None
        got3 = swap(part3, 0, 1)
        got1 = swap(after(part1, part3), 0, 1)
        part2, gw, bias, *near_2 = rows_backward(2, 1, half_b, g_far, out_got, gw, bias)
        if rest_bits:
            join(part2)
        bundle = steps[0]
        (total,) = combine(
            "weights_sum", meta, [near_sum, away_got], [(half, BF, [(0, half, terms(2))])], us=20, deps=(part2,)
        )
        near_all = [v for three in zip(near_0, near_1, near_2, near_3) for v in three]
        shard = (small * 4, width)
        lat_keep, lat_send, c0, c1, c2, c3, small_rows = call(
            backward_far,
            name="backward_far",
            room=6,
            scalars=3,
            ins=[whole((all_lat, wide))] * 3
            + [whole((lat_count, wide))] * 3
            + [whole((lat_count, 4 * HEAD)), whole((all_lat, 4 * HEAD)), whole((lat_count, width)), whole(w_all), whole(w_all)]
            + [whole((8, wide))]
            + [whole((wide, width)), pl.BlockSpec((wide, width), lambda *_: (0, 0), pipeline_mode=pl.Buffered(1))]
            + [par]
            + [whole((8, width))] * 5
            + [whole(v.shape) for v in near_all],
            outs=[out((chip_lat, width))] * 2 + [any_out(shard)] * 4 + [out((32, width), F32)],
            scratch=[vm((4 * wide, width), BF), dma(8)],
            us=8,
            deps=(total, got1, got3),
        )(
            meta, count, image_of_group, qa, ka, va, ql, kl, vl, bundle_own, bundle, normed_lat, w_t, gw, bias, out_grad,
            out_got, params, stats1, stats2, bias_first, bias_near, bias_away, *near_all,
        )

        lat_got = swap(lat_send, 0, 1)
        (there,) = combine(
            "rows_sum", meta, [part2, got3, lat_keep, lat_got],
            [(rows_own, BF, [(0, tok_own, terms(2)), (tok_own, lat_own, [(2, lat_own), (3, lat_own)])])],
            us=2, deps=(total,),
        )
        from_y = swap(there, 0, 2)
        small_rows = small_rows + swap(small_rows, 0, 1)
        small_got = swap(small_rows, 0, 2)
        rows4 = 4 * small
        qkv_parts = (c0,) + cube(None, *(after(v, total) for v in (c1, c2, c3)))
        (qkv,) = combine(
            "qkv_sum", meta, qkv_parts + (small_rows, small_got),
            [(rows4 + 32, BF, [(0, rows4, terms(4)), (rows4, 32, [(4, 0), (5, 0)])])],
            us=2, deps=(there,),
        )
        (grad_rows,) = call(
            final_rows,
            name="final_rows",
            room=6,
            scalars=1,
            ins=[
                pl.BlockSpec((tok_own, width), lambda i, meta: (meta[1], 0), pipeline_mode=pl.Buffered(1)),
                whole((lat_own, width)),
                *[whole((tok_own, width))] * 2,
                whole(big),
                *[whole((chip_lat, width))] * 2,
                whole(big),
                par,
            ],
            outs=[out(big)],
            us=4,
            deps=(qkv,),
        )(meta, tokens, lat_rel, part0, got1, from_y, lat_keep, lat_got, grad_attn, params)

        grad_y = swap(grad_rows, 0, 2)
        grad_c = swap(after(grad_rows, grad_y), 0, 1)
        out_y = swap(after(out_rows, qkv), 0, 2)
        for bit in rest_bits:
            (total,) = combine(
                "rest_sum", meta, [total, swap(total, bit, 0)], [(half, BF, [(0, half, terms(2))])], us=2,
                deps=(there,),
            )
        def all_rows(v, v_y, v_c):
            v_yc = swap(v_y, 0, 1)
            place = lambda n: pl.BlockSpec((n, width), lambda i, meta: (meta[1] ^ i, 0))
            return call(
                place_rows,
                name="place_rows",
                grid=(4,),
                scalars=1,
                ins=[whole(big)] * 4,
                outs=[((tok_count, width), BF, place(tok_own)), ((lat_count, width), BF, place(lat_own))],
                us=4,
            )(meta, v, v_c, v_y, v_yc)

        grad_tok, grad_lat = all_rows(grad_rows, grad_y, grad_c)
        out_tok, out_lat = all_rows(out_rows, out_y, swap(after(out_rows, out_y), 0, 1))
        four = (total,) + cube(total)
        grad_w_up, grad_w_down = combine(
            "weights_out", meta, four,
            [
                (4 * quarter, F32, [(at(d, quarter), quarter, [(i, r * quarter)]) for i, d in enumerate(sides4)])
                for r in (0, 1)
            ]
            ,
            us=5,
            deps=(qkv, out_y, grad_tok),
        )
        for bit in rest_bits:
            (qkv,) = combine("qkv_rest", meta, [qkv, swap(qkv, bit, 0)], [(rows4 + 32, BF, [(0, rows4 + 32, terms(2))])], us=2, deps=(total,))
        four = (qkv,) + tuple(
            swap(after(qkv, v), bit, 0) for v, bit in zip(four[1:], (x_bit, z_bit, x_bit | z_bit))
        )
        grad_w_qkv, grad_w_out, *vectors, grad_b_qv, roots = call(
            projections_out,
            name="qkv_out",
            scalars=1,
            ins=[whole((rows4 + 32, width))] * 4,
            outs=[out((3 * wide, width), F32), out((wide, width), F32)]
            + [((width,), F32, vec)] * 7
            + [out((2, wide), F32), out((8, LANES), F32)],
            us=3,
            deps=(out_tok, grad_w_up),
        )(meta, *four)
        grad_w_qkv = grad_w_qkv.reshape(3, wide, width).transpose(0, 2, 1)


        root_means = roots[0, :3]
        gain1, shift1, b_out_grad, gain2, shift2, b_down_grad, grad_b_up = vectors
        return (
            out_tok,
            out_lat,
            grad_tok,
            grad_lat,
            gain1,
            shift1,
            grad_w_qkv,
            grad_b_qv,
            grad_w_out,
            b_out_grad,
            gain2,
            shift2,
            grad_w_up,
            grad_b_up,
            grad_w_down,
            b_down_grad,
            root_means,
        )

    return per_device


def solution(mesh):
    rows, whole = P("dp", None), P()
    return jax.shard_map(
        make(mesh),
        mesh=mesh,
        in_specs=(
            rows,
            rows,
            whole,
            P("dp"),
            whole,
            whole,
            P(None, None, "mp"),
            P(None, "mp"),
            P("mp", None),
            whole,
            whole,
            whole,
            P(None, "mp"),
            P("mp"),
            P("mp", None),
            whole,
            rows,
            rows,
        ),
        out_specs=(
            rows,
            rows,
            rows,
            rows,
            whole,
            whole,
            P(None, None, "mp"),
            P(None, "mp"),
            P("mp", None),
            whole,
            whole,
            whole,
            P(None, "mp"),
            P("mp"),
            P("mp", None),
            whole,
            whole,
        ),
        check_vma=False,
    )
```
